32 devices in a mesh: shot: 2 (over y), xy: 8 (over z, x), gz: 2 (over core).
Axes of the slice: x: 2, y: 2, z: 4, core: 2. Of those that a mesh axis runs over, the one named last changes fastest.
Arguments:
- wave_p: float32 [256, 8, 640], P(('shot', 'xy'), 'gz'), parts along dimension 0, may hold values from -6 to 6
- wave_q: float32 [256, 8, 640], P(('shot', 'xy'), 'gz'), parts along dimension 0, may hold values from -6 to 6
- prior_p: float32 [256, 8, 640], P(('shot', 'xy'), 'gz'), parts along dimension 0, may hold values from -6 to 6
- prior_q: float32 [256, 8, 640], P(('shot', 'xy'), 'gz'), parts along dimension 0, may hold values from -6 to 6
- courant: bfloat16 [128, 8, 640], P('xy', 'gz'), may hold values from 0.049804688 to 0.19921875
- epsilon: bfloat16 [128, 8, 640], P('xy', 'gz'), may hold values from 0 to 0.3984375
- thomsen_delta: bfloat16 [128, 8, 640], P('xy', 'gz'), may hold values from -0.099609375 to 0.29882812
- tilt_angle: bfloat16 [128, 8, 640], P('xy', 'gz'), may hold values from -3.140625 to 3.140625
- azimuth: bfloat16 [128, 8, 640], P('xy', 'gz'), may hold values from -3.140625 to 3.140625
Outputs:
- next_p: float32 [256, 8, 640], P(('shot', 'xy'), 'gz'), parts along dimension 0
- next_q: float32 [256, 8, 640], P(('shot', 'xy'), 'gz'), parts along dimension 0
- detail_first: float32 [128, 8, 640], P(('shot', 'xy'), 'gz'), parts along dimension 0
- detail_second: float32 [64, 8, 640], P(('shot', 'xy'), 'gz'), parts along dimension 0
- detail_third: float32 [32, 8, 640], P(('shot', 'xy'), 'gz'), parts along dimension 0
- approx_coarse: float32 [32, 8, 640], P(('shot', 'xy'), 'gz'), parts along dimension 0
The draws below stay inside these ranges and needn't reach their ends.
There are 2 independent parts, one for each index of `shot`. The reference program is written for one: setup_inputs(seed, part) draws one part's arguments, and reference() takes and returns one part's arrays. A program takes and returns all parts, laid end to end along the dimension named above; an argument that names none is the same for every part. Nothing has to cross between parts.
All inputs are finite; a program needn't handle non-finite values.
Results may differ from the reference program's by a relative error of at most 0.0003.
Values sent between devices are 32-bit elements; how exact they have to be, the bound alone decides.
No kernel may reach another device: no remote copies, remote signals or barrier semaphores. Data moves between devices by JAX's collectives and lax.ppermute only.
A program may use at most 64 MiB of HBM per device.

```python
import jax
import jax.numpy as jnp
from jax import lax

NY = 640
NX = 128
NZ = 8


def block_scale(rng, dims, pieces, low, high):
    gain, own = 1.0, jax.random.fold_in(rng, 6)
    for axis_at, shards_of in pieces:
        steps = jnp.exp(jax.random.uniform(jax.random.fold_in(own, axis_at), (shards_of,), jnp.float32, low / len(pieces), high / len(pieces)))
        gain = gain * jnp.repeat(steps, dims[axis_at] // shards_of).reshape([-1 if axis == axis_at else 1 for axis in range(len(dims))])
    return gain


def centred(stream_key, extent, deviation, reach, shards=(), held_as=jnp.bfloat16):
    result = deviation * jax.random.normal(stream_key, extent, jnp.float32)
    if shards:
        result = result * block_scale(stream_key, extent, shards, -0.22, 0.18)
    return jnp.clip(result, -reach, reach).astype(held_as)


def setup_inputs(seed: int = 0, part: int = 0) -> dict:
    splits = jax.random.split(jax.random.key(seed), 10)
    part_keys = jax.random.split(jax.random.fold_in(splits[9], part), 10)
    return {
        "wave_p": centred(part_keys[0], (NX, NZ, NY), 1.0, 6.0, ((0, 8), (1, 2)), jnp.float32),
        "wave_q": centred(part_keys[1], (NX, NZ, NY), 1.0, 6.0, ((0, 8), (1, 2)), jnp.float32),
        "prior_p": centred(part_keys[2], (NX, NZ, NY), 1.0, 6.0, ((0, 8), (1, 2)), jnp.float32),
        "prior_q": centred(part_keys[3], (NX, NZ, NY), 1.0, 6.0, ((0, 8), (1, 2)), jnp.float32),
        "courant": jnp.clip(0.049804688 + 0.14941406 * jax.random.uniform(splits[4], (NX, NZ, NY), jnp.float32) ** block_scale(splits[4], (NX, NZ, NY), ((0, 8), (1, 2)), -0.2, 0.2), 0.049804688, 0.19921875).astype(jnp.bfloat16),
        "epsilon": jnp.clip(0.3984375 * jax.random.uniform(splits[5], (NX, NZ, NY), jnp.float32) ** block_scale(splits[5], (NX, NZ, NY), ((0, 8), (1, 2)), -0.2, 0.2), 0.0, 0.3984375).astype(jnp.bfloat16),
        "thomsen_delta": jnp.clip(-0.099609375 + 0.3984375 * jax.random.uniform(splits[6], (NX, NZ, NY), jnp.float32) ** block_scale(splits[6], (NX, NZ, NY), ((0, 8), (1, 2)), -0.2, 0.2), -0.099609375, 0.29882812).astype(jnp.bfloat16),
        "tilt_angle": jnp.clip(jax.random.uniform(splits[7], (NX, NZ, NY), jnp.float32, -3.140625, 3.140625), -3.140625, 3.140625).astype(jnp.bfloat16),
        "azimuth": jnp.clip(jax.random.uniform(splits[8], (NX, NZ, NY), jnp.float32, -3.140625, 3.140625), -3.140625, 3.140625).astype(jnp.bfloat16),
    }


SECOND = (-205.0 / 72.0, 8.0 / 5.0, -1.0 / 5.0, 8.0 / 315.0, -1.0 / 560.0)
FIRST = (4.0 / 5.0, -1.0 / 5.0, 4.0 / 105.0, -1.0 / 280.0)
LIFT = (-1.586134342, -0.05298011854, 0.8829110762, 0.4435068522)
ZETA = 1.149604398

def strip(values, along, offset, length):
    return lax.slice_in_dim(values, offset, offset + length, axis=along)

def first_along(padded, along):
    length = padded.shape[along] - 8
    total = FIRST[0] * (strip(padded, along, 5, length) - strip(padded, along, 3, length))
    for number in range(2, 5):
        total = total + FIRST[number - 1] * (strip(padded, along, 4 + number, length) - strip(padded, along, 4 - number, length))
    return total

def second_along(padded, along):
    length = padded.shape[along] - 8
    total = SECOND[0] * strip(padded, along, 4, length)
    for number in range(1, 5):
        total = total + SECOND[number] * (strip(padded, along, 4 + number, length) + strip(padded, along, 4 - number, length))
    return total

def trim(values, along):
    return strip(values, along, 4, values.shape[along] - 8)

def derivatives(padded):
    dxx = trim(trim(second_along(padded, 0), 1), 2)
    dyy = trim(trim(second_along(padded, 2), 0), 1)
    dzz = trim(trim(second_along(padded, 1), 0), 2)
    dxy = trim(first_along(first_along(padded, 0), 2), 1)
    dzy = trim(first_along(first_along(padded, 1), 2), 0)
    dxz = trim(first_along(first_along(padded, 0), 1), 2)
    return (dxx, dyy, dzz, dxy, dzy, dxz)

def advance(p_padded, q_padded, wave_p, wave_q, prior_p, prior_q, courant, epsilon, thomsen_delta, tilt_angle, azimuth):
    tilt = tilt_angle.astype(jnp.float32)
    turn = azimuth.astype(jnp.float32)
    sine_tilt = jnp.sin(tilt)
    cosine_tilt = jnp.cos(tilt)
    sine_turn = jnp.sin(turn)
    cosine_turn = jnp.cos(turn)
    double_tilt = jnp.sin(2.0 * tilt)
    weights = (sine_tilt * sine_tilt * cosine_turn * cosine_turn, sine_tilt * sine_tilt * sine_turn * sine_turn, cosine_tilt * cosine_tilt, sine_tilt * sine_tilt * jnp.sin(2.0 * turn), double_tilt * sine_turn, double_tilt * cosine_turn)

    def rotated(parts):
        total = weights[0] * parts[0]
        for number in range(1, 6):
            total = total + weights[number] * parts[number]
        return total
    p_parts = derivatives(p_padded)
    h_one_p = rotated(p_parts)
    h_two_p = p_parts[0] + p_parts[1] + p_parts[2] - h_one_p
    h_one_q = rotated(derivatives(q_padded))
    root = jnp.sqrt(1.0 + 2.0 * thomsen_delta.astype(jnp.float32))
    speed = courant.astype(jnp.float32)
    stretch = 1.0 + 2.0 * epsilon.astype(jnp.float32)
    next_p = 2.0 * wave_p - prior_p + speed * (stretch * h_two_p + root * h_one_q)
    next_q = 2.0 * wave_q - prior_q + speed * (root * h_two_p + h_one_q)
    return (next_p, next_q)

def lift_steps(evens, odds, ahead, behind):
    odds = odds + LIFT[0] * (evens + ahead(evens))
    evens = evens + LIFT[1] * (odds + behind(odds))
    odds = odds + LIFT[2] * (evens + ahead(evens))
    evens = evens + LIFT[3] * (odds + behind(odds))
    return (evens * ZETA, odds * (1.0 / ZETA))

def lift_last(values):
    half = values.shape[-1] // 2
    split = values.reshape(values.shape[:-1] + (half, 2))
    return lift_steps(split[..., 0], split[..., 1], lambda field: jnp.roll(field, -1, axis=-1), lambda field: jnp.roll(field, 1, axis=-1))

def lift_first(values):
    half = values.shape[0] // 2
    split = values.reshape((half, 2) + values.shape[1:])
    return lift_steps(split[:, 0], split[:, 1], lambda field: jnp.roll(field, -1, axis=0), lambda field: jnp.roll(field, 1, axis=0))

def transform_last(values):
    details = []
    coarse = values
    for number in range(3):
        coarse, detail = lift_last(coarse)
        details.append(detail)
    return jnp.concatenate(details + [coarse], axis=-1)

def reference(wave_p, wave_q, prior_p, prior_q, courant, epsilon, thomsen_delta, tilt_angle, azimuth):
    next_p, next_q = advance(jnp.pad(wave_p, 4), jnp.pad(wave_q, 4), wave_p, wave_q, prior_p, prior_q, courant, epsilon, thomsen_delta, tilt_angle, azimuth)
    crossline = transform_last(next_p)
    coarse = crossline
    details = []
    for number in range(3):
        coarse, detail = lift_first(coarse)
        details.append(detail)
    return (next_p, next_q, details[0], details[1], details[2], coarse)
```

```python
import functools

import jax
import jax.numpy as jnp
import numpy as np
from jax import lax
from jax.experimental import pallas as pl
from jax.experimental.pallas import tpu as pltpu
from jax.sharding import PartitionSpec as P

SECOND = (-205.0 / 72.0, 8.0 / 5.0, -1.0 / 5.0, 8.0 / 315.0, -1.0 / 560.0)
FIRST = (4.0 / 5.0, -1.0 / 5.0, 4.0 / 105.0, -1.0 / 280.0)
LIFT = (-1.586134342, -0.05298011854, 0.8829110762, 0.4435068522)
ZETA = 1.149604398
LANES = 128


def lift_level(values):
    even, odd = values[0::2], values[1::2]
    odd = odd + LIFT[0] * (even + np.roll(even, -1, 0))
    even = even + LIFT[1] * (odd + np.roll(odd, 1, 0))
    odd = odd + LIFT[2] * (even + np.roll(even, -1, 0))
    even = even + LIFT[3] * (odd + np.roll(odd, 1, 0))
    return even * ZETA, odd * (1.0 / ZETA)


def three_levels(length):
    coarse, members = np.eye(length), []
    for _ in range(3):
        coarse, detail = lift_level(coarse)
        members.append(detail)
    return members + [coarse]


def split_bf16(matrix):
    high = matrix.astype(jnp.bfloat16)
    low = (matrix - high.astype(np.float64)).astype(jnp.bfloat16)
    return high, low


def inline_blocks(rows):
    bricks, brick = 8, 4
    members = three_levels(rows * bricks)
    wanted = np.concatenate(
        [m[brick * len(m) // bricks : (brick + 1) * len(m) // bricks] for m in members]
    )

    def block(offset):
        return wanted[:, rows * (brick + offset) : rows * (brick + offset + 1)]

    factors = {}
    for offset in (-1, 1, -2, 2):
        left, sizes, right = np.linalg.svd(block(offset))
        rank = int((sizes > 1e-12).sum())
        root = np.sqrt(sizes[:rank])
        factors[offset] = (left[:, :rank] * root, root[:, None] * right[:rank])
    return block(0), factors


def sine_cosine(angle):
    turns = jnp.round(angle * (2.0 / np.pi))
    rest = angle - turns * 1.5703125
    rest = rest - turns * 4.837512969970703125e-4
    rest = rest - turns * 7.549789948768648e-8
    square = rest * rest
    sine = rest + rest * square * (
        -1.6666654611e-1 + square * (8.3321608736e-3 + square * -1.9515295891e-4)
    )
    cosine = (
        1.0
        - 0.5 * square
        + square
        * square
        * (4.166664568298827e-2 + square * (-1.388731625493765e-3 + square * 2.443315711809948e-5))
    )
    quarter = turns.astype(jnp.int32)
    swapped = (quarter & 1) == 1
    out_sine = jnp.where(swapped, cosine, sine)
    out_cosine = jnp.where(swapped, sine, cosine)
    out_sine = jnp.where((quarter & 2) == 2, -out_sine, out_sine)
    out_cosine = jnp.where(((quarter + 1) & 2) == 2, -out_cosine, out_cosine)
    return out_sine, out_cosine


def weights_kernel(
    waves, prior_p, prior_q, courant, epsilon, delta, tilt, azimuth, axis_x, axis_y, axis_z, gain_a, gain_b, base
):
    rows = waves.shape[0]
    top = lax.broadcasted_iota(jnp.int32, waves.shape[1:], 0) < 4

    def swap(value):
        return pltpu.roll(value, 4, 0)

    for x in range(rows):
        angles = jnp.concatenate(
            [tilt[x].astype(jnp.float32), azimuth[x].astype(jnp.float32)], axis=0
        )
        sine, cosine = sine_cosine(angles)
        sine_other, cosine_other = swap(sine), swap(cosine)
        sine_tilt = jnp.where(top, sine, sine_other)
        axis_x[x] = sine_tilt * jnp.where(top, cosine_other, cosine)
        axis_y[x] = sine * sine_other
        axis_z[x] = jnp.where(top, cosine, cosine_other)
        speed = courant[x].astype(jnp.float32)
        root = jnp.sqrt(1.0 + 2.0 * delta[x].astype(jnp.float32))
        stretch = 1.0 + 2.0 * epsilon[x].astype(jnp.float32)
        gain_a[x] = jnp.concatenate([speed * stretch, speed], axis=0)
        across = speed * root
        gain_b[x] = jnp.concatenate([across, across], axis=0)
        base[x] = 2.0 * waves[x] - jnp.concatenate([prior_p[x], prior_q[x]], axis=0)


def shifted(value, width):
    wide = jnp.concatenate(
        [value, jnp.zeros((value.shape[0], LANES), jnp.float32)], axis=1
    )
    total = width + LANES
    ahead = [pltpu.roll(wide, total - k, 1)[:, :width] for k in range(1, 5)]
    behind = [pltpu.roll(wide, k, 1)[:, :width] for k in range(1, 5)]
    return ahead, behind


def first_of(ahead, behind):
    total = FIRST[0] * (ahead[0] - behind[0])
    for k in range(1, 4):
        total = total + FIRST[k] * (ahead[k] - behind[k])
    return total


def second_of(centre, ahead, behind):
    total = SECOND[0] * centre
    for k in range(4):
        total = total + SECOND[k + 1] * (ahead[k] + behind[k])
    return total


def dot3(a_high, a_low, b_high, b_low):
    def dot(a, b):
        return jnp.dot(a, b, preferred_element_type=jnp.float32)

    return dot(a_high, b_high) + (dot(a_low, b_high) + dot(a_high, b_low))


def halves(value):
    high = value.astype(jnp.bfloat16)
    return high, (value - high.astype(jnp.float32)).astype(jnp.bfloat16)


def step_kernel(
    gives,
    waves,
    other,
    left,
    right,
    left_cross,
    right_cross,
    axis_x,
    axis_y,
    axis_z,
    gain_a,
    gain_b,
    base,
    across_high,
    across_low,
    inline_high,
    inline_low,
    next_p,
    next_q,
    mine,
    *rest,
):
    sends, (ext, dz_ext, dzz_ext, pressure) = rest[:-4], rest[-4:]
    rows, _, width = waves.shape
    lower = lax.axis_index("gz") == 0
    sub = lax.broadcasted_iota(jnp.int32, waves.shape[1:], 0)
    layer = sub & 3
    top = sub < 4
    above = jnp.where(lower, 1.0, 0.0)
    below = jnp.where(lower, 0.0, 1.0)

    for x in range(rows + 8):
        if x < 4:
            own, far = left[x], left_cross[x]
        elif x < rows + 4:
            own, far = waves[x - 4], other[x - 4]
        else:
            own, far = right[x - rows - 4], right_cross[x - rows - 4]
        ext[x] = own
        up, down = far * above, far * below
        ahead, behind = [], []
        for k in range(1, 4):
            ahead.append(jnp.where(layer < 4 - k, pltpu.roll(own, 8 - k, 0), pltpu.roll(up, 4 - k, 0)))
            behind.append(jnp.where(layer >= k, pltpu.roll(own, k, 0), pltpu.roll(down, 4 + k, 0)))
        ahead.append(up)
        behind.append(down)
        dz_ext[x] = first_of(ahead, behind)
        if 4 <= x < rows + 4:
            dzz_ext[x - 4] = second_of(own, ahead, behind)

    def row(x, carry):
        centre = ext[x + 4]
        ahead = [ext[x + 4 + k] for k in range(1, 5)]
        behind = [ext[x + 4 - k] for k in range(1, 5)]
        dxx = second_of(centre, ahead, behind)
        dx = first_of(ahead, behind)
        dxz = first_of(
            [dz_ext[x + 4 + k] for k in range(1, 5)], [dz_ext[x + 4 - k] for k in range(1, 5)]
        )
        dyy = second_of(centre, *shifted(centre, width))
        dxy = first_of(*shifted(dx, width))
        dzy = first_of(*shifted(dz_ext[x + 4], width))
        dzz = dzz_ext[x]
        n_x, n_y, n_z = axis_x[x], axis_y[x], axis_z[x]
        h_one = (n_x * n_x) * dxx
        h_one = h_one + (n_y * n_y) * dyy
        h_one = h_one + (n_z * n_z) * dzz
        h_one = h_one + 2.0 * (n_x * n_y * dxy + n_z * (n_y * dzy + n_x * dxz))
        h_two = dxx + dyy + dzz - h_one
        mixed = jnp.where(top, h_two, h_one)
        result = base[x] + gain_a[x] * mixed + gain_b[x] * pltpu.roll(mixed, 4, 0)
        next_p[x] = result[:4]
        next_q[x] = result[4:]
        pressure[x] = result
        return carry

    lax.fori_loop(0, rows, row, 0)

    packed = jnp.concatenate(
        [
            jnp.where(top, pressure[x], pltpu.roll(pressure[x + 1], 4, 0))
            for x in range(0, rows, 2)
        ],
        axis=0,
    )
    crossline = dot3(*halves(packed), across_high[...], across_low[...])
    parts = dot3(inline_high[...], inline_low[...], *halves(crossline))
    mine[...] = parts[: 4 * rows]
    for (start, size), send in zip(gives, sends):
        send[...] = parts[start : start + size]


def finish_kernel(takes, mine, *rest):
    received, outs = rest[:4], rest[4:]
    at = 0
    for out in outs:
        for row in range(out.shape[0]):
            total = mine[4 * at : 4 * at + 4]
            for take, got in zip(takes, received):
                for j in range(take.shape[1]):
                    factor = float(take[at, j])
                    if abs(factor) > 1e-13:
                        total = total + factor * got[4 * j : 4 * j + 4]
            out[row] = total
            at += 1


def body(size, wave_p, wave_q, prior_p, prior_q, courant, epsilon, thomsen_delta, tilt_angle, azimuth):
    rows, layers, width = wave_p.shape
    f32 = jnp.float32
    waves = jnp.concatenate([wave_p, wave_q], axis=1)
    up = [(i, i + 1) for i in range(size - 1)]
    down = [(i + 1, i) for i in range(size - 1)]

    def crossed(pairs):
        return [(2 * i + g, 2 * j + 1 - g) for i, j in pairs for g in range(2)]

    last, leading = waves[rows - 4 :], waves[:4]
    other = lax.ppermute(waves, "gz", [(0, 1), (1, 0)])
    left = lax.ppermute(last, "xy", up)
    right = lax.ppermute(leading, "xy", down)
    left_cross = lax.ppermute(last, ("xy", "gz"), crossed(up))
    right_cross = lax.ppermute(leading, ("xy", "gz"), crossed(down))

    stack = jax.ShapeDtypeStruct((rows, 8, width), f32)
    cells = rows * layers * width
    weights = pl.pallas_call(
        weights_kernel,
        out_shape=[stack] * 6,
        cost_estimate=pl.CostEstimate(flops=100 * cells, bytes_accessed=60 * cells, transcendentals=0),
        name="weights",
    )(waves, prior_p, prior_q, courant, epsilon, thomsen_delta, tilt_angle, azimuth)

    own, factors = inline_blocks(rows)
    offsets = (-1, 1, -2, 2)
    pieces, gives, start = [own], [], rows * 4
    for offset in offsets:
        give = factors[offset][1]
        pad = give.shape[0] % 2
        pieces.append(np.pad(give, ((0, pad), (0, 0))))
        gives.append((start, 4 * (give.shape[0] + pad)))
        start += gives[-1][1]
    inline = np.kron(np.concatenate(pieces), np.eye(4))
    across = np.concatenate(three_levels(width)).T
    vmem = 48 * 1024 * 1024
    results = pl.pallas_call(
        functools.partial(step_kernel, gives),
        out_shape=[
            jax.ShapeDtypeStruct(wave_p.shape, f32),
            jax.ShapeDtypeStruct(wave_p.shape, f32),
            jax.ShapeDtypeStruct((4 * rows, width), f32),
        ]
        + [jax.ShapeDtypeStruct((count, width), f32) for _, count in gives],
        scratch_shapes=[
            pltpu.VMEM((rows + 8, 8, width), f32),
            pltpu.VMEM((rows + 8, 8, width), f32),
            pltpu.VMEM((rows, 8, width), f32),
            pltpu.VMEM((rows, 8, width), f32),
        ],
        compiler_params=pltpu.CompilerParams(vmem_limit_bytes=vmem),
        cost_estimate=pl.CostEstimate(flops=400 * cells, bytes_accessed=100 * cells, transcendentals=0),
        name="step",
    )(
        waves,
        other,
        left,
        right,
        left_cross,
        right_cross,
        *weights,
        *[jnp.asarray(m) for m in split_bf16(across)],
        *[jnp.asarray(m) for m in split_bf16(inline)],
    )
    next_p, next_q, mine = results[:3]
    received = [
        lax.ppermute(send, "xy", [(i, (i - offset) % size) for i in range(size)])
        for offset, send in zip(offsets, results[3:])
    ]
    outs = pl.pallas_call(
        functools.partial(finish_kernel, [factors[offset][0] for offset in offsets]),
        out_shape=[
            jax.ShapeDtypeStruct((count, layers, width), f32)
            for count in (rows // 2, rows // 4, rows // 8, rows // 8)
        ],
        name="finish",
    )(mine, *received)
    return (next_p, next_q, *outs)


def solution(mesh):
    split = P(("shot", "xy"), "gz", None)
    shared = P("xy", "gz", None)
    return jax.shard_map(
        functools.partial(body, mesh.shape["xy"]),
        mesh=mesh,
        in_specs=(split,) * 4 + (shared,) * 5,
        out_specs=(split,) * 6,
        check_vma=False,
    )
```

```python
import functools

import jax
import jax.numpy as jnp
import numpy as np
from jax import lax
from jax.experimental import pallas as pl
from jax.experimental.pallas import tpu as pltpu
from jax.sharding import PartitionSpec as P

SECOND = (-205.0 / 72.0, 8.0 / 5.0, -1.0 / 5.0, 8.0 / 315.0, -1.0 / 560.0)
FIRST = (4.0 / 5.0, -1.0 / 5.0, 4.0 / 105.0, -1.0 / 280.0)
LIFT = (-1.586134342, -0.05298011854, 0.8829110762, 0.4435068522)
ZETA = 1.149604398
LANES = 128


def lift_level(values):
    even, odd = values[0::2], values[1::2]
    odd = odd + LIFT[0] * (even + np.roll(even, -1, 0))
    even = even + LIFT[1] * (odd + np.roll(odd, 1, 0))
    odd = odd + LIFT[2] * (even + np.roll(even, -1, 0))
    even = even + LIFT[3] * (odd + np.roll(odd, 1, 0))
    return even * ZETA, odd * (1.0 / ZETA)


def three_levels(length):
    coarse, members = np.eye(length), []
    for _ in range(3):
        coarse, detail = lift_level(coarse)
        members.append(detail)
    return members + [coarse]


def split_bf16(matrix):
    high = matrix.astype(jnp.bfloat16)
    low = (matrix - high.astype(np.float64)).astype(jnp.bfloat16)
    return high, low


def inline_blocks(rows):
    bricks, brick = 8, 4
    members = three_levels(rows * bricks)
    wanted = np.concatenate(
        [m[brick * len(m) // bricks : (brick + 1) * len(m) // bricks] for m in members]
    )

    def block(offset):
        return wanted[:, rows * (brick + offset) : rows * (brick + offset + 1)]

    factors = {}
    for offset in (-1, 1, -2, 2):
        left, sizes, right = np.linalg.svd(block(offset))
        rank = int((sizes > 1e-12).sum())
        root = np.sqrt(sizes[:rank])
        factors[offset] = (left[:, :rank] * root, root[:, None] * right[:rank])
    return block(0), factors


def sine_cosine(angle):
    turns = jnp.round(angle * (2.0 / np.pi))
    rest = angle - turns * 1.5703125
    rest = rest - turns * 4.837512969970703125e-4
    rest = rest - turns * 7.549789948768648e-8
    square = rest * rest
    sine = rest + rest * square * (
        -1.6666654611e-1 + square * (8.3321608736e-3 + square * -1.9515295891e-4)
    )
    cosine = (
        1.0
        - 0.5 * square
        + square
        * square
        * (4.166664568298827e-2 + square * (-1.388731625493765e-3 + square * 2.443315711809948e-5))
    )
    quarter = turns.astype(jnp.int32)
    swapped = (quarter & 1) == 1
    out_sine = jnp.where(swapped, cosine, sine)
    out_cosine = jnp.where(swapped, sine, cosine)
    out_sine = jnp.where((quarter & 2) == 2, -out_sine, out_sine)
    out_cosine = jnp.where(((quarter + 1) & 2) == 2, -out_cosine, out_cosine)
    return out_sine, out_cosine


def weights_kernel(
    waves, prior_p, prior_q, courant, epsilon, delta, tilt, azimuth, axis_x, axis_y, axis_z, gain_a, gain_b, base
):
    rows = waves.shape[0]
    top = lax.broadcasted_iota(jnp.int32, waves.shape[1:], 0) < 4

    def swap(value):
        return pltpu.roll(value, 4, 0)

    for x in range(rows):
        angles = jnp.concatenate(
            [tilt[x].astype(jnp.float32), azimuth[x].astype(jnp.float32)], axis=0
        )
        sine, cosine = sine_cosine(angles)
        sine_other, cosine_other = swap(sine), swap(cosine)
        sine_tilt = jnp.where(top, sine, sine_other)
        axis_x[x] = sine_tilt * jnp.where(top, cosine_other, cosine)
        axis_y[x] = sine * sine_other
        axis_z[x] = jnp.where(top, cosine, cosine_other)
        speed = courant[x].astype(jnp.float32)
        root = jnp.sqrt(1.0 + 2.0 * delta[x].astype(jnp.float32))
        stretch = 1.0 + 2.0 * epsilon[x].astype(jnp.float32)
        gain_a[x] = jnp.concatenate([speed * stretch, speed], axis=0)
        across = speed * root
        gain_b[x] = jnp.concatenate([across, across], axis=0)
        base[x] = 2.0 * waves[x] - jnp.concatenate([prior_p[x], prior_q[x]], axis=0)


def shifted(value, width):
    wide = jnp.concatenate(
        [value, jnp.zeros((value.shape[0], LANES), jnp.float32)], axis=1
    )
    total = width + LANES
    ahead = [pltpu.roll(wide, total - k, 1)[:, :width] for k in range(1, 5)]
    behind = [pltpu.roll(wide, k, 1)[:, :width] for k in range(1, 5)]
    return ahead, behind


def first_of(ahead, behind):
    total = FIRST[0] * (ahead[0] - behind[0])
    for k in range(1, 4):
        total = total + FIRST[k] * (ahead[k] - behind[k])
    return total


def second_of(centre, ahead, behind):
    total = SECOND[0] * centre
    for k in range(4):
        total = total + SECOND[k + 1] * (ahead[k] + behind[k])
    return total


def dot3(a_high, a_low, b_high, b_low):
    def dot(a, b):
        return jnp.dot(a, b, preferred_element_type=jnp.float32)

    return dot(a_high, b_high) + (dot(a_low, b_high) + dot(a_high, b_low))


def halves(value):
    high = value.astype(jnp.bfloat16)
    return high, (value - high.astype(jnp.float32)).astype(jnp.bfloat16)


def step_kernel(
    gives,
    waves,
    other,
    edges,
    edges_other,
    axis_x,
    axis_y,
    axis_z,
    gain_a,
    gain_b,
    base,
    across_high,
    across_low,
    inline_high,
    inline_low,
    next_p,
    next_q,
    mine,
    *rest,
):
    sends, (ext, dz_ext, dzz_ext, pressure) = rest[:-4], rest[-4:]
    rows, _, width = waves.shape
    lower = lax.axis_index("gz") == 0
    sub = lax.broadcasted_iota(jnp.int32, waves.shape[1:], 0)
    layer = sub & 3
    top = sub < 4
    above = jnp.where(lower, 1.0, 0.0)
    below = jnp.where(lower, 0.0, 1.0)

    for x in range(rows + 8):
        if x < 4:
            own, far = edges[x], edges_other[x]
        elif x < rows + 4:
            own, far = waves[x - 4], other[x - 4]
        else:
            own, far = edges[x - rows], edges_other[x - rows]
        ext[x] = own
        up, down = far * above, far * below
        ahead, behind = [], []
        for k in range(1, 4):
            ahead.append(jnp.where(layer < 4 - k, pltpu.roll(own, 8 - k, 0), pltpu.roll(up, 4 - k, 0)))
            behind.append(jnp.where(layer >= k, pltpu.roll(own, k, 0), pltpu.roll(down, 4 + k, 0)))
        ahead.append(up)
        behind.append(down)
        dz_ext[x] = first_of(ahead, behind)
        if 4 <= x < rows + 4:
            dzz_ext[x - 4] = second_of(own, ahead, behind)

    def row(x, carry):
        centre = ext[x + 4]
        ahead = [ext[x + 4 + k] for k in range(1, 5)]
        behind = [ext[x + 4 - k] for k in range(1, 5)]
        dxx = second_of(centre, ahead, behind)
        dx = first_of(ahead, behind)
        dxz = first_of(
            [dz_ext[x + 4 + k] for k in range(1, 5)], [dz_ext[x + 4 - k] for k in range(1, 5)]
        )
        dyy = second_of(centre, *shifted(centre, width))
        dxy = first_of(*shifted(dx, width))
        dzy = first_of(*shifted(dz_ext[x + 4], width))
        dzz = dzz_ext[x]
        n_x, n_y, n_z = axis_x[x], axis_y[x], axis_z[x]
        h_one = (n_x * n_x) * dxx
        h_one = h_one + (n_y * n_y) * dyy
        h_one = h_one + (n_z * n_z) * dzz
        h_one = h_one + 2.0 * (n_x * n_y * dxy + n_z * (n_y * dzy + n_x * dxz))
        h_two = dxx + dyy + dzz - h_one
        mixed = jnp.where(top, h_two, h_one)
        result = base[x] + gain_a[x] * mixed + gain_b[x] * pltpu.roll(mixed, 4, 0)
        next_p[x] = result[:4]
        next_q[x] = result[4:]
        pressure[x] = result
        return carry

    lax.fori_loop(0, rows, row, 0)

    packed = jnp.concatenate(
        [
            jnp.where(top, pressure[x], pltpu.roll(pressure[x + 1], 4, 0))
            for x in range(0, rows, 2)
        ],
        axis=0,
    )
    crossline = dot3(*halves(packed), across_high[...], across_low[...])
    parts = dot3(inline_high[...], inline_low[...], *halves(crossline))
    mine[...] = parts[: 4 * rows]
    for (start, size), send in zip(gives, sends):
        send[...] = parts[start : start + size]


def finish_kernel(takes, mine, *rest):
    received, outs = rest[:4], rest[4:]
    at = 0
    for out in outs:
        for row in range(out.shape[0]):
            total = mine[4 * at : 4 * at + 4]
            for take, got in zip(takes, received):
                for j in range(take.shape[1]):
                    factor = float(take[at, j])
                    if abs(factor) > 1e-13:
                        total = total + factor * got[4 * j : 4 * j + 4]
            out[row] = total
            at += 1


def body(size, wave_p, wave_q, prior_p, prior_q, courant, epsilon, thomsen_delta, tilt_angle, azimuth):
    rows, layers, width = wave_p.shape
    f32 = jnp.float32
    waves = jnp.concatenate([wave_p, wave_q], axis=1)
    up = [(i, i + 1) for i in range(size - 1)]
    down = [(i + 1, i) for i in range(size - 1)]

    last, leading = waves[rows - 4 :], waves[:4]
    other = lax.ppermute(waves, "gz", [(0, 1), (1, 0)])
    left = lax.ppermute(last, "xy", up)
    right = lax.ppermute(leading, "xy", down)
    edges = jnp.concatenate([left, right], axis=0)
    edges_other = lax.ppermute(edges, "gz", [(0, 1), (1, 0)])

    stack = jax.ShapeDtypeStruct((rows, 8, width), f32)
    cells = rows * layers * width
    params = pltpu.CompilerParams(vmem_limit_bytes=16 * 1024 * 1024)
    weights = pl.pallas_call(
        weights_kernel,
        out_shape=[stack] * 6,
        cost_estimate=pl.CostEstimate(flops=100 * cells, bytes_accessed=60 * cells, transcendentals=0),
        compiler_params=params,
        name="weights",
    )(waves, prior_p, prior_q, courant, epsilon, thomsen_delta, tilt_angle, azimuth)

    own, factors = inline_blocks(rows)
    offsets = (-1, 1, -2, 2)
    pieces, gives, start = [own], [], rows * 4
    for offset in offsets:
        give = factors[offset][1]
        pad = give.shape[0] % 2
        pieces.append(np.pad(give, ((0, pad), (0, 0))))
        gives.append((start, 4 * (give.shape[0] + pad)))
        start += gives[-1][1]
    inline = np.kron(np.concatenate(pieces), np.eye(4))
    across = np.concatenate(three_levels(width)).T
    results = pl.pallas_call(
        functools.partial(step_kernel, gives),
        out_shape=[
            jax.ShapeDtypeStruct(wave_p.shape, f32),
            jax.ShapeDtypeStruct(wave_p.shape, f32),
            jax.ShapeDtypeStruct((4 * rows, width), f32),
        ]
        + [jax.ShapeDtypeStruct((count, width), f32) for _, count in gives],
        scratch_shapes=[
            pltpu.VMEM((rows + 8, 8, width), f32),
            pltpu.VMEM((rows + 8, 8, width), f32),
            pltpu.VMEM((rows, 8, width), f32),
            pltpu.VMEM((rows, 8, width), f32),
        ],
        compiler_params=params,
        cost_estimate=pl.CostEstimate(flops=400 * cells, bytes_accessed=100 * cells, transcendentals=0),
        name="step",
    )(
        waves,
        other,
        edges,
        edges_other,
        *weights,
        *[jnp.asarray(m) for m in split_bf16(across)],
        *[jnp.asarray(m) for m in split_bf16(inline)],
    )
    next_p, next_q, mine = results[:3]
    received = [
        lax.ppermute(send, "xy", [(i, (i - offset) % size) for i in range(size)])
        for offset, send in zip(offsets, results[3:])
    ]
    outs = pl.pallas_call(
        functools.partial(finish_kernel, [factors[offset][0] for offset in offsets]),
        out_shape=[
            jax.ShapeDtypeStruct((count, layers, width), f32)
            for count in (rows // 2, rows // 4, rows // 8, rows // 8)
        ],
        compiler_params=params,
        name="finish",
    )(mine, *received)
    return (next_p, next_q, *outs)


def solution(mesh):
    split = P(("shot", "xy"), "gz", None)
    shared = P("xy", "gz", None)
    return jax.shard_map(
        functools.partial(body, mesh.shape["xy"]),
        mesh=mesh,
        in_specs=(split,) * 4 + (shared,) * 5,
        out_specs=(split,) * 6,
        check_vma=False,
    )
```

```python
import functools

import jax
import jax.numpy as jnp
import numpy as np
from jax import lax
from jax.experimental import pallas as pl
from jax.experimental.pallas import tpu as pltpu
from jax.sharding import PartitionSpec as P

SECOND = (-205.0 / 72.0, 8.0 / 5.0, -1.0 / 5.0, 8.0 / 315.0, -1.0 / 560.0)
FIRST = (4.0 / 5.0, -1.0 / 5.0, 4.0 / 105.0, -1.0 / 280.0)
LIFT = (-1.586134342, -0.05298011854, 0.8829110762, 0.4435068522)
ZETA = 1.149604398
LANES = 128


def lift_level(values):
    even, odd = values[0::2], values[1::2]
    odd = odd + LIFT[0] * (even + np.roll(even, -1, 0))
    even = even + LIFT[1] * (odd + np.roll(odd, 1, 0))
    odd = odd + LIFT[2] * (even + np.roll(even, -1, 0))
    even = even + LIFT[3] * (odd + np.roll(odd, 1, 0))
    return even * ZETA, odd * (1.0 / ZETA)


def three_levels(length):
    coarse, members = np.eye(length), []
    for _ in range(3):
        coarse, detail = lift_level(coarse)
        members.append(detail)
    return members + [coarse]


def split_bf16(matrix):
    high = matrix.astype(jnp.bfloat16)
    low = (matrix - high.astype(np.float64)).astype(jnp.bfloat16)
    return high, low


def inline_blocks(rows):
    bricks, brick = 8, 4
    members = three_levels(rows * bricks)
    wanted = np.concatenate(
        [m[brick * len(m) // bricks : (brick + 1) * len(m) // bricks] for m in members]
    )

    def block(offset):
        return wanted[:, rows * (brick + offset) : rows * (brick + offset + 1)]

    factors = {}
    for offset in (-1, 1, -2, 2):
        left, sizes, right = np.linalg.svd(block(offset))
        rank = int((sizes > 1e-12).sum())
        root = np.sqrt(sizes[:rank])
        factors[offset] = (left[:, :rank] * root, root[:, None] * right[:rank])
    return block(0), factors


def sine_cosine(angle):
    turns = jnp.round(angle * (2.0 / np.pi))
    rest = angle - turns * 1.5703125
    rest = rest - turns * 4.837512969970703125e-4
    rest = rest - turns * 7.549789948768648e-8
    square = rest * rest
    sine = rest + rest * square * (
        -1.6666654611e-1 + square * (8.3321608736e-3 + square * -1.9515295891e-4)
    )
    cosine = (
        1.0
        - 0.5 * square
        + square
        * square
        * (4.166664568298827e-2 + square * (-1.388731625493765e-3 + square * 2.443315711809948e-5))
    )
    quarter = turns.astype(jnp.int32)
    swapped = (quarter & 1) == 1
    out_sine = jnp.where(swapped, cosine, sine)
    out_cosine = jnp.where(swapped, sine, cosine)
    out_sine = jnp.where((quarter & 2) == 2, -out_sine, out_sine)
    out_cosine = jnp.where(((quarter + 1) & 2) == 2, -out_cosine, out_cosine)
    return out_sine, out_cosine


def weights_kernel(
    waves, prior_p, prior_q, courant, epsilon, delta, tilt, azimuth, axis_x, axis_y, axis_z, gain_a, gain_b, base
):
    rows = waves.shape[0]
    top = lax.broadcasted_iota(jnp.int32, waves.shape[1:], 0) < 4

    def swap(value):
        return pltpu.roll(value, 4, 0)

    for x in range(rows):
        angles = jnp.concatenate(
            [tilt[x].astype(jnp.float32), azimuth[x].astype(jnp.float32)], axis=0
        )
        sine, cosine = sine_cosine(angles)
        sine_other, cosine_other = swap(sine), swap(cosine)
        sine_tilt = jnp.where(top, sine, sine_other)
        axis_x[x] = sine_tilt * jnp.where(top, cosine_other, cosine)
        axis_y[x] = sine * sine_other
        axis_z[x] = jnp.where(top, cosine, cosine_other)
        speed = courant[x].astype(jnp.float32)
        root = jnp.sqrt(1.0 + 2.0 * delta[x].astype(jnp.float32))
        stretch = 1.0 + 2.0 * epsilon[x].astype(jnp.float32)
        gain_a[x] = jnp.concatenate([speed * stretch, speed], axis=0)
        across = speed * root
        gain_b[x] = jnp.concatenate([across, across], axis=0)
        base[x] = 2.0 * waves[x] - jnp.concatenate([prior_p[x], prior_q[x]], axis=0)


def shifted(value, width):
    wide = jnp.concatenate(
        [value, jnp.zeros((value.shape[0], LANES), jnp.float32)], axis=1
    )
    total = width + LANES
    ahead = [pltpu.roll(wide, total - k, 1)[:, :width] for k in range(1, 5)]
    behind = [pltpu.roll(wide, k, 1)[:, :width] for k in range(1, 5)]
    return ahead, behind


def first_of(ahead, behind):
    total = FIRST[0] * (ahead[0] - behind[0])
    for k in range(1, 4):
        total = total + FIRST[k] * (ahead[k] - behind[k])
    return total


def second_of(centre, ahead, behind):
    total = SECOND[0] * centre
    for k in range(4):
        total = total + SECOND[k + 1] * (ahead[k] + behind[k])
    return total


def dot3(a_high, a_low, b_high, b_low):
    def dot(a, b):
        return jnp.dot(a, b, preferred_element_type=jnp.float32)

    return dot(a_high, b_high) + (dot(a_low, b_high) + dot(a_high, b_low))


def halves(value):
    high = value.astype(jnp.bfloat16)
    return high, (value - high.astype(jnp.float32)).astype(jnp.bfloat16)


def step_kernel(
    size,
    gives,
    waves,
    other,
    edges,
    edges_other,
    axis_x,
    axis_y,
    axis_z,
    gain_a,
    gain_b,
    base,
    across_high,
    across_low,
    inline_high,
    inline_low,
    next_p,
    next_q,
    mine,
    *rest,
):
    sends, (ext, dz_ext, dzz_ext, pressure) = rest[:-4], rest[-4:]
    rows, _, width = waves.shape
    lower = lax.axis_index("gz") == 0
    place = lax.axis_index("xy")
    even, early = place % 2 == 0, place % 4 < 2
    left_at, right_at = jnp.where(even, 4, 0), jnp.where(even, 0, 4)
    left_in = jnp.where(place > 0, 1.0, 0.0)
    right_in = jnp.where(place < size - 1, 1.0, 0.0)
    sub = lax.broadcasted_iota(jnp.int32, waves.shape[1:], 0)
    layer = sub & 3
    top = sub < 4
    above = jnp.where(lower, 1.0, 0.0)
    below = jnp.where(lower, 0.0, 1.0)

    for x in range(rows + 8):
        if x < 4:
            own, far = edges[left_at + x] * left_in, edges_other[left_at + x] * left_in
        elif x < rows + 4:
            own, far = waves[x - 4], other[x - 4]
        else:
            at = right_at + x - rows - 4
            own, far = edges[at] * right_in, edges_other[at] * right_in
        ext[x] = own
        up, down = far * above, far * below
        ahead, behind = [], []
        for k in range(1, 4):
            ahead.append(jnp.where(layer < 4 - k, pltpu.roll(own, 8 - k, 0), pltpu.roll(up, 4 - k, 0)))
            behind.append(jnp.where(layer >= k, pltpu.roll(own, k, 0), pltpu.roll(down, 4 + k, 0)))
        ahead.append(up)
        behind.append(down)
        dz_ext[x] = first_of(ahead, behind)
        if 4 <= x < rows + 4:
            dzz_ext[x - 4] = second_of(own, ahead, behind)

    def row(x, carry):
        centre = ext[x + 4]
        ahead = [ext[x + 4 + k] for k in range(1, 5)]
        behind = [ext[x + 4 - k] for k in range(1, 5)]
        dxx = second_of(centre, ahead, behind)
        dx = first_of(ahead, behind)
        dxz = first_of(
            [dz_ext[x + 4 + k] for k in range(1, 5)], [dz_ext[x + 4 - k] for k in range(1, 5)]
        )
        dyy = second_of(centre, *shifted(centre, width))
        dxy = first_of(*shifted(dx, width))
        dzy = first_of(*shifted(dz_ext[x + 4], width))
        dzz = dzz_ext[x]
        n_x, n_y, n_z = axis_x[x], axis_y[x], axis_z[x]
        h_one = (n_x * n_x) * dxx
        h_one = h_one + (n_y * n_y) * dyy
        h_one = h_one + (n_z * n_z) * dzz
        h_one = h_one + 2.0 * (n_x * n_y * dxy + n_z * (n_y * dzy + n_x * dxz))
        h_two = dxx + dyy + dzz - h_one
        mixed = jnp.where(top, h_two, h_one)
        result = base[x] + gain_a[x] * mixed + gain_b[x] * pltpu.roll(mixed, 4, 0)
        next_p[x] = result[:4]
        next_q[x] = result[4:]
        pressure[x] = result
        return carry

    lax.fori_loop(0, rows, row, 0)

    packed = jnp.concatenate(
        [
            jnp.where(top, pressure[x], pltpu.roll(pressure[x + 1], 4, 0))
            for x in range(0, rows, 2)
        ],
        axis=0,
    )
    crossline = dot3(*halves(packed), across_high[...], across_low[...])
    parts = dot3(inline_high[...], inline_low[...], *halves(crossline))
    mine[...] = parts[: 4 * rows]
    to_next, to_previous, to_second_next, to_second_previous = (
        parts[start : start + count] for start, count in gives
    )
    sends[0][...] = jnp.where(even, to_previous, to_next)
    sends[1][...] = jnp.where(even, to_next, to_previous)
    sends[2][...] = jnp.where(early, to_second_previous, to_second_next)
    sends[3][...] = jnp.where(early, to_second_next, to_second_previous)


def finish_kernel(takes, mine, *rest):
    outer, inner, outer_second, inner_second = (ref[...] for ref in rest[:4])
    outs = rest[4:]
    place = lax.axis_index("xy")
    even, early = place % 2 == 0, place % 4 < 2
    received = (
        jnp.where(even, outer, inner),
        jnp.where(even, inner, outer),
        jnp.where(early, outer_second, inner_second),
        jnp.where(early, inner_second, outer_second),
    )
    at = 0
    for out in outs:
        for row in range(out.shape[0]):
            total = mine[4 * at : 4 * at + 4]
            for take, got in zip(takes, received):
                for j in range(take.shape[1]):
                    factor = float(take[at, j])
                    if abs(factor) > 1e-13:
                        total = total + factor * got[4 * j : 4 * j + 4]
            out[row] = total
            at += 1


def pair_swaps(size):
    one = [1 if i % 2 == 0 else -1 for i in range(size)]
    two = [2 if i % 4 < 2 else -2 for i in range(size)]
    return [
        [(i, (i - one[i]) % size) for i in range(size)],
        [(i, i + one[i]) for i in range(size)],
        [(i, (i - two[i]) % size) for i in range(size)],
        [(i, i + two[i]) for i in range(size)],
    ]


def body(size, wave_p, wave_q, prior_p, prior_q, courant, epsilon, thomsen_delta, tilt_angle, azimuth):
    rows, layers, width = wave_p.shape
    f32 = jnp.float32
    waves = jnp.concatenate([wave_p, wave_q], axis=1)
    even = lax.axis_index("xy") % 2 == 0
    pairs = pair_swaps(size)

    def stacked(start):
        stop = start + 4
        return jnp.concatenate([wave_p[start:stop], wave_q[start:stop]], axis=1)

    last, leading = stacked(rows - 4), stacked(0)
    open_outer = [(i, i) if abs(i - j) > 1 else (i, j) for i, j in pairs[0]]
    outer = lax.ppermute(jnp.where(even, leading, last), "xy", open_outer)
    inner = lax.ppermute(jnp.where(even, last, leading), "xy", pairs[1])
    edges = jnp.concatenate([inner, outer], axis=0)
    other = lax.ppermute(waves, "gz", [(0, 1), (1, 0)])
    edges_other = lax.ppermute(edges, "gz", [(0, 1), (1, 0)])

    stack = jax.ShapeDtypeStruct((rows, 8, width), f32)
    cells = rows * layers * width
    params = pltpu.CompilerParams(vmem_limit_bytes=16 * 1024 * 1024)
    weights = pl.pallas_call(
        weights_kernel,
        out_shape=[stack] * 6,
        cost_estimate=pl.CostEstimate(flops=100 * cells, bytes_accessed=60 * cells, transcendentals=0),
        compiler_params=params,
        name="weights",
    )(waves, prior_p, prior_q, courant, epsilon, thomsen_delta, tilt_angle, azimuth)

    own, factors = inline_blocks(rows)
    offsets = (-1, 1, -2, 2)
    pieces, gives, start = [own], [], rows * 4
    for offset in offsets:
        give = factors[offset][1]
        pad = give.shape[0] % 2
        pieces.append(np.pad(give, ((0, pad), (0, 0))))
        gives.append((start, 4 * (give.shape[0] + pad)))
        start += gives[-1][1]
    inline = np.kron(np.concatenate(pieces), np.eye(4))
    across = np.concatenate(three_levels(width)).T
    results = pl.pallas_call(
        functools.partial(step_kernel, size, gives),
        out_shape=[
            jax.ShapeDtypeStruct(wave_p.shape, f32),
            jax.ShapeDtypeStruct(wave_p.shape, f32),
            jax.ShapeDtypeStruct((4 * rows, width), f32),
        ]
        + [jax.ShapeDtypeStruct((count, width), f32) for _, count in gives],
        scratch_shapes=[
            pltpu.VMEM((rows + 8, 8, width), f32),
            pltpu.VMEM((rows + 8, 8, width), f32),
            pltpu.VMEM((rows, 8, width), f32),
            pltpu.VMEM((rows, 8, width), f32),
        ],
        compiler_params=params,
        cost_estimate=pl.CostEstimate(flops=400 * cells, bytes_accessed=100 * cells, transcendentals=0),
        name="step",
    )(
        waves,
        other,
        edges,
        edges_other,
        *weights,
        *[jnp.asarray(m) for m in split_bf16(across)],
        *[jnp.asarray(m) for m in split_bf16(inline)],
    )
    next_p, next_q, mine = results[:3]
    received = [lax.ppermute(send, "xy", pair) for send, pair in zip(results[3:], pairs)]
    outs = pl.pallas_call(
        functools.partial(finish_kernel, [factors[offset][0] for offset in offsets]),
        out_shape=[
            jax.ShapeDtypeStruct((count, layers, width), f32)
            for count in (rows // 2, rows // 4, rows // 8, rows // 8)
        ],
        compiler_params=params,
        name="finish",
    )(mine, *received)
    return (next_p, next_q, *outs)


def solution(mesh):
    split = P(("shot", "xy"), "gz", None)
    shared = P("xy", "gz", None)
    return jax.shard_map(
        functools.partial(body, mesh.shape["xy"]),
        mesh=mesh,
        in_specs=(split,) * 4 + (shared,) * 5,
        out_specs=(split,) * 6,
        check_vma=False,
    )
```

```python
import functools

import jax
import jax.numpy as jnp
import numpy as np
from jax import lax
from jax.experimental import pallas as pl
from jax.experimental.pallas import tpu as pltpu
from jax.sharding import PartitionSpec as P

SECOND = (-205.0 / 72.0, 8.0 / 5.0, -1.0 / 5.0, 8.0 / 315.0, -1.0 / 560.0)
FIRST = (4.0 / 5.0, -1.0 / 5.0, 4.0 / 105.0, -1.0 / 280.0)
LIFT = (-1.586134342, -0.05298011854, 0.8829110762, 0.4435068522)
ZETA = 1.149604398
LANES = 128


def lift_level(values):
    even, odd = values[0::2], values[1::2]
    odd = odd + LIFT[0] * (even + np.roll(even, -1, 0))
    even = even + LIFT[1] * (odd + np.roll(odd, 1, 0))
    odd = odd + LIFT[2] * (even + np.roll(even, -1, 0))
    even = even + LIFT[3] * (odd + np.roll(odd, 1, 0))
    return even * ZETA, odd * (1.0 / ZETA)


def three_levels(length):
    coarse, members = np.eye(length), []
    for _ in range(3):
        coarse, detail = lift_level(coarse)
        members.append(detail)
    return members + [coarse]


def split_bf16(matrix):
    high = matrix.astype(jnp.bfloat16)
    low = (matrix - high.astype(np.float64)).astype(jnp.bfloat16)
    return high, low


def inline_blocks(rows):
    bricks, brick = 8, 4
    members = three_levels(rows * bricks)
    wanted = np.concatenate(
        [m[brick * len(m) // bricks : (brick + 1) * len(m) // bricks] for m in members]
    )

    def block(offset):
        return wanted[:, rows * (brick + offset) : rows * (brick + offset + 1)]

    factors = {}
    for offset in (-1, 1, -2, 2):
        left, sizes, right = np.linalg.svd(block(offset))
        rank = int((sizes > 1e-12).sum())
        root = np.sqrt(sizes[:rank])
        factors[offset] = (left[:, :rank] * root, root[:, None] * right[:rank])
    return block(0), factors


def sine_cosine(angle):
    turns = jnp.round(angle * (2.0 / np.pi))
    rest = angle - turns * 1.5703125
    rest = rest - turns * 4.837512969970703125e-4
    rest = rest - turns * 7.549789948768648e-8
    square = rest * rest
    sine = rest + rest * square * (
        -1.6666654611e-1 + square * (8.3321608736e-3 + square * -1.9515295891e-4)
    )
    cosine = (
        1.0
        - 0.5 * square
        + square
        * square
        * (4.166664568298827e-2 + square * (-1.388731625493765e-3 + square * 2.443315711809948e-5))
    )
    quarter = turns.astype(jnp.int32)
    swapped = (quarter & 1) == 1
    out_sine = jnp.where(swapped, cosine, sine)
    out_cosine = jnp.where(swapped, sine, cosine)
    out_sine = jnp.where((quarter & 2) == 2, -out_sine, out_sine)
    out_cosine = jnp.where(((quarter + 1) & 2) == 2, -out_cosine, out_cosine)
    return out_sine, out_cosine


def weights_kernel(
    waves, prior_p, prior_q, courant, epsilon, delta, tilt, azimuth, axis_x, axis_y, axis_z, gain_a, gain_b, base
):
    rows = waves.shape[0]
    top = lax.broadcasted_iota(jnp.int32, waves.shape[1:], 0) < 4

    def swap(value):
        return pltpu.roll(value, 4, 0)

    for x in range(rows):
        angles = jnp.concatenate(
            [tilt[x].astype(jnp.float32), azimuth[x].astype(jnp.float32)], axis=0
        )
        sine, cosine = sine_cosine(angles)
        sine_other, cosine_other = swap(sine), swap(cosine)
        sine_tilt = jnp.where(top, sine, sine_other)
        axis_x[x] = sine_tilt * jnp.where(top, cosine_other, cosine)
        axis_y[x] = sine * sine_other
        axis_z[x] = jnp.where(top, cosine, cosine_other)
        speed = courant[x].astype(jnp.float32)
        root = jnp.sqrt(1.0 + 2.0 * delta[x].astype(jnp.float32))
        stretch = 1.0 + 2.0 * epsilon[x].astype(jnp.float32)
        gain_a[x] = jnp.concatenate([speed * stretch, speed], axis=0)
        across = speed * root
        gain_b[x] = jnp.concatenate([across, across], axis=0)
        base[x] = 2.0 * waves[x] - jnp.concatenate([prior_p[x], prior_q[x]], axis=0)


def shifted(value, width):
    wide = jnp.concatenate(
        [value, jnp.zeros((value.shape[0], LANES), jnp.float32)], axis=1
    )
    total = width + LANES
    ahead = [pltpu.roll(wide, total - k, 1)[:, :width] for k in range(1, 5)]
    behind = [pltpu.roll(wide, k, 1)[:, :width] for k in range(1, 5)]
    return ahead, behind


def first_of(ahead, behind):
    total = FIRST[0] * (ahead[0] - behind[0])
    for k in range(1, 4):
        total = total + FIRST[k] * (ahead[k] - behind[k])
    return total


def second_of(centre, ahead, behind):
    total = SECOND[0] * centre
    for k in range(4):
        total = total + SECOND[k + 1] * (ahead[k] + behind[k])
    return total


def dot3(a_high, a_low, b_high, b_low):
    def dot(a, b):
        return jnp.dot(a, b, preferred_element_type=jnp.float32)

    rows = a_high.shape[0]
    both = dot(jnp.concatenate([a_high, a_low], axis=0), b_high)
    return both[:rows] + (both[rows:] + dot(a_high, b_low))


def halves(value):
    high = value.astype(jnp.bfloat16)
    return high, (value - high.astype(jnp.float32)).astype(jnp.bfloat16)


def depth_neighbours(own, far, lower):
    layer = lax.broadcasted_iota(jnp.int32, own.shape, 0) & 3
    up = far * jnp.where(lower, 1.0, 0.0)
    down = far * jnp.where(lower, 0.0, 1.0)
    ahead, behind = [], []
    for k in range(1, 4):
        ahead.append(jnp.where(layer < 4 - k, pltpu.roll(own, 8 - k, 0), pltpu.roll(up, 4 - k, 0)))
        behind.append(jnp.where(layer >= k, pltpu.roll(own, k, 0), pltpu.roll(down, 4 + k, 0)))
    return ahead + [up], behind + [down]


def depth_kernel(waves, other, dz, dzz):
    lower = lax.axis_index("gz") == 0
    for x in range(waves.shape[0]):
        own = waves[x]
        ahead, behind = depth_neighbours(own, other[x], lower)
        dz[x] = first_of(ahead, behind)
        dzz[x] = second_of(own, ahead, behind)


def cross_kernel(waves, dz, dzz, axis_y, axis_z, h_part, sum_part):
    rows, _, width = waves.shape

    def row(x, carry):
        centre = waves[x]
        dyy = second_of(centre, *shifted(centre, width))
        dzy = first_of(*shifted(dz[x], width))
        n_y, n_z = axis_y[x], axis_z[x]
        h_part[x] = (n_y * n_y) * dyy + n_z * (n_z * dzz[x] + 2.0 * n_y * dzy)
        sum_part[x] = dyy + dzz[x]
        return carry

    lax.fori_loop(0, rows, row, 0, unroll=4)


def step_kernel(
    size,
    gives,
    waves,
    edges,
    edges_other,
    dz,
    h_part,
    sum_part,
    axis_x,
    axis_y,
    axis_z,
    gain_a,
    gain_b,
    base,
    across_high,
    across_low,
    inline_high,
    inline_low,
    pressure,
    crossline,
    *rest,
):
    sends, (ext, dz_ext) = rest[:-2], rest[-2:]
    rows, _, width = waves.shape
    lower = lax.axis_index("gz") == 0
    place = lax.axis_index("xy")
    even, early = place % 2 == 0, place % 4 < 2
    left_at, right_at = jnp.where(even, 4, 0), jnp.where(even, 0, 4)
    left_in = jnp.where(place > 0, 1.0, 0.0)
    right_in = jnp.where(place < size - 1, 1.0, 0.0)
    top = lax.broadcasted_iota(jnp.int32, waves.shape[1:], 0) < 4

    for x in range(4):
        for at, inside, to in ((left_at, left_in, x), (right_at, right_in, rows + 4 + x)):
            own, far = edges[at + x] * inside, edges_other[at + x] * inside
            ext[to] = own
            dz_ext[to] = first_of(*depth_neighbours(own, far, lower))
    for x in range(rows):
        ext[x + 4] = waves[x]
        dz_ext[x + 4] = dz[x]

    def row(x, carry):
        ahead = [ext[x + 4 + k] for k in range(1, 5)]
        behind = [ext[x + 4 - k] for k in range(1, 5)]
        dxx = second_of(ext[x + 4], ahead, behind)
        dxy = first_of(*shifted(first_of(ahead, behind), width))
        dxz = first_of(
            [dz_ext[x + 4 + k] for k in range(1, 5)], [dz_ext[x + 4 - k] for k in range(1, 5)]
        )
        n_x = axis_x[x]
        h_one = h_part[x] + n_x * (n_x * dxx + 2.0 * (axis_y[x] * dxy + axis_z[x] * dxz))
        h_two = dxx + sum_part[x] - h_one
        mixed = jnp.where(top, h_two, h_one)
        pressure[x] = base[x] + gain_a[x] * mixed + gain_b[x] * pltpu.roll(mixed, 4, 0)
        return carry

    lax.fori_loop(0, rows, row, 0, unroll=4)

    packed = jnp.concatenate(
        [
            jnp.where(top, pressure[x], pltpu.roll(pressure[x + 1], 4, 0))
            for x in range(0, rows, 2)
        ],
        axis=0,
    )
    transformed = dot3(*halves(packed), across_high[...], across_low[...])
    crossline[...] = transformed
    parts = dot3(inline_high[...], inline_low[...], *halves(transformed))
    to_next, to_previous, to_second_next, to_second_previous = (
        parts[start : start + count] for start, count in gives
    )
    sends[0][...] = jnp.where(even, to_previous, to_next)
    sends[1][...] = jnp.where(even, to_next, to_previous)
    sends[2][...] = jnp.where(early, to_second_previous, to_second_next)
    sends[3][...] = jnp.where(early, to_second_next, to_second_previous)


def own_kernel(pressure, crossline, own_high, own_low, next_p, next_q, mine):
    for x in range(pressure.shape[0]):
        next_p[x] = pressure[x, :4]
        next_q[x] = pressure[x, 4:]
    mine[...] = dot3(own_high[...], own_low[...], *halves(crossline[...]))


def finish_kernel(takes, mine, *rest):
    outer, inner, outer_second, inner_second = (ref[...] for ref in rest[:4])
    outs = rest[4:]
    place = lax.axis_index("xy")
    even, early = place % 2 == 0, place % 4 < 2
    received = (
        jnp.where(even, outer, inner),
        jnp.where(even, inner, outer),
        jnp.where(early, outer_second, inner_second),
        jnp.where(early, inner_second, outer_second),
    )
    at = 0
    for out in outs:
        for row in range(out.shape[0]):
            total = mine[4 * at : 4 * at + 4]
            for take, got in zip(takes, received):
                for j in range(take.shape[1]):
                    factor = float(take[at, j])
                    if abs(factor) > 1e-13:
                        total = total + factor * got[4 * j : 4 * j + 4]
            out[row] = total
            at += 1


def pair_swaps(size):
    one = [1 if i % 2 == 0 else -1 for i in range(size)]
    two = [2 if i % 4 < 2 else -2 for i in range(size)]
    return [
        [(i, (i - one[i]) % size) for i in range(size)],
        [(i, i + one[i]) for i in range(size)],
        [(i, (i - two[i]) % size) for i in range(size)],
        [(i, i + two[i]) for i in range(size)],
    ]


def body(size, wave_p, wave_q, prior_p, prior_q, courant, epsilon, thomsen_delta, tilt_angle, azimuth):
    rows, layers, width = wave_p.shape
    f32 = jnp.float32
    even = lax.axis_index("xy") % 2 == 0
    pairs = pair_swaps(size)
    cores = [(0, 1), (1, 0)]
    waves = lax.optimization_barrier(jnp.concatenate([wave_p, wave_q], axis=1))
    leading, last = waves[:4], waves[rows - 4 :]
    open_outer = [
        (2 * i + g, 2 * i + 1 - g) if abs(i - j) > 1 else (2 * i + g, 2 * j + g)
        for i, j in pairs[0]
        for g in range(2)
    ]
    outer = lax.ppermute(jnp.where(even, leading, last), ("xy", "gz"), open_outer)
    inner = lax.ppermute(jnp.where(even, last, leading), "xy", pairs[1])
    other = lax.ppermute(waves, "gz", cores)

    stack = jax.ShapeDtypeStruct((rows, 8, width), f32)
    cells = rows * layers * width
    params = pltpu.CompilerParams(vmem_limit_bytes=16 * 1024 * 1024)

    def kernel(function, out_shape, work, name, scratch_shapes=()):
        cost = pl.CostEstimate(flops=work * cells, bytes_accessed=40 * cells, transcendentals=0)
        return pl.pallas_call(
            function,
            out_shape=out_shape,
            scratch_shapes=scratch_shapes,
            compiler_params=params,
            cost_estimate=cost,
            name=name,
        )

    axis_x, axis_y, axis_z, *gains = kernel(weights_kernel, [stack] * 6, 100, "weights")(
        waves, prior_p, prior_q, courant, epsilon, thomsen_delta, tilt_angle, azimuth
    )
    dz, dzz = kernel(depth_kernel, [stack] * 2, 100, "depth")(waves, other)
    outer, inner, dz, axis_x = lax.optimization_barrier((outer, inner, dz, axis_x))
    edges = jnp.concatenate([inner, outer], axis=0)
    edges_other = lax.ppermute(edges, "gz", cores)
    h_part, sum_part = kernel(cross_kernel, [stack] * 2, 100, "cross")(waves, dz, dzz, axis_y, axis_z)

    own, factors = inline_blocks(rows)
    offsets = (-1, 1, -2, 2)
    pieces, gives, start = [], [], 0
    for offset in offsets:
        give = factors[offset][1]
        pad = give.shape[0] % 2
        pieces.append(np.pad(give, ((0, pad), (0, 0))))
        gives.append((start, 4 * (give.shape[0] + pad)))
        start += gives[-1][1]

    def parts(matrix):
        return [jnp.asarray(part) for part in split_bf16(matrix)]

    across = parts(np.concatenate(three_levels(width)).T)
    inline = parts(np.kron(np.concatenate(pieces), np.eye(4)))
    inline_own = parts(np.kron(own, np.eye(4)))
    flat = jax.ShapeDtypeStruct((layers * rows, width), f32)
    pressure, crossline, *sends = kernel(
        functools.partial(step_kernel, size, gives),
        [stack, flat] + [jax.ShapeDtypeStruct((count, width), f32) for _, count in gives],
        400,
        "step",
        [pltpu.VMEM((rows + 8, 8, width), f32)] * 2,
    )(waves, edges, edges_other, dz, h_part, sum_part, axis_x, axis_y, axis_z, *gains, *across, *inline)
    received = [lax.ppermute(send, "xy", pair) for send, pair in zip(sends, pairs)]
    grid = jax.ShapeDtypeStruct(wave_p.shape, f32)
    next_p, next_q, mine = kernel(own_kernel, [grid, grid, flat], 100, "own")(
        pressure, crossline, *inline_own
    )
    outs = kernel(
        functools.partial(finish_kernel, [factors[offset][0] for offset in offsets]),
        [
            jax.ShapeDtypeStruct((count, layers, width), f32)
            for count in (rows // 2, rows // 4, rows // 8, rows // 8)
        ],
        20,
        "finish",
    )(mine, *received)
    return (next_p, next_q, *outs)


def solution(mesh):
    split = P(("shot", "xy"), "gz", None)
    shared = P("xy", "gz", None)
    return jax.shard_map(
        functools.partial(body, mesh.shape["xy"]),
        mesh=mesh,
        in_specs=(split,) * 4 + (shared,) * 5,
        out_specs=(split,) * 6,
        check_vma=False,
    )
```

```python
import functools

import jax
import jax.numpy as jnp
import numpy as np
from jax import lax
from jax.experimental import pallas as pl
from jax.experimental.pallas import tpu as pltpu
from jax.sharding import PartitionSpec as P

SECOND = (-205.0 / 72.0, 8.0 / 5.0, -1.0 / 5.0, 8.0 / 315.0, -1.0 / 560.0)
FIRST = (4.0 / 5.0, -1.0 / 5.0, 4.0 / 105.0, -1.0 / 280.0)
LIFT = (-1.586134342, -0.05298011854, 0.8829110762, 0.4435068522)
ZETA = 1.149604398
LANES = 128


def lift_level(values):
    even, odd = values[0::2], values[1::2]
    odd = odd + LIFT[0] * (even + np.roll(even, -1, 0))
    even = even + LIFT[1] * (odd + np.roll(odd, 1, 0))
    odd = odd + LIFT[2] * (even + np.roll(even, -1, 0))
    even = even + LIFT[3] * (odd + np.roll(odd, 1, 0))
    return even * ZETA, odd * (1.0 / ZETA)


def three_levels(length):
    coarse, members = np.eye(length), []
    for _ in range(3):
        coarse, detail = lift_level(coarse)
        members.append(detail)
    return members + [coarse]


def split_bf16(matrix):
    high = matrix.astype(jnp.bfloat16)
    low = (matrix - high.astype(np.float64)).astype(jnp.bfloat16)
    return high, low


def inline_blocks(rows):
    bricks, brick = 8, 4
    members = three_levels(rows * bricks)
    wanted = np.concatenate(
        [m[brick * len(m) // bricks : (brick + 1) * len(m) // bricks] for m in members]
    )

    def block(offset):
        return wanted[:, rows * (brick + offset) : rows * (brick + offset + 1)]

    factors = {}
    for offset in (-1, 1, -2, 2):
        left, sizes, right = np.linalg.svd(block(offset))
        rank = int((sizes > 1e-12).sum())
        root = np.sqrt(sizes[:rank])
        factors[offset] = (left[:, :rank] * root, root[:, None] * right[:rank])
    return block(0), factors


def sine_cosine(angle):
    turns = jnp.round(angle * (2.0 / np.pi))
    rest = angle - turns * 1.5703125
    rest = rest - turns * 4.837512969970703125e-4
    rest = rest - turns * 7.549789948768648e-8
    square = rest * rest
    sine = rest + rest * square * (
        -1.6666654611e-1 + square * (8.3321608736e-3 + square * -1.9515295891e-4)
    )
    cosine = (
        1.0
        - 0.5 * square
        + square
        * square
        * (4.166664568298827e-2 + square * (-1.388731625493765e-3 + square * 2.443315711809948e-5))
    )
    quarter = turns.astype(jnp.int32)
    swapped = (quarter & 1) == 1
    out_sine = jnp.where(swapped, cosine, sine)
    out_cosine = jnp.where(swapped, sine, cosine)
    out_sine = jnp.where((quarter & 2) == 2, -out_sine, out_sine)
    out_cosine = jnp.where(((quarter + 1) & 2) == 2, -out_cosine, out_cosine)
    return out_sine, out_cosine


def weights_kernel(
    waves, prior_p, prior_q, courant, epsilon, delta, tilt, azimuth, axis_x, axis_y, axis_z, gain_a, gain_b, base
):
    rows = waves.shape[0]
    top = lax.broadcasted_iota(jnp.int32, waves.shape[1:], 0) < 4

    def swap(value):
        return pltpu.roll(value, 4, 0)

    for x in range(rows):
        angles = jnp.concatenate(
            [tilt[x].astype(jnp.float32), azimuth[x].astype(jnp.float32)], axis=0
        )
        sine, cosine = sine_cosine(angles)
        sine_other, cosine_other = swap(sine), swap(cosine)
        sine_tilt = jnp.where(top, sine, sine_other)
        axis_x[x] = sine_tilt * jnp.where(top, cosine_other, cosine)
        axis_y[x] = sine * sine_other
        axis_z[x] = jnp.where(top, cosine, cosine_other)
        speed = courant[x].astype(jnp.float32)
        root = jnp.sqrt(1.0 + 2.0 * delta[x].astype(jnp.float32))
        stretch = 1.0 + 2.0 * epsilon[x].astype(jnp.float32)
        gain_a[x] = jnp.concatenate([speed * stretch, speed], axis=0)
        across = speed * root
        gain_b[x] = jnp.concatenate([across, across], axis=0)
        base[x] = 2.0 * waves[x] - jnp.concatenate([prior_p[x], prior_q[x]], axis=0)


def shifted(value, width):
    wide = jnp.concatenate(
        [value, jnp.zeros((value.shape[0], LANES), jnp.float32)], axis=1
    )
    total = width + LANES
    ahead = [pltpu.roll(wide, total - k, 1)[:, :width] for k in range(1, 5)]
    behind = [pltpu.roll(wide, k, 1)[:, :width] for k in range(1, 5)]
    return ahead, behind


def first_of(ahead, behind):
    total = FIRST[0] * (ahead[0] - behind[0])
    for k in range(1, 4):
        total = total + FIRST[k] * (ahead[k] - behind[k])
    return total


def second_of(centre, ahead, behind):
    total = SECOND[0] * centre
    for k in range(4):
        total = total + SECOND[k + 1] * (ahead[k] + behind[k])
    return total


def dot3(a_high, a_low, b_high, b_low):
    def dot(a, b):
        return jnp.dot(a, b, preferred_element_type=jnp.float32)

    rows = a_high.shape[0]
    both = dot(jnp.concatenate([a_high, a_low], axis=0), b_high)
    return both[:rows] + (both[rows:] + dot(a_high, b_low))


def halves(value):
    high = value.astype(jnp.bfloat16)
    return high, (value - high.astype(jnp.float32)).astype(jnp.bfloat16)


def depth_neighbours(own, far, lower):
    layer = lax.broadcasted_iota(jnp.int32, own.shape, 0) & 3
    up = far * jnp.where(lower, 1.0, 0.0)
    down = far * jnp.where(lower, 0.0, 1.0)
    ahead, behind = [], []
    for k in range(1, 4):
        ahead.append(jnp.where(layer < 4 - k, pltpu.roll(own, 8 - k, 0), pltpu.roll(up, 4 - k, 0)))
        behind.append(jnp.where(layer >= k, pltpu.roll(own, k, 0), pltpu.roll(down, 4 + k, 0)))
    return ahead + [up], behind + [down]


def depth_kernel(waves, other, dz, dzz):
    lower = lax.axis_index("gz") == 0
    for x in range(waves.shape[0]):
        own = waves[x]
        ahead, behind = depth_neighbours(own, other[x], lower)
        dz[x] = first_of(ahead, behind)
        dzz[x] = second_of(own, ahead, behind)


def cross_kernel(waves, dz, dzz, axis_y, axis_z, h_part, sum_part):
    rows, _, width = waves.shape

    def row(x, carry):
        centre = waves[x]
        dyy = second_of(centre, *shifted(centre, width))
        dzy = first_of(*shifted(dz[x], width))
        n_y, n_z = axis_y[x], axis_z[x]
        h_part[x] = (n_y * n_y) * dyy + n_z * (n_z * dzz[x] + 2.0 * n_y * dzy)
        sum_part[x] = dyy + dzz[x]
        return carry

    lax.fori_loop(0, rows, row, 0, unroll=4)


def halo_places(size, rows):
    place = lax.axis_index("xy")
    even = place % 2 == 0
    left_at, right_at = jnp.where(even, 4, 0), jnp.where(even, 0, 4)
    left_in = jnp.where(place > 0, 1.0, 0.0)
    right_in = jnp.where(place < size - 1, 1.0, 0.0)
    for x in range(4):
        yield left_at + x, x, left_in
        yield right_at + x, rows + 4 + x, right_in


def inline_kernel(size, waves, edges, axis_x, axis_y, h_part, sum_part, h_more, sum_all, ext):
    rows, _, width = waves.shape
    for at, to, inside in halo_places(size, rows):
        ext[to] = edges[at] * inside
    for x in range(rows):
        ext[x + 4] = waves[x]

    def row(x, carry):
        ahead = [ext[x + 4 + k] for k in range(1, 5)]
        behind = [ext[x + 4 - k] for k in range(1, 5)]
        dxx = second_of(ext[x + 4], ahead, behind)
        dxy = first_of(*shifted(first_of(ahead, behind), width))
        n_x = axis_x[x]
        h_more[x] = h_part[x] + n_x * (n_x * dxx + 2.0 * (axis_y[x] * dxy))
        sum_all[x] = sum_part[x] + dxx
        return carry

    lax.fori_loop(0, rows, row, 0, unroll=4)


def step_kernel(
    size,
    gives,
    edges,
    edges_other,
    dz,
    h_more,
    sum_all,
    axis_x,
    axis_z,
    gain_a,
    gain_b,
    base,
    across_high,
    across_low,
    inline_high,
    inline_low,
    pressure,
    crossline,
    *rest,
):
    sends, dz_ext = rest[:-1], rest[-1]
    rows, _, width = dz.shape
    lower = lax.axis_index("gz") == 0
    place = lax.axis_index("xy")
    even, early = place % 2 == 0, place % 4 < 2
    top = lax.broadcasted_iota(jnp.int32, dz.shape[1:], 0) < 4

    for at, to, inside in halo_places(size, rows):
        own, far = edges[at] * inside, edges_other[at] * inside
        dz_ext[to] = first_of(*depth_neighbours(own, far, lower))
    for x in range(rows):
        dz_ext[x + 4] = dz[x]

    for x in range(rows):
        dxz = first_of(
            [dz_ext[x + 4 + k] for k in range(1, 5)], [dz_ext[x + 4 - k] for k in range(1, 5)]
        )
        h_one = h_more[x] + 2.0 * (axis_x[x] * axis_z[x] * dxz)
        h_two = sum_all[x] - h_one
        mixed = jnp.where(top, h_two, h_one)
        pressure[x] = base[x] + gain_a[x] * mixed + gain_b[x] * pltpu.roll(mixed, 4, 0)

    packed = jnp.concatenate(
        [
            jnp.where(top, pressure[x], pltpu.roll(pressure[x + 1], 4, 0))
            for x in range(0, rows, 2)
        ],
        axis=0,
    )
    transformed = dot3(*halves(packed), across_high[...], across_low[...])
    crossline[...] = transformed
    parts = dot3(inline_high[...], inline_low[...], *halves(transformed))
    to_next, to_previous, to_second_next, to_second_previous = (
        parts[start : start + count] for start, count in gives
    )
    sends[0][...] = jnp.where(even, to_previous, to_next)
    sends[1][...] = jnp.where(even, to_next, to_previous)
    sends[2][...] = jnp.where(early, to_second_next, to_second_previous)
    sends[3][...] = jnp.where(early, to_second_previous, to_second_next)


def own_kernel(pressure, crossline, own_high, own_low, next_p, next_q, mine):
    for x in range(pressure.shape[0]):
        next_p[x] = pressure[x, :4]
        next_q[x] = pressure[x, 4:]
    mine[...] = dot3(own_high[...], own_low[...], *halves(crossline[...]))


def finish_kernel(takes, mine, *rest):
    outer, inner, inner_second, outer_second = (ref[...] for ref in rest[:4])
    outs = rest[4:]
    place = lax.axis_index("xy")
    even, early = place % 2 == 0, place % 4 < 2
    received = (
        jnp.where(even, outer, inner),
        jnp.where(even, inner, outer),
        jnp.where(early, outer_second, inner_second),
        jnp.where(early, inner_second, outer_second),
    )
    at = 0
    for out in outs:
        for row in range(out.shape[0]):
            total = mine[4 * at : 4 * at + 4]
            for take, got in zip(takes, received):
                for j in range(take.shape[1]):
                    factor = float(take[at, j])
                    if abs(factor) > 1e-13:
                        total = total + factor * got[4 * j : 4 * j + 4]
            out[row] = total
            at += 1


def pair_swaps(size):
    one = [1 if i % 2 == 0 else -1 for i in range(size)]
    two = [2 if i % 4 < 2 else -2 for i in range(size)]
    return [
        [(i, (i - one[i]) % size) for i in range(size)],
        [(i, i + one[i]) for i in range(size)],
        [(i, i + two[i]) for i in range(size)],
        [(i, (i - two[i]) % size) for i in range(size)],
    ]


def body(size, wave_p, wave_q, prior_p, prior_q, courant, epsilon, thomsen_delta, tilt_angle, azimuth):
    rows, layers, width = wave_p.shape
    f32 = jnp.float32
    even = lax.axis_index("xy") % 2 == 0
    pairs = pair_swaps(size)
    cores = [(0, 1), (1, 0)]
    waves = lax.optimization_barrier(jnp.concatenate([wave_p, wave_q], axis=1))
    leading, last = waves[:4], waves[rows - 4 :]
    open_outer = [
        (2 * i + g, 2 * i + 1 - g) if abs(i - j) > 1 else (2 * i + g, 2 * j + g)
        for i, j in pairs[0]
        for g in range(2)
    ]
    outer = lax.ppermute(jnp.where(even, leading, last), ("xy", "gz"), open_outer)
    inner = lax.ppermute(jnp.where(even, last, leading), "xy", pairs[1])
    other = lax.ppermute(waves, "gz", cores)

    stack = jax.ShapeDtypeStruct((rows, 8, width), f32)
    cells = rows * layers * width
    params = pltpu.CompilerParams(vmem_limit_bytes=16 * 1024 * 1024)

    def kernel(function, out_shape, work, name, scratch_shapes=()):
        cost = pl.CostEstimate(flops=work * cells, bytes_accessed=40 * cells, transcendentals=0)
        return pl.pallas_call(
            function,
            out_shape=out_shape,
            scratch_shapes=scratch_shapes,
            compiler_params=params,
            cost_estimate=cost,
            name=name,
        )

    axis_x, axis_y, axis_z, *gains = kernel(weights_kernel, [stack] * 6, 100, "weights")(
        waves, prior_p, prior_q, courant, epsilon, thomsen_delta, tilt_angle, azimuth
    )
    dz, dzz = kernel(depth_kernel, [stack] * 2, 100, "depth")(waves, other)
    h_part, sum_part = kernel(cross_kernel, [stack] * 2, 100, "cross")(waves, dz, dzz, axis_y, axis_z)
    outer, inner, h_part, sum_part = lax.optimization_barrier((outer, inner, h_part, sum_part))
    edges = jnp.concatenate([inner, outer], axis=0)
    edges_other = lax.ppermute(edges, "gz", cores)
    h_more, sum_all = kernel(
        functools.partial(inline_kernel, size),
        [stack] * 2,
        100,
        "inline",
        [pltpu.VMEM((rows + 8, 8, width), f32)],
    )(waves, edges, axis_x, axis_y, h_part, sum_part)

    own, factors = inline_blocks(rows)
    offsets = (-1, 1, -2, 2)
    pieces, gives, start = [], [], 0
    for offset in offsets:
        give = factors[offset][1]
        pad = give.shape[0] % 2
        pieces.append(np.pad(give, ((0, pad), (0, 0))))
        gives.append((start, 4 * (give.shape[0] + pad)))
        start += gives[-1][1]

    def parts(matrix):
        return [jnp.asarray(part) for part in split_bf16(matrix)]

    across = parts(np.concatenate(three_levels(width)).T)
    inline = parts(np.kron(np.concatenate(pieces), np.eye(4)))
    inline_own = parts(np.kron(own, np.eye(4)))
    flat = jax.ShapeDtypeStruct((layers * rows, width), f32)
    pressure, crossline, *sends = kernel(
        functools.partial(step_kernel, size, gives),
        [stack, flat] + [jax.ShapeDtypeStruct((count, width), f32) for _, count in gives],
        400,
        "step",
        [pltpu.VMEM((rows + 8, 8, width), f32)],
    )(edges, edges_other, dz, h_more, sum_all, axis_x, axis_z, *gains, *across, *inline)
    received = [lax.ppermute(send, "xy", pair) for send, pair in zip(sends, pairs)]
    grid = jax.ShapeDtypeStruct(wave_p.shape, f32)
    next_p, next_q, mine = kernel(own_kernel, [grid, grid, flat], 100, "own")(
        pressure, crossline, *inline_own
    )
    outs = kernel(
        functools.partial(finish_kernel, [factors[offset][0] for offset in offsets]),
        [
            jax.ShapeDtypeStruct((count, layers, width), f32)
            for count in (rows // 2, rows // 4, rows // 8, rows // 8)
        ],
        20,
        "finish",
    )(mine, *received)
    return (next_p, next_q, *outs)


def solution(mesh):
    split = P(("shot", "xy"), "gz", None)
    shared = P("xy", "gz", None)
    return jax.shard_map(
        functools.partial(body, mesh.shape["xy"]),
        mesh=mesh,
        in_specs=(split,) * 4 + (shared,) * 5,
        out_specs=(split,) * 6,
        check_vma=False,
    )
```

```python
import functools

import jax
import jax.numpy as jnp
import numpy as np
from jax import lax
from jax.experimental import pallas as pl
from jax.experimental.pallas import tpu as pltpu
from jax.sharding import PartitionSpec as P

SECOND = (-205.0 / 72.0, 8.0 / 5.0, -1.0 / 5.0, 8.0 / 315.0, -1.0 / 560.0)
FIRST = (4.0 / 5.0, -1.0 / 5.0, 4.0 / 105.0, -1.0 / 280.0)
LIFT = (-1.586134342, -0.05298011854, 0.8829110762, 0.4435068522)
ZETA = 1.149604398
LANES = 128
SCALE_FIRST, SCALE_SECOND = 840.0, 5040.0


def lift_level(values):
    even, odd = values[0::2], values[1::2]
    odd = odd + LIFT[0] * (even + np.roll(even, -1, 0))
    even = even + LIFT[1] * (odd + np.roll(odd, 1, 0))
    odd = odd + LIFT[2] * (even + np.roll(even, -1, 0))
    even = even + LIFT[3] * (odd + np.roll(odd, 1, 0))
    return even * ZETA, odd * (1.0 / ZETA)


def three_levels(length):
    coarse, members = np.eye(length), []
    for _ in range(3):
        coarse, detail = lift_level(coarse)
        members.append(detail)
    return members + [coarse]


def band(width, taps, sign, scale):
    matrix = np.zeros((width, width))
    for k, tap in enumerate(taps, 1):
        value = float(np.round(tap * scale))
        matrix += value * np.eye(width, k=-k) + sign * value * np.eye(width, k=k)
    return jnp.asarray(matrix.astype(jnp.bfloat16))


def split_bf16(matrix):
    high = matrix.astype(jnp.bfloat16)
    low = (matrix - high.astype(np.float64)).astype(jnp.bfloat16)
    return high, low


def inline_blocks(rows):
    bricks, brick = 8, 4
    members = three_levels(rows * bricks)
    wanted = np.concatenate(
        [m[brick * len(m) // bricks : (brick + 1) * len(m) // bricks] for m in members]
    )

    def block(offset):
        return wanted[:, rows * (brick + offset) : rows * (brick + offset + 1)]

    factors = {}
    for offset in (-1, 1, -2, 2):
        left, sizes, right = np.linalg.svd(block(offset))
        rank = int((sizes > 1e-12).sum())
        root = np.sqrt(sizes[:rank])
        factors[offset] = (left[:, :rank] * root, root[:, None] * right[:rank])
    return block(0), factors


def sine_cosine(angle):
    turns = jnp.round(angle * (2.0 / np.pi))
    rest = angle - turns * 1.5703125
    rest = rest - turns * 4.837512969970703125e-4
    rest = rest - turns * 7.549789948768648e-8
    square = rest * rest
    sine = rest + rest * square * (
        -1.6666654611e-1 + square * (8.3321608736e-3 + square * -1.9515295891e-4)
    )
    cosine = (
        1.0
        - 0.5 * square
        + square
        * square
        * (4.166664568298827e-2 + square * (-1.388731625493765e-3 + square * 2.443315711809948e-5))
    )
    quarter = turns.astype(jnp.int32)
    swapped = (quarter & 1) == 1
    out_sine = jnp.where(swapped, cosine, sine)
    out_cosine = jnp.where(swapped, sine, cosine)
    out_sine = jnp.where((quarter & 2) == 2, -out_sine, out_sine)
    out_cosine = jnp.where(((quarter + 1) & 2) == 2, -out_cosine, out_cosine)
    return out_sine, out_cosine


def weights_kernel(
    waves, prior_p, prior_q, courant, epsilon, delta, tilt, azimuth, axis_x, axis_y, axis_z, gain_a, gain_b, base
):
    rows = waves.shape[0]
    top = lax.broadcasted_iota(jnp.int32, waves.shape[1:], 0) < 4

    def swap(value):
        return pltpu.roll(value, 4, 0)

    for x in range(rows):
        angles = jnp.concatenate(
            [tilt[x].astype(jnp.float32), azimuth[x].astype(jnp.float32)], axis=0
        )
        sine, cosine = sine_cosine(angles)
        sine_other, cosine_other = swap(sine), swap(cosine)
        sine_tilt = jnp.where(top, sine, sine_other)
        axis_x[x] = sine_tilt * jnp.where(top, cosine_other, cosine)
        axis_y[x] = sine * sine_other
        axis_z[x] = jnp.where(top, cosine, cosine_other)
        speed = courant[x].astype(jnp.float32)
        root = jnp.sqrt(1.0 + 2.0 * delta[x].astype(jnp.float32))
        stretch = 1.0 + 2.0 * epsilon[x].astype(jnp.float32)
        gain_a[x] = jnp.concatenate([speed * stretch, speed], axis=0)
        across = speed * root
        gain_b[x] = jnp.concatenate([across, across], axis=0)
        base[x] = 2.0 * waves[x] - jnp.concatenate([prior_p[x], prior_q[x]], axis=0)


def first_of(ahead, behind):
    total = FIRST[0] * (ahead[0] - behind[0])
    for k in range(1, 4):
        total = total + FIRST[k] * (ahead[k] - behind[k])
    return total


def second_of(centre, ahead, behind):
    total = SECOND[0] * centre
    for k in range(4):
        total = total + SECOND[k + 1] * (ahead[k] + behind[k])
    return total


def dot3(a_high, a_low, b_high, b_low):
    def dot(a, b):
        return jnp.dot(a, b, preferred_element_type=jnp.float32)

    rows = a_high.shape[0]
    both = dot(jnp.concatenate([a_high, a_low], axis=0), b_high)
    return both[:rows] + (both[rows:] + dot(a_high, b_low))


def halves(value):
    high = value.astype(jnp.bfloat16)
    return high, (value - high.astype(jnp.float32)).astype(jnp.bfloat16)


def depth_neighbours(own, far, lower):
    layer = lax.broadcasted_iota(jnp.int32, own.shape, 0) & 3
    up = far * jnp.where(lower, 1.0, 0.0)
    down = far * jnp.where(lower, 0.0, 1.0)
    ahead, behind = [], []
    for k in range(1, 4):
        ahead.append(jnp.where(layer < 4 - k, pltpu.roll(own, 8 - k, 0), pltpu.roll(up, 4 - k, 0)))
        behind.append(jnp.where(layer >= k, pltpu.roll(own, k, 0), pltpu.roll(down, 4 + k, 0)))
    return ahead + [up], behind + [down]


def across(parts, taps):
    width = parts.shape[1]
    blocks = []
    for start in range(0, width, 2 * LANES):
        stop = min(start + 2 * LANES, width)
        low, high = max(start - LANES, 0), min(stop + LANES, width)
        blocks.append(
            jnp.dot(
                parts[:, low:high], taps[low:high, start:stop], preferred_element_type=jnp.float32
            )
        )
    return jnp.concatenate(blocks, axis=1)


def joined(parts, rows):
    return parts[:rows] + parts[rows:]


def interior_kernel(
    waves, other, axis_x, axis_y, axis_z, taps_first, taps_second, h_own, sum_own, dz, dzz, dy, dyy, dzy
):
    rows, sub, width = waves.shape
    flat = rows * sub
    lower = lax.axis_index("gz") == 0
    for x in range(rows):
        own = waves[x]
        ahead, behind = depth_neighbours(own, other[x], lower)
        dz[x] = first_of(ahead, behind)
        dzz[x] = second_of(own, ahead, behind)
    field = jnp.concatenate(halves(waves[...].reshape(flat, width)), axis=0)
    slope = jnp.concatenate(halves(dz[...].reshape(flat, width)), axis=0)
    dyy[...] = joined(across(field, taps_second), flat).reshape(waves.shape)
    dy[...] = joined(across(field, taps_first), flat).reshape(waves.shape)
    dzy[...] = joined(across(slope, taps_first), flat).reshape(waves.shape)
    for x in range(rows):
        centre = waves[x]
        dxx = SECOND[0] * centre
        dxy = jnp.zeros_like(centre)
        dxz = jnp.zeros_like(centre)
        for k in range(1, 5):
            for step in (k, -k):
                if 0 <= x + step < rows:
                    weight = FIRST[k - 1] if step > 0 else -FIRST[k - 1]
                    dxx = dxx + SECOND[k] * waves[x + step]
                    dxy = dxy + (weight / SCALE_FIRST) * dy[x + step]
                    dxz = dxz + weight * dz[x + step]
        cross = SECOND[0] * centre + (1.0 / SCALE_SECOND) * dyy[x]
        n_x, n_y, n_z = axis_x[x], axis_y[x], axis_z[x]
        h_one = n_x * (n_x * dxx + 2.0 * (n_y * dxy + n_z * dxz))
        h_one = h_one + n_y * (n_y * cross + (2.0 / SCALE_FIRST) * (n_z * dzy[x]))
        h_own[x] = h_one + n_z * (n_z * dzz[x])
        sum_own[x] = dxx + cross + dzz[x]


def halo_rows(size, edges):
    place = lax.axis_index("xy")
    even = place % 2 == 0
    left_at, right_at = jnp.where(even, 4, 0), jnp.where(even, 0, 4)
    left_in = jnp.where(place > 0, 1.0, 0.0)
    right_in = jnp.where(place < size - 1, 1.0, 0.0)
    before = [edges[left_at + x] * left_in for x in range(4)]
    return before + [edges[right_at + x] * right_in for x in range(4)]


def reach(values, row, coefficients, sign):
    total = None
    for k in range(1, 5):
        at = row + 4 - k if row < 4 else row + k - 4
        if (row < 4 and 0 <= at < 4) or (row >= 4 and 4 <= at < 8):
            term = (coefficients[k - 1] * (sign if row < 4 else 1.0)) * values[at]
            total = term if total is None else total + term
    return total


def halo_kernel(size, edges, axis_x, axis_y, h_own, sum_own, taps_first, h_edge, sum_edge):
    rows, sub, width = h_own.shape
    values = halo_rows(size, edges)
    parts = jnp.concatenate(halves(jnp.concatenate(values, axis=0)), axis=0)
    slopes = joined(across(parts, taps_first), 8 * sub)
    slopes = [slopes[sub * x : sub * x + sub] for x in range(8)]
    for row in range(8):
        x = row if row < 4 else rows - 8 + row
        dxx = reach(values, row, SECOND[1:], 1.0)
        dxy = reach(slopes, row, [c / SCALE_FIRST for c in FIRST], -1.0)
        n_x = axis_x[x]
        h_edge[row] = h_own[x] + n_x * (n_x * dxx + 2.0 * (axis_y[x] * dxy))
        sum_edge[row] = sum_own[x] + dxx


def step_kernel(
    size,
    gives,
    edges,
    edges_other,
    h_own,
    sum_own,
    h_edge,
    sum_edge,
    axis_x,
    axis_z,
    gain_a,
    gain_b,
    base,
    across_high,
    across_low,
    inline_high,
    inline_low,
    pressure,
    crossline,
    *sends,
):
    rows, sub, width = h_own.shape
    lower = lax.axis_index("gz") == 0
    place = lax.axis_index("xy")
    even, early = place % 2 == 0, place % 4 < 2
    top = lax.broadcasted_iota(jnp.int32, (sub, width), 0) < 4

    slopes = [
        first_of(*depth_neighbours(own, far, lower))
        for own, far in zip(halo_rows(size, edges), halo_rows(size, edges_other))
    ]
    for x in range(rows):
        row = x if x < 4 else x - rows + 8
        if 4 <= x < rows - 4:
            h_one, total = h_own[x], sum_own[x]
        else:
            dxz = reach(slopes, row, FIRST, -1.0)
            h_one, total = h_edge[row] + 2.0 * (axis_x[x] * axis_z[x] * dxz), sum_edge[row]
        mixed = jnp.where(top, total - h_one, h_one)
        pressure[x] = base[x] + gain_a[x] * mixed + gain_b[x] * pltpu.roll(mixed, 4, 0)

    packed = jnp.concatenate(
        [
            jnp.where(top, pressure[x], pltpu.roll(pressure[x + 1], 4, 0))
            for x in range(0, rows, 2)
        ],
        axis=0,
    )
    transformed = dot3(*halves(packed), across_high[...], across_low[...])
    crossline[...] = transformed
    parts = dot3(inline_high[...], inline_low[...], *halves(transformed))
    to_next, to_previous, to_second_next, to_second_previous = (
        parts[start : start + count] for start, count in gives
    )
    sends[0][...] = jnp.where(even, to_previous, to_next)
    sends[1][...] = jnp.where(even, to_next, to_previous)
    sends[2][...] = jnp.where(early, to_second_previous, to_second_next)
    sends[3][...] = jnp.where(early, to_second_next, to_second_previous)


def own_kernel(pressure, crossline, own_high, own_low, next_p, next_q, mine):
    for x in range(pressure.shape[0]):
        next_p[x] = pressure[x, :4]
        next_q[x] = pressure[x, 4:]
    mine[...] = dot3(own_high[...], own_low[...], *halves(crossline[...]))


def finish_kernel(takes, mine, *rest):
    outer, inner, outer_second, inner_second = (ref[...] for ref in rest[:4])
    outs = rest[4:]
    place = lax.axis_index("xy")
    even, early = place % 2 == 0, place % 4 < 2
    received = (
        jnp.where(even, outer, inner),
        jnp.where(even, inner, outer),
        jnp.where(early, outer_second, inner_second),
        jnp.where(early, inner_second, outer_second),
    )
    at = 0
    for out in outs:
        for row in range(out.shape[0]):
            total = mine[4 * at : 4 * at + 4]
            for take, got in zip(takes, received):
                for j in range(take.shape[1]):
                    factor = float(take[at, j])
                    if abs(factor) > 1e-13:
                        total = total + factor * got[4 * j : 4 * j + 4]
            out[row] = total
            at += 1


def pair_swaps(size):
    one = [1 if i % 2 == 0 else -1 for i in range(size)]
    two = [2 if i % 4 < 2 else -2 for i in range(size)]
    return [
        [(i, (i - one[i]) % size) for i in range(size)],
        [(i, i + one[i]) for i in range(size)],
        [(i, (i - two[i]) % size) for i in range(size)],
        [(i, i + two[i]) for i in range(size)],
    ]


def body(size, wave_p, wave_q, prior_p, prior_q, courant, epsilon, thomsen_delta, tilt_angle, azimuth):
    rows, layers, width = wave_p.shape
    f32 = jnp.float32
    even = lax.axis_index("xy") % 2 == 0
    pairs = pair_swaps(size)
    cores = [(0, 1), (1, 0)]
    waves = lax.optimization_barrier(jnp.concatenate([wave_p, wave_q], axis=1))
    leading, last = waves[:4], waves[rows - 4 :]
    open_outer = [
        (2 * i + g, 2 * i + 1 - g) if abs(i - j) > 1 else (2 * i + g, 2 * j + g)
        for i, j in pairs[0]
        for g in range(2)
    ]
    other = lax.ppermute(waves, "gz", cores)
    inner = lax.ppermute(jnp.where(even, last, leading), "xy", pairs[1])
    outer = lax.ppermute(jnp.where(even, leading, last), ("xy", "gz"), open_outer)

    stack = jax.ShapeDtypeStruct((rows, 8, width), f32)
    cells = rows * layers * width
    params = pltpu.CompilerParams(vmem_limit_bytes=16 * 1024 * 1024)

    def kernel(function, out_shape, work, name, scratch_shapes=()):
        cost = pl.CostEstimate(flops=work * cells, bytes_accessed=40 * cells, transcendentals=0)
        return pl.pallas_call(
            function,
            out_shape=out_shape,
            scratch_shapes=scratch_shapes,
            compiler_params=params,
            cost_estimate=cost,
            name=name,
        )

    axis_x, axis_y, axis_z, *gains = kernel(weights_kernel, [stack] * 6, 100, "weights")(
        waves, prior_p, prior_q, courant, epsilon, thomsen_delta, tilt_angle, azimuth
    )
    taps_first = band(width, FIRST, -1.0, SCALE_FIRST)
    taps_second = band(width, SECOND[1:], 1.0, SCALE_SECOND)
    work = pltpu.VMEM((rows, 8, width), f32)
    h_own, sum_own = kernel(interior_kernel, [stack] * 2, 100, "interior", [work] * 5)(
        waves, other, axis_x, axis_y, axis_z, taps_first, taps_second
    )
    outer, inner, h_own, sum_own = lax.optimization_barrier((outer, inner, h_own, sum_own))
    edges = jnp.concatenate([inner, outer], axis=0)
    edges_other = lax.ppermute(edges, "gz", cores)
    edge = jax.ShapeDtypeStruct((8, 8, width), f32)
    h_edge, sum_edge = kernel(functools.partial(halo_kernel, size), [edge] * 2, 100, "halo")(
        edges, axis_x, axis_y, h_own, sum_own, taps_first
    )

    own, factors = inline_blocks(rows)
    offsets = (-1, 1, -2, 2)
    pieces, gives, start = [], [], 0
    for offset in offsets:
        give = factors[offset][1]
        pad = give.shape[0] % 2
        pieces.append(np.pad(give, ((0, pad), (0, 0))))
        gives.append((start, 4 * (give.shape[0] + pad)))
        start += gives[-1][1]

    def parts(matrix):
        return [jnp.asarray(part) for part in split_bf16(matrix)]

    inline = parts(np.kron(np.concatenate(pieces), np.eye(4)))
    inline_own = parts(np.kron(own, np.eye(4)))
    flat = jax.ShapeDtypeStruct((layers * rows, width), f32)
    pressure, crossline, *sends = kernel(
        functools.partial(step_kernel, size, gives),
        [stack, flat] + [jax.ShapeDtypeStruct((count, width), f32) for _, count in gives],
        400,
        "step",
    )(
        edges,
        edges_other,
        h_own,
        sum_own,
        h_edge,
        sum_edge,
        axis_x,
        axis_z,
        *gains,
        *parts(np.concatenate(three_levels(width)).T),
        *inline,
    )
    received = [lax.ppermute(send, "xy", pair) for send, pair in zip(sends, pairs)]
    grid = jax.ShapeDtypeStruct(wave_p.shape, f32)
    next_p, next_q, mine = kernel(own_kernel, [grid, grid, flat], 100, "own")(
        pressure, crossline, *inline_own
    )
    outs = kernel(
        functools.partial(finish_kernel, [factors[offset][0] for offset in offsets]),
        [
            jax.ShapeDtypeStruct((count, layers, width), f32)
            for count in (rows // 2, rows // 4, rows // 8, rows // 8)
        ],
        20,
        "finish",
    )(mine, *received)
    return (next_p, next_q, *outs)


def solution(mesh):
    split = P(("shot", "xy"), "gz", None)
    shared = P("xy", "gz", None)
    return jax.shard_map(
        functools.partial(body, mesh.shape["xy"]),
        mesh=mesh,
        in_specs=(split,) * 4 + (shared,) * 5,
        out_specs=(split,) * 6,
        check_vma=False,
    )
```

```python
import functools

import jax
import jax.numpy as jnp
import numpy as np
from jax import lax
from jax.experimental import pallas as pl
from jax.experimental.pallas import tpu as pltpu
from jax.sharding import PartitionSpec as P

SECOND = (-205.0 / 72.0, 8.0 / 5.0, -1.0 / 5.0, 8.0 / 315.0, -1.0 / 560.0)
FIRST = (4.0 / 5.0, -1.0 / 5.0, 4.0 / 105.0, -1.0 / 280.0)
LIFT = (-1.586134342, -0.05298011854, 0.8829110762, 0.4435068522)
ZETA = 1.149604398
LANES = 128
SCALE_FIRST, SCALE_SECOND = 840.0, 5040.0


def lift_level(values):
    even, odd = values[0::2], values[1::2]
    odd = odd + LIFT[0] * (even + np.roll(even, -1, 0))
    even = even + LIFT[1] * (odd + np.roll(odd, 1, 0))
    odd = odd + LIFT[2] * (even + np.roll(even, -1, 0))
    even = even + LIFT[3] * (odd + np.roll(odd, 1, 0))
    return even * ZETA, odd * (1.0 / ZETA)


def three_levels(length):
    coarse, members = np.eye(length), []
    for _ in range(3):
        coarse, detail = lift_level(coarse)
        members.append(detail)
    return members + [coarse]


def band(taps, sign, scale):
    offset = np.arange(4 * LANES)[:, None] - LANES - np.arange(2 * LANES)[None]
    matrix = np.zeros(offset.shape)
    for k, tap in enumerate(taps, 1):
        value = float(np.round(tap * scale))
        matrix += value * (offset == k) + sign * value * (offset == -k)
    return jnp.asarray(matrix.astype(jnp.bfloat16))


def split_bf16(matrix):
    high = matrix.astype(jnp.bfloat16)
    low = (matrix - high.astype(np.float64)).astype(jnp.bfloat16)
    return high, low


def inline_blocks(rows):
    bricks, brick = 8, 4
    members = three_levels(rows * bricks)
    wanted = np.concatenate(
        [m[brick * len(m) // bricks : (brick + 1) * len(m) // bricks] for m in members]
    )

    def block(offset):
        return wanted[:, rows * (brick + offset) : rows * (brick + offset + 1)]

    factors = {}
    for offset in (-1, 1, -2, 2):
        left, sizes, right = np.linalg.svd(block(offset))
        rank = int((sizes > 1e-12).sum())
        root = np.sqrt(sizes[:rank])
        factors[offset] = (left[:, :rank] * root, root[:, None] * right[:rank])
    return block(0), factors


def sine_cosine(angle):
    turns = jnp.round(angle * (2.0 / np.pi))
    rest = angle - turns * 1.5703125
    rest = rest - turns * 4.837512969970703125e-4
    rest = rest - turns * 7.549789948768648e-8
    square = rest * rest
    sine = rest + rest * square * (
        -1.6666654611e-1 + square * (8.3321608736e-3 + square * -1.9515295891e-4)
    )
    cosine = (
        1.0
        - 0.5 * square
        + square
        * square
        * (4.166664568298827e-2 + square * (-1.388731625493765e-3 + square * 2.443315711809948e-5))
    )
    quarter = turns.astype(jnp.int32)
    swapped = (quarter & 1) == 1
    out_sine = jnp.where(swapped, cosine, sine)
    out_cosine = jnp.where(swapped, sine, cosine)
    out_sine = jnp.where((quarter & 2) == 2, -out_sine, out_sine)
    out_cosine = jnp.where(((quarter + 1) & 2) == 2, -out_cosine, out_cosine)
    return out_sine, out_cosine


def load_kernel(wave_p, wave_q, *rest):
    count = (len(rest) - 4) // 2
    sources, waves, targets = rest[:count], rest[count], rest[count + 1 : 2 * count + 1]
    field_p, field_q, arrived = rest[2 * count + 1 :]
    copies = [
        pltpu.make_async_copy(source, target, arrived.at[k])
        for k, (source, target) in enumerate(
            zip((wave_p, wave_q) + sources, (field_p, field_q) + targets)
        )
    ]
    for copy in copies:
        copy.start()
    for copy in copies[:2]:
        copy.wait()
    for x in range(waves.shape[0]):
        waves[x] = jnp.concatenate([field_p[x], field_q[x]], axis=0)
    for copy in copies[2:]:
        copy.wait()


def weights_kernel(
    waves, prior_p, prior_q, courant, epsilon, delta, tilt, azimuth, axis_x, axis_y, axis_z, gain_a, gain_b, base
):
    rows = waves.shape[0]
    top = lax.broadcasted_iota(jnp.int32, waves.shape[1:], 0) < 4

    def swap(value):
        return pltpu.roll(value, 4, 0)

    for x in range(rows):
        angles = jnp.concatenate(
            [tilt[x].astype(jnp.float32), azimuth[x].astype(jnp.float32)], axis=0
        )
        sine, cosine = sine_cosine(angles)
        sine_other, cosine_other = swap(sine), swap(cosine)
        sine_tilt = jnp.where(top, sine, sine_other)
        axis_x[x] = sine_tilt * jnp.where(top, cosine_other, cosine)
        axis_y[x] = sine * sine_other
        axis_z[x] = jnp.where(top, cosine, cosine_other)
        speed = courant[x].astype(jnp.float32)
        root = jnp.sqrt(1.0 + 2.0 * delta[x].astype(jnp.float32))
        stretch = 1.0 + 2.0 * epsilon[x].astype(jnp.float32)
        gain_a[x] = jnp.concatenate([speed * stretch, speed], axis=0)
        across = speed * root
        gain_b[x] = jnp.concatenate([across, across], axis=0)
        base[x] = 2.0 * waves[x] - jnp.concatenate([prior_p[x], prior_q[x]], axis=0)


def first_of(ahead, behind):
    total = FIRST[0] * (ahead[0] - behind[0])
    for k in range(1, 4):
        total = total + FIRST[k] * (ahead[k] - behind[k])
    return total


def second_of(centre, ahead, behind):
    total = SECOND[0] * centre
    for k in range(4):
        total = total + SECOND[k + 1] * (ahead[k] + behind[k])
    return total


def dot3(a_high, a_low, b_high, b_low):
    def dot(a, b):
        return jnp.dot(a, b, preferred_element_type=jnp.float32)

    rows = a_high.shape[0]
    both = dot(jnp.concatenate([a_high, a_low], axis=0), b_high)
    return both[:rows] + (both[rows:] + dot(a_high, b_low))


def halves(value):
    high = value.astype(jnp.bfloat16)
    return high, (value - high.astype(jnp.float32)).astype(jnp.bfloat16)


def depth_neighbours(own, far, lower):
    layer = lax.broadcasted_iota(jnp.int32, own.shape, 0) & 3
    up = far * jnp.where(lower, 1.0, 0.0)
    down = far * jnp.where(lower, 0.0, 1.0)
    ahead, behind = [], []
    for k in range(1, 4):
        ahead.append(jnp.where(layer < 4 - k, pltpu.roll(own, 8 - k, 0), pltpu.roll(up, 4 - k, 0)))
        behind.append(jnp.where(layer >= k, pltpu.roll(own, k, 0), pltpu.roll(down, 4 + k, 0)))
    return ahead + [up], behind + [down]


def across(parts, taps):
    width = parts.shape[1]
    blocks = []
    for start in range(0, width, 2 * LANES):
        stop = min(start + 2 * LANES, width)
        first = start - LANES
        low, high = max(first, 0), min(stop + LANES, width)
        block = taps[low - first : high - first, : stop - start]
        blocks.append(jnp.dot(parts[:, low:high], block, preferred_element_type=jnp.float32))
    return jnp.concatenate(blocks, axis=1)


def joined(parts, rows):
    return parts[:rows] + parts[rows:]


def interior_kernel(
    waves, other, axis_x, axis_y, axis_z, taps_first, taps_second, h_own, sum_own, dz, dzz, dy, dyy, dzy
):
    rows, sub, width = waves.shape
    flat = rows * sub
    lower = lax.axis_index("gz") == 0
    for x in range(rows):
        own = waves[x]
        ahead, behind = depth_neighbours(own, other[x], lower)
        dz[x] = first_of(ahead, behind)
        dzz[x] = second_of(own, ahead, behind)
    field = jnp.concatenate(halves(waves[...].reshape(flat, width)), axis=0)
    slope = jnp.concatenate(halves(dz[...].reshape(flat, width)), axis=0)
    dyy[...] = joined(across(field, taps_second), flat).reshape(waves.shape)
    dy[...] = joined(across(field, taps_first), flat).reshape(waves.shape)
    dzy[...] = joined(across(slope, taps_first), flat).reshape(waves.shape)
    for x in range(rows):
        centre = waves[x]
        dxx = SECOND[0] * centre
        dxy = jnp.zeros_like(centre)
        dxz = jnp.zeros_like(centre)
        for k in range(1, 5):
            for step in (k, -k):
                if 0 <= x + step < rows:
                    weight = FIRST[k - 1] if step > 0 else -FIRST[k - 1]
                    dxx = dxx + SECOND[k] * waves[x + step]
                    dxy = dxy + (weight / SCALE_FIRST) * dy[x + step]
                    dxz = dxz + weight * dz[x + step]
        cross = SECOND[0] * centre + (1.0 / SCALE_SECOND) * dyy[x]
        n_x, n_y, n_z = axis_x[x], axis_y[x], axis_z[x]
        h_one = n_x * (n_x * dxx + 2.0 * (n_y * dxy + n_z * dxz))
        h_one = h_one + n_y * (n_y * cross + (2.0 / SCALE_FIRST) * (n_z * dzy[x]))
        h_own[x] = h_one + n_z * (n_z * dzz[x])
        sum_own[x] = dxx + cross + dzz[x]


def halo_rows(size, edges):
    place = lax.axis_index("xy")
    even = place % 2 == 0
    left_at, right_at = jnp.where(even, 4, 0), jnp.where(even, 0, 4)
    left_in = jnp.where(place > 0, 1.0, 0.0)
    right_in = jnp.where(place < size - 1, 1.0, 0.0)
    before = [edges[left_at + x] * left_in for x in range(4)]
    return before + [edges[right_at + x] * right_in for x in range(4)]


def reach(values, row, coefficients, sign):
    total = None
    for k in range(1, 5):
        at = row + 4 - k if row < 4 else row + k - 4
        if (row < 4 and 0 <= at < 4) or (row >= 4 and 4 <= at < 8):
            term = (coefficients[k - 1] * (sign if row < 4 else 1.0)) * values[at]
            total = term if total is None else total + term
    return total


def halo_kernel(size, edges, axis_x, axis_y, h_own, sum_own, taps_first, h_edge, sum_edge):
    rows, sub, width = h_own.shape
    values = halo_rows(size, edges)
    parts = jnp.concatenate(halves(jnp.concatenate(values, axis=0)), axis=0)
    slopes = joined(across(parts, taps_first), 8 * sub)
    slopes = [slopes[sub * x : sub * x + sub] for x in range(8)]
    for row in range(8):
        x = row if row < 4 else rows - 8 + row
        dxx = reach(values, row, SECOND[1:], 1.0)
        dxy = reach(slopes, row, [c / SCALE_FIRST for c in FIRST], -1.0)
        n_x = axis_x[x]
        h_edge[row] = h_own[x] + n_x * (n_x * dxx + 2.0 * (axis_y[x] * dxy))
        sum_edge[row] = sum_own[x] + dxx


def step_kernel(
    size,
    gives,
    edges,
    edges_other,
    h_own,
    sum_own,
    h_edge,
    sum_edge,
    axis_x,
    axis_z,
    gain_a,
    gain_b,
    base,
    across_high,
    across_low,
    inline_high,
    inline_low,
    pressure,
    crossline,
    *sends,
):
    rows, sub, width = h_own.shape
    lower = lax.axis_index("gz") == 0
    place = lax.axis_index("xy")
    even, early = place % 2 == 0, place % 4 < 2
    top = lax.broadcasted_iota(jnp.int32, (sub, width), 0) < 4

    slopes = [
        first_of(*depth_neighbours(own, far, lower))
        for own, far in zip(halo_rows(size, edges), halo_rows(size, edges_other))
    ]
    for x in range(rows):
        row = x if x < 4 else x - rows + 8
        if 4 <= x < rows - 4:
            h_one, total = h_own[x], sum_own[x]
        else:
            dxz = reach(slopes, row, FIRST, -1.0)
            h_one, total = h_edge[row] + 2.0 * (axis_x[x] * axis_z[x] * dxz), sum_edge[row]
        mixed = jnp.where(top, total - h_one, h_one)
        pressure[x] = base[x] + gain_a[x] * mixed + gain_b[x] * pltpu.roll(mixed, 4, 0)

    packed = jnp.concatenate(
        [
            jnp.where(top, pressure[x], pltpu.roll(pressure[x + 1], 4, 0))
            for x in range(0, rows, 2)
        ],
        axis=0,
    )
    transformed = dot3(*halves(packed), across_high[...], across_low[...])
    crossline[...] = transformed
    parts = dot3(inline_high[...], inline_low[...], *halves(transformed))
    to_next, to_previous, to_second_next, to_second_previous = (
        parts[start : start + count] for start, count in gives
    )
    sends[0][...] = jnp.where(even, to_previous, to_next)
    sends[1][...] = jnp.where(even, to_next, to_previous)
    sends[2][...] = jnp.where(early, to_second_previous, to_second_next)
    sends[3][...] = jnp.where(early, to_second_next, to_second_previous)


def own_kernel(pressure, crossline, own_high, own_low, next_p, next_q, mine):
    for x in range(pressure.shape[0]):
        next_p[x] = pressure[x, :4]
        next_q[x] = pressure[x, 4:]
    mine[...] = dot3(own_high[...], own_low[...], *halves(crossline[...]))


def finish_kernel(takes, mine, *rest):
    outer, inner, outer_second, inner_second = (ref[...] for ref in rest[:4])
    outs = rest[4:]
    place = lax.axis_index("xy")
    even, early = place % 2 == 0, place % 4 < 2
    received = (
        jnp.where(even, outer, inner),
        jnp.where(even, inner, outer),
        jnp.where(early, outer_second, inner_second),
        jnp.where(early, inner_second, outer_second),
    )
    at = 0
    for out in outs:
        for row in range(out.shape[0]):
            total = mine[4 * at : 4 * at + 4]
            for take, got in zip(takes, received):
                for j in range(take.shape[1]):
                    factor = float(take[at, j])
                    if abs(factor) > 1e-13:
                        total = total + factor * got[4 * j : 4 * j + 4]
            out[row] = total
            at += 1


def pair_swaps(size):
    one = [1 if i % 2 == 0 else -1 for i in range(size)]
    two = [2 if i % 4 < 2 else -2 for i in range(size)]
    return [
        [(i, (i - one[i]) % size) for i in range(size)],
        [(i, i + one[i]) for i in range(size)],
        [(i, (i - two[i]) % size) for i in range(size)],
        [(i, i + two[i]) for i in range(size)],
    ]


def body(size, wave_p, wave_q, prior_p, prior_q, courant, epsilon, thomsen_delta, tilt_angle, azimuth):
    rows, layers, width = wave_p.shape
    f32 = jnp.float32
    even = lax.axis_index("xy") % 2 == 0
    pairs = pair_swaps(size)
    cores = [(0, 1), (1, 0)]
    stack = jax.ShapeDtypeStruct((rows, 8, width), f32)
    cells = rows * layers * width
    params = pltpu.CompilerParams(vmem_limit_bytes=16 * 1024 * 1024)

    def kernel(function, out_shape, work, name, scratch_shapes=(), **specs):
        cost = pl.CostEstimate(flops=work * cells, bytes_accessed=40 * cells, transcendentals=0)
        return pl.pallas_call(
            function,
            out_shape=out_shape,
            scratch_shapes=scratch_shapes,
            compiler_params=params,
            cost_estimate=cost,
            name=name,
            **specs,
        )

    others = (prior_p, prior_q, courant, epsilon, thomsen_delta, tilt_angle, azimuth)
    field = pltpu.VMEM(wave_p.shape, f32)
    waves, *others = kernel(
        load_kernel,
        [stack] + [jax.ShapeDtypeStruct(array.shape, array.dtype) for array in others],
        10,
        "load",
        [field, field, pltpu.SemaphoreType.DMA((2 + len(others),))],
        in_specs=[pl.BlockSpec(memory_space=pltpu.HBM)] * (2 + len(others)),
        out_specs=[pl.BlockSpec(memory_space=pltpu.VMEM)] * (1 + len(others)),
    )(wave_p, wave_q, *others)
    leading, last = waves[:4], waves[rows - 4 :]
    open_outer = [
        (2 * i + g, 2 * i + 1 - g) if abs(i - j) > 1 else (2 * i + g, 2 * j + g)
        for i, j in pairs[0]
        for g in range(2)
    ]
    other = lax.ppermute(waves, "gz", cores)
    inner = lax.ppermute(jnp.where(even, last, leading), "xy", pairs[1])
    outer = lax.ppermute(jnp.where(even, leading, last), ("xy", "gz"), open_outer)

    axis_x, axis_y, axis_z, *gains = kernel(weights_kernel, [stack] * 6, 100, "weights")(
        waves, *others
    )
    taps_first = band(FIRST, -1.0, SCALE_FIRST)
    taps_second = band(SECOND[1:], 1.0, SCALE_SECOND)
    work = pltpu.VMEM((rows, 8, width), f32)
    h_own, sum_own = kernel(interior_kernel, [stack] * 2, 100, "interior", [work] * 5)(
        waves, other, axis_x, axis_y, axis_z, taps_first, taps_second
    )
    outer, inner, h_own, sum_own = lax.optimization_barrier((outer, inner, h_own, sum_own))
    edges = jnp.concatenate([inner, outer], axis=0)
    edges_other = lax.ppermute(edges, "gz", cores)
    edge = jax.ShapeDtypeStruct((8, 8, width), f32)
    h_edge, sum_edge = kernel(functools.partial(halo_kernel, size), [edge] * 2, 100, "halo")(
        edges, axis_x, axis_y, h_own, sum_own, taps_first
    )

    own, factors = inline_blocks(rows)
    offsets = (-1, 1, -2, 2)
    pieces, gives, start = [], [], 0
    for offset in offsets:
        give = factors[offset][1]
        pad = give.shape[0] % 2
        pieces.append(np.pad(give, ((0, pad), (0, 0))))
        gives.append((start, 4 * (give.shape[0] + pad)))
        start += gives[-1][1]

    def parts(matrix):
        return [jnp.asarray(part) for part in split_bf16(matrix)]

    inline = parts(np.kron(np.concatenate(pieces), np.eye(4)))
    inline_own = parts(np.kron(own, np.eye(4)))
    flat = jax.ShapeDtypeStruct((layers * rows, width), f32)
    pressure, crossline, *sends = kernel(
        functools.partial(step_kernel, size, gives),
        [stack, flat] + [jax.ShapeDtypeStruct((count, width), f32) for _, count in gives],
        400,
        "step",
    )(
        edges,
        edges_other,
        h_own,
        sum_own,
        h_edge,
        sum_edge,
        axis_x,
        axis_z,
        *gains,
        *parts(np.concatenate(three_levels(width)).T),
        *inline,
    )
    received = [lax.ppermute(send, "xy", pair) for send, pair in zip(sends, pairs)]
    grid = jax.ShapeDtypeStruct(wave_p.shape, f32)
    next_p, next_q, mine = kernel(own_kernel, [grid, grid, flat], 100, "own")(
        pressure, crossline, *inline_own
    )
    outs = kernel(
        functools.partial(finish_kernel, [factors[offset][0] for offset in offsets]),
        [
            jax.ShapeDtypeStruct((count, layers, width), f32)
            for count in (rows // 2, rows // 4, rows // 8, rows // 8)
        ],
        20,
        "finish",
    )(mine, *received)
    return (next_p, next_q, *outs)


def solution(mesh):
    split = P(("shot", "xy"), "gz", None)
    shared = P("xy", "gz", None)
    return jax.shard_map(
        functools.partial(body, mesh.shape["xy"]),
        mesh=mesh,
        in_specs=(split,) * 4 + (shared,) * 5,
        out_specs=(split,) * 6,
        check_vma=False,
    )
```

```python
import functools

import jax
import jax.numpy as jnp
import numpy as np
from jax import lax
from jax.experimental import pallas as pl
from jax.experimental.pallas import tpu as pltpu
from jax.sharding import PartitionSpec as P

SECOND = (-205.0 / 72.0, 8.0 / 5.0, -1.0 / 5.0, 8.0 / 315.0, -1.0 / 560.0)
FIRST = (4.0 / 5.0, -1.0 / 5.0, 4.0 / 105.0, -1.0 / 280.0)
LIFT = (-1.586134342, -0.05298011854, 0.8829110762, 0.4435068522)
ZETA = 1.149604398
LANES = 128
SCALE_FIRST, SCALE_SECOND = 840.0, 5040.0


def lift_level(values):
    even, odd = values[0::2], values[1::2]
    odd = odd + LIFT[0] * (even + np.roll(even, -1, 0))
    even = even + LIFT[1] * (odd + np.roll(odd, 1, 0))
    odd = odd + LIFT[2] * (even + np.roll(even, -1, 0))
    even = even + LIFT[3] * (odd + np.roll(odd, 1, 0))
    return even * ZETA, odd * (1.0 / ZETA)


def three_levels(length):
    coarse, members = np.eye(length), []
    for _ in range(3):
        coarse, detail = lift_level(coarse)
        members.append(detail)
    return members + [coarse]


def split_bf16(matrix):
    high = matrix.astype(jnp.bfloat16)
    low = (matrix - high.astype(np.float64)).astype(jnp.bfloat16)
    return high, low


def inline_blocks(rows):
    bricks, brick = 8, 4
    members = three_levels(rows * bricks)
    wanted = np.concatenate(
        [m[brick * len(m) // bricks : (brick + 1) * len(m) // bricks] for m in members]
    )

    def block(offset):
        return wanted[:, rows * (brick + offset) : rows * (brick + offset + 1)]

    factors = {}
    for offset in (-1, 1, -2, 2):
        left, sizes, right = np.linalg.svd(block(offset))
        rank = int((sizes > 1e-12).sum())
        root = np.sqrt(sizes[:rank])
        factors[offset] = (left[:, :rank] * root, root[:, None] * right[:rank])
    return block(0), factors


def sine_cosine(angle):
    turns = jnp.round(angle * (2.0 / np.pi))
    rest = angle - turns * 1.5703125
    rest = rest - turns * 4.837512969970703125e-4
    rest = rest - turns * 7.549789948768648e-8
    square = rest * rest
    sine = rest + rest * square * (
        -1.6666654611e-1 + square * (8.3321608736e-3 + square * -1.9515295891e-4)
    )
    cosine = (
        1.0
        - 0.5 * square
        + square
        * square
        * (4.166664568298827e-2 + square * (-1.388731625493765e-3 + square * 2.443315711809948e-5))
    )
    quarter = turns.astype(jnp.int32)
    swapped = (quarter & 1) == 1
    out_sine = jnp.where(swapped, cosine, sine)
    out_cosine = jnp.where(swapped, sine, cosine)
    out_sine = jnp.where((quarter & 2) == 2, -out_sine, out_sine)
    out_cosine = jnp.where(((quarter + 1) & 2) == 2, -out_cosine, out_cosine)
    return out_sine, out_cosine


def band(shape, taps, sign, scale):
    offset = lax.broadcasted_iota(jnp.int32, shape, 0) - LANES
    offset = offset - lax.broadcasted_iota(jnp.int32, shape, 1)
    values = jnp.zeros(shape, jnp.float32)
    for k, tap in enumerate(taps, 1):
        values = jnp.where(jnp.abs(offset) == k, float(np.round(tap * scale)), values)
    if sign < 0:
        values = jnp.where(offset < 0, -values, values)
    return values.astype(jnp.bfloat16)


def weights_kernel(
    waves,
    prior_p,
    prior_q,
    courant,
    epsilon,
    delta,
    tilt,
    azimuth,
    axis_x,
    axis_y,
    axis_z,
    gain_a,
    gain_b,
    base,
    taps_first,
    taps_second,
):
    rows = waves.shape[0]
    taps_first[...] = band(taps_first.shape, FIRST, -1.0, SCALE_FIRST)
    taps_second[...] = band(taps_second.shape, SECOND[1:], 1.0, SCALE_SECOND)
    top = lax.broadcasted_iota(jnp.int32, waves.shape[1:], 0) < 4

    def swap(value):
        return pltpu.roll(value, 4, 0)

    for x in range(rows):
        angles = jnp.concatenate(
            [tilt[x].astype(jnp.float32), azimuth[x].astype(jnp.float32)], axis=0
        )
        sine, cosine = sine_cosine(angles)
        sine_other, cosine_other = swap(sine), swap(cosine)
        sine_tilt = jnp.where(top, sine, sine_other)
        axis_x[x] = sine_tilt * jnp.where(top, cosine_other, cosine)
        axis_y[x] = sine * sine_other
        axis_z[x] = jnp.where(top, cosine, cosine_other)
        speed = courant[x].astype(jnp.float32)
        root = jnp.sqrt(1.0 + 2.0 * delta[x].astype(jnp.float32))
        stretch = 1.0 + 2.0 * epsilon[x].astype(jnp.float32)
        gain_a[x] = jnp.concatenate([speed * stretch, speed], axis=0)
        across = speed * root
        gain_b[x] = jnp.concatenate([across, across], axis=0)
        base[x] = 2.0 * waves[x] - jnp.concatenate([prior_p[x], prior_q[x]], axis=0)


def first_of(ahead, behind):
    total = FIRST[0] * (ahead[0] - behind[0])
    for k in range(1, 4):
        total = total + FIRST[k] * (ahead[k] - behind[k])
    return total


def second_of(centre, ahead, behind):
    total = SECOND[0] * centre
    for k in range(4):
        total = total + SECOND[k + 1] * (ahead[k] + behind[k])
    return total


def dot3(a_high, a_low, b_high, b_low):
    def dot(a, b):
        return jnp.dot(a, b, preferred_element_type=jnp.float32)

    rows = a_high.shape[0]
    both = dot(jnp.concatenate([a_high, a_low], axis=0), b_high)
    return both[:rows] + (both[rows:] + dot(a_high, b_low))


def halves(value):
    high = value.astype(jnp.bfloat16)
    return high, (value - high.astype(jnp.float32)).astype(jnp.bfloat16)


def depth_neighbours(own, far, lower):
    layer = lax.broadcasted_iota(jnp.int32, own.shape, 0) & 3
    up = far * jnp.where(lower, 1.0, 0.0)
    down = far * jnp.where(lower, 0.0, 1.0)
    ahead, behind = [], []
    for k in range(1, 4):
        ahead.append(jnp.where(layer < 4 - k, pltpu.roll(own, 8 - k, 0), pltpu.roll(up, 4 - k, 0)))
        behind.append(jnp.where(layer >= k, pltpu.roll(own, k, 0), pltpu.roll(down, 4 + k, 0)))
    return ahead + [up], behind + [down]


def across(parts, taps):
    width = parts.shape[1]
    blocks = []
    for start in range(0, width, 2 * LANES):
        stop = min(start + 2 * LANES, width)
        first = start - LANES
        low, high = max(first, 0), min(stop + LANES, width)
        block = taps[low - first : high - first, : stop - start]
        blocks.append(jnp.dot(parts[:, low:high], block, preferred_element_type=jnp.float32))
    return jnp.concatenate(blocks, axis=1)


def joined(parts, rows):
    return parts[:rows] + parts[rows:]


def interior_kernel(
    waves, other, axis_x, axis_y, axis_z, taps_first, taps_second, h_own, sum_own, dz, dzz, dy, dyy, dzy
):
    rows, sub, width = waves.shape
    flat = rows * sub
    lower = lax.axis_index("gz") == 0
    for x in range(rows):
        own = waves[x]
        ahead, behind = depth_neighbours(own, other[x], lower)
        dz[x] = first_of(ahead, behind)
        dzz[x] = second_of(own, ahead, behind)
    field = jnp.concatenate(halves(waves[...].reshape(flat, width)), axis=0)
    slope = jnp.concatenate(halves(dz[...].reshape(flat, width)), axis=0)
    dyy[...] = joined(across(field, taps_second), flat).reshape(waves.shape)
    dy[...] = joined(across(field, taps_first), flat).reshape(waves.shape)
    dzy[...] = joined(across(slope, taps_first), flat).reshape(waves.shape)
    for x in range(rows):
        centre = waves[x]
        dxx = SECOND[0] * centre
        dxy = jnp.zeros_like(centre)
        dxz = jnp.zeros_like(centre)
        for k in range(1, 5):
            for step in (k, -k):
                if 0 <= x + step < rows:
                    weight = FIRST[k - 1] if step > 0 else -FIRST[k - 1]
                    dxx = dxx + SECOND[k] * waves[x + step]
                    dxy = dxy + (weight / SCALE_FIRST) * dy[x + step]
                    dxz = dxz + weight * dz[x + step]
        cross = SECOND[0] * centre + (1.0 / SCALE_SECOND) * dyy[x]
        n_x, n_y, n_z = axis_x[x], axis_y[x], axis_z[x]
        h_one = n_x * (n_x * dxx + 2.0 * (n_y * dxy + n_z * dxz))
        h_one = h_one + n_y * (n_y * cross + (2.0 / SCALE_FIRST) * (n_z * dzy[x]))
        h_own[x] = h_one + n_z * (n_z * dzz[x])
        sum_own[x] = dxx + cross + dzz[x]


def halo_rows(size, edges):
    place = lax.axis_index("xy")
    even = place % 2 == 0
    left_at, right_at = jnp.where(even, 0, 4), jnp.where(even, 4, 0)
    left_in = jnp.where(place > 0, 1.0, 0.0)
    right_in = jnp.where(place < size - 1, 1.0, 0.0)
    before = [edges[left_at + x] * left_in for x in range(4)]
    return before + [edges[right_at + x] * right_in for x in range(4)]


def reach(values, row, coefficients, sign):
    total = None
    for k in range(1, 5):
        at = row + 4 - k if row < 4 else row + k - 4
        if (row < 4 and 0 <= at < 4) or (row >= 4 and 4 <= at < 8):
            term = (coefficients[k - 1] * (sign if row < 4 else 1.0)) * values[at]
            total = term if total is None else total + term
    return total


def halo_kernel(size, edges, axis_x, axis_y, h_own, sum_own, taps_first, h_edge, sum_edge):
    rows, sub, width = h_own.shape
    values = halo_rows(size, edges)
    parts = jnp.concatenate(halves(jnp.concatenate(values, axis=0)), axis=0)
    slopes = joined(across(parts, taps_first), 8 * sub)
    slopes = [slopes[sub * x : sub * x + sub] for x in range(8)]
    for row in range(8):
        x = row if row < 4 else rows - 8 + row
        dxx = reach(values, row, SECOND[1:], 1.0)
        dxy = reach(slopes, row, [c / SCALE_FIRST for c in FIRST], -1.0)
        n_x = axis_x[x]
        h_edge[row] = h_own[x] + n_x * (n_x * dxx + 2.0 * (axis_y[x] * dxy))
        sum_edge[row] = sum_own[x] + dxx


def step_kernel(
    size,
    gives,
    edges,
    edges_other,
    h_own,
    sum_own,
    h_edge,
    sum_edge,
    axis_x,
    axis_z,
    gain_a,
    gain_b,
    base,
    across_high,
    across_low,
    inline_high,
    inline_low,
    pressure,
    crossline,
    *sends,
):
    rows, sub, width = h_own.shape
    lower = lax.axis_index("gz") == 0
    place = lax.axis_index("xy")
    even, early = place % 2 == 0, place % 4 < 2
    top = lax.broadcasted_iota(jnp.int32, (sub, width), 0) < 4

    slopes = [
        first_of(*depth_neighbours(own, far, lower))
        for own, far in zip(halo_rows(size, edges), halo_rows(size, edges_other))
    ]
    for x in range(rows):
        row = x if x < 4 else x - rows + 8
        if 4 <= x < rows - 4:
            h_one, total = h_own[x], sum_own[x]
        else:
            dxz = reach(slopes, row, FIRST, -1.0)
            h_one, total = h_edge[row] + 2.0 * (axis_x[x] * axis_z[x] * dxz), sum_edge[row]
        mixed = jnp.where(top, total - h_one, h_one)
        pressure[x] = base[x] + gain_a[x] * mixed + gain_b[x] * pltpu.roll(mixed, 4, 0)

    packed = jnp.concatenate(
        [
            jnp.where(top, pressure[x], pltpu.roll(pressure[x + 1], 4, 0))
            for x in range(0, rows, 2)
        ],
        axis=0,
    )
    transformed = dot3(*halves(packed), across_high[...], across_low[...])
    crossline[...] = transformed
    parts = dot3(inline_high[...], inline_low[...], *halves(transformed))
    to_next, to_previous, to_second_next, to_second_previous = (
        parts[start : start + count] for start, count in gives
    )
    sends[0][...] = jnp.where(even, to_previous, to_next)
    sends[1][...] = jnp.where(even, to_next, to_previous)
    sends[2][...] = jnp.where(early, to_second_previous, to_second_next)
    sends[3][...] = jnp.where(early, to_second_next, to_second_previous)


def own_kernel(pressure, crossline, own_high, own_low, next_p, next_q, mine):
    for x in range(pressure.shape[0]):
        next_p[x] = pressure[x, :4]
        next_q[x] = pressure[x, 4:]
    mine[...] = dot3(own_high[...], own_low[...], *halves(crossline[...]))


def finish_kernel(takes, mine, *rest):
    outer, inner, outer_second, inner_second = (ref[...] for ref in rest[:4])
    outs = rest[4:]
    place = lax.axis_index("xy")
    even, early = place % 2 == 0, place % 4 < 2
    received = (
        jnp.where(even, outer, inner),
        jnp.where(even, inner, outer),
        jnp.where(early, outer_second, inner_second),
        jnp.where(early, inner_second, outer_second),
    )
    at = 0
    for out in outs:
        for row in range(out.shape[0]):
            total = mine[4 * at : 4 * at + 4]
            for take, got in zip(takes, received):
                for j in range(take.shape[1]):
                    factor = float(take[at, j])
                    if abs(factor) > 1e-13:
                        total = total + factor * got[4 * j : 4 * j + 4]
            out[row] = total
            at += 1


def pair_swaps(size):
    one = [1 if i % 2 == 0 else -1 for i in range(size)]
    two = [2 if i % 4 < 2 else -2 for i in range(size)]
    return [
        [(i, (i - one[i]) % size) for i in range(size)],
        [(i, i + one[i]) for i in range(size)],
        [(i, (i - two[i]) % size) for i in range(size)],
        [(i, i + two[i]) for i in range(size)],
    ]


def body(size, wave_p, wave_q, prior_p, prior_q, courant, epsilon, thomsen_delta, tilt_angle, azimuth):
    rows, layers, width = wave_p.shape
    f32 = jnp.float32
    even = lax.axis_index("xy") % 2 == 0
    pairs = pair_swaps(size)
    cores = [(0, 1), (1, 0)]
    stack = jax.ShapeDtypeStruct((rows, 8, width), f32)
    cells = rows * layers * width
    params = pltpu.CompilerParams(vmem_limit_bytes=16 * 1024 * 1024)

    def kernel(function, out_shape, work, name, scratch_shapes=()):
        cost = pl.CostEstimate(flops=work * cells, bytes_accessed=40 * cells, transcendentals=0)
        return pl.pallas_call(
            function,
            out_shape=out_shape,
            scratch_shapes=scratch_shapes,
            compiler_params=params,
            cost_estimate=cost,
            name=name,
        )

    waves = lax.optimization_barrier(jnp.concatenate([wave_p, wave_q], axis=1))
    leading, last = waves[:4], waves[rows - 4 :]
    open_outer = [
        (2 * i + g, 2 * i + 1 - g) if abs(i - j) > 1 else (2 * i + g, 2 * j + g)
        for i, j in pairs[0]
        for g in range(2)
    ]
    other = lax.ppermute(waves, "gz", cores)
    inner = lax.ppermute(jnp.where(even, last, leading), "xy", pairs[1])
    outer = lax.ppermute(jnp.where(even, leading, last), ("xy", "gz"), open_outer)

    taps = jax.ShapeDtypeStruct((4 * LANES, 2 * LANES), jnp.bfloat16)
    axis_x, axis_y, axis_z, *gains, taps_first, taps_second = kernel(
        weights_kernel, [stack] * 6 + [taps] * 2, 100, "weights"
    )(waves, prior_p, prior_q, courant, epsilon, thomsen_delta, tilt_angle, azimuth)
    work = pltpu.VMEM((rows, 8, width), f32)
    h_own, sum_own = kernel(interior_kernel, [stack] * 2, 100, "interior", [work] * 5)(
        waves, other, axis_x, axis_y, axis_z, taps_first, taps_second
    )
    outer, inner, h_own, sum_own = lax.optimization_barrier((outer, inner, h_own, sum_own))
    edges = jnp.concatenate([outer, inner], axis=0)
    edges_other = lax.ppermute(edges, "gz", cores)
    edge = jax.ShapeDtypeStruct((8, 8, width), f32)
    h_edge, sum_edge = kernel(functools.partial(halo_kernel, size), [edge] * 2, 100, "halo")(
        edges, axis_x, axis_y, h_own, sum_own, taps_first
    )

    own, factors = inline_blocks(rows)
    offsets = (-1, 1, -2, 2)
    pieces, gives, start = [], [], 0
    for offset in offsets:
        give = factors[offset][1]
        pad = give.shape[0] % 2
        pieces.append(np.pad(give, ((0, pad), (0, 0))))
        gives.append((start, 4 * (give.shape[0] + pad)))
        start += gives[-1][1]

    def parts(matrix):
        return [jnp.asarray(part) for part in split_bf16(matrix)]

    inline = parts(np.kron(np.concatenate(pieces), np.eye(4)))
    inline_own = parts(np.kron(own, np.eye(4)))
    flat = jax.ShapeDtypeStruct((layers * rows, width), f32)
    pressure, crossline, *sends = kernel(
        functools.partial(step_kernel, size, gives),
        [stack, flat] + [jax.ShapeDtypeStruct((count, width), f32) for _, count in gives],
        400,
        "step",
    )(
        edges,
        edges_other,
        h_own,
        sum_own,
        h_edge,
        sum_edge,
        axis_x,
        axis_z,
        *gains,
        *parts(np.concatenate(three_levels(width)).T),
        *inline,
    )
    received = [lax.ppermute(send, "xy", pair) for send, pair in zip(sends, pairs)]
    grid = jax.ShapeDtypeStruct(wave_p.shape, f32)
    next_p, next_q, mine = kernel(own_kernel, [grid, grid, flat], 100, "own")(
        pressure, crossline, *inline_own
    )
    outs = kernel(
        functools.partial(finish_kernel, [factors[offset][0] for offset in offsets]),
        [
            jax.ShapeDtypeStruct((count, layers, width), f32)
            for count in (rows // 2, rows // 4, rows // 8, rows // 8)
        ],
        20,
        "finish",
    )(mine, *received)
    return (next_p, next_q, *outs)


def solution(mesh):
    split = P(("shot", "xy"), "gz", None)
    shared = P("xy", "gz", None)
    return jax.shard_map(
        functools.partial(body, mesh.shape["xy"]),
        mesh=mesh,
        in_specs=(split,) * 4 + (shared,) * 5,
        out_specs=(split,) * 6,
        check_vma=False,
    )
```

```python
import functools

import jax
import jax.numpy as jnp
import numpy as np
from jax import lax
from jax.experimental import pallas as pl
from jax.experimental.pallas import tpu as pltpu
from jax.sharding import PartitionSpec as P

SECOND = (-205.0 / 72.0, 8.0 / 5.0, -1.0 / 5.0, 8.0 / 315.0, -1.0 / 560.0)
FIRST = (4.0 / 5.0, -1.0 / 5.0, 4.0 / 105.0, -1.0 / 280.0)
LIFT = (-1.586134342, -0.05298011854, 0.8829110762, 0.4435068522)
ZETA = 1.149604398
LANES = 128
SCALE_FIRST, SCALE_SECOND = 840.0, 5040.0


def lift_level(values):
    even, odd = values[0::2], values[1::2]
    odd = odd + LIFT[0] * (even + np.roll(even, -1, 0))
    even = even + LIFT[1] * (odd + np.roll(odd, 1, 0))
    odd = odd + LIFT[2] * (even + np.roll(even, -1, 0))
    even = even + LIFT[3] * (odd + np.roll(odd, 1, 0))
    return even * ZETA, odd * (1.0 / ZETA)


def three_levels(length):
    coarse, members = np.eye(length), []
    for _ in range(3):
        coarse, detail = lift_level(coarse)
        members.append(detail)
    return members + [coarse]


def split_bf16(matrix):
    high = matrix.astype(jnp.bfloat16)
    low = (matrix - high.astype(np.float64)).astype(jnp.bfloat16)
    return high, low


def inline_blocks(rows):
    bricks, brick = 8, 4
    members = three_levels(rows * bricks)
    wanted = np.concatenate(
        [m[brick * len(m) // bricks : (brick + 1) * len(m) // bricks] for m in members]
    )

    def block(offset):
        return wanted[:, rows * (brick + offset) : rows * (brick + offset + 1)]

    factors = {}
    for offset in (-1, 1, -2, 2):
        left, sizes, right = np.linalg.svd(block(offset))
        rank = int((sizes > 1e-12).sum())
        root = np.sqrt(sizes[:rank])
        factors[offset] = (left[:, :rank] * root, root[:, None] * right[:rank])
    return block(0), factors


def sine_cosine(angle):
    turns = jnp.round(angle * (2.0 / np.pi))
    rest = angle - turns * 1.5703125
    rest = rest - turns * 4.837512969970703125e-4
    rest = rest - turns * 7.549789948768648e-8
    square = rest * rest
    sine = rest + rest * square * (
        -1.6666654611e-1 + square * (8.3321608736e-3 + square * -1.9515295891e-4)
    )
    cosine = (
        1.0
        - 0.5 * square
        + square
        * square
        * (4.166664568298827e-2 + square * (-1.388731625493765e-3 + square * 2.443315711809948e-5))
    )
    quarter = turns.astype(jnp.int32)
    swapped = (quarter & 1) == 1
    out_sine = jnp.where(swapped, cosine, sine)
    out_cosine = jnp.where(swapped, sine, cosine)
    out_sine = jnp.where((quarter & 2) == 2, -out_sine, out_sine)
    out_cosine = jnp.where(((quarter + 1) & 2) == 2, -out_cosine, out_cosine)
    return out_sine, out_cosine


def band(shape, taps, sign, scale):
    offset = lax.broadcasted_iota(jnp.int32, shape, 0) - LANES
    offset = offset - lax.broadcasted_iota(jnp.int32, shape, 1)
    values = jnp.zeros(shape, jnp.float32)
    for k, tap in enumerate(taps, 1):
        values = jnp.where(jnp.abs(offset) == k, float(np.round(tap * scale)), values)
    if sign < 0:
        values = jnp.where(offset < 0, -values, values)
    return values.astype(jnp.bfloat16)


def weights_kernel(
    waves,
    prior_p,
    prior_q,
    courant,
    epsilon,
    delta,
    tilt,
    azimuth,
    axis_x,
    axis_y,
    axis_z,
    gain_a,
    gain_b,
    base,
    taps_first,
    taps_second,
):
    rows = waves.shape[0]
    taps_first[...] = band(taps_first.shape, FIRST, -1.0, SCALE_FIRST)
    taps_second[...] = band(taps_second.shape, SECOND[1:], 1.0, SCALE_SECOND)
    top = lax.broadcasted_iota(jnp.int32, waves.shape[1:], 0) < 4

    def swap(value):
        return pltpu.roll(value, 4, 0)

    for x in range(rows):
        angles = jnp.concatenate(
            [tilt[x].astype(jnp.float32), azimuth[x].astype(jnp.float32)], axis=0
        )
        sine, cosine = sine_cosine(angles)
        sine_other, cosine_other = swap(sine), swap(cosine)
        sine_tilt = jnp.where(top, sine, sine_other)
        axis_x[x] = sine_tilt * jnp.where(top, cosine_other, cosine)
        axis_y[x] = sine * sine_other
        axis_z[x] = jnp.where(top, cosine, cosine_other)
        speed = courant[x].astype(jnp.float32)
        root = jnp.sqrt(1.0 + 2.0 * delta[x].astype(jnp.float32))
        stretch = 1.0 + 2.0 * epsilon[x].astype(jnp.float32)
        gain_a[x] = jnp.concatenate([speed * stretch, speed], axis=0)
        across = speed * root
        gain_b[x] = jnp.concatenate([across, across], axis=0)
        base[x] = 2.0 * waves[x] - jnp.concatenate([prior_p[x], prior_q[x]], axis=0)


def first_of(ahead, behind):
    total = FIRST[0] * (ahead[0] - behind[0])
    for k in range(1, 4):
        total = total + FIRST[k] * (ahead[k] - behind[k])
    return total


def second_of(centre, ahead, behind):
    total = SECOND[0] * centre
    for k in range(4):
        total = total + SECOND[k + 1] * (ahead[k] + behind[k])
    return total


def dot3(a_high, a_low, b_high, b_low):
    def dot(a, b):
        return jnp.dot(a, b, preferred_element_type=jnp.float32)

    rows = a_high.shape[0]
    both = dot(jnp.concatenate([a_high, a_low], axis=0), b_high)
    return both[:rows] + (both[rows:] + dot(a_high, b_low))


def halves(value):
    high = value.astype(jnp.bfloat16)
    return high, (value - high.astype(jnp.float32)).astype(jnp.bfloat16)


def depth_neighbours(own, far, lower):
    layer = lax.broadcasted_iota(jnp.int32, own.shape, 0) & 3
    up = far * jnp.where(lower, 1.0, 0.0)
    down = far * jnp.where(lower, 0.0, 1.0)
    ahead, behind = [], []
    for k in range(1, 4):
        ahead.append(jnp.where(layer < 4 - k, pltpu.roll(own, 8 - k, 0), pltpu.roll(up, 4 - k, 0)))
        behind.append(jnp.where(layer >= k, pltpu.roll(own, k, 0), pltpu.roll(down, 4 + k, 0)))
    return ahead + [up], behind + [down]


def across(parts, taps):
    width = parts.shape[1]
    blocks = []
    for start in range(0, width, 2 * LANES):
        stop = min(start + 2 * LANES, width)
        first = start - LANES
        low, high = max(first, 0), min(stop + LANES, width)
        block = taps[low - first : high - first, : stop - start]
        blocks.append(jnp.dot(parts[:, low:high], block, preferred_element_type=jnp.float32))
    return jnp.concatenate(blocks, axis=1)


def joined(parts, rows):
    return parts[:rows] + parts[rows:]


def interior_kernel(
    waves, other, axis_x, axis_y, axis_z, taps_first, taps_second, h_own, sum_own, dz, dzz, dy, dyy, dzy
):
    rows, sub, width = waves.shape
    flat = rows * sub
    lower = lax.axis_index("gz") == 0
    for x in range(rows):
        own = waves[x]
        ahead, behind = depth_neighbours(own, other[x], lower)
        dz[x] = first_of(ahead, behind)
        dzz[x] = second_of(own, ahead, behind)
    field = jnp.concatenate(halves(waves[...].reshape(flat, width)), axis=0)
    slope = jnp.concatenate(halves(dz[...].reshape(flat, width)), axis=0)
    dyy[...] = joined(across(field, taps_second), flat).reshape(waves.shape)
    dy[...] = joined(across(field, taps_first), flat).reshape(waves.shape)
    dzy[...] = joined(across(slope, taps_first), flat).reshape(waves.shape)
    for x in range(rows):
        centre = waves[x]
        dxx = SECOND[0] * centre
        dxy = jnp.zeros_like(centre)
        dxz = jnp.zeros_like(centre)
        for k in range(1, 5):
            for step in (k, -k):
                if 0 <= x + step < rows:
                    weight = FIRST[k - 1] if step > 0 else -FIRST[k - 1]
                    dxx = dxx + SECOND[k] * waves[x + step]
                    dxy = dxy + (weight / SCALE_FIRST) * dy[x + step]
                    dxz = dxz + weight * dz[x + step]
        cross = SECOND[0] * centre + (1.0 / SCALE_SECOND) * dyy[x]
        n_x, n_y, n_z = axis_x[x], axis_y[x], axis_z[x]
        h_one = n_x * (n_x * dxx + 2.0 * (n_y * dxy + n_z * dxz))
        h_one = h_one + n_y * (n_y * cross + (2.0 / SCALE_FIRST) * (n_z * dzy[x]))
        h_own[x] = h_one + n_z * (n_z * dzz[x])
        sum_own[x] = dxx + cross + dzz[x]


def halo_rows(size, edges):
    place = lax.axis_index("xy")
    even = place % 2 == 0
    left_at, right_at = jnp.where(even, 0, 4), jnp.where(even, 4, 0)
    left_in = jnp.where(place > 0, 1.0, 0.0)
    right_in = jnp.where(place < size - 1, 1.0, 0.0)
    before = [edges[left_at + x] * left_in for x in range(4)]
    return before + [edges[right_at + x] * right_in for x in range(4)]


def reach(values, row, coefficients, sign):
    total = None
    for k in range(1, 5):
        at = row + 4 - k if row < 4 else row + k - 4
        if (row < 4 and 0 <= at < 4) or (row >= 4 and 4 <= at < 8):
            term = (coefficients[k - 1] * (sign if row < 4 else 1.0)) * values[at]
            total = term if total is None else total + term
    return total


def halo_kernel(size, edges, axis_x, axis_y, h_own, sum_own, taps_first, h_edge, sum_edge):
    rows, sub, width = h_own.shape
    values = halo_rows(size, edges)
    parts = jnp.concatenate(halves(jnp.concatenate(values, axis=0)), axis=0)
    slopes = joined(across(parts, taps_first), 8 * sub)
    slopes = [slopes[sub * x : sub * x + sub] for x in range(8)]
    for row in range(8):
        x = row if row < 4 else rows - 8 + row
        dxx = reach(values, row, SECOND[1:], 1.0)
        dxy = reach(slopes, row, [c / SCALE_FIRST for c in FIRST], -1.0)
        n_x = axis_x[x]
        h_edge[row] = h_own[x] + n_x * (n_x * dxx + 2.0 * (axis_y[x] * dxy))
        sum_edge[row] = sum_own[x] + dxx


def step_kernel(
    size,
    gives,
    edges,
    edges_other,
    h_own,
    sum_own,
    h_edge,
    sum_edge,
    axis_x,
    axis_z,
    gain_a,
    gain_b,
    base,
    across_high,
    across_low,
    inline_high,
    inline_low,
    pressure,
    crossline,
    *sends,
):
    rows, sub, width = h_own.shape
    lower = lax.axis_index("gz") == 0
    place = lax.axis_index("xy")
    even, early = place % 2 == 0, place % 4 < 2
    top = lax.broadcasted_iota(jnp.int32, (sub, width), 0) < 4

    slopes = [
        first_of(*depth_neighbours(own, far, lower))
        for own, far in zip(halo_rows(size, edges), halo_rows(size, edges_other))
    ]
    for x in range(rows):
        row = x if x < 4 else x - rows + 8
        if 4 <= x < rows - 4:
            h_one, total = h_own[x], sum_own[x]
        else:
            dxz = reach(slopes, row, FIRST, -1.0)
            h_one, total = h_edge[row] + 2.0 * (axis_x[x] * axis_z[x] * dxz), sum_edge[row]
        mixed = jnp.where(top, total - h_one, h_one)
        pressure[x] = base[x] + gain_a[x] * mixed + gain_b[x] * pltpu.roll(mixed, 4, 0)

    packed = jnp.concatenate(
        [
            jnp.where(top, pressure[x], pltpu.roll(pressure[x + 1], 4, 0))
            for x in range(0, rows, 2)
        ],
        axis=0,
    )
    transformed = dot3(*halves(packed), across_high[...], across_low[...])
    crossline[...] = transformed
    parts = dot3(inline_high[...], inline_low[...], *halves(transformed))
    to_next, to_previous, to_second_next, to_second_previous = (
        parts[start : start + count] for start, count in gives
    )
    sends[0][...] = jnp.where(even, to_previous, to_next)
    sends[1][...] = jnp.where(even, to_next, to_previous)
    sends[2][...] = jnp.where(early, to_second_previous, to_second_next)
    sends[3][...] = jnp.where(early, to_second_next, to_second_previous)


def own_kernel(pressure, crossline, own_high, own_low, next_p, next_q, mine):
    for x in range(pressure.shape[0]):
        next_p[x] = pressure[x, :4]
        next_q[x] = pressure[x, 4:]
    mine[...] = dot3(own_high[...], own_low[...], *halves(crossline[...]))


def finish_kernel(takes, mine, *rest):
    outer, inner, outer_second, inner_second = (ref[...] for ref in rest[:4])
    outs = rest[4:]
    place = lax.axis_index("xy")
    even, early = place % 2 == 0, place % 4 < 2
    received = (
        jnp.where(even, outer, inner),
        jnp.where(even, inner, outer),
        jnp.where(early, outer_second, inner_second),
        jnp.where(early, inner_second, outer_second),
    )
    at = 0
    for out in outs:
        for row in range(out.shape[0]):
            total = mine[4 * at : 4 * at + 4]
            for take, got in zip(takes, received):
                for j in range(take.shape[1]):
                    factor = float(take[at, j])
                    if abs(factor) > 1e-13:
                        total = total + factor * got[4 * j : 4 * j + 4]
            out[row] = total
            at += 1


def pair_swaps(size):
    one = [1 if i % 2 == 0 else -1 for i in range(size)]
    two = [2 if i % 4 < 2 else -2 for i in range(size)]
    return [
        [(i, (i - one[i]) % size) for i in range(size)],
        [(i, i + one[i]) for i in range(size)],
        [(i, (i - two[i]) % size) for i in range(size)],
        [(i, i + two[i]) for i in range(size)],
    ]


def body(size, wave_p, wave_q, prior_p, prior_q, courant, epsilon, thomsen_delta, tilt_angle, azimuth):
    rows, layers, width = wave_p.shape
    f32 = jnp.float32
    even = lax.axis_index("xy") % 2 == 0
    pairs = pair_swaps(size)
    cores = [(0, 1), (1, 0)]
    stack = jax.ShapeDtypeStruct((rows, 8, width), f32)
    cells = rows * layers * width
    params = pltpu.CompilerParams(vmem_limit_bytes=16 * 1024 * 1024)

    def kernel(function, out_shape, work, name, scratch_shapes=()):
        cost = pl.CostEstimate(flops=work * cells, bytes_accessed=40 * cells, transcendentals=0)
        return pl.pallas_call(
            function,
            out_shape=out_shape,
            scratch_shapes=scratch_shapes,
            compiler_params=params,
            cost_estimate=cost,
            name=name,
        )

    waves = lax.optimization_barrier(jnp.concatenate([wave_p, wave_q], axis=1))
    leading, last = waves[:4], waves[rows - 4 :]
    open_outer = [
        (2 * i + g, 2 * i + 1 - g) if abs(i - j) > 1 else (2 * i + g, 2 * j + g)
        for i, j in pairs[0]
        for g in range(2)
    ]
    other = lax.ppermute(waves, "gz", cores)
    inner = lax.ppermute(jnp.where(even, last, leading), "xy", pairs[1])
    outer = lax.ppermute(jnp.where(even, leading, last), ("xy", "gz"), open_outer)

    taps = jax.ShapeDtypeStruct((4 * LANES, 2 * LANES), jnp.bfloat16)
    axis_x, axis_y, axis_z, *gains, taps_first, taps_second = kernel(
        weights_kernel, [stack] * 6 + [taps] * 2, 100, "weights"
    )(waves, prior_p, prior_q, courant, epsilon, thomsen_delta, tilt_angle, azimuth)
    work = pltpu.VMEM((rows, 8, width), f32)
    h_own, sum_own = kernel(interior_kernel, [stack] * 2, 100, "interior", [work] * 5)(
        waves, other, axis_x, axis_y, axis_z, taps_first, taps_second
    )
    h_own, sum_own, inner, outer = lax.optimization_barrier((h_own, sum_own, inner, outer))
    edges = jnp.concatenate([outer, inner], axis=0)
    edges_other = lax.ppermute(edges, "gz", cores)
    edge = jax.ShapeDtypeStruct((8, 8, width), f32)
    h_edge, sum_edge = kernel(functools.partial(halo_kernel, size), [edge] * 2, 100, "halo")(
        edges, axis_x, axis_y, h_own, sum_own, taps_first
    )

    own, factors = inline_blocks(rows)
    offsets = (-1, 1, -2, 2)
    pieces, gives, start = [], [], 0
    for offset in offsets:
        give = factors[offset][1]
        pad = give.shape[0] % 2
        pieces.append(np.pad(give, ((0, pad), (0, 0))))
        gives.append((start, 4 * (give.shape[0] + pad)))
        start += gives[-1][1]

    def parts(matrix):
        return [jnp.asarray(part) for part in split_bf16(matrix)]

    inline = parts(np.kron(np.concatenate(pieces), np.eye(4)))
    inline_own = parts(np.kron(own, np.eye(4)))
    flat = jax.ShapeDtypeStruct((layers * rows, width), f32)
    pressure, crossline, *sends = kernel(
        functools.partial(step_kernel, size, gives),
        [stack, flat] + [jax.ShapeDtypeStruct((count, width), f32) for _, count in gives],
        400,
        "step",
    )(
        edges,
        edges_other,
        h_own,
        sum_own,
        h_edge,
        sum_edge,
        axis_x,
        axis_z,
        *gains,
        *parts(np.concatenate(three_levels(width)).T),
        *inline,
    )
    received = [lax.ppermute(send, "xy", pair) for send, pair in zip(sends, pairs)]
    grid = jax.ShapeDtypeStruct(wave_p.shape, f32)
    next_p, next_q, mine = kernel(own_kernel, [grid, grid, flat], 100, "own")(
        pressure, crossline, *inline_own
    )
    outs = kernel(
        functools.partial(finish_kernel, [factors[offset][0] for offset in offsets]),
        [
            jax.ShapeDtypeStruct((count, layers, width), f32)
            for count in (rows // 2, rows // 4, rows // 8, rows // 8)
        ],
        20,
        "finish",
    )(mine, *received)
    return (next_p, next_q, *outs)


def solution(mesh):
    split = P(("shot", "xy"), "gz", None)
    shared = P("xy", "gz", None)
    return jax.shard_map(
        functools.partial(body, mesh.shape["xy"]),
        mesh=mesh,
        in_specs=(split,) * 4 + (shared,) * 5,
        out_specs=(split,) * 6,
        check_vma=False,
    )
```

```python
import functools

import jax
import jax.numpy as jnp
import numpy as np
from jax import lax
from jax.experimental import pallas as pl
from jax.experimental.pallas import tpu as pltpu
from jax.sharding import PartitionSpec as P

SECOND = (-205.0 / 72.0, 8.0 / 5.0, -1.0 / 5.0, 8.0 / 315.0, -1.0 / 560.0)
FIRST = (4.0 / 5.0, -1.0 / 5.0, 4.0 / 105.0, -1.0 / 280.0)
LIFT = (-1.586134342, -0.05298011854, 0.8829110762, 0.4435068522)
ZETA = 1.149604398
LANES = 128
SCALE_FIRST, SCALE_SECOND = 840.0, 5040.0


def lift_level(values):
    even, odd = values[0::2], values[1::2]
    odd = odd + LIFT[0] * (even + np.roll(even, -1, 0))
    even = even + LIFT[1] * (odd + np.roll(odd, 1, 0))
    odd = odd + LIFT[2] * (even + np.roll(even, -1, 0))
    even = even + LIFT[3] * (odd + np.roll(odd, 1, 0))
    return even * ZETA, odd * (1.0 / ZETA)


def three_levels(length):
    coarse, members = np.eye(length), []
    for _ in range(3):
        coarse, detail = lift_level(coarse)
        members.append(detail)
    return members + [coarse]


def split_bf16(matrix):
    high = matrix.astype(jnp.bfloat16)
    low = (matrix - high.astype(np.float64)).astype(jnp.bfloat16)
    return high, low


def inline_blocks(rows):
    bricks, brick = 8, 4
    members = three_levels(rows * bricks)
    wanted = np.concatenate(
        [m[brick * len(m) // bricks : (brick + 1) * len(m) // bricks] for m in members]
    )

    def block(offset):
        return wanted[:, rows * (brick + offset) : rows * (brick + offset + 1)]

    factors = {}
    for offset in (-1, 1, -2, 2):
        left, sizes, right = np.linalg.svd(block(offset))
        rank = int((sizes > 1e-12).sum())
        root = np.sqrt(sizes[:rank])
        factors[offset] = (left[:, :rank] * root, root[:, None] * right[:rank])
    return block(0), factors


def sine_cosine(angle):
    turns = jnp.round(angle * (2.0 / np.pi))
    rest = angle - turns * 1.5703125
    rest = rest - turns * 4.837512969970703125e-4
    rest = rest - turns * 7.549789948768648e-8
    square = rest * rest
    sine = rest + rest * square * (
        -1.6666654611e-1 + square * (8.3321608736e-3 + square * -1.9515295891e-4)
    )
    cosine = (
        1.0
        - 0.5 * square
        + square
        * square
        * (4.166664568298827e-2 + square * (-1.388731625493765e-3 + square * 2.443315711809948e-5))
    )
    quarter = turns.astype(jnp.int32)
    swapped = (quarter & 1) == 1
    out_sine = jnp.where(swapped, cosine, sine)
    out_cosine = jnp.where(swapped, sine, cosine)
    out_sine = jnp.where((quarter & 2) == 2, -out_sine, out_sine)
    out_cosine = jnp.where(((quarter + 1) & 2) == 2, -out_cosine, out_cosine)
    return out_sine, out_cosine


def band(shape, taps, sign, scale):
    offset = lax.broadcasted_iota(jnp.int32, shape, 0) - LANES
    offset = offset - lax.broadcasted_iota(jnp.int32, shape, 1)
    values = jnp.zeros(shape, jnp.float32)
    for k, tap in enumerate(taps, 1):
        values = jnp.where(jnp.abs(offset) == k, float(np.round(tap * scale)), values)
    if sign < 0:
        values = jnp.where(offset < 0, -values, values)
    return values.astype(jnp.bfloat16)


def weights_kernel(
    waves,
    prior_p,
    prior_q,
    courant,
    epsilon,
    delta,
    tilt,
    azimuth,
    axis_x,
    axis_y,
    axis_z,
    gain_a,
    gain_b,
    base,
    taps_first,
    taps_second,
):
    rows = waves.shape[0]
    taps_first[...] = band(taps_first.shape, FIRST, -1.0, SCALE_FIRST)
    taps_second[...] = band(taps_second.shape, SECOND[1:], 1.0, SCALE_SECOND)
    top = lax.broadcasted_iota(jnp.int32, waves.shape[1:], 0) < 4

    def swap(value):
        return pltpu.roll(value, 4, 0)

    for x in range(rows):
        angles = jnp.concatenate(
            [tilt[x].astype(jnp.float32), azimuth[x].astype(jnp.float32)], axis=0
        )
        sine, cosine = sine_cosine(angles)
        sine_other, cosine_other = swap(sine), swap(cosine)
        sine_tilt = jnp.where(top, sine, sine_other)
        axis_x[x] = sine_tilt * jnp.where(top, cosine_other, cosine)
        axis_y[x] = sine * sine_other
        axis_z[x] = jnp.where(top, cosine, cosine_other)
        speed = courant[x].astype(jnp.float32)
        root = jnp.sqrt(1.0 + 2.0 * delta[x].astype(jnp.float32))
        stretch = 1.0 + 2.0 * epsilon[x].astype(jnp.float32)
        gain_a[x] = jnp.concatenate([speed * stretch, speed], axis=0)
        across = speed * root
        gain_b[x] = jnp.concatenate([across, across], axis=0)
        base[x] = 2.0 * waves[x] - jnp.concatenate([prior_p[x], prior_q[x]], axis=0)


def first_of(ahead, behind):
    total = FIRST[0] * (ahead[0] - behind[0])
    for k in range(1, 4):
        total = total + FIRST[k] * (ahead[k] - behind[k])
    return total


def second_of(centre, ahead, behind):
    total = SECOND[0] * centre
    for k in range(4):
        total = total + SECOND[k + 1] * (ahead[k] + behind[k])
    return total


def dot3(a_high, a_low, b_high, b_low):
    def dot(a, b):
        return jnp.dot(a, b, preferred_element_type=jnp.float32)

    rows = a_high.shape[0]
    both = dot(jnp.concatenate([a_high, a_low], axis=0), b_high)
    return both[:rows] + (both[rows:] + dot(a_high, b_low))


def halves(value):
    high = value.astype(jnp.bfloat16)
    return high, (value - high.astype(jnp.float32)).astype(jnp.bfloat16)


def depth_neighbours(own, far, lower):
    layer = lax.broadcasted_iota(jnp.int32, own.shape, 0) & 3
    up = far * jnp.where(lower, 1.0, 0.0)
    down = far * jnp.where(lower, 0.0, 1.0)
    ahead, behind = [], []
    for k in range(1, 4):
        ahead.append(jnp.where(layer < 4 - k, pltpu.roll(own, 8 - k, 0), pltpu.roll(up, 4 - k, 0)))
        behind.append(jnp.where(layer >= k, pltpu.roll(own, k, 0), pltpu.roll(down, 4 + k, 0)))
    return ahead + [up], behind + [down]


def across(parts, taps):
    width = parts.shape[1]
    blocks = []
    for start in range(0, width, 2 * LANES):
        stop = min(start + 2 * LANES, width)
        first = start - LANES
        low, high = max(first, 0), min(stop + LANES, width)
        block = taps[low - first : high - first, : stop - start]
        blocks.append(jnp.dot(parts[:, low:high], block, preferred_element_type=jnp.float32))
    return jnp.concatenate(blocks, axis=1)


def joined(parts, rows):
    return parts[:rows] + parts[rows:]


def interior_kernel(waves, axis_x, axis_y, taps_first, taps_second, h_part, sum_part, dy, dyy):
    rows, sub, width = waves.shape
    flat = rows * sub
    field = jnp.concatenate(halves(waves[...].reshape(flat, width)), axis=0)
    dyy[...] = joined(across(field, taps_second), flat).reshape(waves.shape)
    dy[...] = joined(across(field, taps_first), flat).reshape(waves.shape)
    for x in range(rows):
        dxx = SECOND[0] * waves[x]
        cross = dxx + (1.0 / SCALE_SECOND) * dyy[x]
        dxy = jnp.zeros_like(dxx)
        for k in range(1, 5):
            for step in (k, -k):
                if 0 <= x + step < rows:
                    weight = FIRST[k - 1] if step > 0 else -FIRST[k - 1]
                    dxx = dxx + SECOND[k] * waves[x + step]
                    dxy = dxy + (weight / SCALE_FIRST) * dy[x + step]
        n_x, n_y = axis_x[x], axis_y[x]
        h_part[x] = n_x * (n_x * dxx + 2.0 * (n_y * dxy)) + n_y * (n_y * cross)
        sum_part[x] = dxx + cross


def halo_rows(size, edges):
    place = lax.axis_index("xy")
    even = place % 2 == 0
    left_at, right_at = jnp.where(even, 0, 4), jnp.where(even, 4, 0)
    left_in = jnp.where(place > 0, 1.0, 0.0)
    right_in = jnp.where(place < size - 1, 1.0, 0.0)
    before = [edges[left_at + x] * left_in for x in range(4)]
    return before + [edges[right_at + x] * right_in for x in range(4)]


def reach(values, row, coefficients, sign):
    total = None
    for k in range(1, 5):
        at = row + 4 - k if row < 4 else row + k - 4
        if (row < 4 and 0 <= at < 4) or (row >= 4 and 4 <= at < 8):
            term = (coefficients[k - 1] * (sign if row < 4 else 1.0)) * values[at]
            total = term if total is None else total + term
    return total


def depth_kernel(
    size,
    waves,
    other,
    edges,
    axis_x,
    axis_y,
    axis_z,
    h_part,
    sum_part,
    taps_first,
    h_own,
    sum_own,
    dz,
    dzz,
    dzy,
):
    rows, sub, width = waves.shape
    flat = rows * sub
    lower = lax.axis_index("gz") == 0
    for x in range(rows):
        own = waves[x]
        ahead, behind = depth_neighbours(own, other[x], lower)
        dz[x] = first_of(ahead, behind)
        dzz[x] = second_of(own, ahead, behind)
    slope = jnp.concatenate(halves(dz[...].reshape(flat, width)), axis=0)
    dzy[...] = joined(across(slope, taps_first), flat).reshape(waves.shape)
    values = halo_rows(size, edges)
    parts = jnp.concatenate(halves(jnp.concatenate(values, axis=0)), axis=0)
    slopes = joined(across(parts, taps_first), 8 * sub)
    slopes = [slopes[sub * x : sub * x + sub] for x in range(8)]
    for x in range(rows):
        n_x, n_y, n_z = axis_x[x], axis_y[x], axis_z[x]
        dxz = jnp.zeros_like(n_x)
        for k in range(1, 5):
            for step in (k, -k):
                if 0 <= x + step < rows:
                    weight = FIRST[k - 1] if step > 0 else -FIRST[k - 1]
                    dxz = dxz + weight * dz[x + step]
        mixed = n_x * dxz + (1.0 / SCALE_FIRST) * (n_y * dzy[x])
        h_one = h_part[x] + n_z * (n_z * dzz[x] + 2.0 * mixed)
        total = sum_part[x] + dzz[x]
        if x < 4 or x >= rows - 4:
            row = x if x < 4 else x - rows + 8
            dxx = reach(values, row, SECOND[1:], 1.0)
            dxy = reach(slopes, row, [c / SCALE_FIRST for c in FIRST], -1.0)
            h_one = h_one + n_x * (n_x * dxx + 2.0 * (n_y * dxy))
            total = total + dxx
        h_own[x] = h_one
        sum_own[x] = total


def step_kernel(
    size,
    gives,
    edges,
    edges_other,
    h_own,
    sum_own,
    axis_x,
    axis_z,
    gain_a,
    gain_b,
    base,
    across_high,
    across_low,
    inline_high,
    inline_low,
    pressure,
    crossline,
    *sends,
):
    rows, sub, width = h_own.shape
    lower = lax.axis_index("gz") == 0
    place = lax.axis_index("xy")
    even, early = place % 2 == 0, place % 4 < 2
    top = lax.broadcasted_iota(jnp.int32, (sub, width), 0) < 4

    slopes = [
        first_of(*depth_neighbours(own, far, lower))
        for own, far in zip(halo_rows(size, edges), halo_rows(size, edges_other))
    ]
    for x in range(rows):
        h_one = h_own[x]
        if x < 4 or x >= rows - 4:
            dxz = reach(slopes, x if x < 4 else x - rows + 8, FIRST, -1.0)
            h_one = h_one + 2.0 * (axis_x[x] * axis_z[x] * dxz)
        mixed = jnp.where(top, sum_own[x] - h_one, h_one)
        pressure[x] = base[x] + gain_a[x] * mixed + gain_b[x] * pltpu.roll(mixed, 4, 0)

    packed = jnp.concatenate(
        [
            jnp.where(top, pressure[x], pltpu.roll(pressure[x + 1], 4, 0))
            for x in range(0, rows, 2)
        ],
        axis=0,
    )
    transformed = dot3(*halves(packed), across_high[...], across_low[...])
    crossline[...] = transformed
    parts = dot3(inline_high[...], inline_low[...], *halves(transformed))
    to_next, to_previous, to_second_next, to_second_previous = (
        parts[start : start + count] for start, count in gives
    )
    sends[0][...] = jnp.where(even, to_previous, to_next)
    sends[1][...] = jnp.where(even, to_next, to_previous)
    sends[2][...] = jnp.where(early, to_second_previous, to_second_next)
    sends[3][...] = jnp.where(early, to_second_next, to_second_previous)


def own_kernel(pressure, crossline, own_high, own_low, next_p, next_q, mine):
    for x in range(pressure.shape[0]):
        next_p[x] = pressure[x, :4]
        next_q[x] = pressure[x, 4:]
    mine[...] = dot3(own_high[...], own_low[...], *halves(crossline[...]))


def finish_kernel(takes, mine, *rest):
    outer, inner, outer_second, inner_second = (ref[...] for ref in rest[:4])
    outs = rest[4:]
    place = lax.axis_index("xy")
    even, early = place % 2 == 0, place % 4 < 2
    received = (
        jnp.where(even, outer, inner),
        jnp.where(even, inner, outer),
        jnp.where(early, outer_second, inner_second),
        jnp.where(early, inner_second, outer_second),
    )
    at = 0
    for out in outs:
        for row in range(out.shape[0]):
            total = mine[4 * at : 4 * at + 4]
            for take, got in zip(takes, received):
                for j in range(take.shape[1]):
                    factor = float(take[at, j])
                    if abs(factor) > 1e-13:
                        total = total + factor * got[4 * j : 4 * j + 4]
            out[row] = total
            at += 1


def pair_swaps(size):
    one = [1 if i % 2 == 0 else -1 for i in range(size)]
    two = [2 if i % 4 < 2 else -2 for i in range(size)]
    return [
        [(i, (i - one[i]) % size) for i in range(size)],
        [(i, i + one[i]) for i in range(size)],
        [(i, (i - two[i]) % size) for i in range(size)],
        [(i, i + two[i]) for i in range(size)],
    ]


def body(size, wave_p, wave_q, prior_p, prior_q, courant, epsilon, thomsen_delta, tilt_angle, azimuth):
    rows, layers, width = wave_p.shape
    f32 = jnp.float32
    even = lax.axis_index("xy") % 2 == 0
    pairs = pair_swaps(size)
    cores = [(0, 1), (1, 0)]
    stack = jax.ShapeDtypeStruct((rows, 8, width), f32)
    cells = rows * layers * width
    params = pltpu.CompilerParams(vmem_limit_bytes=16 * 1024 * 1024)

    def kernel(function, out_shape, work, name, scratch_shapes=()):
        cost = pl.CostEstimate(flops=work * cells, bytes_accessed=40 * cells, transcendentals=0)
        return pl.pallas_call(
            function,
            out_shape=out_shape,
            scratch_shapes=scratch_shapes,
            compiler_params=params,
            cost_estimate=cost,
            name=name,
        )

    waves = lax.optimization_barrier(jnp.concatenate([wave_p, wave_q], axis=1))
    leading, last = waves[:4], waves[rows - 4 :]
    open_outer = [
        (2 * i + g, 2 * i + 1 - g) if abs(i - j) > 1 else (2 * i + g, 2 * j + g)
        for i, j in pairs[0]
        for g in range(2)
    ]
    to_inner, to_outer = jnp.where(even, last, leading), jnp.where(even, leading, last)
    to_inner, to_outer, fields = lax.optimization_barrier((to_inner, to_outer, waves))
    outer = lax.ppermute(to_outer, ("xy", "gz"), open_outer)
    inner = lax.ppermute(to_inner, "xy", pairs[1])
    other = lax.ppermute(fields, "gz", cores)

    taps = jax.ShapeDtypeStruct((4 * LANES, 2 * LANES), jnp.bfloat16)
    axis_x, axis_y, axis_z, *gains, taps_first, taps_second = kernel(
        weights_kernel, [stack] * 6 + [taps] * 2, 100, "weights"
    )(waves, prior_p, prior_q, courant, epsilon, thomsen_delta, tilt_angle, azimuth)
    work = pltpu.VMEM((rows, 8, width), f32)
    h_part, sum_part = kernel(interior_kernel, [stack] * 2, 100, "interior", [work] * 2)(
        waves, axis_x, axis_y, taps_first, taps_second
    )
    h_part, outer, inner = lax.optimization_barrier((h_part, outer, inner))
    edges, other = lax.optimization_barrier((jnp.concatenate([outer, inner], axis=0), other))
    edges_other = lax.ppermute(edges, "gz", cores)
    h_own, sum_own = kernel(functools.partial(depth_kernel, size), [stack] * 2, 100, "depth", [work] * 3)(
        waves, other, edges, axis_x, axis_y, axis_z, h_part, sum_part, taps_first
    )

    own, factors = inline_blocks(rows)
    offsets = (-1, 1, -2, 2)
    pieces, gives, start = [], [], 0
    for offset in offsets:
        give = factors[offset][1]
        pad = give.shape[0] % 2
        pieces.append(np.pad(give, ((0, pad), (0, 0))))
        gives.append((start, 4 * (give.shape[0] + pad)))
        start += gives[-1][1]

    def parts(matrix):
        return [jnp.asarray(part) for part in split_bf16(matrix)]

    inline = parts(np.kron(np.concatenate(pieces), np.eye(4)))
    inline_own = parts(np.kron(own, np.eye(4)))
    flat = jax.ShapeDtypeStruct((layers * rows, width), f32)
    pressure, crossline, *sends = kernel(
        functools.partial(step_kernel, size, gives),
        [stack, flat] + [jax.ShapeDtypeStruct((count, width), f32) for _, count in gives],
        400,
        "step",
    )(
        edges,
        edges_other,
        h_own,
        sum_own,
        axis_x,
        axis_z,
        *gains,
        *parts(np.concatenate(three_levels(width)).T),
        *inline,
    )
    received = [lax.ppermute(send, "xy", pair) for send, pair in zip(sends, pairs)]
    grid = jax.ShapeDtypeStruct(wave_p.shape, f32)
    next_p, next_q, mine = kernel(own_kernel, [grid, grid, flat], 100, "own")(
        pressure, crossline, *inline_own
    )
    outs = kernel(
        functools.partial(finish_kernel, [factors[offset][0] for offset in offsets]),
        [
            jax.ShapeDtypeStruct((count, layers, width), f32)
            for count in (rows // 2, rows // 4, rows // 8, rows // 8)
        ],
        20,
        "finish",
    )(mine, *received)
    return (next_p, next_q, *outs)


def solution(mesh):
    split = P(("shot", "xy"), "gz", None)
    shared = P("xy", "gz", None)
    return jax.shard_map(
        functools.partial(body, mesh.shape["xy"]),
        mesh=mesh,
        in_specs=(split,) * 4 + (shared,) * 5,
        out_specs=(split,) * 6,
        check_vma=False,
    )
```

```python
import functools

import jax
import jax.numpy as jnp
import numpy as np
from jax import lax
from jax.experimental import pallas as pl
from jax.experimental.pallas import tpu as pltpu
from jax.sharding import PartitionSpec as P

SECOND = (-205.0 / 72.0, 8.0 / 5.0, -1.0 / 5.0, 8.0 / 315.0, -1.0 / 560.0)
FIRST = (4.0 / 5.0, -1.0 / 5.0, 4.0 / 105.0, -1.0 / 280.0)
LIFT = (-1.586134342, -0.05298011854, 0.8829110762, 0.4435068522)
ZETA = 1.149604398
LANES = 128
SCALE_FIRST, SCALE_SECOND = 840.0, 5040.0


def lift_level(values):
    even, odd = values[0::2], values[1::2]
    odd = odd + LIFT[0] * (even + np.roll(even, -1, 0))
    even = even + LIFT[1] * (odd + np.roll(odd, 1, 0))
    odd = odd + LIFT[2] * (even + np.roll(even, -1, 0))
    even = even + LIFT[3] * (odd + np.roll(odd, 1, 0))
    return even * ZETA, odd * (1.0 / ZETA)


def three_levels(length):
    coarse, members = np.eye(length), []
    for _ in range(3):
        coarse, detail = lift_level(coarse)
        members.append(detail)
    return members + [coarse]


def split_bf16(matrix):
    high = matrix.astype(jnp.bfloat16)
    low = (matrix - high.astype(np.float64)).astype(jnp.bfloat16)
    return high, low


def inline_blocks(rows):
    bricks, brick = 8, 4
    members = three_levels(rows * bricks)
    wanted = np.concatenate(
        [m[brick * len(m) // bricks : (brick + 1) * len(m) // bricks] for m in members]
    )

    def block(offset):
        return wanted[:, rows * (brick + offset) : rows * (brick + offset + 1)]

    factors = {}
    for offset in (-1, 1, -2, 2):
        left, sizes, right = np.linalg.svd(block(offset))
        rank = int((sizes > 1e-12).sum())
        root = np.sqrt(sizes[:rank])
        factors[offset] = (left[:, :rank] * root, root[:, None] * right[:rank])
    return block(0), factors


def sine_cosine(angle):
    turns = jnp.round(angle * (2.0 / np.pi))
    rest = angle - turns * 1.5703125
    rest = rest - turns * 4.837512969970703125e-4
    rest = rest - turns * 7.549789948768648e-8
    square = rest * rest
    sine = rest + rest * square * (
        -1.6666654611e-1 + square * (8.3321608736e-3 + square * -1.9515295891e-4)
    )
    cosine = (
        1.0
        - 0.5 * square
        + square
        * square
        * (4.166664568298827e-2 + square * (-1.388731625493765e-3 + square * 2.443315711809948e-5))
    )
    quarter = turns.astype(jnp.int32)
    swapped = (quarter & 1) == 1
    out_sine = jnp.where(swapped, cosine, sine)
    out_cosine = jnp.where(swapped, sine, cosine)
    out_sine = jnp.where((quarter & 2) == 2, -out_sine, out_sine)
    out_cosine = jnp.where(((quarter + 1) & 2) == 2, -out_cosine, out_cosine)
    return out_sine, out_cosine


def band(shape, taps, sign, scale):
    offset = lax.broadcasted_iota(jnp.int32, shape, 0) - LANES
    offset = offset - lax.broadcasted_iota(jnp.int32, shape, 1)
    values = jnp.zeros(shape, jnp.float32)
    for k, tap in enumerate(taps, 1):
        values = jnp.where(jnp.abs(offset) == k, float(np.round(tap * scale)), values)
    if sign < 0:
        values = jnp.where(offset < 0, -values, values)
    return values.astype(jnp.bfloat16)


def weights_kernel(
    waves,
    prior_p,
    prior_q,
    courant,
    epsilon,
    delta,
    tilt,
    azimuth,
    axis_x,
    axis_y,
    axis_z,
    gain_a,
    gain_b,
    base,
    taps_first,
    taps_second,
):
    rows = waves.shape[0]
    taps_first[...] = band(taps_first.shape, FIRST, -1.0, SCALE_FIRST)
    taps_second[...] = band(taps_second.shape, SECOND[1:], 1.0, SCALE_SECOND)
    top = lax.broadcasted_iota(jnp.int32, waves.shape[1:], 0) < 4

    def swap(value):
        return pltpu.roll(value, 4, 0)

    for x in range(rows):
        angles = jnp.concatenate(
            [tilt[x].astype(jnp.float32), azimuth[x].astype(jnp.float32)], axis=0
        )
        sine, cosine = sine_cosine(angles)
        sine_other, cosine_other = swap(sine), swap(cosine)
        sine_tilt = jnp.where(top, sine, sine_other)
        axis_x[x] = sine_tilt * jnp.where(top, cosine_other, cosine)
        axis_y[x] = sine * sine_other
        axis_z[x] = jnp.where(top, cosine, cosine_other)
        speed = courant[x].astype(jnp.float32)
        root = jnp.sqrt(1.0 + 2.0 * delta[x].astype(jnp.float32))
        stretch = 1.0 + 2.0 * epsilon[x].astype(jnp.float32)
        gain_a[x] = jnp.concatenate([speed * stretch, speed], axis=0)
        across = speed * root
        gain_b[x] = jnp.concatenate([across, across], axis=0)
        base[x] = 2.0 * waves[x] - jnp.concatenate([prior_p[x], prior_q[x]], axis=0)


def first_of(ahead, behind):
    total = FIRST[0] * (ahead[0] - behind[0])
    for k in range(1, 4):
        total = total + FIRST[k] * (ahead[k] - behind[k])
    return total


def second_of(centre, ahead, behind):
    total = SECOND[0] * centre
    for k in range(4):
        total = total + SECOND[k + 1] * (ahead[k] + behind[k])
    return total


def dot3(a_high, a_low, b_high, b_low):
    def dot(a, b):
        return jnp.dot(a, b, preferred_element_type=jnp.float32)

    rows = a_high.shape[0]
    both = dot(jnp.concatenate([a_high, a_low], axis=0), b_high)
    return both[:rows] + (both[rows:] + dot(a_high, b_low))


def halves(value):
    high = value.astype(jnp.bfloat16)
    return high, (value - high.astype(jnp.float32)).astype(jnp.bfloat16)


def depth_neighbours(own, far, lower):
    layer = lax.broadcasted_iota(jnp.int32, own.shape, 0) & 3
    up = far * jnp.where(lower, 1.0, 0.0)
    down = far * jnp.where(lower, 0.0, 1.0)
    ahead, behind = [], []
    for k in range(1, 4):
        ahead.append(jnp.where(layer < 4 - k, pltpu.roll(own, 8 - k, 0), pltpu.roll(up, 4 - k, 0)))
        behind.append(jnp.where(layer >= k, pltpu.roll(own, k, 0), pltpu.roll(down, 4 + k, 0)))
    return ahead + [up], behind + [down]


def across(parts, taps):
    width = parts.shape[1]
    blocks = []
    for start in range(0, width, 2 * LANES):
        stop = min(start + 2 * LANES, width)
        first = start - LANES
        low, high = max(first, 0), min(stop + LANES, width)
        block = taps[low - first : high - first, : stop - start]
        blocks.append(jnp.dot(parts[:, low:high], block, preferred_element_type=jnp.float32))
    return jnp.concatenate(blocks, axis=1)


def joined(parts, rows):
    return parts[:rows] + parts[rows:]


def interior_kernel(waves, axis_x, axis_y, taps_first, taps_second, h_part, sum_part, dy, dyy):
    rows, sub, width = waves.shape
    flat = rows * sub
    field = jnp.concatenate(halves(waves[...].reshape(flat, width)), axis=0)
    dyy[...] = joined(across(field, taps_second), flat).reshape(waves.shape)
    dy[...] = joined(across(field, taps_first), flat).reshape(waves.shape)
    for x in range(rows):
        dxx = SECOND[0] * waves[x]
        cross = dxx + (1.0 / SCALE_SECOND) * dyy[x]
        dxy = jnp.zeros_like(dxx)
        for k in range(1, 5):
            for step in (k, -k):
                if 0 <= x + step < rows:
                    weight = FIRST[k - 1] if step > 0 else -FIRST[k - 1]
                    dxx = dxx + SECOND[k] * waves[x + step]
                    dxy = dxy + (weight / SCALE_FIRST) * dy[x + step]
        n_x, n_y = axis_x[x], axis_y[x]
        h_part[x] = n_x * (n_x * dxx + 2.0 * (n_y * dxy)) + n_y * (n_y * cross)
        sum_part[x] = dxx + cross


def halo_rows(size, edges):
    place = lax.axis_index("xy")
    even = place % 2 == 0
    left_at, right_at = jnp.where(even, 0, 4), jnp.where(even, 4, 0)
    left_in = jnp.where(place > 0, 1.0, 0.0)
    right_in = jnp.where(place < size - 1, 1.0, 0.0)
    before = [edges[left_at + x] * left_in for x in range(4)]
    return before + [edges[right_at + x] * right_in for x in range(4)]


def reach(values, row, coefficients, sign):
    total = None
    for k in range(1, 5):
        at = row + 4 - k if row < 4 else row + k - 4
        if (row < 4 and 0 <= at < 4) or (row >= 4 and 4 <= at < 8):
            term = (coefficients[k - 1] * (sign if row < 4 else 1.0)) * values[at]
            total = term if total is None else total + term
    return total


def depth_kernel(
    size,
    waves,
    layers_p,
    layers_q,
    edges,
    axis_x,
    axis_y,
    axis_z,
    h_part,
    sum_part,
    taps_first,
    h_own,
    sum_own,
    dz,
    dzz,
    dzy,
):
    rows, sub, width = waves.shape
    flat = rows * sub
    half = lax.axis_index("gz")
    lower = half == 0
    for x in range(rows):
        own = waves[x]
        far = jnp.concatenate([layers_p[1 - half, x], layers_q[1 - half, x]], axis=0)
        ahead, behind = depth_neighbours(own, far, lower)
        dz[x] = first_of(ahead, behind)
        dzz[x] = second_of(own, ahead, behind)
    slope = jnp.concatenate(halves(dz[...].reshape(flat, width)), axis=0)
    dzy[...] = joined(across(slope, taps_first), flat).reshape(waves.shape)
    values = halo_rows(size, edges)
    parts = jnp.concatenate(halves(jnp.concatenate(values, axis=0)), axis=0)
    slopes = joined(across(parts, taps_first), 8 * sub)
    slopes = [slopes[sub * x : sub * x + sub] for x in range(8)]
    for x in range(rows):
        n_x, n_y, n_z = axis_x[x], axis_y[x], axis_z[x]
        dxz = jnp.zeros_like(n_x)
        for k in range(1, 5):
            for step in (k, -k):
                if 0 <= x + step < rows:
                    weight = FIRST[k - 1] if step > 0 else -FIRST[k - 1]
                    dxz = dxz + weight * dz[x + step]
        mixed = n_x * dxz + (1.0 / SCALE_FIRST) * (n_y * dzy[x])
        h_one = h_part[x] + n_z * (n_z * dzz[x] + 2.0 * mixed)
        total = sum_part[x] + dzz[x]
        if x < 4 or x >= rows - 4:
            row = x if x < 4 else x - rows + 8
            dxx = reach(values, row, SECOND[1:], 1.0)
            dxy = reach(slopes, row, [c / SCALE_FIRST for c in FIRST], -1.0)
            h_one = h_one + n_x * (n_x * dxx + 2.0 * (n_y * dxy))
            total = total + dxx
        h_own[x] = h_one
        sum_own[x] = total


def step_kernel(
    size,
    gives,
    edges,
    edges_other,
    h_own,
    sum_own,
    axis_x,
    axis_z,
    gain_a,
    gain_b,
    base,
    across_high,
    across_low,
    inline_high,
    inline_low,
    pressure,
    crossline,
    *sends,
):
    rows, sub, width = h_own.shape
    lower = lax.axis_index("gz") == 0
    place = lax.axis_index("xy")
    even, early = place % 2 == 0, place % 4 < 2
    top = lax.broadcasted_iota(jnp.int32, (sub, width), 0) < 4

    slopes = [
        first_of(*depth_neighbours(own, far, lower))
        for own, far in zip(halo_rows(size, edges), halo_rows(size, edges_other))
    ]
    for x in range(rows):
        h_one = h_own[x]
        if x < 4 or x >= rows - 4:
            dxz = reach(slopes, x if x < 4 else x - rows + 8, FIRST, -1.0)
            h_one = h_one + 2.0 * (axis_x[x] * axis_z[x] * dxz)
        mixed = jnp.where(top, sum_own[x] - h_one, h_one)
        pressure[x] = base[x] + gain_a[x] * mixed + gain_b[x] * pltpu.roll(mixed, 4, 0)

    packed = jnp.concatenate(
        [
            jnp.where(top, pressure[x], pltpu.roll(pressure[x + 1], 4, 0))
            for x in range(0, rows, 2)
        ],
        axis=0,
    )
    transformed = dot3(*halves(packed), across_high[...], across_low[...])
    crossline[...] = transformed
    parts = dot3(inline_high[...], inline_low[...], *halves(transformed))
    to_next, to_previous, to_second_next, to_second_previous = (
        parts[start : start + count] for start, count in gives
    )
    sends[0][...] = jnp.where(even, to_previous, to_next)
    sends[1][...] = jnp.where(even, to_next, to_previous)
    sends[2][...] = jnp.where(early, to_second_previous, to_second_next)
    sends[3][...] = jnp.where(early, to_second_next, to_second_previous)


def own_kernel(pressure, crossline, own_high, own_low, next_p, next_q, mine):
    for x in range(pressure.shape[0]):
        next_p[x] = pressure[x, :4]
        next_q[x] = pressure[x, 4:]
    mine[...] = dot3(own_high[...], own_low[...], *halves(crossline[...]))


def finish_kernel(takes, mine, *rest):
    outer, inner, outer_second, inner_second = (ref[...] for ref in rest[:4])
    outs = rest[4:]
    place = lax.axis_index("xy")
    even, early = place % 2 == 0, place % 4 < 2
    received = (
        jnp.where(even, outer, inner),
        jnp.where(even, inner, outer),
        jnp.where(early, outer_second, inner_second),
        jnp.where(early, inner_second, outer_second),
    )
    at = 0
    for out in outs:
        for row in range(out.shape[0]):
            total = mine[4 * at : 4 * at + 4]
            for take, got in zip(takes, received):
                for j in range(take.shape[1]):
                    factor = float(take[at, j])
                    if abs(factor) > 1e-13:
                        total = total + factor * got[4 * j : 4 * j + 4]
            out[row] = total
            at += 1


def pair_swaps(size):
    one = [1 if i % 2 == 0 else -1 for i in range(size)]
    two = [2 if i % 4 < 2 else -2 for i in range(size)]
    return [
        [(i, (i - one[i]) % size) for i in range(size)],
        [(i, i + one[i]) for i in range(size)],
        [(i, (i - two[i]) % size) for i in range(size)],
        [(i, i + two[i]) for i in range(size)],
    ]


def body(size, wave_p, wave_q, prior_p, prior_q, courant, epsilon, thomsen_delta, tilt_angle, azimuth):
    rows, layers, width = wave_p.shape
    f32 = jnp.float32
    even = lax.axis_index("xy") % 2 == 0
    pairs = pair_swaps(size)
    cores = [(0, 1), (1, 0)]
    stack = jax.ShapeDtypeStruct((rows, 8, width), f32)
    cells = rows * layers * width
    params = pltpu.CompilerParams(vmem_limit_bytes=16 * 1024 * 1024)

    def kernel(function, out_shape, work, name, scratch_shapes=()):
        cost = pl.CostEstimate(flops=work * cells, bytes_accessed=40 * cells, transcendentals=0)
        return pl.pallas_call(
            function,
            out_shape=out_shape,
            scratch_shapes=scratch_shapes,
            compiler_params=params,
            cost_estimate=cost,
            name=name,
        )

    waves = lax.optimization_barrier(jnp.concatenate([wave_p, wave_q], axis=1))
    leading, last = waves[:4], waves[rows - 4 :]
    open_outer = [
        (2 * i + g, 2 * i + 1 - g) if abs(i - j) > 1 else (2 * i + g, 2 * j + g)
        for i, j in pairs[0]
        for g in range(2)
    ]
    outer = lax.ppermute(jnp.where(even, leading, last), ("xy", "gz"), open_outer)
    inner = lax.ppermute(jnp.where(even, last, leading), "xy", pairs[1])
    layers_p, layers_q = lax.all_gather(wave_p, "gz"), lax.all_gather(wave_q, "gz")

    taps = jax.ShapeDtypeStruct((4 * LANES, 2 * LANES), jnp.bfloat16)
    axis_x, axis_y, axis_z, *gains, taps_first, taps_second = kernel(
        weights_kernel, [stack] * 6 + [taps] * 2, 100, "weights"
    )(waves, prior_p, prior_q, courant, epsilon, thomsen_delta, tilt_angle, azimuth)
    work = pltpu.VMEM((rows, 8, width), f32)
    h_part, sum_part = kernel(interior_kernel, [stack] * 2, 100, "interior", [work] * 2)(
        waves, axis_x, axis_y, taps_first, taps_second
    )
    h_part, layers_p, layers_q, outer, inner = lax.optimization_barrier(
        (h_part, layers_p, layers_q, outer, inner)
    )
    edges = jnp.concatenate([outer, inner], axis=0)
    edges_other = lax.ppermute(edges, "gz", cores)
    h_own, sum_own = kernel(functools.partial(depth_kernel, size), [stack] * 2, 100, "depth", [work] * 3)(
        waves, layers_p, layers_q, edges, axis_x, axis_y, axis_z, h_part, sum_part, taps_first
    )

    own, factors = inline_blocks(rows)
    offsets = (-1, 1, -2, 2)
    pieces, gives, start = [], [], 0
    for offset in offsets:
        give = factors[offset][1]
        pad = give.shape[0] % 2
        pieces.append(np.pad(give, ((0, pad), (0, 0))))
        gives.append((start, 4 * (give.shape[0] + pad)))
        start += gives[-1][1]

    def parts(matrix):
        return [jnp.asarray(part) for part in split_bf16(matrix)]

    inline = parts(np.kron(np.concatenate(pieces), np.eye(4)))
    inline_own = parts(np.kron(own, np.eye(4)))
    flat = jax.ShapeDtypeStruct((layers * rows, width), f32)
    pressure, crossline, *sends = kernel(
        functools.partial(step_kernel, size, gives),
        [stack, flat] + [jax.ShapeDtypeStruct((count, width), f32) for _, count in gives],
        400,
        "step",
    )(
        edges,
        edges_other,
        h_own,
        sum_own,
        axis_x,
        axis_z,
        *gains,
        *parts(np.concatenate(three_levels(width)).T),
        *inline,
    )
    received = [lax.ppermute(send, "xy", pair) for send, pair in zip(sends, pairs)]
    grid = jax.ShapeDtypeStruct(wave_p.shape, f32)
    next_p, next_q, mine = kernel(own_kernel, [grid, grid, flat], 100, "own")(
        pressure, crossline, *inline_own
    )
    outs = kernel(
        functools.partial(finish_kernel, [factors[offset][0] for offset in offsets]),
        [
            jax.ShapeDtypeStruct((count, layers, width), f32)
            for count in (rows // 2, rows // 4, rows // 8, rows // 8)
        ],
        20,
        "finish",
    )(mine, *received)
    return (next_p, next_q, *outs)


def solution(mesh):
    split = P(("shot", "xy"), "gz", None)
    shared = P("xy", "gz", None)
    return jax.shard_map(
        functools.partial(body, mesh.shape["xy"]),
        mesh=mesh,
        in_specs=(split,) * 4 + (shared,) * 5,
        out_specs=(split,) * 6,
        check_vma=False,
    )
```

```python
import functools

import jax
import jax.numpy as jnp
import numpy as np
from jax import lax
from jax.experimental import pallas as pl
from jax.experimental.pallas import tpu as pltpu
from jax.sharding import PartitionSpec as P

SECOND = (-205.0 / 72.0, 8.0 / 5.0, -1.0 / 5.0, 8.0 / 315.0, -1.0 / 560.0)
FIRST = (4.0 / 5.0, -1.0 / 5.0, 4.0 / 105.0, -1.0 / 280.0)
LIFT = (-1.586134342, -0.05298011854, 0.8829110762, 0.4435068522)
ZETA = 1.149604398
LANES = 128
SCALE_FIRST, SCALE_SECOND = 840.0, 5040.0


def lift_level(values):
    even, odd = values[0::2], values[1::2]
    odd = odd + LIFT[0] * (even + np.roll(even, -1, 0))
    even = even + LIFT[1] * (odd + np.roll(odd, 1, 0))
    odd = odd + LIFT[2] * (even + np.roll(even, -1, 0))
    even = even + LIFT[3] * (odd + np.roll(odd, 1, 0))
    return even * ZETA, odd * (1.0 / ZETA)


def three_levels(length):
    coarse, members = np.eye(length), []
    for _ in range(3):
        coarse, detail = lift_level(coarse)
        members.append(detail)
    return members + [coarse]


def split_bf16(matrix):
    high = matrix.astype(jnp.bfloat16)
    low = (matrix - high.astype(np.float64)).astype(jnp.bfloat16)
    return high, low


def inline_blocks(rows):
    bricks, brick = 8, 4
    members = three_levels(rows * bricks)
    wanted = np.concatenate(
        [m[brick * len(m) // bricks : (brick + 1) * len(m) // bricks] for m in members]
    )

    def block(offset):
        return wanted[:, rows * (brick + offset) : rows * (brick + offset + 1)]

    factors = {}
    for offset in (-1, 1, -2, 2):
        left, sizes, right = np.linalg.svd(block(offset))
        rank = int((sizes > 1e-12).sum())
        root = np.sqrt(sizes[:rank])
        factors[offset] = (left[:, :rank] * root, root[:, None] * right[:rank])
    return block(0), factors


def sine_cosine(angle):
    turns = jnp.round(angle * (2.0 / np.pi))
    rest = angle - turns * 1.5703125
    rest = rest - turns * 4.837512969970703125e-4
    rest = rest - turns * 7.549789948768648e-8
    square = rest * rest
    sine = rest + rest * square * (
        -1.6666654611e-1 + square * (8.3321608736e-3 + square * -1.9515295891e-4)
    )
    cosine = (
        1.0
        - 0.5 * square
        + square
        * square
        * (4.166664568298827e-2 + square * (-1.388731625493765e-3 + square * 2.443315711809948e-5))
    )
    quarter = turns.astype(jnp.int32)
    swapped = (quarter & 1) == 1
    out_sine = jnp.where(swapped, cosine, sine)
    out_cosine = jnp.where(swapped, sine, cosine)
    out_sine = jnp.where((quarter & 2) == 2, -out_sine, out_sine)
    out_cosine = jnp.where(((quarter + 1) & 2) == 2, -out_cosine, out_cosine)
    return out_sine, out_cosine


def band(shape, taps, sign, scale):
    offset = lax.broadcasted_iota(jnp.int32, shape, 0) - LANES
    offset = offset - lax.broadcasted_iota(jnp.int32, shape, 1)
    values = jnp.zeros(shape, jnp.float32)
    for k, tap in enumerate(taps, 1):
        values = jnp.where(jnp.abs(offset) == k, float(np.round(tap * scale)), values)
    if sign < 0:
        values = jnp.where(offset < 0, -values, values)
    return values.astype(jnp.bfloat16)


def weights_kernel(
    waves,
    prior_p,
    prior_q,
    courant,
    epsilon,
    delta,
    tilt,
    azimuth,
    axis_x,
    axis_y,
    axis_z,
    gain_a,
    gain_b,
    base,
    taps_first,
    taps_second,
):
    rows = waves.shape[0]
    taps_first[...] = band(taps_first.shape, FIRST, -1.0, SCALE_FIRST)
    taps_second[...] = band(taps_second.shape, SECOND[1:], 1.0, SCALE_SECOND)
    top = lax.broadcasted_iota(jnp.int32, waves.shape[1:], 0) < 4

    def swap(value):
        return pltpu.roll(value, 4, 0)

    for x in range(rows):
        angles = jnp.concatenate(
            [tilt[x].astype(jnp.float32), azimuth[x].astype(jnp.float32)], axis=0
        )
        sine, cosine = sine_cosine(angles)
        sine_other, cosine_other = swap(sine), swap(cosine)
        sine_tilt = jnp.where(top, sine, sine_other)
        axis_x[x] = sine_tilt * jnp.where(top, cosine_other, cosine)
        axis_y[x] = sine * sine_other
        axis_z[x] = jnp.where(top, cosine, cosine_other)
        speed = courant[x].astype(jnp.float32)
        root = jnp.sqrt(1.0 + 2.0 * delta[x].astype(jnp.float32))
        stretch = 1.0 + 2.0 * epsilon[x].astype(jnp.float32)
        gain_a[x] = jnp.concatenate([speed * stretch, speed], axis=0)
        across = speed * root
        gain_b[x] = jnp.concatenate([across, across], axis=0)
        base[x] = 2.0 * waves[x] - jnp.concatenate([prior_p[x], prior_q[x]], axis=0)


def first_of(ahead, behind):
    total = FIRST[0] * (ahead[0] - behind[0])
    for k in range(1, 4):
        total = total + FIRST[k] * (ahead[k] - behind[k])
    return total


def second_of(centre, ahead, behind):
    total = SECOND[0] * centre
    for k in range(4):
        total = total + SECOND[k + 1] * (ahead[k] + behind[k])
    return total


def dot3(a_high, a_low, b_high, b_low):
    def dot(a, b):
        return jnp.dot(a, b, preferred_element_type=jnp.float32)

    rows = a_high.shape[0]
    both = dot(jnp.concatenate([a_high, a_low], axis=0), b_high)
    return both[:rows] + (both[rows:] + dot(a_high, b_low))


def halves(value):
    high = value.astype(jnp.bfloat16)
    return high, (value - high.astype(jnp.float32)).astype(jnp.bfloat16)


def depth_neighbours(own, far, lower):
    layer = lax.broadcasted_iota(jnp.int32, own.shape, 0) & 3
    up = far * jnp.where(lower, 1.0, 0.0)
    down = far * jnp.where(lower, 0.0, 1.0)
    ahead, behind = [], []
    for k in range(1, 4):
        ahead.append(jnp.where(layer < 4 - k, pltpu.roll(own, 8 - k, 0), pltpu.roll(up, 4 - k, 0)))
        behind.append(jnp.where(layer >= k, pltpu.roll(own, k, 0), pltpu.roll(down, 4 + k, 0)))
    return ahead + [up], behind + [down]


def across(parts, taps):
    width = parts.shape[1]
    blocks = []
    for start in range(0, width, 2 * LANES):
        stop = min(start + 2 * LANES, width)
        first = start - LANES
        low, high = max(first, 0), min(stop + LANES, width)
        block = taps[low - first : high - first, : stop - start]
        blocks.append(jnp.dot(parts[:, low:high], block, preferred_element_type=jnp.float32))
    return jnp.concatenate(blocks, axis=1)


def joined(parts, rows):
    return parts[:rows] + parts[rows:]


def interior_kernel(waves, axis_x, axis_y, taps_first, taps_second, h_part, sum_part, dy, dyy):
    rows, sub, width = waves.shape
    flat = rows * sub
    field = jnp.concatenate(halves(waves[...].reshape(flat, width)), axis=0)
    dyy[...] = joined(across(field, taps_second), flat).reshape(waves.shape)
    dy[...] = joined(across(field, taps_first), flat).reshape(waves.shape)
    for x in range(rows):
        dxx = SECOND[0] * waves[x]
        cross = dxx + (1.0 / SCALE_SECOND) * dyy[x]
        dxy = jnp.zeros_like(dxx)
        for k in range(1, 5):
            for step in (k, -k):
                if 0 <= x + step < rows:
                    weight = FIRST[k - 1] if step > 0 else -FIRST[k - 1]
                    dxx = dxx + SECOND[k] * waves[x + step]
                    dxy = dxy + (weight / SCALE_FIRST) * dy[x + step]
        n_x, n_y = axis_x[x], axis_y[x]
        h_part[x] = n_x * (n_x * dxx + 2.0 * (n_y * dxy)) + n_y * (n_y * cross)
        sum_part[x] = dxx + cross


def halo_rows(size, edges):
    place = lax.axis_index("xy")
    even = place % 2 == 0
    left_at, right_at = jnp.where(even, 0, 4), jnp.where(even, 4, 0)
    left_in = jnp.where(place > 0, 1.0, 0.0)
    right_in = jnp.where(place < size - 1, 1.0, 0.0)
    before = [edges[left_at + x] * left_in for x in range(4)]
    return before + [edges[right_at + x] * right_in for x in range(4)]


def reach(values, row, coefficients, sign):
    total = None
    for k in range(1, 5):
        at = row + 4 - k if row < 4 else row + k - 4
        if (row < 4 and 0 <= at < 4) or (row >= 4 and 4 <= at < 8):
            term = (coefficients[k - 1] * (sign if row < 4 else 1.0)) * values[at]
            total = term if total is None else total + term
    return total


def depth_kernel(
    size,
    waves,
    all_layers,
    edges,
    axis_x,
    axis_y,
    axis_z,
    h_part,
    sum_part,
    taps_first,
    h_own,
    sum_own,
    dz,
    dzz,
    dzy,
):
    rows, sub, width = waves.shape
    flat = rows * sub
    half = lax.axis_index("gz")
    lower = half == 0
    for x in range(rows):
        own = waves[x]
        ahead, behind = depth_neighbours(own, all_layers[1 - half, x], lower)
        dz[x] = first_of(ahead, behind)
        dzz[x] = second_of(own, ahead, behind)
    slope = jnp.concatenate(halves(dz[...].reshape(flat, width)), axis=0)
    dzy[...] = joined(across(slope, taps_first), flat).reshape(waves.shape)
    values = halo_rows(size, edges)
    parts = jnp.concatenate(halves(jnp.concatenate(values, axis=0)), axis=0)
    slopes = joined(across(parts, taps_first), 8 * sub)
    slopes = [slopes[sub * x : sub * x + sub] for x in range(8)]
    for x in range(rows):
        n_x, n_y, n_z = axis_x[x], axis_y[x], axis_z[x]
        dxz = jnp.zeros_like(n_x)
        for k in range(1, 5):
            for step in (k, -k):
                if 0 <= x + step < rows:
                    weight = FIRST[k - 1] if step > 0 else -FIRST[k - 1]
                    dxz = dxz + weight * dz[x + step]
        mixed = n_x * dxz + (1.0 / SCALE_FIRST) * (n_y * dzy[x])
        h_one = h_part[x] + n_z * (n_z * dzz[x] + 2.0 * mixed)
        total = sum_part[x] + dzz[x]
        if x < 4 or x >= rows - 4:
            row = x if x < 4 else x - rows + 8
            dxx = reach(values, row, SECOND[1:], 1.0)
            dxy = reach(slopes, row, [c / SCALE_FIRST for c in FIRST], -1.0)
            h_one = h_one + n_x * (n_x * dxx + 2.0 * (n_y * dxy))
            total = total + dxx
        h_own[x] = h_one
        sum_own[x] = total


def step_kernel(
    size,
    gives,
    edges,
    edges_other,
    h_own,
    sum_own,
    axis_x,
    axis_z,
    gain_a,
    gain_b,
    base,
    across_high,
    across_low,
    inline_high,
    inline_low,
    pressure,
    crossline,
    *sends,
):
    rows, sub, width = h_own.shape
    lower = lax.axis_index("gz") == 0
    place = lax.axis_index("xy")
    even, early = place % 2 == 0, place % 4 < 2
    top = lax.broadcasted_iota(jnp.int32, (sub, width), 0) < 4

    slopes = [
        first_of(*depth_neighbours(own, far, lower))
        for own, far in zip(halo_rows(size, edges), halo_rows(size, edges_other))
    ]
    for x in range(rows):
        h_one = h_own[x]
        if x < 4 or x >= rows - 4:
            dxz = reach(slopes, x if x < 4 else x - rows + 8, FIRST, -1.0)
            h_one = h_one + 2.0 * (axis_x[x] * axis_z[x] * dxz)
        mixed = jnp.where(top, sum_own[x] - h_one, h_one)
        pressure[x] = base[x] + gain_a[x] * mixed + gain_b[x] * pltpu.roll(mixed, 4, 0)

    packed = jnp.concatenate(
        [
            jnp.where(top, pressure[x], pltpu.roll(pressure[x + 1], 4, 0))
            for x in range(0, rows, 2)
        ],
        axis=0,
    )
    transformed = dot3(*halves(packed), across_high[...], across_low[...])
    crossline[...] = transformed
    parts = dot3(inline_high[...], inline_low[...], *halves(transformed))
    to_next, to_previous, to_second_next, to_second_previous = (
        parts[start : start + count] for start, count in gives
    )
    sends[0][...] = jnp.where(even, to_previous, to_next)
    sends[1][...] = jnp.where(even, to_next, to_previous)
    sends[2][...] = jnp.where(early, to_second_previous, to_second_next)
    sends[3][...] = jnp.where(early, to_second_next, to_second_previous)


def own_kernel(pressure, crossline, own_high, own_low, next_p, next_q, mine):
    for x in range(pressure.shape[0]):
        next_p[x] = pressure[x, :4]
        next_q[x] = pressure[x, 4:]
    mine[...] = dot3(own_high[...], own_low[...], *halves(crossline[...]))


def finish_kernel(takes, mine, *rest):
    outer, inner, outer_second, inner_second = (ref[...] for ref in rest[:4])
    outs = rest[4:]
    place = lax.axis_index("xy")
    even, early = place % 2 == 0, place % 4 < 2
    received = (
        jnp.where(even, outer, inner),
        jnp.where(even, inner, outer),
        jnp.where(early, outer_second, inner_second),
        jnp.where(early, inner_second, outer_second),
    )
    at = 0
    for out in outs:
        for row in range(out.shape[0]):
            total = mine[4 * at : 4 * at + 4]
            for take, got in zip(takes, received):
                for j in range(take.shape[1]):
                    factor = float(take[at, j])
                    if abs(factor) > 1e-13:
                        total = total + factor * got[4 * j : 4 * j + 4]
            out[row] = total
            at += 1


def pair_swaps(size):
    one = [1 if i % 2 == 0 else -1 for i in range(size)]
    two = [2 if i % 4 < 2 else -2 for i in range(size)]
    return [
        [(i, (i - one[i]) % size) for i in range(size)],
        [(i, i + one[i]) for i in range(size)],
        [(i, (i - two[i]) % size) for i in range(size)],
        [(i, i + two[i]) for i in range(size)],
    ]


def body(size, wave_p, wave_q, prior_p, prior_q, courant, epsilon, thomsen_delta, tilt_angle, azimuth):
    rows, layers, width = wave_p.shape
    f32 = jnp.float32
    even = lax.axis_index("xy") % 2 == 0
    pairs = pair_swaps(size)
    cores = [(0, 1), (1, 0)]
    stack = jax.ShapeDtypeStruct((rows, 8, width), f32)
    cells = rows * layers * width
    params = pltpu.CompilerParams(vmem_limit_bytes=16 * 1024 * 1024)

    def kernel(function, out_shape, work, name, scratch_shapes=()):
        cost = pl.CostEstimate(flops=work * cells, bytes_accessed=40 * cells, transcendentals=0)
        return pl.pallas_call(
            function,
            out_shape=out_shape,
            scratch_shapes=scratch_shapes,
            compiler_params=params,
            cost_estimate=cost,
            name=name,
        )

    waves = lax.optimization_barrier(jnp.concatenate([wave_p, wave_q], axis=1))
    leading, last = waves[:4], waves[rows - 4 :]
    open_outer = [
        (2 * i + g, 2 * i + 1 - g) if abs(i - j) > 1 else (2 * i + g, 2 * j + g)
        for i, j in pairs[0]
        for g in range(2)
    ]
    outer = lax.ppermute(jnp.where(even, leading, last), ("xy", "gz"), open_outer)
    inner = lax.ppermute(jnp.where(even, last, leading), "xy", pairs[1])
    all_layers = lax.all_gather(waves, "gz")

    taps = jax.ShapeDtypeStruct((4 * LANES, 2 * LANES), jnp.bfloat16)
    axis_x, axis_y, axis_z, *gains, taps_first, taps_second = kernel(
        weights_kernel, [stack] * 6 + [taps] * 2, 100, "weights"
    )(waves, prior_p, prior_q, courant, epsilon, thomsen_delta, tilt_angle, azimuth)
    work = pltpu.VMEM((rows, 8, width), f32)
    h_part, sum_part = kernel(interior_kernel, [stack] * 2, 100, "interior", [work] * 2)(
        waves, axis_x, axis_y, taps_first, taps_second
    )
    h_part, all_layers, outer, inner = lax.optimization_barrier((h_part, all_layers, outer, inner))
    edges = jnp.concatenate([outer, inner], axis=0)
    edges_other = lax.ppermute(edges, "gz", cores)
    h_own, sum_own = kernel(functools.partial(depth_kernel, size), [stack] * 2, 100, "depth", [work] * 3)(
        waves, all_layers, edges, axis_x, axis_y, axis_z, h_part, sum_part, taps_first
    )

    own, factors = inline_blocks(rows)
    offsets = (-1, 1, -2, 2)
    pieces, gives, start = [], [], 0
    for offset in offsets:
        give = factors[offset][1]
        pad = give.shape[0] % 2
        pieces.append(np.pad(give, ((0, pad), (0, 0))))
        gives.append((start, 4 * (give.shape[0] + pad)))
        start += gives[-1][1]

    def parts(matrix):
        return [jnp.asarray(part) for part in split_bf16(matrix)]

    inline = parts(np.kron(np.concatenate(pieces), np.eye(4)))
    inline_own = parts(np.kron(own, np.eye(4)))
    flat = jax.ShapeDtypeStruct((layers * rows, width), f32)
    pressure, crossline, *sends = kernel(
        functools.partial(step_kernel, size, gives),
        [stack, flat] + [jax.ShapeDtypeStruct((count, width), f32) for _, count in gives],
        400,
        "step",
    )(
        edges,
        edges_other,
        h_own,
        sum_own,
        axis_x,
        axis_z,
        *gains,
        *parts(np.concatenate(three_levels(width)).T),
        *inline,
    )
    received = [lax.ppermute(send, "xy", pair) for send, pair in zip(sends, pairs)]
    grid = jax.ShapeDtypeStruct(wave_p.shape, f32)
    next_p, next_q, mine = kernel(own_kernel, [grid, grid, flat], 100, "own")(
        pressure, crossline, *inline_own
    )
    outs = kernel(
        functools.partial(finish_kernel, [factors[offset][0] for offset in offsets]),
        [
            jax.ShapeDtypeStruct((count, layers, width), f32)
            for count in (rows // 2, rows // 4, rows // 8, rows // 8)
        ],
        20,
        "finish",
    )(mine, *received)
    return (next_p, next_q, *outs)


def solution(mesh):
    split = P(("shot", "xy"), "gz", None)
    shared = P("xy", "gz", None)
    return jax.shard_map(
        functools.partial(body, mesh.shape["xy"]),
        mesh=mesh,
        in_specs=(split,) * 4 + (shared,) * 5,
        out_specs=(split,) * 6,
        check_vma=False,
    )
```

```python
import functools

import jax
import jax.numpy as jnp
import numpy as np
from jax import lax
from jax.experimental import pallas as pl
from jax.experimental.pallas import tpu as pltpu
from jax.sharding import PartitionSpec as P

SECOND = (-205.0 / 72.0, 8.0 / 5.0, -1.0 / 5.0, 8.0 / 315.0, -1.0 / 560.0)
FIRST = (4.0 / 5.0, -1.0 / 5.0, 4.0 / 105.0, -1.0 / 280.0)
LIFT = (-1.586134342, -0.05298011854, 0.8829110762, 0.4435068522)
ZETA = 1.149604398
LANES = 128
SCALE_FIRST, SCALE_SECOND = 840.0, 5040.0


def lift_level(values):
    even, odd = values[0::2], values[1::2]
    odd = odd + LIFT[0] * (even + np.roll(even, -1, 0))
    even = even + LIFT[1] * (odd + np.roll(odd, 1, 0))
    odd = odd + LIFT[2] * (even + np.roll(even, -1, 0))
    even = even + LIFT[3] * (odd + np.roll(odd, 1, 0))
    return even * ZETA, odd * (1.0 / ZETA)


def three_levels(length):
    coarse, members = np.eye(length), []
    for _ in range(3):
        coarse, detail = lift_level(coarse)
        members.append(detail)
    return members + [coarse]


def split_bf16(matrix):
    high = matrix.astype(jnp.bfloat16)
    low = (matrix - high.astype(np.float64)).astype(jnp.bfloat16)
    return high, low


def inline_blocks(rows):
    bricks, brick = 8, 4
    members = three_levels(rows * bricks)
    wanted = np.concatenate(
        [m[brick * len(m) // bricks : (brick + 1) * len(m) // bricks] for m in members]
    )

    def block(offset):
        return wanted[:, rows * (brick + offset) : rows * (brick + offset + 1)]

    factors = {}
    for offset in (-1, 1, -2, 2):
        left, sizes, right = np.linalg.svd(block(offset))
        rank = int((sizes > 1e-12).sum())
        root = np.sqrt(sizes[:rank])
        factors[offset] = (left[:, :rank] * root, root[:, None] * right[:rank])
    return block(0), factors


def sine_cosine(angle):
    turns = jnp.round(angle * (2.0 / np.pi))
    rest = angle - turns * 1.5703125
    rest = rest - turns * 4.837512969970703125e-4
    rest = rest - turns * 7.549789948768648e-8
    square = rest * rest
    sine = rest + rest * square * (
        -1.6666654611e-1 + square * (8.3321608736e-3 + square * -1.9515295891e-4)
    )
    cosine = (
        1.0
        - 0.5 * square
        + square
        * square
        * (4.166664568298827e-2 + square * (-1.388731625493765e-3 + square * 2.443315711809948e-5))
    )
    quarter = turns.astype(jnp.int32)
    swapped = (quarter & 1) == 1
    out_sine = jnp.where(swapped, cosine, sine)
    out_cosine = jnp.where(swapped, sine, cosine)
    out_sine = jnp.where((quarter & 2) == 2, -out_sine, out_sine)
    out_cosine = jnp.where(((quarter + 1) & 2) == 2, -out_cosine, out_cosine)
    return out_sine, out_cosine


def band(shape, taps, sign, scale):
    offset = lax.broadcasted_iota(jnp.int32, shape, 0) - LANES
    offset = offset - lax.broadcasted_iota(jnp.int32, shape, 1)
    values = jnp.zeros(shape, jnp.float32)
    for k, tap in enumerate(taps, 1):
        values = jnp.where(jnp.abs(offset) == k, float(np.round(tap * scale)), values)
    if sign < 0:
        values = jnp.where(offset < 0, -values, values)
    return values.astype(jnp.bfloat16)


def weights_kernel(
    waves,
    prior_p,
    prior_q,
    courant,
    epsilon,
    delta,
    tilt,
    azimuth,
    axis_x,
    axis_y,
    axis_z,
    gain_a,
    gain_b,
    base,
    taps_first,
    taps_second,
):
    rows = waves.shape[0]
    taps_first[...] = band(taps_first.shape, FIRST, -1.0, SCALE_FIRST)
    taps_second[...] = band(taps_second.shape, SECOND[1:], 1.0, SCALE_SECOND)
    top = lax.broadcasted_iota(jnp.int32, waves.shape[1:], 0) < 4

    def swap(value):
        return pltpu.roll(value, 4, 0)

    for x in range(rows):
        angles = jnp.concatenate(
            [tilt[x].astype(jnp.float32), azimuth[x].astype(jnp.float32)], axis=0
        )
        sine, cosine = sine_cosine(angles)
        sine_other, cosine_other = swap(sine), swap(cosine)
        sine_tilt = jnp.where(top, sine, sine_other)
        axis_x[x] = sine_tilt * jnp.where(top, cosine_other, cosine)
        axis_y[x] = sine * sine_other
        axis_z[x] = jnp.where(top, cosine, cosine_other)
        speed = courant[x].astype(jnp.float32)
        root = jnp.sqrt(1.0 + 2.0 * delta[x].astype(jnp.float32))
        stretch = 1.0 + 2.0 * epsilon[x].astype(jnp.float32)
        gain_a[x] = jnp.concatenate([speed * stretch, speed], axis=0)
        across = speed * root
        gain_b[x] = jnp.concatenate([across, across], axis=0)
        base[x] = 2.0 * waves[x] - jnp.concatenate([prior_p[x], prior_q[x]], axis=0)


def first_of(ahead, behind):
    total = FIRST[0] * (ahead[0] - behind[0])
    for k in range(1, 4):
        total = total + FIRST[k] * (ahead[k] - behind[k])
    return total


def second_of(centre, ahead, behind):
    total = SECOND[0] * centre
    for k in range(4):
        total = total + SECOND[k + 1] * (ahead[k] + behind[k])
    return total


def dot3(a_high, a_low, b_high, b_low):
    def dot(a, b):
        return jnp.dot(a, b, preferred_element_type=jnp.float32)

    rows = a_high.shape[0]
    both = dot(jnp.concatenate([a_high, a_low], axis=0), b_high)
    return both[:rows] + (both[rows:] + dot(a_high, b_low))


def halves(value):
    high = value.astype(jnp.bfloat16)
    return high, (value - high.astype(jnp.float32)).astype(jnp.bfloat16)


def depth_neighbours(own, far, lower):
    layer = lax.broadcasted_iota(jnp.int32, own.shape, 0) & 3
    up = far * jnp.where(lower, 1.0, 0.0)
    down = far * jnp.where(lower, 0.0, 1.0)
    ahead, behind = [], []
    for k in range(1, 4):
        ahead.append(jnp.where(layer < 4 - k, pltpu.roll(own, 8 - k, 0), pltpu.roll(up, 4 - k, 0)))
        behind.append(jnp.where(layer >= k, pltpu.roll(own, k, 0), pltpu.roll(down, 4 + k, 0)))
    return ahead + [up], behind + [down]


def across(parts, taps):
    width = parts.shape[1]
    blocks = []
    for start in range(0, width, 2 * LANES):
        stop = min(start + 2 * LANES, width)
        first = start - LANES
        low, high = max(first, 0), min(stop + LANES, width)
        block = taps[low - first : high - first, : stop - start]
        blocks.append(jnp.dot(parts[:, low:high], block, preferred_element_type=jnp.float32))
    return jnp.concatenate(blocks, axis=1)


def joined(parts, rows):
    return parts[:rows] + parts[rows:]


def interior_kernel(
    waves, other, axis_x, axis_y, axis_z, taps_first, taps_second, h_own, sum_own, dz, dzz, dy, dyy, dzy
):
    rows, sub, width = waves.shape
    flat = rows * sub
    lower = lax.axis_index("gz") == 0
    for x in range(rows):
        own = waves[x]
        ahead, behind = depth_neighbours(own, other[x], lower)
        dz[x] = first_of(ahead, behind)
        dzz[x] = second_of(own, ahead, behind)
    field = jnp.concatenate(halves(waves[...].reshape(flat, width)), axis=0)
    slope = jnp.concatenate(halves(dz[...].reshape(flat, width)), axis=0)
    dyy[...] = joined(across(field, taps_second), flat).reshape(waves.shape)
    dy[...] = joined(across(field, taps_first), flat).reshape(waves.shape)
    dzy[...] = joined(across(slope, taps_first), flat).reshape(waves.shape)
    for x in range(rows):
        centre = waves[x]
        dxx = SECOND[0] * centre
        dxy = jnp.zeros_like(centre)
        dxz = jnp.zeros_like(centre)
        for k in range(1, 5):
            for step in (k, -k):
                if 0 <= x + step < rows:
                    weight = FIRST[k - 1] if step > 0 else -FIRST[k - 1]
                    dxx = dxx + SECOND[k] * waves[x + step]
                    dxy = dxy + (weight / SCALE_FIRST) * dy[x + step]
                    dxz = dxz + weight * dz[x + step]
        cross = SECOND[0] * centre + (1.0 / SCALE_SECOND) * dyy[x]
        n_x, n_y, n_z = axis_x[x], axis_y[x], axis_z[x]
        h_one = n_x * (n_x * dxx + 2.0 * (n_y * dxy + n_z * dxz))
        h_one = h_one + n_y * (n_y * cross + (2.0 / SCALE_FIRST) * (n_z * dzy[x]))
        h_own[x] = h_one + n_z * (n_z * dzz[x])
        sum_own[x] = dxx + cross + dzz[x]


def halo_rows(size, edges):
    place = lax.axis_index("xy")
    even = place % 2 == 0
    left_at, right_at = jnp.where(even, 0, 4), jnp.where(even, 4, 0)
    left_in = jnp.where(place > 0, 1.0, 0.0)
    right_in = jnp.where(place < size - 1, 1.0, 0.0)
    before = [edges[left_at + x] * left_in for x in range(4)]
    return before + [edges[right_at + x] * right_in for x in range(4)]


def reach(values, row, coefficients, sign):
    total = None
    for k in range(1, 5):
        at = row + 4 - k if row < 4 else row + k - 4
        if (row < 4 and 0 <= at < 4) or (row >= 4 and 4 <= at < 8):
            term = (coefficients[k - 1] * (sign if row < 4 else 1.0)) * values[at]
            total = term if total is None else total + term
    return total


def halo_kernel(size, edges, axis_x, axis_y, h_own, sum_own, taps_first, h_edge, sum_edge):
    rows, sub, width = h_own.shape
    values = halo_rows(size, edges)
    parts = jnp.concatenate(halves(jnp.concatenate(values, axis=0)), axis=0)
    slopes = joined(across(parts, taps_first), 8 * sub)
    slopes = [slopes[sub * x : sub * x + sub] for x in range(8)]
    for row in range(8):
        x = row if row < 4 else rows - 8 + row
        dxx = reach(values, row, SECOND[1:], 1.0)
        dxy = reach(slopes, row, [c / SCALE_FIRST for c in FIRST], -1.0)
        n_x = axis_x[x]
        h_edge[row] = h_own[x] + n_x * (n_x * dxx + 2.0 * (axis_y[x] * dxy))
        sum_edge[row] = sum_own[x] + dxx


def step_kernel(
    size,
    gives,
    edges,
    edges_other,
    h_own,
    sum_own,
    h_edge,
    sum_edge,
    axis_x,
    axis_z,
    gain_a,
    gain_b,
    base,
    across_high,
    across_low,
    inline_high,
    inline_low,
    pressure,
    crossline,
    *sends,
):
    rows, sub, width = h_own.shape
    lower = lax.axis_index("gz") == 0
    place = lax.axis_index("xy")
    even = place % 2 == 0
    top = lax.broadcasted_iota(jnp.int32, (sub, width), 0) < 4

    slopes = [
        first_of(*depth_neighbours(own, far, lower))
        for own, far in zip(halo_rows(size, edges), halo_rows(size, edges_other))
    ]
    for x in range(rows):
        row = x if x < 4 else x - rows + 8
        if 4 <= x < rows - 4:
            h_one, total = h_own[x], sum_own[x]
        else:
            dxz = reach(slopes, row, FIRST, -1.0)
            h_one, total = h_edge[row] + 2.0 * (axis_x[x] * axis_z[x] * dxz), sum_edge[row]
        mixed = jnp.where(top, total - h_one, h_one)
        pressure[x] = base[x] + gain_a[x] * mixed + gain_b[x] * pltpu.roll(mixed, 4, 0)

    packed = jnp.concatenate(
        [
            jnp.where(top, pressure[x], pltpu.roll(pressure[x + 1], 4, 0))
            for x in range(0, rows, 2)
        ],
        axis=0,
    )
    transformed = dot3(*halves(packed), across_high[...], across_low[...])
    crossline[...] = transformed
    parts = dot3(inline_high[...], inline_low[...], *halves(transformed))
    to_next, to_previous, to_second_next, to_second_previous = (
        parts[start : start + count] for start, count in gives
    )
    sends[0][...] = jnp.where(even, to_previous, to_next)
    sends[1][...] = jnp.where(even, to_next, to_previous)
    sends[2][...] = jnp.concatenate([to_second_next, to_second_previous], axis=0)


def finish_kernel(
    takes, pressure, crossline, own_high, own_low, outer, inner, second, next_p, next_q, *outs
):
    for x in range(pressure.shape[0]):
        next_p[x] = pressure[x, :4]
        next_q[x] = pressure[x, 4:]
    mine = dot3(own_high[...], own_low[...], *halves(crossline[...]))
    place = lax.axis_index("xy")
    even = place % 2 == 0
    count, rows = second.shape[0], second.shape[1] // 2
    before, after = (place // 2 + count - 1) % count, (place // 2 + 1) % count
    received = (
        jnp.where(even, outer[...], inner[...]),
        jnp.where(even, inner[...], outer[...]),
        second[before, :rows],
        second[after, rows:],
    )
    at = 0
    for out in outs:
        for row in range(out.shape[0]):
            total = mine[4 * at : 4 * at + 4]
            for take, got in zip(takes, received):
                for j in range(take.shape[1]):
                    factor = float(take[at, j])
                    if abs(factor) > 1e-13:
                        total = total + factor * got[4 * j : 4 * j + 4]
            out[row] = total
            at += 1


def pair_swaps(size):
    one = [1 if i % 2 == 0 else -1 for i in range(size)]
    return [
        [(i, (i - one[i]) % size) for i in range(size)],
        [(i, i + one[i]) for i in range(size)],
    ]


def body(size, wave_p, wave_q, prior_p, prior_q, courant, epsilon, thomsen_delta, tilt_angle, azimuth):
    rows, layers, width = wave_p.shape
    f32 = jnp.float32
    even = lax.axis_index("xy") % 2 == 0
    pairs = pair_swaps(size)
    cores = [(0, 1), (1, 0)]
    stack = jax.ShapeDtypeStruct((rows, 8, width), f32)
    cells = rows * layers * width
    params = pltpu.CompilerParams(vmem_limit_bytes=16 * 1024 * 1024)

    def kernel(function, out_shape, work, name, scratch_shapes=()):
        cost = pl.CostEstimate(flops=work * cells, bytes_accessed=40 * cells, transcendentals=0)
        return pl.pallas_call(
            function,
            out_shape=out_shape,
            scratch_shapes=scratch_shapes,
            compiler_params=params,
            cost_estimate=cost,
            name=name,
        )

    waves = lax.optimization_barrier(jnp.concatenate([wave_p, wave_q], axis=1))
    leading, last = waves[:4], waves[rows - 4 :]
    open_outer = [
        (2 * i + g, 2 * i + 1 - g) if abs(i - j) > 1 else (2 * i + g, 2 * j + g)
        for i, j in pairs[0]
        for g in range(2)
    ]
    other = lax.ppermute(waves, "gz", cores)
    inner = lax.ppermute(jnp.where(even, last, leading), "xy", pairs[1])
    outer = lax.ppermute(jnp.where(even, leading, last), ("xy", "gz"), open_outer)

    taps = jax.ShapeDtypeStruct((4 * LANES, 2 * LANES), jnp.bfloat16)
    axis_x, axis_y, axis_z, *gains, taps_first, taps_second = kernel(
        weights_kernel, [stack] * 6 + [taps] * 2, 100, "weights"
    )(waves, prior_p, prior_q, courant, epsilon, thomsen_delta, tilt_angle, azimuth)
    work = pltpu.VMEM((rows, 8, width), f32)
    h_own, sum_own = kernel(interior_kernel, [stack] * 2, 100, "interior", [work] * 5)(
        waves, other, axis_x, axis_y, axis_z, taps_first, taps_second
    )
    h_own, sum_own, inner, outer = lax.optimization_barrier((h_own, sum_own, inner, outer))
    edges = jnp.concatenate([outer, inner], axis=0)
    edges_other = lax.ppermute(edges, "gz", cores)
    edge = jax.ShapeDtypeStruct((8, 8, width), f32)
    h_edge, sum_edge = kernel(functools.partial(halo_kernel, size), [edge] * 2, 100, "halo")(
        edges, axis_x, axis_y, h_own, sum_own, taps_first
    )

    own, factors = inline_blocks(rows)
    offsets = (-1, 1, -2, 2)
    pieces, gives, start = [], [], 0
    for offset in offsets:
        give = factors[offset][1]
        pad = give.shape[0] % 2
        pieces.append(np.pad(give, ((0, pad), (0, 0))))
        gives.append((start, 4 * (give.shape[0] + pad)))
        start += gives[-1][1]

    def parts(matrix):
        return [jnp.asarray(part) for part in split_bf16(matrix)]

    inline = parts(np.kron(np.concatenate(pieces), np.eye(4)))
    inline_own = parts(np.kron(own, np.eye(4)))
    flat = jax.ShapeDtypeStruct((layers * rows, width), f32)
    first, second = gives[0][1], gives[2][1]
    pressure, crossline, *sends = kernel(
        functools.partial(step_kernel, size, gives),
        [stack, flat] + [jax.ShapeDtypeStruct((count, width), f32) for count in (first, first, 2 * second)],
        400,
        "step",
    )(
        edges,
        edges_other,
        h_own,
        sum_own,
        h_edge,
        sum_edge,
        axis_x,
        axis_z,
        *gains,
        *parts(np.concatenate(three_levels(width)).T),
        *inline,
    )
    received = [lax.ppermute(send, "xy", pair) for send, pair in zip(sends, pairs)]
    lines = [list(range(first, size, 2)) for first in range(2)]
    received.append(lax.all_gather(sends[2], "xy", axis_index_groups=lines))
    grid = jax.ShapeDtypeStruct(wave_p.shape, f32)
    next_p, next_q, *outs = kernel(
        functools.partial(finish_kernel, [factors[offset][0] for offset in offsets]),
        [grid, grid]
        + [
            jax.ShapeDtypeStruct((count, layers, width), f32)
            for count in (rows // 2, rows // 4, rows // 8, rows // 8)
        ],
        20,
        "finish",
    )(pressure, crossline, *inline_own, *received)
    return (next_p, next_q, *outs)


def solution(mesh):
    split = P(("shot", "xy"), "gz", None)
    shared = P("xy", "gz", None)
    return jax.shard_map(
        functools.partial(body, mesh.shape["xy"]),
        mesh=mesh,
        in_specs=(split,) * 4 + (shared,) * 5,
        out_specs=(split,) * 6,
        check_vma=False,
    )
```

```python
import functools

import jax
import jax.numpy as jnp
import numpy as np
from jax import lax
from jax.experimental import pallas as pl
from jax.experimental.pallas import tpu as pltpu
from jax.sharding import PartitionSpec as P

SECOND = (-205.0 / 72.0, 8.0 / 5.0, -1.0 / 5.0, 8.0 / 315.0, -1.0 / 560.0)
FIRST = (4.0 / 5.0, -1.0 / 5.0, 4.0 / 105.0, -1.0 / 280.0)
LIFT = (-1.586134342, -0.05298011854, 0.8829110762, 0.4435068522)
ZETA = 1.149604398
LANES = 128
SCALE_FIRST, SCALE_SECOND = 840.0, 5040.0


def lift_level(values):
    even, odd = values[0::2], values[1::2]
    odd = odd + LIFT[0] * (even + np.roll(even, -1, 0))
    even = even + LIFT[1] * (odd + np.roll(odd, 1, 0))
    odd = odd + LIFT[2] * (even + np.roll(even, -1, 0))
    even = even + LIFT[3] * (odd + np.roll(odd, 1, 0))
    return even * ZETA, odd * (1.0 / ZETA)


def three_levels(length):
    coarse, members = np.eye(length), []
    for _ in range(3):
        coarse, detail = lift_level(coarse)
        members.append(detail)
    return members + [coarse]


def crossline_block(width):
    tiles = width // LANES
    members = three_levels(width)
    tile = tiles // 2
    wanted = np.concatenate(
        [m[tile * len(m) // tiles : (tile + 1) * len(m) // tiles] for m in members]
    )
    return wanted[:, (tile - 1) * LANES : (tile + 2) * LANES].T


def split_bf16(matrix):
    high = matrix.astype(jnp.bfloat16)
    low = (matrix - high.astype(np.float64)).astype(jnp.bfloat16)
    return high, low


def inline_blocks(rows):
    bricks, brick = 8, 4
    members = three_levels(rows * bricks)
    wanted = np.concatenate(
        [m[brick * len(m) // bricks : (brick + 1) * len(m) // bricks] for m in members]
    )

    def block(offset):
        return wanted[:, rows * (brick + offset) : rows * (brick + offset + 1)]

    factors = {}
    for offset in (-1, 1, -2, 2):
        left, sizes, right = np.linalg.svd(block(offset))
        rank = int((sizes > 1e-12).sum())
        root = np.sqrt(sizes[:rank])
        factors[offset] = (left[:, :rank] * root, root[:, None] * right[:rank])
    return block(0), factors


def sine_cosine(angle):
    turns = jnp.round(angle * (2.0 / np.pi))
    rest = angle - turns * 1.5703125
    rest = rest - turns * 4.837512969970703125e-4
    rest = rest - turns * 7.549789948768648e-8
    square = rest * rest
    sine = rest + rest * square * (
        -1.6666654611e-1 + square * (8.3321608736e-3 + square * -1.9515295891e-4)
    )
    cosine = (
        1.0
        - 0.5 * square
        + square
        * square
        * (4.166664568298827e-2 + square * (-1.388731625493765e-3 + square * 2.443315711809948e-5))
    )
    quarter = turns.astype(jnp.int32)
    swapped = (quarter & 1) == 1
    out_sine = jnp.where(swapped, cosine, sine)
    out_cosine = jnp.where(swapped, sine, cosine)
    out_sine = jnp.where((quarter & 2) == 2, -out_sine, out_sine)
    out_cosine = jnp.where(((quarter + 1) & 2) == 2, -out_cosine, out_cosine)
    return out_sine, out_cosine


def band(shape, taps, sign, scale):
    offset = lax.broadcasted_iota(jnp.int32, shape, 0) - LANES
    offset = offset - lax.broadcasted_iota(jnp.int32, shape, 1)
    values = jnp.zeros(shape, jnp.float32)
    for k, tap in enumerate(taps, 1):
        values = jnp.where(jnp.abs(offset) == k, float(np.round(tap * scale)), values)
    if sign < 0:
        values = jnp.where(offset < 0, -values, values)
    return values.astype(jnp.bfloat16)


def weights_kernel(
    waves,
    prior_p,
    prior_q,
    courant,
    epsilon,
    delta,
    tilt,
    azimuth,
    axis_x,
    axis_y,
    axis_z,
    gain_a,
    gain_b,
    base,
    taps_first,
    taps_second,
):
    rows = waves.shape[0]
    taps_first[...] = band(taps_first.shape, FIRST, -1.0, SCALE_FIRST)
    taps_second[...] = band(taps_second.shape, SECOND[1:], 1.0, SCALE_SECOND)
    top = lax.broadcasted_iota(jnp.int32, waves.shape[1:], 0) < 4

    def swap(value):
        return pltpu.roll(value, 4, 0)

    for x in range(rows):
        angles = jnp.concatenate(
            [tilt[x].astype(jnp.float32), azimuth[x].astype(jnp.float32)], axis=0
        )
        sine, cosine = sine_cosine(angles)
        sine_other, cosine_other = swap(sine), swap(cosine)
        sine_tilt = jnp.where(top, sine, sine_other)
        axis_x[x] = sine_tilt * jnp.where(top, cosine_other, cosine)
        axis_y[x] = sine * sine_other
        axis_z[x] = jnp.where(top, cosine, cosine_other)
        speed = courant[x].astype(jnp.float32)
        root = jnp.sqrt(1.0 + 2.0 * delta[x].astype(jnp.float32))
        stretch = 1.0 + 2.0 * epsilon[x].astype(jnp.float32)
        gain_a[x] = jnp.concatenate([speed * stretch, speed], axis=0)
        across = speed * root
        gain_b[x] = jnp.concatenate([across, across], axis=0)
        base[x] = 2.0 * waves[x] - jnp.concatenate([prior_p[x], prior_q[x]], axis=0)


def first_of(ahead, behind):
    total = FIRST[0] * (ahead[0] - behind[0])
    for k in range(1, 4):
        total = total + FIRST[k] * (ahead[k] - behind[k])
    return total


def second_of(centre, ahead, behind):
    total = SECOND[0] * centre
    for k in range(4):
        total = total + SECOND[k + 1] * (ahead[k] + behind[k])
    return total


def dot3(a_high, a_low, b_high, b_low):
    def dot(a, b):
        return jnp.dot(a, b, preferred_element_type=jnp.float32)

    rows = a_high.shape[0]
    both = dot(jnp.concatenate([a_high, a_low], axis=0), b_high)
    return both[:rows] + (both[rows:] + dot(a_high, b_low))


def halves(value):
    high = value.astype(jnp.bfloat16)
    return high, (value - high.astype(jnp.float32)).astype(jnp.bfloat16)


def packed_rows(rows):
    top = lax.broadcasted_iota(jnp.int32, rows[0].shape, 0) < 4
    return jnp.concatenate(
        [
            jnp.where(top, rows[x], pltpu.roll(rows[x + 1], 4, 0))
            for x in range(0, len(rows), 2)
        ],
        axis=0,
    )


def crossline_of(rows, block_high, block_low):
    count, width = rows.shape
    tiles = width // LANES

    def windows(values):
        parts = [values[:, LANES * t : LANES * (t + 1)] for t in range(tiles)]
        return [
            jnp.concatenate([parts[t - 1], parts[t], parts[(t + 1) % tiles]], axis=1)
            for t in range(tiles)
        ]

    high, low = (jnp.concatenate(windows(part), axis=0) for part in halves(rows))
    result = dot3(high, low, block_high, block_low)
    lane = lax.broadcasted_iota(jnp.int32, (count, LANES), 1)
    ordered = [jnp.zeros((count, LANES), jnp.float32)] * tiles
    source, target = 0, 0
    for size in (LANES // 2, LANES // 4, LANES // 8, LANES // 8):
        for t in range(tiles):
            tile, offset = divmod(target + size * t, LANES)
            piece = result[count * t : count * (t + 1)]
            shift = (offset - source) % LANES
            if shift:
                piece = pltpu.roll(piece, shift, 1)
            inside = (lane >= offset) & (lane < offset + size)
            ordered[tile] = jnp.where(inside, piece, ordered[tile])
        source += size
        target += size * tiles
    return jnp.concatenate(ordered, axis=1)


def pressure_of(h_one, total, gain_a, gain_b, base):
    top = lax.broadcasted_iota(jnp.int32, h_one.shape, 0) < 4
    mixed = jnp.where(top, total - h_one, h_one)
    return base + gain_a * mixed + gain_b * pltpu.roll(mixed, 4, 0)


def depth_neighbours(own, far, lower):
    layer = lax.broadcasted_iota(jnp.int32, own.shape, 0) & 3
    up = far * jnp.where(lower, 1.0, 0.0)
    down = far * jnp.where(lower, 0.0, 1.0)
    ahead, behind = [], []
    for k in range(1, 4):
        ahead.append(jnp.where(layer < 4 - k, pltpu.roll(own, 8 - k, 0), pltpu.roll(up, 4 - k, 0)))
        behind.append(jnp.where(layer >= k, pltpu.roll(own, k, 0), pltpu.roll(down, 4 + k, 0)))
    return ahead + [up], behind + [down]


def across(parts, taps):
    width = parts.shape[1]
    blocks = []
    for start in range(0, width, 2 * LANES):
        stop = min(start + 2 * LANES, width)
        first = start - LANES
        low, high = max(first, 0), min(stop + LANES, width)
        block = taps[low - first : high - first, : stop - start]
        blocks.append(jnp.dot(parts[:, low:high], block, preferred_element_type=jnp.float32))
    return jnp.concatenate(blocks, axis=1)


def joined(parts, rows):
    return parts[:rows] + parts[rows:]


def interior_kernel(
    waves,
    other,
    axis_x,
    axis_y,
    axis_z,
    gain_a,
    gain_b,
    base,
    taps_first,
    taps_second,
    block_high,
    block_low,
    h_own,
    sum_own,
    inside,
    crossline,
    dz,
    dzz,
    dy,
    dyy,
    dzy,
):
    rows, sub, width = waves.shape
    flat = rows * sub
    lower = lax.axis_index("gz") == 0
    for x in range(rows):
        own = waves[x]
        ahead, behind = depth_neighbours(own, other[x], lower)
        dz[x] = first_of(ahead, behind)
        dzz[x] = second_of(own, ahead, behind)
    field = jnp.concatenate(halves(waves[...].reshape(flat, width)), axis=0)
    slope = jnp.concatenate(halves(dz[...].reshape(flat, width)), axis=0)
    dyy[...] = joined(across(field, taps_second), flat).reshape(waves.shape)
    dy[...] = joined(across(field, taps_first), flat).reshape(waves.shape)
    dzy[...] = joined(across(slope, taps_first), flat).reshape(waves.shape)
    for x in range(rows):
        centre = waves[x]
        dxx = SECOND[0] * centre
        dxy = jnp.zeros_like(centre)
        dxz = jnp.zeros_like(centre)
        for k in range(1, 5):
            for step in (k, -k):
                if 0 <= x + step < rows:
                    weight = FIRST[k - 1] if step > 0 else -FIRST[k - 1]
                    dxx = dxx + SECOND[k] * waves[x + step]
                    dxy = dxy + (weight / SCALE_FIRST) * dy[x + step]
                    dxz = dxz + weight * dz[x + step]
        cross = SECOND[0] * centre + (1.0 / SCALE_SECOND) * dyy[x]
        n_x, n_y, n_z = axis_x[x], axis_y[x], axis_z[x]
        h_one = n_x * (n_x * dxx + 2.0 * (n_y * dxy + n_z * dxz))
        h_one = h_one + n_y * (n_y * cross + (2.0 / SCALE_FIRST) * (n_z * dzy[x]))
        h_one = h_one + n_z * (n_z * dzz[x])
        total = dxx + cross + dzz[x]
        if 4 <= x < rows - 4:
            inside[x - 4] = pressure_of(h_one, total, gain_a[x], gain_b[x], base[x])
        else:
            row = x if x < 4 else x - rows + 8
            h_own[row], sum_own[row] = h_one, total
    ready = packed_rows([inside[x] for x in range(rows - 8)])
    crossline[...] = crossline_of(ready, block_high[...], block_low[...])


def halo_rows(size, edges):
    place = lax.axis_index("xy")
    even = place % 2 == 0
    left_at, right_at = jnp.where(even, 0, 4), jnp.where(even, 4, 0)
    left_in = jnp.where(place > 0, 1.0, 0.0)
    right_in = jnp.where(place < size - 1, 1.0, 0.0)
    before = [edges[left_at + x] * left_in for x in range(4)]
    return before + [edges[right_at + x] * right_in for x in range(4)]


def reach(values, row, coefficients, sign):
    total = None
    for k in range(1, 5):
        at = row + 4 - k if row < 4 else row + k - 4
        if (row < 4 and 0 <= at < 4) or (row >= 4 and 4 <= at < 8):
            term = (coefficients[k - 1] * (sign if row < 4 else 1.0)) * values[at]
            total = term if total is None else total + term
    return total


def halo_kernel(size, edges, axis_x, axis_y, h_own, sum_own, taps_first, h_edge, sum_edge):
    rows, sub, _ = axis_x.shape
    values = halo_rows(size, edges)
    parts = jnp.concatenate(halves(jnp.concatenate(values, axis=0)), axis=0)
    slopes = joined(across(parts, taps_first), 8 * sub)
    slopes = [slopes[sub * x : sub * x + sub] for x in range(8)]
    for row in range(8):
        x = row if row < 4 else rows - 8 + row
        dxx = reach(values, row, SECOND[1:], 1.0)
        dxy = reach(slopes, row, [c / SCALE_FIRST for c in FIRST], -1.0)
        n_x = axis_x[x]
        h_edge[row] = h_own[row] + n_x * (n_x * dxx + 2.0 * (axis_y[x] * dxy))
        sum_edge[row] = sum_own[row] + dxx


def step_kernel(
    size,
    gives,
    edges,
    edges_other,
    h_edge,
    sum_edge,
    axis_x,
    axis_z,
    gain_a,
    gain_b,
    base,
    block_high,
    block_low,
    crossline_inside,
    inline_high,
    inline_low,
    outside,
    crossline,
    *sends,
):
    rows = axis_x.shape[0]
    lower = lax.axis_index("gz") == 0
    place = lax.axis_index("xy")
    even, early = place % 2 == 0, place % 4 < 2

    slopes = [
        first_of(*depth_neighbours(own, far, lower))
        for own, far in zip(halo_rows(size, edges), halo_rows(size, edges_other))
    ]
    for row in range(8):
        x = row if row < 4 else rows - 8 + row
        dxz = reach(slopes, row, FIRST, -1.0)
        h_one = h_edge[row] + 2.0 * (axis_x[x] * axis_z[x] * dxz)
        outside[row] = pressure_of(h_one, sum_edge[row], gain_a[x], gain_b[x], base[x])
    ready = packed_rows([outside[row] for row in range(8)])
    edge = crossline_of(ready, block_high[...], block_low[...])
    transformed = jnp.concatenate([edge[:16], crossline_inside[...], edge[16:]], axis=0)
    crossline[...] = transformed
    parts = dot3(inline_high[...], inline_low[...], *halves(transformed))
    to_next, to_previous, to_second_next, to_second_previous = (
        parts[start : start + count] for start, count in gives
    )
    sends[0][...] = jnp.where(even, to_previous, to_next)
    sends[1][...] = jnp.where(even, to_next, to_previous)
    sends[2][...] = jnp.where(early, to_second_previous, to_second_next)
    sends[3][...] = jnp.where(early, to_second_next, to_second_previous)


def own_kernel(inside, outside, crossline, own_high, own_low, next_p, next_q, mine):
    rows = next_p.shape[0]
    for x in range(rows):
        if 4 <= x < rows - 4:
            value = inside[x - 4]
        else:
            value = outside[x if x < 4 else x - rows + 8]
        next_p[x] = value[:4]
        next_q[x] = value[4:]
    mine[...] = dot3(own_high[...], own_low[...], *halves(crossline[...]))


def finish_kernel(at, takes, mine, *rest):
    received, outs = [ref[...] for ref in rest[: len(takes)]], rest[len(takes) :]
    place = lax.axis_index("xy")
    for first, near in zip(range(0, len(takes), 2), (place % 2 == 0, place % 4 < 2)):
        outer, inner = received[first : first + 2]
        received[first : first + 2] = jnp.where(near, outer, inner), jnp.where(near, inner, outer)
    for out in outs:
        for row in range(out.shape[0]):
            total = mine[4 * at : 4 * at + 4]
            for take, got in zip(takes, received):
                for j in range(take.shape[1]):
                    factor = float(take[at, j])
                    if abs(factor) > 1e-13:
                        total = total + factor * got[4 * j : 4 * j + 4]
            out[row] = total
            at += 1


def pair_swaps(size):
    one = [1 if i % 2 == 0 else -1 for i in range(size)]
    two = [2 if i % 4 < 2 else -2 for i in range(size)]
    return [
        [(i, (i - one[i]) % size) for i in range(size)],
        [(i, i + one[i]) for i in range(size)],
        [(i, (i - two[i]) % size) for i in range(size)],
        [(i, i + two[i]) for i in range(size)],
    ]


def body(size, wave_p, wave_q, prior_p, prior_q, courant, epsilon, thomsen_delta, tilt_angle, azimuth):
    rows, layers, width = wave_p.shape
    f32 = jnp.float32
    even = lax.axis_index("xy") % 2 == 0
    pairs = pair_swaps(size)
    cores = [(0, 1), (1, 0)]
    stack = jax.ShapeDtypeStruct((rows, 8, width), f32)

    def parts(matrix):
        return [jnp.asarray(part) for part in split_bf16(matrix)]

    cells = rows * layers * width
    params = pltpu.CompilerParams(vmem_limit_bytes=16 * 1024 * 1024)

    def kernel(function, out_shape, work, name, scratch_shapes=()):
        cost = pl.CostEstimate(flops=work * cells, bytes_accessed=40 * cells, transcendentals=0)
        return pl.pallas_call(
            function,
            out_shape=out_shape,
            scratch_shapes=scratch_shapes,
            compiler_params=params,
            cost_estimate=cost,
            name=name,
        )

    waves = lax.optimization_barrier(jnp.concatenate([wave_p, wave_q], axis=1))
    leading, last = waves[:4], waves[rows - 4 :]
    open_outer = [
        (2 * i + g, 2 * i + 1 - g) if abs(i - j) > 1 else (2 * i + g, 2 * j + g)
        for i, j in pairs[0]
        for g in range(2)
    ]
    other = lax.ppermute(waves, "gz", cores)
    inner = lax.ppermute(jnp.where(even, last, leading), "xy", pairs[1])
    outer = lax.ppermute(jnp.where(even, leading, last), ("xy", "gz"), open_outer)

    taps = jax.ShapeDtypeStruct((4 * LANES, 2 * LANES), jnp.bfloat16)
    axis_x, axis_y, axis_z, *gains, taps_first, taps_second = kernel(
        weights_kernel, [stack] * 6 + [taps] * 2, 100, "weights"
    )(waves, prior_p, prior_q, courant, epsilon, thomsen_delta, tilt_angle, azimuth)
    block = parts(crossline_block(width))
    work = pltpu.VMEM((rows, 8, width), f32)
    edge = jax.ShapeDtypeStruct((8, 8, width), f32)
    inside = jax.ShapeDtypeStruct((rows - 8, 8, width), f32)
    ready = jax.ShapeDtypeStruct((layers * (rows - 8), width), f32)
    h_own, sum_own, inside, crossline = kernel(
        interior_kernel, [edge, edge, inside, ready], 100, "interior", [work] * 5
    )(waves, other, axis_x, axis_y, axis_z, *gains, taps_first, taps_second, *block)
    h_own, sum_own, inner, outer = lax.optimization_barrier((h_own, sum_own, inner, outer))
    edges = jnp.concatenate([outer, inner], axis=0)
    edges_other = lax.ppermute(edges, "gz", cores)
    h_edge, sum_edge = kernel(functools.partial(halo_kernel, size), [edge] * 2, 100, "halo")(
        edges, axis_x, axis_y, h_own, sum_own, taps_first
    )

    own, factors = inline_blocks(rows)
    offsets = (-1, 1, -2, 2)
    pieces, gives, start = [], [], 0
    for offset in offsets:
        give = factors[offset][1]
        pad = give.shape[0] % 2
        pieces.append(np.pad(give, ((0, pad), (0, 0))))
        gives.append((start, 4 * (give.shape[0] + pad)))
        start += gives[-1][1]

    inline = parts(np.kron(np.concatenate(pieces), np.eye(4)))
    inline_own = parts(np.kron(own, np.eye(4)))
    flat = jax.ShapeDtypeStruct((layers * rows, width), f32)
    outside, crossline, *sends = kernel(
        functools.partial(step_kernel, size, gives),
        [edge, flat] + [jax.ShapeDtypeStruct((count, width), f32) for _, count in gives],
        400,
        "step",
    )(edges, edges_other, h_edge, sum_edge, axis_x, axis_z, *gains, *block, crossline, *inline)
    received = [lax.ppermute(send, "xy", pair) for send, pair in zip(sends, pairs)]
    grid = jax.ShapeDtypeStruct(wave_p.shape, f32)
    next_p, next_q, mine = kernel(own_kernel, [grid, grid, flat], 100, "own")(
        inside, outside, crossline, *inline_own
    )
    takes = [factors[offset][0] for offset in offsets]
    counts = (rows // 2, rows // 4, rows // 8, rows // 8)
    outs = [jax.ShapeDtypeStruct((count, layers, width), f32) for count in counts]
    first, second = kernel(functools.partial(finish_kernel, 0, takes[:2]), outs[:2], 20, "fine")(
        mine, *received[:2]
    )
    first, *received[2:] = lax.optimization_barrier((first, *received[2:]))
    third, coarse = kernel(
        functools.partial(finish_kernel, counts[0] + counts[1], takes), outs[2:], 20, "coarse"
    )(mine, *received)
    return (next_p, next_q, first, second, third, coarse)


def solution(mesh):
    split = P(("shot", "xy"), "gz", None)
    shared = P("xy", "gz", None)
    return jax.shard_map(
        functools.partial(body, mesh.shape["xy"]),
        mesh=mesh,
        in_specs=(split,) * 4 + (shared,) * 5,
        out_specs=(split,) * 6,
        check_vma=False,
    )
```

```python
import functools

import jax
import jax.numpy as jnp
import numpy as np
from jax import lax
from jax.experimental import pallas as pl
from jax.experimental.pallas import tpu as pltpu
from jax.sharding import PartitionSpec as P

SECOND = (-205.0 / 72.0, 8.0 / 5.0, -1.0 / 5.0, 8.0 / 315.0, -1.0 / 560.0)
FIRST = (4.0 / 5.0, -1.0 / 5.0, 4.0 / 105.0, -1.0 / 280.0)
LIFT = (-1.586134342, -0.05298011854, 0.8829110762, 0.4435068522)
ZETA = 1.149604398
LANES = 128
LONG = 25_000_000
SCALE_FIRST, SCALE_SECOND = 840.0, 5040.0


def lift_level(values):
    even, odd = values[0::2], values[1::2]
    odd = odd + LIFT[0] * (even + np.roll(even, -1, 0))
    even = even + LIFT[1] * (odd + np.roll(odd, 1, 0))
    odd = odd + LIFT[2] * (even + np.roll(even, -1, 0))
    even = even + LIFT[3] * (odd + np.roll(odd, 1, 0))
    return even * ZETA, odd * (1.0 / ZETA)


def three_levels(length):
    coarse, members = np.eye(length), []
    for _ in range(3):
        coarse, detail = lift_level(coarse)
        members.append(detail)
    return members + [coarse]


def crossline_block(width):
    tiles = width // LANES
    members = three_levels(width)
    tile = tiles // 2
    wanted = np.concatenate(
        [m[tile * len(m) // tiles : (tile + 1) * len(m) // tiles] for m in members]
    )
    return wanted[:, (tile - 1) * LANES : (tile + 2) * LANES].T


def split_bf16(matrix):
    high = matrix.astype(jnp.bfloat16)
    low = (matrix - high.astype(np.float64)).astype(jnp.bfloat16)
    return high, low


def inline_blocks(rows):
    bricks, brick = 8, 4
    members = three_levels(rows * bricks)
    wanted = np.concatenate(
        [m[brick * len(m) // bricks : (brick + 1) * len(m) // bricks] for m in members]
    )

    def block(offset):
        return wanted[:, rows * (brick + offset) : rows * (brick + offset + 1)]

    factors = {}
    for offset in (-1, 1, -2, 2):
        left, sizes, right = np.linalg.svd(block(offset))
        rank = int((sizes > 1e-12).sum())
        root = np.sqrt(sizes[:rank])
        factors[offset] = (left[:, :rank] * root, root[:, None] * right[:rank])
    return block(0), factors


def sine_cosine(angle):
    turns = jnp.round(angle * (2.0 / np.pi))
    rest = angle - turns * 1.5703125
    rest = rest - turns * 4.837512969970703125e-4
    rest = rest - turns * 7.549789948768648e-8
    square = rest * rest
    sine = rest + rest * square * (
        -1.6666654611e-1 + square * (8.3321608736e-3 + square * -1.9515295891e-4)
    )
    cosine = (
        1.0
        - 0.5 * square
        + square
        * square
        * (4.166664568298827e-2 + square * (-1.388731625493765e-3 + square * 2.443315711809948e-5))
    )
    quarter = turns.astype(jnp.int32)
    swapped = (quarter & 1) == 1
    out_sine = jnp.where(swapped, cosine, sine)
    out_cosine = jnp.where(swapped, sine, cosine)
    out_sine = jnp.where((quarter & 2) == 2, -out_sine, out_sine)
    out_cosine = jnp.where(((quarter + 1) & 2) == 2, -out_cosine, out_cosine)
    return out_sine, out_cosine


def band(shape, taps, sign, scale):
    offset = lax.broadcasted_iota(jnp.int32, shape, 0) - LANES
    offset = offset - lax.broadcasted_iota(jnp.int32, shape, 1)
    values = jnp.zeros(shape, jnp.float32)
    for k, tap in enumerate(taps, 1):
        values = jnp.where(jnp.abs(offset) == k, float(np.round(tap * scale)), values)
    if sign < 0:
        values = jnp.where(offset < 0, -values, values)
    return values.astype(jnp.bfloat16)


def weights_kernel(
    waves,
    prior_p,
    prior_q,
    courant,
    epsilon,
    delta,
    tilt,
    azimuth,
    axis_x,
    axis_y,
    axis_z,
    gain_a,
    gain_b,
    base,
    taps_first,
    taps_second,
):
    rows = waves.shape[0]
    taps_first[...] = band(taps_first.shape, FIRST, -1.0, SCALE_FIRST)
    taps_second[...] = band(taps_second.shape, SECOND[1:], 1.0, SCALE_SECOND)
    top = lax.broadcasted_iota(jnp.int32, waves.shape[1:], 0) < 4

    def swap(value):
        return pltpu.roll(value, 4, 0)

    for x in range(rows):
        angles = jnp.concatenate(
            [tilt[x].astype(jnp.float32), azimuth[x].astype(jnp.float32)], axis=0
        )
        sine, cosine = sine_cosine(angles)
        sine_other, cosine_other = swap(sine), swap(cosine)
        sine_tilt = jnp.where(top, sine, sine_other)
        axis_x[x] = sine_tilt * jnp.where(top, cosine_other, cosine)
        axis_y[x] = sine * sine_other
        axis_z[x] = jnp.where(top, cosine, cosine_other)
        speed = courant[x].astype(jnp.float32)
        root = jnp.sqrt(1.0 + 2.0 * delta[x].astype(jnp.float32))
        stretch = 1.0 + 2.0 * epsilon[x].astype(jnp.float32)
        gain_a[x] = jnp.concatenate([speed * stretch, speed], axis=0)
        across = speed * root
        gain_b[x] = jnp.concatenate([across, across], axis=0)
        base[x] = 2.0 * waves[x] - jnp.concatenate([prior_p[x], prior_q[x]], axis=0)


def first_of(ahead, behind):
    total = FIRST[0] * (ahead[0] - behind[0])
    for k in range(1, 4):
        total = total + FIRST[k] * (ahead[k] - behind[k])
    return total


def second_of(centre, ahead, behind):
    total = SECOND[0] * centre
    for k in range(4):
        total = total + SECOND[k + 1] * (ahead[k] + behind[k])
    return total


def dot3(a_high, a_low, b_high, b_low):
    def dot(a, b):
        return jnp.dot(a, b, preferred_element_type=jnp.float32)

    rows = a_high.shape[0]
    both = dot(jnp.concatenate([a_high, a_low], axis=0), b_high)
    return both[:rows] + (both[rows:] + dot(a_high, b_low))


def halves(value):
    high = value.astype(jnp.bfloat16)
    return high, (value - high.astype(jnp.float32)).astype(jnp.bfloat16)


def packed_rows(rows):
    top = lax.broadcasted_iota(jnp.int32, rows[0].shape, 0) < 4
    return jnp.concatenate(
        [
            jnp.where(top, rows[x], pltpu.roll(rows[x + 1], 4, 0))
            for x in range(0, len(rows), 2)
        ],
        axis=0,
    )


def crossline_of(rows, block_high, block_low):
    count, width = rows.shape
    tiles = width // LANES

    def windows(values):
        parts = [values[:, LANES * t : LANES * (t + 1)] for t in range(tiles)]
        return [
            jnp.concatenate([parts[t - 1], parts[t], parts[(t + 1) % tiles]], axis=1)
            for t in range(tiles)
        ]

    high, low = (jnp.concatenate(windows(part), axis=0) for part in halves(rows))
    result = dot3(high, low, block_high, block_low)
    lane = lax.broadcasted_iota(jnp.int32, (count, LANES), 1)
    ordered = [jnp.zeros((count, LANES), jnp.float32)] * tiles
    source, target = 0, 0
    for size in (LANES // 2, LANES // 4, LANES // 8, LANES // 8):
        for t in range(tiles):
            tile, offset = divmod(target + size * t, LANES)
            piece = result[count * t : count * (t + 1)]
            shift = (offset - source) % LANES
            if shift:
                piece = pltpu.roll(piece, shift, 1)
            inside = (lane >= offset) & (lane < offset + size)
            ordered[tile] = jnp.where(inside, piece, ordered[tile])
        source += size
        target += size * tiles
    return jnp.concatenate(ordered, axis=1)


def pressure_of(h_one, total, gain_a, gain_b, base):
    top = lax.broadcasted_iota(jnp.int32, h_one.shape, 0) < 4
    mixed = jnp.where(top, total - h_one, h_one)
    return base + gain_a * mixed + gain_b * pltpu.roll(mixed, 4, 0)


def depth_neighbours(own, far, lower):
    layer = lax.broadcasted_iota(jnp.int32, own.shape, 0) & 3
    up = far * jnp.where(lower, 1.0, 0.0)
    down = far * jnp.where(lower, 0.0, 1.0)
    ahead, behind = [], []
    for k in range(1, 4):
        ahead.append(jnp.where(layer < 4 - k, pltpu.roll(own, 8 - k, 0), pltpu.roll(up, 4 - k, 0)))
        behind.append(jnp.where(layer >= k, pltpu.roll(own, k, 0), pltpu.roll(down, 4 + k, 0)))
    return ahead + [up], behind + [down]


def across(parts, taps):
    width = parts.shape[1]
    blocks = []
    for start in range(0, width, 2 * LANES):
        stop = min(start + 2 * LANES, width)
        first = start - LANES
        low, high = max(first, 0), min(stop + LANES, width)
        block = taps[low - first : high - first, : stop - start]
        blocks.append(jnp.dot(parts[:, low:high], block, preferred_element_type=jnp.float32))
    return jnp.concatenate(blocks, axis=1)


def joined(parts, rows):
    return parts[:rows] + parts[rows:]


def interior_kernel(
    waves,
    other,
    axis_x,
    axis_y,
    axis_z,
    gain_a,
    gain_b,
    base,
    taps_first,
    taps_second,
    block_high,
    block_low,
    h_own,
    sum_own,
    inside,
    crossline,
    dz,
    dzz,
    dy,
    dyy,
    dzy,
):
    rows, sub, width = waves.shape
    flat = rows * sub
    lower = lax.axis_index("gz") == 0
    for x in range(rows):
        own = waves[x]
        ahead, behind = depth_neighbours(own, other[x], lower)
        dz[x] = first_of(ahead, behind)
        dzz[x] = second_of(own, ahead, behind)
    field = jnp.concatenate(halves(waves[...].reshape(flat, width)), axis=0)
    slope = jnp.concatenate(halves(dz[...].reshape(flat, width)), axis=0)
    dyy[...] = joined(across(field, taps_second), flat).reshape(waves.shape)
    dy[...] = joined(across(field, taps_first), flat).reshape(waves.shape)
    dzy[...] = joined(across(slope, taps_first), flat).reshape(waves.shape)
    for x in range(rows):
        centre = waves[x]
        dxx = SECOND[0] * centre
        dxy = jnp.zeros_like(centre)
        dxz = jnp.zeros_like(centre)
        for k in range(1, 5):
            for step in (k, -k):
                if 0 <= x + step < rows:
                    weight = FIRST[k - 1] if step > 0 else -FIRST[k - 1]
                    dxx = dxx + SECOND[k] * waves[x + step]
                    dxy = dxy + (weight / SCALE_FIRST) * dy[x + step]
                    dxz = dxz + weight * dz[x + step]
        cross = SECOND[0] * centre + (1.0 / SCALE_SECOND) * dyy[x]
        n_x, n_y, n_z = axis_x[x], axis_y[x], axis_z[x]
        h_one = n_x * (n_x * dxx + 2.0 * (n_y * dxy + n_z * dxz))
        h_one = h_one + n_y * (n_y * cross + (2.0 / SCALE_FIRST) * (n_z * dzy[x]))
        h_one = h_one + n_z * (n_z * dzz[x])
        total = dxx + cross + dzz[x]
        if 4 <= x < rows - 4:
            inside[x - 4] = pressure_of(h_one, total, gain_a[x], gain_b[x], base[x])
        else:
            row = x if x < 4 else x - rows + 8
            h_own[row], sum_own[row] = h_one, total
    ready = packed_rows([inside[x] for x in range(rows - 8)])
    crossline[...] = crossline_of(ready, block_high[...], block_low[...])


def halo_rows(size, edges):
    place = lax.axis_index("xy")
    even = place % 2 == 0
    left_at, right_at = jnp.where(even, 0, 4), jnp.where(even, 4, 0)
    left_in = jnp.where(place > 0, 1.0, 0.0)
    right_in = jnp.where(place < size - 1, 1.0, 0.0)
    before = [edges[left_at + x] * left_in for x in range(4)]
    return before + [edges[right_at + x] * right_in for x in range(4)]


def reach(values, row, coefficients, sign):
    total = None
    for k in range(1, 5):
        at = row + 4 - k if row < 4 else row + k - 4
        if (row < 4 and 0 <= at < 4) or (row >= 4 and 4 <= at < 8):
            term = (coefficients[k - 1] * (sign if row < 4 else 1.0)) * values[at]
            total = term if total is None else total + term
    return total


def halo_kernel(size, edges, axis_x, axis_y, h_own, sum_own, taps_first, h_edge, sum_edge):
    rows, sub, _ = axis_x.shape
    values = halo_rows(size, edges)
    parts = jnp.concatenate(halves(jnp.concatenate(values, axis=0)), axis=0)
    slopes = joined(across(parts, taps_first), 8 * sub)
    slopes = [slopes[sub * x : sub * x + sub] for x in range(8)]
    for row in range(8):
        x = row if row < 4 else rows - 8 + row
        dxx = reach(values, row, SECOND[1:], 1.0)
        dxy = reach(slopes, row, [c / SCALE_FIRST for c in FIRST], -1.0)
        n_x = axis_x[x]
        h_edge[row] = h_own[row] + n_x * (n_x * dxx + 2.0 * (axis_y[x] * dxy))
        sum_edge[row] = sum_own[row] + dxx


def step_kernel(
    size,
    gives,
    edges,
    edges_other,
    h_edge,
    sum_edge,
    axis_x,
    axis_z,
    gain_a,
    gain_b,
    base,
    block_high,
    block_low,
    crossline_inside,
    inline_high,
    inline_low,
    outside,
    crossline,
    *sends,
):
    rows = axis_x.shape[0]
    lower = lax.axis_index("gz") == 0
    place = lax.axis_index("xy")
    even, early = place % 2 == 0, place % 4 < 2

    slopes = [
        first_of(*depth_neighbours(own, far, lower))
        for own, far in zip(halo_rows(size, edges), halo_rows(size, edges_other))
    ]
    for row in range(8):
        x = row if row < 4 else rows - 8 + row
        dxz = reach(slopes, row, FIRST, -1.0)
        h_one = h_edge[row] + 2.0 * (axis_x[x] * axis_z[x] * dxz)
        outside[row] = pressure_of(h_one, sum_edge[row], gain_a[x], gain_b[x], base[x])
    ready = packed_rows([outside[row] for row in range(8)])
    edge = crossline_of(ready, block_high[...], block_low[...])
    transformed = jnp.concatenate([edge[:16], crossline_inside[...], edge[16:]], axis=0)
    crossline[...] = transformed
    parts = dot3(inline_high[...], inline_low[...], *halves(transformed))
    to_next, to_previous, to_second_next, to_second_previous = (
        parts[start : start + count] for start, count in gives
    )
    sends[0][...] = jnp.where(even, to_previous, to_next)
    sends[1][...] = jnp.where(early, to_second_previous, to_second_next)
    sends[2][...] = jnp.where(even, to_next, to_previous)
    sends[3][...] = jnp.where(early, to_second_next, to_second_previous)


def own_kernel(inside, outside, crossline, own_high, own_low, next_p, next_q, mine):
    rows = next_p.shape[0]
    for x in range(rows):
        if 4 <= x < rows - 4:
            value = inside[x - 4]
        else:
            value = outside[x if x < 4 else x - rows + 8]
        next_p[x] = value[:4]
        next_q[x] = value[4:]
    mine[...] = dot3(own_high[...], own_low[...], *halves(crossline[...]))


def finish_kernel(takes, mine, *rest):
    outer, outer_second, inner, inner_second = (ref[...] for ref in rest[:4])
    outs = rest[4:]
    place = lax.axis_index("xy")
    even, early = place % 2 == 0, place % 4 < 2
    received = (
        jnp.where(even, outer, inner),
        jnp.where(even, inner, outer),
        jnp.where(early, outer_second, inner_second),
        jnp.where(early, inner_second, outer_second),
    )
    at = 0
    for out in outs:
        for row in range(out.shape[0]):
            total = mine[4 * at : 4 * at + 4]
            for take, got in zip(takes, received):
                for j in range(take.shape[1]):
                    factor = float(take[at, j])
                    if abs(factor) > 1e-13:
                        total = total + factor * got[4 * j : 4 * j + 4]
            out[row] = total
            at += 1


def pair_swaps(size):
    one = [1 if i % 2 == 0 else -1 for i in range(size)]
    two = [2 if i % 4 < 2 else -2 for i in range(size)]
    return [
        [(i, (i - one[i]) % size) for i in range(size)],
        [(i, (i - two[i]) % size) for i in range(size)],
        [(i, i + one[i]) for i in range(size)],
        [(i, i + two[i]) for i in range(size)],
    ]


def body(size, wave_p, wave_q, prior_p, prior_q, courant, epsilon, thomsen_delta, tilt_angle, azimuth):
    rows, layers, width = wave_p.shape
    f32 = jnp.float32
    even = lax.axis_index("xy") % 2 == 0
    pairs = pair_swaps(size)
    cores = [(0, 1), (1, 0)]
    stack = jax.ShapeDtypeStruct((rows, 8, width), f32)

    def parts(matrix):
        return [jnp.asarray(part) for part in split_bf16(matrix)]

    cells = rows * layers * width
    params = pltpu.CompilerParams(vmem_limit_bytes=16 * 1024 * 1024)

    def kernel(function, out_shape, work, name, scratch_shapes=()):
        cost = pl.CostEstimate(flops=work * cells, bytes_accessed=40 * cells, transcendentals=0)
        return pl.pallas_call(
            function,
            out_shape=out_shape,
            scratch_shapes=scratch_shapes,
            compiler_params=params,
            cost_estimate=cost,
            name=name,
        )

    waves = lax.optimization_barrier(jnp.concatenate([wave_p, wave_q], axis=1))
    leading, last = waves[:4], waves[rows - 4 :]
    open_outer = [
        (2 * i + g, 2 * i + 1 - g) if abs(i - j) > 1 else (2 * i + g, 2 * j + g)
        for i, j in pairs[0]
        for g in range(2)
    ]
    to_outer, to_inner = jnp.where(even, leading, last), jnp.where(even, last, leading)
    to_outer, to_inner, fields = lax.optimization_barrier((to_outer, to_inner, waves))
    outer = lax.ppermute(to_outer, ("xy", "gz"), open_outer)
    inner = lax.ppermute(to_inner, "xy", pairs[2])
    other = lax.ppermute(fields, "gz", cores)

    taps = jax.ShapeDtypeStruct((4 * LANES, 2 * LANES), jnp.bfloat16)
    axis_x, axis_y, axis_z, *gains, taps_first, taps_second = kernel(
        weights_kernel, [stack] * 6 + [taps] * 2, LONG, "weights"
    )(waves, prior_p, prior_q, courant, epsilon, thomsen_delta, tilt_angle, azimuth)
    block = parts(crossline_block(width))
    work = pltpu.VMEM((rows, 8, width), f32)
    edge = jax.ShapeDtypeStruct((8, 8, width), f32)
    inside = jax.ShapeDtypeStruct((rows - 8, 8, width), f32)
    ready = jax.ShapeDtypeStruct((layers * (rows - 8), width), f32)
    h_own, sum_own, inside, crossline = kernel(
        interior_kernel, [edge, edge, inside, ready], 100, "interior", [work] * 5
    )(waves, other, axis_x, axis_y, axis_z, *gains, taps_first, taps_second, *block)
    h_own, sum_own, inner, outer = lax.optimization_barrier((h_own, sum_own, inner, outer))
    edges = jnp.concatenate([outer, inner], axis=0)
    edges_other = lax.ppermute(edges, "gz", cores)
    h_edge, sum_edge = kernel(functools.partial(halo_kernel, size), [edge] * 2, 100, "halo")(
        edges, axis_x, axis_y, h_own, sum_own, taps_first
    )

    own, factors = inline_blocks(rows)
    offsets = (-1, 1, -2, 2)
    pieces, gives, start = [], [], 0
    for offset in offsets:
        give = factors[offset][1]
        pad = give.shape[0] % 2
        pieces.append(np.pad(give, ((0, pad), (0, 0))))
        gives.append((start, 4 * (give.shape[0] + pad)))
        start += gives[-1][1]

    inline = parts(np.kron(np.concatenate(pieces), np.eye(4)))
    inline_own = parts(np.kron(own, np.eye(4)))
    flat = jax.ShapeDtypeStruct((layers * rows, width), f32)
    sizes = [gives[k][1] for k in (0, 2, 1, 3)]
    outside, crossline, *sends = kernel(
        functools.partial(step_kernel, size, gives),
        [edge, flat] + [jax.ShapeDtypeStruct((count, width), f32) for count in sizes],
        400,
        "step",
    )(edges, edges_other, h_edge, sum_edge, axis_x, axis_z, *gains, *block, crossline, *inline)
    received = [lax.ppermute(send, "xy", pair) for send, pair in zip(sends, pairs)]
    grid = jax.ShapeDtypeStruct(wave_p.shape, f32)
    next_p, next_q, mine = kernel(own_kernel, [grid, grid, flat], LONG, "own")(
        inside, outside, crossline, *inline_own
    )
    outs = kernel(
        functools.partial(finish_kernel, [factors[offset][0] for offset in offsets]),
        [
            jax.ShapeDtypeStruct((count, layers, width), f32)
            for count in (rows // 2, rows // 4, rows // 8, rows // 8)
        ],
        20,
        "finish",
    )(mine, *received)
    return (next_p, next_q, *outs)


def solution(mesh):
    split = P(("shot", "xy"), "gz", None)
    shared = P("xy", "gz", None)
    return jax.shard_map(
        functools.partial(body, mesh.shape["xy"]),
        mesh=mesh,
        in_specs=(split,) * 4 + (shared,) * 5,
        out_specs=(split,) * 6,
        check_vma=False,
    )
```

```python
import functools

import jax
import jax.numpy as jnp
import numpy as np
from jax import lax
from jax.experimental import pallas as pl
from jax.experimental.pallas import tpu as pltpu
from jax.sharding import PartitionSpec as P

SECOND = (-205.0 / 72.0, 8.0 / 5.0, -1.0 / 5.0, 8.0 / 315.0, -1.0 / 560.0)
FIRST = (4.0 / 5.0, -1.0 / 5.0, 4.0 / 105.0, -1.0 / 280.0)
LIFT = (-1.586134342, -0.05298011854, 0.8829110762, 0.4435068522)
ZETA = 1.149604398
LANES = 128
LONG = 250_000
SCALE_FIRST, SCALE_SECOND = 840.0, 5040.0


def lift_level(values):
    even, odd = values[0::2], values[1::2]
    odd = odd + LIFT[0] * (even + np.roll(even, -1, 0))
    even = even + LIFT[1] * (odd + np.roll(odd, 1, 0))
    odd = odd + LIFT[2] * (even + np.roll(even, -1, 0))
    even = even + LIFT[3] * (odd + np.roll(odd, 1, 0))
    return even * ZETA, odd * (1.0 / ZETA)


def three_levels(length):
    coarse, members = np.eye(length), []
    for _ in range(3):
        coarse, detail = lift_level(coarse)
        members.append(detail)
    return members + [coarse]


def crossline_block(width):
    tiles = width // LANES
    members = three_levels(width)
    tile = tiles // 2
    wanted = np.concatenate(
        [m[tile * len(m) // tiles : (tile + 1) * len(m) // tiles] for m in members]
    )
    return wanted[:, (tile - 1) * LANES : (tile + 2) * LANES].T


def split_bf16(matrix):
    high = matrix.astype(jnp.bfloat16)
    low = (matrix - high.astype(np.float64)).astype(jnp.bfloat16)
    return high, low


def inline_blocks(rows):
    bricks, brick = 8, 4
    members = three_levels(rows * bricks)
    wanted = np.concatenate(
        [m[brick * len(m) // bricks : (brick + 1) * len(m) // bricks] for m in members]
    )

    def block(offset):
        return wanted[:, rows * (brick + offset) : rows * (brick + offset + 1)]

    factors = {}
    for offset in (-1, 1, -2, 2):
        left, sizes, right = np.linalg.svd(block(offset))
        rank = int((sizes > 1e-12).sum())
        root = np.sqrt(sizes[:rank])
        factors[offset] = (left[:, :rank] * root, root[:, None] * right[:rank])
    return block(0), factors


def sine_cosine(angle):
    turns = jnp.round(angle * (2.0 / np.pi))
    rest = angle - turns * 1.5703125
    rest = rest - turns * 4.837512969970703125e-4
    rest = rest - turns * 7.549789948768648e-8
    square = rest * rest
    sine = rest + rest * square * (
        -1.6666654611e-1 + square * (8.3321608736e-3 + square * -1.9515295891e-4)
    )
    cosine = (
        1.0
        - 0.5 * square
        + square
        * square
        * (4.166664568298827e-2 + square * (-1.388731625493765e-3 + square * 2.443315711809948e-5))
    )
    quarter = turns.astype(jnp.int32)
    swapped = (quarter & 1) == 1
    out_sine = jnp.where(swapped, cosine, sine)
    out_cosine = jnp.where(swapped, sine, cosine)
    out_sine = jnp.where((quarter & 2) == 2, -out_sine, out_sine)
    out_cosine = jnp.where(((quarter + 1) & 2) == 2, -out_cosine, out_cosine)
    return out_sine, out_cosine


def band(shape, taps, sign, scale):
    offset = lax.broadcasted_iota(jnp.int32, shape, 0) - LANES
    offset = offset - lax.broadcasted_iota(jnp.int32, shape, 1)
    values = jnp.zeros(shape, jnp.float32)
    for k, tap in enumerate(taps, 1):
        values = jnp.where(jnp.abs(offset) == k, float(np.round(tap * scale)), values)
    if sign < 0:
        values = jnp.where(offset < 0, -values, values)
    return values.astype(jnp.bfloat16)


def taps_kernel(taps_first, taps_second):
    taps_first[...] = band(taps_first.shape, FIRST, -1.0, SCALE_FIRST)
    taps_second[...] = band(taps_second.shape, SECOND[1:], 1.0, SCALE_SECOND)


def weights_kernel(
    waves,
    prior_p,
    prior_q,
    courant,
    epsilon,
    delta,
    tilt,
    azimuth,
    axis_x,
    axis_y,
    axis_z,
    gain_a,
    gain_b,
    base,
):
    rows = waves.shape[0]
    top = lax.broadcasted_iota(jnp.int32, waves.shape[1:], 0) < 4

    def swap(value):
        return pltpu.roll(value, 4, 0)

    for x in range(rows):
        angles = jnp.concatenate(
            [tilt[x].astype(jnp.float32), azimuth[x].astype(jnp.float32)], axis=0
        )
        sine, cosine = sine_cosine(angles)
        sine_other, cosine_other = swap(sine), swap(cosine)
        sine_tilt = jnp.where(top, sine, sine_other)
        axis_x[x] = sine_tilt * jnp.where(top, cosine_other, cosine)
        axis_y[x] = sine * sine_other
        axis_z[x] = jnp.where(top, cosine, cosine_other)
        speed = courant[x].astype(jnp.float32)
        root = jnp.sqrt(1.0 + 2.0 * delta[x].astype(jnp.float32))
        stretch = 1.0 + 2.0 * epsilon[x].astype(jnp.float32)
        gain_a[x] = jnp.concatenate([speed * stretch, speed], axis=0)
        across = speed * root
        gain_b[x] = jnp.concatenate([across, across], axis=0)
        base[x] = 2.0 * waves[x] - jnp.concatenate([prior_p[x], prior_q[x]], axis=0)


def first_of(ahead, behind):
    total = FIRST[0] * (ahead[0] - behind[0])
    for k in range(1, 4):
        total = total + FIRST[k] * (ahead[k] - behind[k])
    return total


def second_of(centre, ahead, behind):
    total = SECOND[0] * centre
    for k in range(4):
        total = total + SECOND[k + 1] * (ahead[k] + behind[k])
    return total


def dot3(a_high, a_low, b_high, b_low):
    def dot(a, b):
        return jnp.dot(a, b, preferred_element_type=jnp.float32)

    rows = a_high.shape[0]
    both = dot(jnp.concatenate([a_high, a_low], axis=0), b_high)
    return both[:rows] + (both[rows:] + dot(a_high, b_low))


def halves(value):
    high = value.astype(jnp.bfloat16)
    return high, (value - high.astype(jnp.float32)).astype(jnp.bfloat16)


def packed_rows(rows):
    top = lax.broadcasted_iota(jnp.int32, rows[0].shape, 0) < 4
    return jnp.concatenate(
        [
            jnp.where(top, rows[x], pltpu.roll(rows[x + 1], 4, 0))
            for x in range(0, len(rows), 2)
        ],
        axis=0,
    )


def crossline_of(rows, block_high, block_low):
    count, width = rows.shape
    tiles = width // LANES

    def windows(values):
        parts = [values[:, LANES * t : LANES * (t + 1)] for t in range(tiles)]
        return [
            jnp.concatenate([parts[t - 1], parts[t], parts[(t + 1) % tiles]], axis=1)
            for t in range(tiles)
        ]

    high, low = (jnp.concatenate(windows(part), axis=0) for part in halves(rows))
    result = dot3(high, low, block_high, block_low)
    lane = lax.broadcasted_iota(jnp.int32, (count, LANES), 1)
    ordered = [jnp.zeros((count, LANES), jnp.float32)] * tiles
    source, target = 0, 0
    for size in (LANES // 2, LANES // 4, LANES // 8, LANES // 8):
        for t in range(tiles):
            tile, offset = divmod(target + size * t, LANES)
            piece = result[count * t : count * (t + 1)]
            shift = (offset - source) % LANES
            if shift:
                piece = pltpu.roll(piece, shift, 1)
            inside = (lane >= offset) & (lane < offset + size)
            ordered[tile] = jnp.where(inside, piece, ordered[tile])
        source += size
        target += size * tiles
    return jnp.concatenate(ordered, axis=1)


def pressure_of(h_one, total, gain_a, gain_b, base):
    top = lax.broadcasted_iota(jnp.int32, h_one.shape, 0) < 4
    mixed = jnp.where(top, total - h_one, h_one)
    return base + gain_a * mixed + gain_b * pltpu.roll(mixed, 4, 0)


def depth_neighbours(own, far, lower):
    layer = lax.broadcasted_iota(jnp.int32, own.shape, 0) & 3
    up = far * jnp.where(lower, 1.0, 0.0)
    down = far * jnp.where(lower, 0.0, 1.0)
    ahead, behind = [], []
    for k in range(1, 4):
        ahead.append(jnp.where(layer < 4 - k, pltpu.roll(own, 8 - k, 0), pltpu.roll(up, 4 - k, 0)))
        behind.append(jnp.where(layer >= k, pltpu.roll(own, k, 0), pltpu.roll(down, 4 + k, 0)))
    return ahead + [up], behind + [down]


def across(parts, taps):
    width = parts.shape[1]
    blocks = []
    for start in range(0, width, 2 * LANES):
        stop = min(start + 2 * LANES, width)
        first = start - LANES
        low, high = max(first, 0), min(stop + LANES, width)
        block = taps[low - first : high - first, : stop - start]
        blocks.append(jnp.dot(parts[:, low:high], block, preferred_element_type=jnp.float32))
    return jnp.concatenate(blocks, axis=1)


def joined(parts, rows):
    return parts[:rows] + parts[rows:]


def interior_kernel(
    waves,
    other,
    axis_x,
    axis_y,
    axis_z,
    gain_a,
    gain_b,
    base,
    taps_first,
    taps_second,
    block_high,
    block_low,
    h_own,
    sum_own,
    inside,
    crossline,
    dz,
    dzz,
    dy,
    dyy,
    dzy,
):
    rows, sub, width = waves.shape
    flat = rows * sub
    lower = lax.axis_index("gz") == 0
    for x in range(rows):
        own = waves[x]
        ahead, behind = depth_neighbours(own, other[x], lower)
        dz[x] = first_of(ahead, behind)
        dzz[x] = second_of(own, ahead, behind)
    field = jnp.concatenate(halves(waves[...].reshape(flat, width)), axis=0)
    slope = jnp.concatenate(halves(dz[...].reshape(flat, width)), axis=0)
    dyy[...] = joined(across(field, taps_second), flat).reshape(waves.shape)
    dy[...] = joined(across(field, taps_first), flat).reshape(waves.shape)
    dzy[...] = joined(across(slope, taps_first), flat).reshape(waves.shape)
    for x in range(rows):
        centre = waves[x]
        dxx = SECOND[0] * centre
        dxy = jnp.zeros_like(centre)
        dxz = jnp.zeros_like(centre)
        for k in range(1, 5):
            for step in (k, -k):
                if 0 <= x + step < rows:
                    weight = FIRST[k - 1] if step > 0 else -FIRST[k - 1]
                    dxx = dxx + SECOND[k] * waves[x + step]
                    dxy = dxy + (weight / SCALE_FIRST) * dy[x + step]
                    dxz = dxz + weight * dz[x + step]
        cross = SECOND[0] * centre + (1.0 / SCALE_SECOND) * dyy[x]
        n_x, n_y, n_z = axis_x[x], axis_y[x], axis_z[x]
        h_one = n_x * (n_x * dxx + 2.0 * (n_y * dxy + n_z * dxz))
        h_one = h_one + n_y * (n_y * cross + (2.0 / SCALE_FIRST) * (n_z * dzy[x]))
        h_one = h_one + n_z * (n_z * dzz[x])
        total = dxx + cross + dzz[x]
        if 4 <= x < rows - 4:
            inside[x - 4] = pressure_of(h_one, total, gain_a[x], gain_b[x], base[x])
        else:
            row = x if x < 4 else x - rows + 8
            h_own[row], sum_own[row] = h_one, total
    ready = packed_rows([inside[x] for x in range(rows - 8)])
    crossline[...] = crossline_of(ready, block_high[...], block_low[...])


def halo_rows(size, edges):
    place = lax.axis_index("xy")
    even = place % 2 == 0
    left_at, right_at = jnp.where(even, 0, 4), jnp.where(even, 4, 0)
    left_in = jnp.where(place > 0, 1.0, 0.0)
    right_in = jnp.where(place < size - 1, 1.0, 0.0)
    before = [edges[left_at + x] * left_in for x in range(4)]
    return before + [edges[right_at + x] * right_in for x in range(4)]


def reach(values, row, coefficients, sign):
    total = None
    for k in range(1, 5):
        at = row + 4 - k if row < 4 else row + k - 4
        if (row < 4 and 0 <= at < 4) or (row >= 4 and 4 <= at < 8):
            term = (coefficients[k - 1] * (sign if row < 4 else 1.0)) * values[at]
            total = term if total is None else total + term
    return total


def halo_kernel(size, edges, axis_x, axis_y, h_own, sum_own, taps_first, h_edge, sum_edge):
    rows, sub, _ = axis_x.shape
    values = halo_rows(size, edges)
    parts = jnp.concatenate(halves(jnp.concatenate(values, axis=0)), axis=0)
    slopes = joined(across(parts, taps_first), 8 * sub)
    slopes = [slopes[sub * x : sub * x + sub] for x in range(8)]
    for row in range(8):
        x = row if row < 4 else rows - 8 + row
        dxx = reach(values, row, SECOND[1:], 1.0)
        dxy = reach(slopes, row, [c / SCALE_FIRST for c in FIRST], -1.0)
        n_x = axis_x[x]
        h_edge[row] = h_own[row] + n_x * (n_x * dxx + 2.0 * (axis_y[x] * dxy))
        sum_edge[row] = sum_own[row] + dxx


def step_kernel(
    size,
    gives,
    edges,
    edges_other,
    h_edge,
    sum_edge,
    axis_x,
    axis_z,
    gain_a,
    gain_b,
    base,
    block_high,
    block_low,
    crossline_inside,
    inline_high,
    inline_low,
    outside,
    crossline,
    *sends,
):
    rows = axis_x.shape[0]
    lower = lax.axis_index("gz") == 0
    place = lax.axis_index("xy")
    even, early = place % 2 == 0, place % 4 < 2

    slopes = [
        first_of(*depth_neighbours(own, far, lower))
        for own, far in zip(halo_rows(size, edges), halo_rows(size, edges_other))
    ]
    for row in range(8):
        x = row if row < 4 else rows - 8 + row
        dxz = reach(slopes, row, FIRST, -1.0)
        h_one = h_edge[row] + 2.0 * (axis_x[x] * axis_z[x] * dxz)
        outside[row] = pressure_of(h_one, sum_edge[row], gain_a[x], gain_b[x], base[x])
    ready = packed_rows([outside[row] for row in range(8)])
    edge = crossline_of(ready, block_high[...], block_low[...])
    transformed = jnp.concatenate([edge[:16], crossline_inside[...], edge[16:]], axis=0)
    crossline[...] = transformed
    parts = dot3(inline_high[...], inline_low[...], *halves(transformed))
    to_next, to_previous, to_second_next, to_second_previous = (
        parts[start : start + count] for start, count in gives
    )
    sends[0][...] = jnp.where(even, to_previous, to_next)
    sends[1][...] = jnp.where(early, to_second_previous, to_second_next)
    sends[2][...] = jnp.where(even, to_next, to_previous)
    sends[3][...] = jnp.where(early, to_second_next, to_second_previous)


def own_kernel(inside, outside, crossline, own_high, own_low, next_p, next_q, mine):
    rows = next_p.shape[0]
    for x in range(rows):
        if 4 <= x < rows - 4:
            value = inside[x - 4]
        else:
            value = outside[x if x < 4 else x - rows + 8]
        next_p[x] = value[:4]
        next_q[x] = value[4:]
    mine[...] = dot3(own_high[...], own_low[...], *halves(crossline[...]))


def finish_kernel(takes, mine, *rest):
    outer, outer_second, inner, inner_second = (ref[...] for ref in rest[:4])
    outs = rest[4:]
    place = lax.axis_index("xy")
    even, early = place % 2 == 0, place % 4 < 2
    received = (
        jnp.where(even, outer, inner),
        jnp.where(even, inner, outer),
        jnp.where(early, outer_second, inner_second),
        jnp.where(early, inner_second, outer_second),
    )
    at = 0
    for out in outs:
        for row in range(out.shape[0]):
            total = mine[4 * at : 4 * at + 4]
            for take, got in zip(takes, received):
                for j in range(take.shape[1]):
                    factor = float(take[at, j])
                    if abs(factor) > 1e-13:
                        total = total + factor * got[4 * j : 4 * j + 4]
            out[row] = total
            at += 1


def pair_swaps(size):
    one = [1 if i % 2 == 0 else -1 for i in range(size)]
    two = [2 if i % 4 < 2 else -2 for i in range(size)]
    return [
        [(i, (i - one[i]) % size) for i in range(size)],
        [(i, (i - two[i]) % size) for i in range(size)],
        [(i, i + one[i]) for i in range(size)],
        [(i, i + two[i]) for i in range(size)],
    ]


def body(size, wave_p, wave_q, prior_p, prior_q, courant, epsilon, thomsen_delta, tilt_angle, azimuth):
    rows, layers, width = wave_p.shape
    f32 = jnp.float32
    even = lax.axis_index("xy") % 2 == 0
    pairs = pair_swaps(size)
    cores = [(0, 1), (1, 0)]
    stack = jax.ShapeDtypeStruct((rows, 8, width), f32)

    def parts(matrix):
        return [jnp.asarray(part) for part in split_bf16(matrix)]

    cells = rows * layers * width
    params = pltpu.CompilerParams(vmem_limit_bytes=16 * 1024 * 1024)

    def kernel(function, out_shape, work, name, scratch_shapes=()):
        cost = pl.CostEstimate(flops=work * cells, bytes_accessed=40 * cells, transcendentals=0)
        return pl.pallas_call(
            function,
            out_shape=out_shape,
            scratch_shapes=scratch_shapes,
            compiler_params=params,
            cost_estimate=cost,
            name=name,
        )

    waves = lax.optimization_barrier(jnp.concatenate([wave_p, wave_q], axis=1))
    leading, last = waves[:4], waves[rows - 4 :]
    open_outer = [
        (2 * i + g, 2 * i + 1 - g) if abs(i - j) > 1 else (2 * i + g, 2 * j + g)
        for i, j in pairs[0]
        for g in range(2)
    ]
    to_outer, to_inner = jnp.where(even, leading, last), jnp.where(even, last, leading)
    to_outer, to_inner, fields = lax.optimization_barrier((to_outer, to_inner, waves))
    outer = lax.ppermute(to_outer, ("xy", "gz"), open_outer)
    inner = lax.ppermute(to_inner, "xy", pairs[2])
    other = lax.ppermute(fields, "gz", cores)

    taps = jax.ShapeDtypeStruct((4 * LANES, 2 * LANES), jnp.bfloat16)
    taps_first, taps_second = kernel(taps_kernel, [taps] * 2, LONG, "taps")()
    axis_x, axis_y, axis_z, *gains = kernel(weights_kernel, [stack] * 6, 100, "weights")(
        waves, prior_p, prior_q, courant, epsilon, thomsen_delta, tilt_angle, azimuth
    )
    block = parts(crossline_block(width))
    work = pltpu.VMEM((rows, 8, width), f32)
    edge = jax.ShapeDtypeStruct((8, 8, width), f32)
    inside = jax.ShapeDtypeStruct((rows - 8, 8, width), f32)
    ready = jax.ShapeDtypeStruct((layers * (rows - 8), width), f32)
    h_own, sum_own, inside, crossline = kernel(
        interior_kernel, [edge, edge, inside, ready], 100, "interior", [work] * 5
    )(waves, other, axis_x, axis_y, axis_z, *gains, taps_first, taps_second, *block)
    h_own, sum_own, inner, outer = lax.optimization_barrier((h_own, sum_own, inner, outer))
    edges = jnp.concatenate([outer, inner], axis=0)
    edges_other = lax.ppermute(edges, "gz", cores)
    h_edge, sum_edge = kernel(functools.partial(halo_kernel, size), [edge] * 2, 100, "halo")(
        edges, axis_x, axis_y, h_own, sum_own, taps_first
    )

    own, factors = inline_blocks(rows)
    offsets = (-1, 1, -2, 2)
    pieces, gives, start = [], [], 0
    for offset in offsets:
        give = factors[offset][1]
        pad = give.shape[0] % 2
        pieces.append(np.pad(give, ((0, pad), (0, 0))))
        gives.append((start, 4 * (give.shape[0] + pad)))
        start += gives[-1][1]

    inline = parts(np.kron(np.concatenate(pieces), np.eye(4)))
    inline_own = parts(np.kron(own, np.eye(4)))
    flat = jax.ShapeDtypeStruct((layers * rows, width), f32)
    sizes = [gives[k][1] for k in (0, 2, 1, 3)]
    outside, crossline, *sends = kernel(
        functools.partial(step_kernel, size, gives),
        [edge, flat] + [jax.ShapeDtypeStruct((count, width), f32) for count in sizes],
        400,
        "step",
    )(edges, edges_other, h_edge, sum_edge, axis_x, axis_z, *gains, *block, crossline, *inline)
    received = [lax.ppermute(send, "xy", pair) for send, pair in zip(sends, pairs)]
    grid = jax.ShapeDtypeStruct(wave_p.shape, f32)
    next_p, next_q, mine = kernel(own_kernel, [grid, grid, flat], 100, "own")(
        inside, outside, crossline, *inline_own
    )
    outs = kernel(
        functools.partial(finish_kernel, [factors[offset][0] for offset in offsets]),
        [
            jax.ShapeDtypeStruct((count, layers, width), f32)
            for count in (rows // 2, rows // 4, rows // 8, rows // 8)
        ],
        20,
        "finish",
    )(mine, *received)
    return (next_p, next_q, *outs)


def solution(mesh):
    split = P(("shot", "xy"), "gz", None)
    shared = P("xy", "gz", None)
    return jax.shard_map(
        functools.partial(body, mesh.shape["xy"]),
        mesh=mesh,
        in_specs=(split,) * 4 + (shared,) * 5,
        out_specs=(split,) * 6,
        check_vma=False,
    )
```

```python
import functools

import jax
import jax.numpy as jnp
import numpy as np
from jax import lax
from jax.experimental import pallas as pl
from jax.experimental.pallas import tpu as pltpu
from jax.sharding import PartitionSpec as P

SECOND = (-205.0 / 72.0, 8.0 / 5.0, -1.0 / 5.0, 8.0 / 315.0, -1.0 / 560.0)
FIRST = (4.0 / 5.0, -1.0 / 5.0, 4.0 / 105.0, -1.0 / 280.0)
LIFT = (-1.586134342, -0.05298011854, 0.8829110762, 0.4435068522)
ZETA = 1.149604398
LANES = 128
LONG = 250_000
OUTER = 14_000
SCALE_FIRST, SCALE_SECOND = 840.0, 5040.0


def lift_level(values):
    even, odd = values[0::2], values[1::2]
    odd = odd + LIFT[0] * (even + np.roll(even, -1, 0))
    even = even + LIFT[1] * (odd + np.roll(odd, 1, 0))
    odd = odd + LIFT[2] * (even + np.roll(even, -1, 0))
    even = even + LIFT[3] * (odd + np.roll(odd, 1, 0))
    return even * ZETA, odd * (1.0 / ZETA)


def three_levels(length):
    coarse, members = np.eye(length), []
    for _ in range(3):
        coarse, detail = lift_level(coarse)
        members.append(detail)
    return members + [coarse]


def crossline_block(width):
    tiles = width // LANES
    members = three_levels(width)
    tile = tiles // 2
    wanted = np.concatenate(
        [m[tile * len(m) // tiles : (tile + 1) * len(m) // tiles] for m in members]
    )
    return wanted[:, (tile - 1) * LANES : (tile + 2) * LANES].T


def split_bf16(matrix):
    high = matrix.astype(jnp.bfloat16)
    low = (matrix - high.astype(np.float64)).astype(jnp.bfloat16)
    return high, low


def inline_blocks(rows):
    bricks, brick = 8, 4
    members = three_levels(rows * bricks)
    wanted = np.concatenate(
        [m[brick * len(m) // bricks : (brick + 1) * len(m) // bricks] for m in members]
    )

    def block(offset):
        return wanted[:, rows * (brick + offset) : rows * (brick + offset + 1)]

    factors = {}
    for offset in (-1, 1, -2, 2):
        left, sizes, right = np.linalg.svd(block(offset))
        rank = int((sizes > 1e-12).sum())
        root = np.sqrt(sizes[:rank])
        factors[offset] = (left[:, :rank] * root, root[:, None] * right[:rank])
    return block(0), factors


def sine_cosine(angle):
    turns = jnp.round(angle * (2.0 / np.pi))
    rest = angle - turns * 1.5703125
    rest = rest - turns * 4.837512969970703125e-4
    rest = rest - turns * 7.549789948768648e-8
    square = rest * rest
    sine = rest + rest * square * (
        -1.6666654611e-1 + square * (8.3321608736e-3 + square * -1.9515295891e-4)
    )
    cosine = (
        1.0
        - 0.5 * square
        + square
        * square
        * (4.166664568298827e-2 + square * (-1.388731625493765e-3 + square * 2.443315711809948e-5))
    )
    quarter = turns.astype(jnp.int32)
    swapped = (quarter & 1) == 1
    out_sine = jnp.where(swapped, cosine, sine)
    out_cosine = jnp.where(swapped, sine, cosine)
    out_sine = jnp.where((quarter & 2) == 2, -out_sine, out_sine)
    out_cosine = jnp.where(((quarter + 1) & 2) == 2, -out_cosine, out_cosine)
    return out_sine, out_cosine


def band(shape, taps, sign, scale):
    offset = lax.broadcasted_iota(jnp.int32, shape, 0) - LANES
    offset = offset - lax.broadcasted_iota(jnp.int32, shape, 1)
    values = jnp.zeros(shape, jnp.float32)
    for k, tap in enumerate(taps, 1):
        values = jnp.where(jnp.abs(offset) == k, float(np.round(tap * scale)), values)
    if sign < 0:
        values = jnp.where(offset < 0, -values, values)
    return values.astype(jnp.bfloat16)


def taps_kernel(taps_first, taps_second):
    taps_first[...] = band(taps_first.shape, FIRST, -1.0, SCALE_FIRST)
    taps_second[...] = band(taps_second.shape, SECOND[1:], 1.0, SCALE_SECOND)


def weights_kernel(
    waves,
    prior_p,
    prior_q,
    courant,
    epsilon,
    delta,
    tilt,
    azimuth,
    axis_x,
    axis_y,
    axis_z,
    gain_a,
    gain_b,
    base,
):
    rows = waves.shape[0]
    top = lax.broadcasted_iota(jnp.int32, waves.shape[1:], 0) < 4

    def swap(value):
        return pltpu.roll(value, 4, 0)

    for x in range(rows):
        angles = jnp.concatenate(
            [tilt[x].astype(jnp.float32), azimuth[x].astype(jnp.float32)], axis=0
        )
        sine, cosine = sine_cosine(angles)
        sine_other, cosine_other = swap(sine), swap(cosine)
        sine_tilt = jnp.where(top, sine, sine_other)
        axis_x[x] = sine_tilt * jnp.where(top, cosine_other, cosine)
        axis_y[x] = sine * sine_other
        axis_z[x] = jnp.where(top, cosine, cosine_other)
        speed = courant[x].astype(jnp.float32)
        root = jnp.sqrt(1.0 + 2.0 * delta[x].astype(jnp.float32))
        stretch = 1.0 + 2.0 * epsilon[x].astype(jnp.float32)
        gain_a[x] = jnp.concatenate([speed * stretch, speed], axis=0)
        across = speed * root
        gain_b[x] = jnp.concatenate([across, across], axis=0)
        base[x] = 2.0 * waves[x] - jnp.concatenate([prior_p[x], prior_q[x]], axis=0)


def first_of(ahead, behind):
    total = FIRST[0] * (ahead[0] - behind[0])
    for k in range(1, 4):
        total = total + FIRST[k] * (ahead[k] - behind[k])
    return total


def second_of(centre, ahead, behind):
    total = SECOND[0] * centre
    for k in range(4):
        total = total + SECOND[k + 1] * (ahead[k] + behind[k])
    return total


def dot3(a_high, a_low, b_high, b_low):
    def dot(a, b):
        return jnp.dot(a, b, preferred_element_type=jnp.float32)

    rows = a_high.shape[0]
    both = dot(jnp.concatenate([a_high, a_low], axis=0), b_high)
    return both[:rows] + (both[rows:] + dot(a_high, b_low))


def halves(value):
    high = value.astype(jnp.bfloat16)
    return high, (value - high.astype(jnp.float32)).astype(jnp.bfloat16)


def packed_rows(rows):
    top = lax.broadcasted_iota(jnp.int32, rows[0].shape, 0) < 4
    return jnp.concatenate(
        [
            jnp.where(top, rows[x], pltpu.roll(rows[x + 1], 4, 0))
            for x in range(0, len(rows), 2)
        ],
        axis=0,
    )


def crossline_of(rows, block_high, block_low):
    count, width = rows.shape
    tiles = width // LANES

    def windows(values):
        parts = [values[:, LANES * t : LANES * (t + 1)] for t in range(tiles)]
        return [
            jnp.concatenate([parts[t - 1], parts[t], parts[(t + 1) % tiles]], axis=1)
            for t in range(tiles)
        ]

    high, low = (jnp.concatenate(windows(part), axis=0) for part in halves(rows))
    result = dot3(high, low, block_high, block_low)
    lane = lax.broadcasted_iota(jnp.int32, (count, LANES), 1)
    ordered = [jnp.zeros((count, LANES), jnp.float32)] * tiles
    source, target = 0, 0
    for size in (LANES // 2, LANES // 4, LANES // 8, LANES // 8):
        for t in range(tiles):
            tile, offset = divmod(target + size * t, LANES)
            piece = result[count * t : count * (t + 1)]
            shift = (offset - source) % LANES
            if shift:
                piece = pltpu.roll(piece, shift, 1)
            inside = (lane >= offset) & (lane < offset + size)
            ordered[tile] = jnp.where(inside, piece, ordered[tile])
        source += size
        target += size * tiles
    return jnp.concatenate(ordered, axis=1)


def pressure_of(h_one, total, gain_a, gain_b, base):
    top = lax.broadcasted_iota(jnp.int32, h_one.shape, 0) < 4
    mixed = jnp.where(top, total - h_one, h_one)
    return base + gain_a * mixed + gain_b * pltpu.roll(mixed, 4, 0)


def depth_neighbours(own, far, lower):
    layer = lax.broadcasted_iota(jnp.int32, own.shape, 0) & 3
    up = far * jnp.where(lower, 1.0, 0.0)
    down = far * jnp.where(lower, 0.0, 1.0)
    ahead, behind = [], []
    for k in range(1, 4):
        ahead.append(jnp.where(layer < 4 - k, pltpu.roll(own, 8 - k, 0), pltpu.roll(up, 4 - k, 0)))
        behind.append(jnp.where(layer >= k, pltpu.roll(own, k, 0), pltpu.roll(down, 4 + k, 0)))
    return ahead + [up], behind + [down]


def across(parts, taps):
    width = parts.shape[1]
    blocks = []
    for start in range(0, width, 2 * LANES):
        stop = min(start + 2 * LANES, width)
        first = start - LANES
        low, high = max(first, 0), min(stop + LANES, width)
        block = taps[low - first : high - first, : stop - start]
        blocks.append(jnp.dot(parts[:, low:high], block, preferred_element_type=jnp.float32))
    return jnp.concatenate(blocks, axis=1)


def joined(parts, rows):
    return parts[:rows] + parts[rows:]


def interior_kernel(
    waves,
    other,
    axis_x,
    axis_y,
    axis_z,
    gain_a,
    gain_b,
    base,
    taps_first,
    taps_second,
    block_high,
    block_low,
    h_own,
    sum_own,
    inside,
    crossline,
    dz,
    dzz,
    dy,
    dyy,
    dzy,
):
    rows, sub, width = waves.shape
    flat = rows * sub
    lower = lax.axis_index("gz") == 0
    for x in range(rows):
        own = waves[x]
        ahead, behind = depth_neighbours(own, other[x], lower)
        dz[x] = first_of(ahead, behind)
        dzz[x] = second_of(own, ahead, behind)
    field = jnp.concatenate(halves(waves[...].reshape(flat, width)), axis=0)
    slope = jnp.concatenate(halves(dz[...].reshape(flat, width)), axis=0)
    dyy[...] = joined(across(field, taps_second), flat).reshape(waves.shape)
    dy[...] = joined(across(field, taps_first), flat).reshape(waves.shape)
    dzy[...] = joined(across(slope, taps_first), flat).reshape(waves.shape)
    for x in range(rows):
        centre = waves[x]
        dxx = SECOND[0] * centre
        dxy = jnp.zeros_like(centre)
        dxz = jnp.zeros_like(centre)
        for k in range(1, 5):
            for step in (k, -k):
                if 0 <= x + step < rows:
                    weight = FIRST[k - 1] if step > 0 else -FIRST[k - 1]
                    dxx = dxx + SECOND[k] * waves[x + step]
                    dxy = dxy + (weight / SCALE_FIRST) * dy[x + step]
                    dxz = dxz + weight * dz[x + step]
        cross = SECOND[0] * centre + (1.0 / SCALE_SECOND) * dyy[x]
        n_x, n_y, n_z = axis_x[x], axis_y[x], axis_z[x]
        h_one = n_x * (n_x * dxx + 2.0 * (n_y * dxy + n_z * dxz))
        h_one = h_one + n_y * (n_y * cross + (2.0 / SCALE_FIRST) * (n_z * dzy[x]))
        h_one = h_one + n_z * (n_z * dzz[x])
        total = dxx + cross + dzz[x]
        if 4 <= x < rows - 4:
            inside[x - 4] = pressure_of(h_one, total, gain_a[x], gain_b[x], base[x])
        else:
            row = x if x < 4 else x - rows + 8
            h_own[row], sum_own[row] = h_one, total
    ready = packed_rows([inside[x] for x in range(rows - 8)])
    crossline[...] = crossline_of(ready, block_high[...], block_low[...])


def halo_rows(size, edges):
    place = lax.axis_index("xy")
    even = place % 2 == 0
    left_at, right_at = jnp.where(even, 0, 4), jnp.where(even, 4, 0)
    left_in = jnp.where(place > 0, 1.0, 0.0)
    right_in = jnp.where(place < size - 1, 1.0, 0.0)
    before = [edges[left_at + x] * left_in for x in range(4)]
    return before + [edges[right_at + x] * right_in for x in range(4)]


def reach(values, row, coefficients, sign):
    total = None
    for k in range(1, 5):
        at = row + 4 - k if row < 4 else row + k - 4
        if (row < 4 and 0 <= at < 4) or (row >= 4 and 4 <= at < 8):
            term = (coefficients[k - 1] * (sign if row < 4 else 1.0)) * values[at]
            total = term if total is None else total + term
    return total


def halo_kernel(size, edges, axis_x, axis_y, h_own, sum_own, taps_first, h_edge, sum_edge):
    rows, sub, _ = axis_x.shape
    values = halo_rows(size, edges)
    parts = jnp.concatenate(halves(jnp.concatenate(values, axis=0)), axis=0)
    slopes = joined(across(parts, taps_first), 8 * sub)
    slopes = [slopes[sub * x : sub * x + sub] for x in range(8)]
    for row in range(8):
        x = row if row < 4 else rows - 8 + row
        dxx = reach(values, row, SECOND[1:], 1.0)
        dxy = reach(slopes, row, [c / SCALE_FIRST for c in FIRST], -1.0)
        n_x = axis_x[x]
        h_edge[row] = h_own[row] + n_x * (n_x * dxx + 2.0 * (axis_y[x] * dxy))
        sum_edge[row] = sum_own[row] + dxx


def step_kernel(
    size,
    gives,
    edges,
    edges_other,
    h_edge,
    sum_edge,
    axis_x,
    axis_z,
    gain_a,
    gain_b,
    base,
    block_high,
    block_low,
    crossline_inside,
    inline_high,
    inline_low,
    outside,
    crossline,
    *sends,
):
    rows = axis_x.shape[0]
    lower = lax.axis_index("gz") == 0
    place = lax.axis_index("xy")
    even, early = place % 2 == 0, place % 4 < 2

    slopes = [
        first_of(*depth_neighbours(own, far, lower))
        for own, far in zip(halo_rows(size, edges), halo_rows(size, edges_other))
    ]
    for row in range(8):
        x = row if row < 4 else rows - 8 + row
        dxz = reach(slopes, row, FIRST, -1.0)
        h_one = h_edge[row] + 2.0 * (axis_x[x] * axis_z[x] * dxz)
        outside[row] = pressure_of(h_one, sum_edge[row], gain_a[x], gain_b[x], base[x])
    ready = packed_rows([outside[row] for row in range(8)])
    edge = crossline_of(ready, block_high[...], block_low[...])
    transformed = jnp.concatenate([edge[:16], crossline_inside[...], edge[16:]], axis=0)
    crossline[...] = transformed
    parts = dot3(inline_high[...], inline_low[...], *halves(transformed))
    to_next, to_previous, to_second_next, to_second_previous = (
        parts[start : start + count] for start, count in gives
    )
    sends[0][...] = jnp.where(even, to_previous, to_next)
    sends[1][...] = jnp.where(early, to_second_previous, to_second_next)
    sends[2][...] = jnp.where(even, to_next, to_previous)
    sends[3][...] = jnp.where(early, to_second_next, to_second_previous)


def own_kernel(inside, outside, crossline, own_high, own_low, next_p, next_q, mine):
    rows = next_p.shape[0]
    for x in range(rows):
        if 4 <= x < rows - 4:
            value = inside[x - 4]
        else:
            value = outside[x if x < 4 else x - rows + 8]
        next_p[x] = value[:4]
        next_q[x] = value[4:]
    mine[...] = dot3(own_high[...], own_low[...], *halves(crossline[...]))


def added(takes, total, at, previous, following, second_previous, second_following):
    received = (previous, following, second_previous, second_following)
    for take, got in zip(takes, received):
        for j in range(take.shape[1]):
            factor = float(take[at, j])
            if got is not None and abs(factor) > 1e-13:
                total = total + factor * got[4 * j : 4 * j + 4]
    return total


def halves_by_place(outer, inner, outer_second, inner_second):
    place = lax.axis_index("xy")
    even, early = place % 2 == 0, place % 4 < 2
    return (
        jnp.where(even, outer, inner),
        jnp.where(even, inner, outer),
        jnp.where(early, outer_second, inner_second),
        jnp.where(early, inner_second, outer_second),
    )


def outer_kernel(takes, mine, outer, outer_second, with_outer):
    received = halves_by_place(outer[...], 0.0, outer_second[...], 0.0)
    for at in range(mine.shape[0] // 4):
        with_outer[4 * at : 4 * at + 4] = added(takes, mine[4 * at : 4 * at + 4], at, *received)


def finish_kernel(takes, mine, inner, inner_second, *outs):
    received = halves_by_place(0.0, inner[...], 0.0, inner_second[...])
    at = 0
    for out in outs:
        for row in range(out.shape[0]):
            out[row] = added(takes, mine[4 * at : 4 * at + 4], at, *received)
            at += 1


def pair_swaps(size):
    one = [1 if i % 2 == 0 else -1 for i in range(size)]
    two = [2 if i % 4 < 2 else -2 for i in range(size)]
    return [
        [(i, (i - one[i]) % size) for i in range(size)],
        [(i, (i - two[i]) % size) for i in range(size)],
        [(i, i + one[i]) for i in range(size)],
        [(i, i + two[i]) for i in range(size)],
    ]


def body(size, wave_p, wave_q, prior_p, prior_q, courant, epsilon, thomsen_delta, tilt_angle, azimuth):
    rows, layers, width = wave_p.shape
    f32 = jnp.float32
    even = lax.axis_index("xy") % 2 == 0
    pairs = pair_swaps(size)
    cores = [(0, 1), (1, 0)]
    stack = jax.ShapeDtypeStruct((rows, 8, width), f32)

    def parts(matrix):
        return [jnp.asarray(part) for part in split_bf16(matrix)]

    cells = rows * layers * width
    params = pltpu.CompilerParams(vmem_limit_bytes=16 * 1024 * 1024)

    def kernel(function, out_shape, work, name, scratch_shapes=(), bytes_accessed=40 * cells):
        cost = pl.CostEstimate(flops=work * cells, bytes_accessed=bytes_accessed, transcendentals=0)
        return pl.pallas_call(
            function,
            out_shape=out_shape,
            scratch_shapes=scratch_shapes,
            compiler_params=params,
            cost_estimate=cost,
            name=name,
        )

    waves = lax.optimization_barrier(jnp.concatenate([wave_p, wave_q], axis=1))
    leading, last = waves[:4], waves[rows - 4 :]
    open_outer = [
        (2 * i + g, 2 * i + 1 - g) if abs(i - j) > 1 else (2 * i + g, 2 * j + g)
        for i, j in pairs[0]
        for g in range(2)
    ]
    to_outer, to_inner = jnp.where(even, leading, last), jnp.where(even, last, leading)
    to_outer, to_inner, fields = lax.optimization_barrier((to_outer, to_inner, waves))
    outer = lax.ppermute(to_outer, ("xy", "gz"), open_outer)
    inner = lax.ppermute(to_inner, "xy", pairs[2])
    other = lax.ppermute(fields, "gz", cores)

    taps = jax.ShapeDtypeStruct((4 * LANES, 2 * LANES), jnp.bfloat16)
    taps_first, taps_second = kernel(taps_kernel, [taps] * 2, LONG, "taps")()
    axis_x, axis_y, axis_z, *gains = kernel(weights_kernel, [stack] * 6, 100, "weights")(
        waves, prior_p, prior_q, courant, epsilon, thomsen_delta, tilt_angle, azimuth
    )
    block = parts(crossline_block(width))
    work = pltpu.VMEM((rows, 8, width), f32)
    edge = jax.ShapeDtypeStruct((8, 8, width), f32)
    inside = jax.ShapeDtypeStruct((rows - 8, 8, width), f32)
    ready = jax.ShapeDtypeStruct((layers * (rows - 8), width), f32)
    h_own, sum_own, inside, crossline = kernel(
        interior_kernel, [edge, edge, inside, ready], 100, "interior", [work] * 5
    )(waves, other, axis_x, axis_y, axis_z, *gains, taps_first, taps_second, *block)
    h_own, sum_own, inner, outer = lax.optimization_barrier((h_own, sum_own, inner, outer))
    edges = jnp.concatenate([outer, inner], axis=0)
    edges_other = lax.ppermute(edges, "gz", cores)
    h_edge, sum_edge = kernel(functools.partial(halo_kernel, size), [edge] * 2, 100, "halo")(
        edges, axis_x, axis_y, h_own, sum_own, taps_first
    )

    own, factors = inline_blocks(rows)
    offsets = (-1, 1, -2, 2)
    pieces, gives, start = [], [], 0
    for offset in offsets:
        give = factors[offset][1]
        pad = give.shape[0] % 2
        pieces.append(np.pad(give, ((0, pad), (0, 0))))
        gives.append((start, 4 * (give.shape[0] + pad)))
        start += gives[-1][1]

    inline = parts(np.kron(np.concatenate(pieces), np.eye(4)))
    inline_own = parts(np.kron(own, np.eye(4)))
    flat = jax.ShapeDtypeStruct((layers * rows, width), f32)
    sizes = [gives[k][1] for k in (0, 2, 1, 3)]
    outside, crossline, *sends = kernel(
        functools.partial(step_kernel, size, gives),
        [edge, flat] + [jax.ShapeDtypeStruct((count, width), f32) for count in sizes],
        400,
        "step",
    )(edges, edges_other, h_edge, sum_edge, axis_x, axis_z, *gains, *block, crossline, *inline)
    received = [lax.ppermute(send, "xy", pair) for send, pair in zip(sends, pairs)]
    grid = jax.ShapeDtypeStruct(wave_p.shape, f32)
    next_p, next_q, mine = kernel(own_kernel, [grid, grid, flat], 100, "own")(
        inside, outside, crossline, *inline_own
    )
    outer, outer_second, inner, inner_second = received
    takes = [factors[offset][0] for offset in offsets]
    with_outer = kernel(functools.partial(outer_kernel, takes), flat, OUTER, "outer", bytes_accessed=10**8)(
        mine, outer, outer_second
    )
    with_outer, inner, inner_second = lax.optimization_barrier((with_outer, inner, inner_second))
    outs = kernel(
        functools.partial(finish_kernel, takes),
        [
            jax.ShapeDtypeStruct((count, layers, width), f32)
            for count in (rows // 2, rows // 4, rows // 8, rows // 8)
        ],
        20,
        "finish",
    )(with_outer, inner, inner_second)
    return (next_p, next_q, *outs)


def solution(mesh):
    split = P(("shot", "xy"), "gz", None)
    shared = P("xy", "gz", None)
    return jax.shard_map(
        functools.partial(body, mesh.shape["xy"]),
        mesh=mesh,
        in_specs=(split,) * 4 + (shared,) * 5,
        out_specs=(split,) * 6,
        check_vma=False,
    )
```

```python
import functools

import jax
import jax.numpy as jnp
import numpy as np
from jax import lax
from jax.experimental import pallas as pl
from jax.experimental.pallas import tpu as pltpu
from jax.sharding import PartitionSpec as P

SECOND = (-205.0 / 72.0, 8.0 / 5.0, -1.0 / 5.0, 8.0 / 315.0, -1.0 / 560.0)
FIRST = (4.0 / 5.0, -1.0 / 5.0, 4.0 / 105.0, -1.0 / 280.0)
LIFT = (-1.586134342, -0.05298011854, 0.8829110762, 0.4435068522)
ZETA = 1.149604398
LANES = 128
SCALE_FIRST, SCALE_SECOND = 840.0, 5040.0


def lift_level(values):
    even, odd = values[0::2], values[1::2]
    odd = odd + LIFT[0] * (even + np.roll(even, -1, 0))
    even = even + LIFT[1] * (odd + np.roll(odd, 1, 0))
    odd = odd + LIFT[2] * (even + np.roll(even, -1, 0))
    even = even + LIFT[3] * (odd + np.roll(odd, 1, 0))
    return even * ZETA, odd * (1.0 / ZETA)


def three_levels(length):
    coarse, members = np.eye(length), []
    for _ in range(3):
        coarse, detail = lift_level(coarse)
        members.append(detail)
    return members + [coarse]


def crossline_block(width):
    tiles = width // LANES
    members = three_levels(width)
    tile = tiles // 2
    wanted = np.concatenate(
        [m[tile * len(m) // tiles : (tile + 1) * len(m) // tiles] for m in members]
    )
    return wanted[:, (tile - 1) * LANES : (tile + 2) * LANES].T


def split_bf16(matrix):
    high = matrix.astype(jnp.bfloat16)
    low = (matrix - high.astype(np.float64)).astype(jnp.bfloat16)
    return high, low


def inline_blocks(rows):
    bricks, brick = 8, 4
    members = three_levels(rows * bricks)
    wanted = np.concatenate(
        [m[brick * len(m) // bricks : (brick + 1) * len(m) // bricks] for m in members]
    )

    def block(offset):
        return wanted[:, rows * (brick + offset) : rows * (brick + offset + 1)]

    factors = {}
    for offset in (-1, 1, -2, 2):
        left, sizes, right = np.linalg.svd(block(offset))
        rank = int((sizes > 1e-12).sum())
        root = np.sqrt(sizes[:rank])
        factors[offset] = (left[:, :rank] * root, root[:, None] * right[:rank])
    return block(0), factors


def sine_cosine(angle):
    turns = jnp.round(angle * (2.0 / np.pi))
    rest = angle - turns * 1.5703125
    rest = rest - turns * 4.837512969970703125e-4
    rest = rest - turns * 7.549789948768648e-8
    square = rest * rest
    sine = rest + rest * square * (
        -1.6666654611e-1 + square * (8.3321608736e-3 + square * -1.9515295891e-4)
    )
    cosine = (
        1.0
        - 0.5 * square
        + square
        * square
        * (4.166664568298827e-2 + square * (-1.388731625493765e-3 + square * 2.443315711809948e-5))
    )
    quarter = turns.astype(jnp.int32)
    swapped = (quarter & 1) == 1
    out_sine = jnp.where(swapped, cosine, sine)
    out_cosine = jnp.where(swapped, sine, cosine)
    out_sine = jnp.where((quarter & 2) == 2, -out_sine, out_sine)
    out_cosine = jnp.where(((quarter + 1) & 2) == 2, -out_cosine, out_cosine)
    return out_sine, out_cosine


def band(shape, taps, sign, scale):
    offset = lax.broadcasted_iota(jnp.int32, shape, 0) - LANES
    offset = offset - lax.broadcasted_iota(jnp.int32, shape, 1)
    values = jnp.zeros(shape, jnp.float32)
    for k, tap in enumerate(taps, 1):
        values = jnp.where(jnp.abs(offset) == k, float(np.round(tap * scale)), values)
    if sign < 0:
        values = jnp.where(offset < 0, -values, values)
    return values.astype(jnp.bfloat16)


def weights_kernel(
    waves,
    prior_p,
    prior_q,
    courant,
    epsilon,
    delta,
    tilt,
    azimuth,
    axis_x,
    axis_y,
    axis_z,
    gain_a,
    gain_b,
    base,
    taps_first,
    taps_second,
):
    rows = waves.shape[0]
    taps_first[...] = band(taps_first.shape, FIRST, -1.0, SCALE_FIRST)
    taps_second[...] = band(taps_second.shape, SECOND[1:], 1.0, SCALE_SECOND)
    top = lax.broadcasted_iota(jnp.int32, waves.shape[1:], 0) < 4

    def swap(value):
        return pltpu.roll(value, 4, 0)

    for x in range(rows):
        angles = jnp.concatenate(
            [tilt[x].astype(jnp.float32), azimuth[x].astype(jnp.float32)], axis=0
        )
        sine, cosine = sine_cosine(angles)
        sine_other, cosine_other = swap(sine), swap(cosine)
        sine_tilt = jnp.where(top, sine, sine_other)
        axis_x[x] = sine_tilt * jnp.where(top, cosine_other, cosine)
        axis_y[x] = sine * sine_other
        axis_z[x] = jnp.where(top, cosine, cosine_other)
        speed = courant[x].astype(jnp.float32)
        root = jnp.sqrt(1.0 + 2.0 * delta[x].astype(jnp.float32))
        stretch = 1.0 + 2.0 * epsilon[x].astype(jnp.float32)
        gain_a[x] = jnp.concatenate([speed * stretch, speed], axis=0)
        across = speed * root
        gain_b[x] = jnp.concatenate([across, across], axis=0)
        base[x] = 2.0 * waves[x] - jnp.concatenate([prior_p[x], prior_q[x]], axis=0)


def first_of(ahead, behind):
    total = FIRST[0] * (ahead[0] - behind[0])
    for k in range(1, 4):
        total = total + FIRST[k] * (ahead[k] - behind[k])
    return total


def second_of(centre, ahead, behind):
    total = SECOND[0] * centre
    for k in range(4):
        total = total + SECOND[k + 1] * (ahead[k] + behind[k])
    return total


def dot3(a_high, a_low, b_high, b_low):
    def dot(a, b):
        return jnp.dot(a, b, preferred_element_type=jnp.float32)

    rows = a_high.shape[0]
    both = dot(jnp.concatenate([a_high, a_low], axis=0), b_high)
    return both[:rows] + (both[rows:] + dot(a_high, b_low))


def halves(value):
    high = value.astype(jnp.bfloat16)
    return high, (value - high.astype(jnp.float32)).astype(jnp.bfloat16)


def packed_rows(rows):
    top = lax.broadcasted_iota(jnp.int32, rows[0].shape, 0) < 4
    return jnp.concatenate(
        [
            jnp.where(top, rows[x], pltpu.roll(rows[x + 1], 4, 0))
            for x in range(0, len(rows), 2)
        ],
        axis=0,
    )


def crossline_of(rows, block_high, block_low):
    count, width = rows.shape
    tiles = width // LANES

    def windows(values):
        parts = [values[:, LANES * t : LANES * (t + 1)] for t in range(tiles)]
        return [
            jnp.concatenate([parts[t - 1], parts[t], parts[(t + 1) % tiles]], axis=1)
            for t in range(tiles)
        ]

    high, low = (jnp.concatenate(windows(part), axis=0) for part in halves(rows))
    result = dot3(high, low, block_high, block_low)
    lane = lax.broadcasted_iota(jnp.int32, (count, LANES), 1)
    ordered = [jnp.zeros((count, LANES), jnp.float32)] * tiles
    source, target = 0, 0
    for size in (LANES // 2, LANES // 4, LANES // 8, LANES // 8):
        for t in range(tiles):
            tile, offset = divmod(target + size * t, LANES)
            piece = result[count * t : count * (t + 1)]
            shift = (offset - source) % LANES
            if shift:
                piece = pltpu.roll(piece, shift, 1)
            inside = (lane >= offset) & (lane < offset + size)
            ordered[tile] = jnp.where(inside, piece, ordered[tile])
        source += size
        target += size * tiles
    return jnp.concatenate(ordered, axis=1)


def pressure_of(h_one, total, gain_a, gain_b, base):
    top = lax.broadcasted_iota(jnp.int32, h_one.shape, 0) < 4
    mixed = jnp.where(top, total - h_one, h_one)
    return base + gain_a * mixed + gain_b * pltpu.roll(mixed, 4, 0)


def depth_neighbours(own, far, lower):
    layer = lax.broadcasted_iota(jnp.int32, own.shape, 0) & 3
    up = far * jnp.where(lower, 1.0, 0.0)
    down = far * jnp.where(lower, 0.0, 1.0)
    ahead, behind = [], []
    for k in range(1, 4):
        ahead.append(jnp.where(layer < 4 - k, pltpu.roll(own, 8 - k, 0), pltpu.roll(up, 4 - k, 0)))
        behind.append(jnp.where(layer >= k, pltpu.roll(own, k, 0), pltpu.roll(down, 4 + k, 0)))
    return ahead + [up], behind + [down]


def across(parts, taps):
    width = parts.shape[1]
    blocks = []
    for start in range(0, width, 2 * LANES):
        stop = min(start + 2 * LANES, width)
        first = start - LANES
        low, high = max(first, 0), min(stop + LANES, width)
        block = taps[low - first : high - first, : stop - start]
        blocks.append(jnp.dot(parts[:, low:high], block, preferred_element_type=jnp.float32))
    return jnp.concatenate(blocks, axis=1)


def joined(parts, rows):
    return parts[:rows] + parts[rows:]


def interior_kernel(
    waves,
    other,
    axis_x,
    axis_y,
    axis_z,
    gain_a,
    gain_b,
    base,
    taps_first,
    taps_second,
    block_high,
    block_low,
    h_own,
    sum_own,
    inside,
    crossline,
    dz,
    dzz,
    dy,
    dyy,
    dzy,
):
    rows, sub, width = waves.shape
    flat = rows * sub
    lower = lax.axis_index("gz") == 0
    for x in range(rows):
        own = waves[x]
        ahead, behind = depth_neighbours(own, other[x], lower)
        dz[x] = first_of(ahead, behind)
        dzz[x] = second_of(own, ahead, behind)
    field = jnp.concatenate(halves(waves[...].reshape(flat, width)), axis=0)
    slope = jnp.concatenate(halves(dz[...].reshape(flat, width)), axis=0)
    dyy[...] = joined(across(field, taps_second), flat).reshape(waves.shape)
    dy[...] = joined(across(field, taps_first), flat).reshape(waves.shape)
    dzy[...] = joined(across(slope, taps_first), flat).reshape(waves.shape)
    for x in range(rows):
        centre = waves[x]
        dxx = SECOND[0] * centre
        dxy = jnp.zeros_like(centre)
        dxz = jnp.zeros_like(centre)
        for k in range(1, 5):
            for step in (k, -k):
                if 0 <= x + step < rows:
                    weight = FIRST[k - 1] if step > 0 else -FIRST[k - 1]
                    dxx = dxx + SECOND[k] * waves[x + step]
                    dxy = dxy + (weight / SCALE_FIRST) * dy[x + step]
                    dxz = dxz + weight * dz[x + step]
        cross = SECOND[0] * centre + (1.0 / SCALE_SECOND) * dyy[x]
        n_x, n_y, n_z = axis_x[x], axis_y[x], axis_z[x]
        h_one = n_x * (n_x * dxx + 2.0 * (n_y * dxy + n_z * dxz))
        h_one = h_one + n_y * (n_y * cross + (2.0 / SCALE_FIRST) * (n_z * dzy[x]))
        h_one = h_one + n_z * (n_z * dzz[x])
        total = dxx + cross + dzz[x]
        if 4 <= x < rows - 4:
            inside[x - 4] = pressure_of(h_one, total, gain_a[x], gain_b[x], base[x])
        else:
            row = x if x < 4 else x - rows + 8
            h_own[row], sum_own[row] = h_one, total
    ready = packed_rows([inside[x] for x in range(rows - 8)])
    crossline[...] = crossline_of(ready, block_high[...], block_low[...])


def halo_rows(size, outer, inner):
    place = lax.axis_index("xy")
    even = place % 2 == 0
    left_in = jnp.where(place > 0, 1.0, 0.0)
    right_in = jnp.where(place < size - 1, 1.0, 0.0)
    before = [jnp.where(even, outer[x], inner[x]) * left_in for x in range(4)]
    return before + [jnp.where(even, inner[x], outer[x]) * right_in for x in range(4)]


def reach(values, row, coefficients, sign):
    total = None
    for k in range(1, 5):
        at = row + 4 - k if row < 4 else row + k - 4
        if (row < 4 and 0 <= at < 4) or (row >= 4 and 4 <= at < 8):
            term = (coefficients[k - 1] * (sign if row < 4 else 1.0)) * values[at]
            total = term if total is None else total + term
    return total


NOTHING = [0.0] * 4


def depth_slopes(edges, other, lower):
    return [first_of(*depth_neighbours(edges[x], other[x], lower)) for x in range(4)]


def halo_part(values, row, x, axis_x, axis_y, h_before, sum_before, slopes):
    dxx = reach(values, row, SECOND[1:], 1.0)
    dxy = reach(slopes, row, [c / SCALE_FIRST for c in FIRST], -1.0)
    n_x = axis_x[x]
    h_one = h_before[row] + n_x * (n_x * dxx + 2.0 * (axis_y[x] * dxy))
    return h_one, sum_before[row] + dxx


def crossline_slopes(values, sub, taps_first):
    parts = jnp.concatenate(halves(jnp.concatenate(values, axis=0)), axis=0)
    slopes = joined(across(parts, taps_first), 8 * sub)
    return [slopes[sub * x : sub * x + sub] for x in range(8)]


def inner_kernel(size, inner, axis_x, axis_y, h_before, sum_before, taps_first, h_edge, sum_edge):
    rows, sub, _ = axis_x.shape
    values = halo_rows(size, NOTHING, inner)
    slopes = crossline_slopes(values, sub, taps_first)
    for row in range(8):
        x = row if row < 4 else rows - 8 + row
        h_edge[row], sum_edge[row] = halo_part(
            values, row, x, axis_x, axis_y, h_before, sum_before, slopes
        )


def outer_kernel(
    size,
    outer,
    inner,
    inner_other,
    axis_x,
    axis_y,
    axis_z,
    h_before,
    sum_before,
    taps_first,
    h_edge,
    sum_edge,
):
    rows, sub, _ = axis_x.shape
    lower = lax.axis_index("gz") == 0
    values = halo_rows(size, outer, NOTHING)
    slopes = crossline_slopes(values, sub, taps_first)
    depth = halo_rows(size, NOTHING, depth_slopes(inner, inner_other, lower))
    for row in range(8):
        x = row if row < 4 else rows - 8 + row
        h_one, sum_edge[row] = halo_part(
            values, row, x, axis_x, axis_y, h_before, sum_before, slopes
        )
        dxz = reach(depth, row, FIRST, -1.0)
        h_edge[row] = h_one + 2.0 * (axis_x[x] * axis_z[x] * dxz)


def step_kernel(
    size,
    gives,
    outer,
    outer_other,
    h_edge,
    sum_edge,
    axis_x,
    axis_z,
    gain_a,
    gain_b,
    base,
    block_high,
    block_low,
    crossline_inside,
    inline_high,
    inline_low,
    outside,
    crossline,
    *sends,
):
    rows = axis_x.shape[0]
    lower = lax.axis_index("gz") == 0
    place = lax.axis_index("xy")
    even, early = place % 2 == 0, place % 4 < 2

    slopes = halo_rows(size, depth_slopes(outer, outer_other, lower), NOTHING)
    for row in range(8):
        x = row if row < 4 else rows - 8 + row
        dxz = reach(slopes, row, FIRST, -1.0)
        h_one = h_edge[row] + 2.0 * (axis_x[x] * axis_z[x] * dxz)
        outside[row] = pressure_of(h_one, sum_edge[row], gain_a[x], gain_b[x], base[x])
    ready = packed_rows([outside[row] for row in range(8)])
    edge = crossline_of(ready, block_high[...], block_low[...])
    transformed = jnp.concatenate([edge[:16], crossline_inside[...], edge[16:]], axis=0)
    crossline[...] = transformed
    parts = dot3(inline_high[...], inline_low[...], *halves(transformed))
    to_next, to_previous, to_second_next, to_second_previous = (
        parts[start : start + count] for start, count in gives
    )
    sends[0][...] = jnp.where(even, to_previous, to_next)
    sends[1][...] = jnp.where(even, to_next, to_previous)
    sends[2][...] = jnp.where(early, to_second_previous, to_second_next)
    sends[3][...] = jnp.where(early, to_second_next, to_second_previous)


def own_kernel(inside, outside, crossline, own_high, own_low, next_p, next_q, mine):
    rows = next_p.shape[0]
    for x in range(rows):
        if 4 <= x < rows - 4:
            value = inside[x - 4]
        else:
            value = outside[x if x < 4 else x - rows + 8]
        next_p[x] = value[:4]
        next_q[x] = value[4:]
    mine[...] = dot3(own_high[...], own_low[...], *halves(crossline[...]))


def finish_kernel(at, takes, mine, *rest):
    received, outs = [ref[...] for ref in rest[: len(takes)]], rest[len(takes) :]
    place = lax.axis_index("xy")
    for first, near in zip(range(0, len(takes), 2), (place % 2 == 0, place % 4 < 2)):
        outer, inner = received[first : first + 2]
        received[first : first + 2] = jnp.where(near, outer, inner), jnp.where(near, inner, outer)
    for out in outs:
        for row in range(out.shape[0]):
            total = mine[4 * at : 4 * at + 4]
            for take, got in zip(takes, received):
                for j in range(take.shape[1]):
                    factor = float(take[at, j])
                    if abs(factor) > 1e-13:
                        total = total + factor * got[4 * j : 4 * j + 4]
            out[row] = total
            at += 1


def pair_swaps(size):
    one = [1 if i % 2 == 0 else -1 for i in range(size)]
    two = [2 if i % 4 < 2 else -2 for i in range(size)]
    return [
        [(i, (i - one[i]) % size) for i in range(size)],
        [(i, i + one[i]) for i in range(size)],
        [(i, (i - two[i]) % size) for i in range(size)],
        [(i, i + two[i]) for i in range(size)],
    ]


def body(size, wave_p, wave_q, prior_p, prior_q, courant, epsilon, thomsen_delta, tilt_angle, azimuth):
    rows, layers, width = wave_p.shape
    f32 = jnp.float32
    even = lax.axis_index("xy") % 2 == 0
    pairs = pair_swaps(size)
    cores = [(0, 1), (1, 0)]
    stack = jax.ShapeDtypeStruct((rows, 8, width), f32)

    def parts(matrix):
        return [jnp.asarray(part) for part in split_bf16(matrix)]

    cells = rows * layers * width
    params = pltpu.CompilerParams(vmem_limit_bytes=16 * 1024 * 1024)

    def kernel(function, out_shape, work, name, scratch_shapes=()):
        cost = pl.CostEstimate(flops=work * cells, bytes_accessed=40 * cells, transcendentals=0)
        return pl.pallas_call(
            function,
            out_shape=out_shape,
            scratch_shapes=scratch_shapes,
            compiler_params=params,
            cost_estimate=cost,
            name=name,
        )

    waves = lax.optimization_barrier(jnp.concatenate([wave_p, wave_q], axis=1))
    leading, last = waves[:4], waves[rows - 4 :]
    open_outer = [
        (2 * i + g, 2 * i + 1 - g) if abs(i - j) > 1 else (2 * i + g, 2 * j + g)
        for i, j in pairs[0]
        for g in range(2)
    ]
    other = lax.ppermute(waves, "gz", cores)
    inner = lax.ppermute(jnp.where(even, last, leading), "xy", pairs[1])
    outer = lax.ppermute(jnp.where(even, leading, last), ("xy", "gz"), open_outer)

    taps = jax.ShapeDtypeStruct((4 * LANES, 2 * LANES), jnp.bfloat16)
    axis_x, axis_y, axis_z, *gains, taps_first, taps_second = kernel(
        weights_kernel, [stack] * 6 + [taps] * 2, 100, "weights"
    )(waves, prior_p, prior_q, courant, epsilon, thomsen_delta, tilt_angle, azimuth)
    block = parts(crossline_block(width))
    work = pltpu.VMEM((rows, 8, width), f32)
    edge = jax.ShapeDtypeStruct((8, 8, width), f32)
    inside = jax.ShapeDtypeStruct((rows - 8, 8, width), f32)
    ready = jax.ShapeDtypeStruct((layers * (rows - 8), width), f32)
    h_own, sum_own, inside, crossline = kernel(
        interior_kernel, [edge, edge, inside, ready], 100, "interior", [work] * 5
    )(waves, other, axis_x, axis_y, axis_z, *gains, taps_first, taps_second, *block)
    h_own, sum_own, inner = lax.optimization_barrier((h_own, sum_own, inner))
    inner_other = lax.ppermute(inner, "gz", cores)
    h_inner, sum_inner = kernel(functools.partial(inner_kernel, size), [edge] * 2, 100, "inner")(
        inner, axis_x, axis_y, h_own, sum_own, taps_first
    )
    h_inner, sum_inner, outer = lax.optimization_barrier((h_inner, sum_inner, outer))
    outer_other = lax.ppermute(outer, "gz", cores)
    h_edge, sum_edge = kernel(functools.partial(outer_kernel, size), [edge] * 2, 100, "outer")(
        outer, inner, inner_other, axis_x, axis_y, axis_z, h_inner, sum_inner, taps_first
    )

    own, factors = inline_blocks(rows)
    offsets = (-1, 1, -2, 2)
    pieces, gives, start = [], [], 0
    for offset in offsets:
        give = factors[offset][1]
        pad = give.shape[0] % 2
        pieces.append(np.pad(give, ((0, pad), (0, 0))))
        gives.append((start, 4 * (give.shape[0] + pad)))
        start += gives[-1][1]

    inline = parts(np.kron(np.concatenate(pieces), np.eye(4)))
    inline_own = parts(np.kron(own, np.eye(4)))
    flat = jax.ShapeDtypeStruct((layers * rows, width), f32)
    outside, crossline, *sends = kernel(
        functools.partial(step_kernel, size, gives),
        [edge, flat] + [jax.ShapeDtypeStruct((count, width), f32) for _, count in gives],
        400,
        "step",
    )(
        outer,
        outer_other,
        h_edge,
        sum_edge,
        axis_x,
        axis_z,
        *gains,
        *block,
        crossline,
        *inline,
    )
    received = [lax.ppermute(send, "xy", pair) for send, pair in zip(sends, pairs)]
    grid = jax.ShapeDtypeStruct(wave_p.shape, f32)
    next_p, next_q, mine = kernel(own_kernel, [grid, grid, flat], 100, "own")(
        inside, outside, crossline, *inline_own
    )
    takes = [factors[offset][0] for offset in offsets]
    counts = (rows // 2, rows // 4, rows // 8, rows // 8)
    outs = [jax.ShapeDtypeStruct((count, layers, width), f32) for count in counts]
    first, second = kernel(functools.partial(finish_kernel, 0, takes[:2]), outs[:2], 20, "fine")(
        mine, *received[:2]
    )
    first, *received[2:] = lax.optimization_barrier((first, *received[2:]))
    third, coarse = kernel(
        functools.partial(finish_kernel, counts[0] + counts[1], takes), outs[2:], 20, "coarse"
    )(mine, *received)
    return (next_p, next_q, first, second, third, coarse)


def solution(mesh):
    split = P(("shot", "xy"), "gz", None)
    shared = P("xy", "gz", None)
    return jax.shard_map(
        functools.partial(body, mesh.shape["xy"]),
        mesh=mesh,
        in_specs=(split,) * 4 + (shared,) * 5,
        out_specs=(split,) * 6,
        check_vma=False,
    )
```

```python
import functools

import jax
import jax.numpy as jnp
import numpy as np
from jax import lax
from jax.experimental import pallas as pl
from jax.experimental.pallas import tpu as pltpu
from jax.sharding import PartitionSpec as P

SECOND = (-205.0 / 72.0, 8.0 / 5.0, -1.0 / 5.0, 8.0 / 315.0, -1.0 / 560.0)
FIRST = (4.0 / 5.0, -1.0 / 5.0, 4.0 / 105.0, -1.0 / 280.0)
LIFT = (-1.586134342, -0.05298011854, 0.8829110762, 0.4435068522)
ZETA = 1.149604398
LANES = 128
LONG = 250_000
SCALE_FIRST, SCALE_SECOND = 840.0, 5040.0


def lift_level(values):
    even, odd = values[0::2], values[1::2]
    odd = odd + LIFT[0] * (even + np.roll(even, -1, 0))
    even = even + LIFT[1] * (odd + np.roll(odd, 1, 0))
    odd = odd + LIFT[2] * (even + np.roll(even, -1, 0))
    even = even + LIFT[3] * (odd + np.roll(odd, 1, 0))
    return even * ZETA, odd * (1.0 / ZETA)


def three_levels(length):
    coarse, members = np.eye(length), []
    for _ in range(3):
        coarse, detail = lift_level(coarse)
        members.append(detail)
    return members + [coarse]


def crossline_block(width):
    tiles = width // LANES
    members = three_levels(width)
    tile = tiles // 2
    wanted = np.concatenate(
        [m[tile * len(m) // tiles : (tile + 1) * len(m) // tiles] for m in members]
    )
    return wanted[:, (tile - 1) * LANES : (tile + 2) * LANES].T


def split_bf16(matrix):
    high = matrix.astype(jnp.bfloat16)
    low = (matrix - high.astype(np.float64)).astype(jnp.bfloat16)
    return high, low


def inline_blocks(rows):
    bricks, brick = 8, 4
    members = three_levels(rows * bricks)
    wanted = np.concatenate(
        [m[brick * len(m) // bricks : (brick + 1) * len(m) // bricks] for m in members]
    )

    def block(offset):
        return wanted[:, rows * (brick + offset) : rows * (brick + offset + 1)]

    factors = {}
    for offset in (-1, 1, -2, 2):
        left, sizes, right = np.linalg.svd(block(offset))
        rank = int((sizes > 1e-12).sum())
        root = np.sqrt(sizes[:rank])
        factors[offset] = (left[:, :rank] * root, root[:, None] * right[:rank])
    return block(0), factors


def sine_cosine(angle):
    turns = jnp.round(angle * (2.0 / np.pi))
    rest = angle - turns * 1.5703125
    rest = rest - turns * 4.837512969970703125e-4
    rest = rest - turns * 7.549789948768648e-8
    square = rest * rest
    sine = rest + rest * square * (
        -1.6666654611e-1 + square * (8.3321608736e-3 + square * -1.9515295891e-4)
    )
    cosine = (
        1.0
        - 0.5 * square
        + square
        * square
        * (4.166664568298827e-2 + square * (-1.388731625493765e-3 + square * 2.443315711809948e-5))
    )
    quarter = turns.astype(jnp.int32)
    swapped = (quarter & 1) == 1
    out_sine = jnp.where(swapped, cosine, sine)
    out_cosine = jnp.where(swapped, sine, cosine)
    out_sine = jnp.where((quarter & 2) == 2, -out_sine, out_sine)
    out_cosine = jnp.where(((quarter + 1) & 2) == 2, -out_cosine, out_cosine)
    return out_sine, out_cosine


def band(shape, taps, sign, scale):
    offset = lax.broadcasted_iota(jnp.int32, shape, 0) - LANES
    offset = offset - lax.broadcasted_iota(jnp.int32, shape, 1)
    values = jnp.zeros(shape, jnp.float32)
    for k, tap in enumerate(taps, 1):
        values = jnp.where(jnp.abs(offset) == k, float(np.round(tap * scale)), values)
    if sign < 0:
        values = jnp.where(offset < 0, -values, values)
    return values.astype(jnp.bfloat16)


def taps_kernel(taps_first, taps_second):
    taps_first[...] = band(taps_first.shape, FIRST, -1.0, SCALE_FIRST)
    taps_second[...] = band(taps_second.shape, SECOND[1:], 1.0, SCALE_SECOND)


def weights_kernel(
    waves,
    prior_p,
    prior_q,
    courant,
    epsilon,
    delta,
    tilt,
    azimuth,
    axis_x,
    axis_y,
    axis_z,
    gain_a,
    gain_b,
    base,
):
    rows = waves.shape[0]
    top = lax.broadcasted_iota(jnp.int32, waves.shape[1:], 0) < 4

    def swap(value):
        return pltpu.roll(value, 4, 0)

    for x in range(rows):
        angles = jnp.concatenate(
            [tilt[x].astype(jnp.float32), azimuth[x].astype(jnp.float32)], axis=0
        )
        sine, cosine = sine_cosine(angles)
        sine_other, cosine_other = swap(sine), swap(cosine)
        sine_tilt = jnp.where(top, sine, sine_other)
        axis_x[x] = sine_tilt * jnp.where(top, cosine_other, cosine)
        axis_y[x] = sine * sine_other
        axis_z[x] = jnp.where(top, cosine, cosine_other)
        speed = courant[x].astype(jnp.float32)
        root = jnp.sqrt(1.0 + 2.0 * delta[x].astype(jnp.float32))
        stretch = 1.0 + 2.0 * epsilon[x].astype(jnp.float32)
        gain_a[x] = jnp.concatenate([speed * stretch, speed], axis=0)
        across = speed * root
        gain_b[x] = jnp.concatenate([across, across], axis=0)
        base[x] = 2.0 * waves[x] - jnp.concatenate([prior_p[x], prior_q[x]], axis=0)


def first_of(ahead, behind):
    total = FIRST[0] * (ahead[0] - behind[0])
    for k in range(1, 4):
        total = total + FIRST[k] * (ahead[k] - behind[k])
    return total


def second_of(centre, ahead, behind):
    total = SECOND[0] * centre
    for k in range(4):
        total = total + SECOND[k + 1] * (ahead[k] + behind[k])
    return total


def dot3(a_high, a_low, b_high, b_low):
    def dot(a, b):
        return jnp.dot(a, b, preferred_element_type=jnp.float32)

    rows = a_high.shape[0]
    both = dot(jnp.concatenate([a_high, a_low], axis=0), b_high)
    return both[:rows] + (both[rows:] + dot(a_high, b_low))


def halves(value):
    high = value.astype(jnp.bfloat16)
    return high, (value - high.astype(jnp.float32)).astype(jnp.bfloat16)


def packed_rows(rows):
    top = lax.broadcasted_iota(jnp.int32, rows[0].shape, 0) < 4
    return jnp.concatenate(
        [
            jnp.where(top, rows[x], pltpu.roll(rows[x + 1], 4, 0))
            for x in range(0, len(rows), 2)
        ],
        axis=0,
    )


def crossline_of(rows, block_high, block_low):
    count, width = rows.shape
    tiles = width // LANES

    def windows(values):
        parts = [values[:, LANES * t : LANES * (t + 1)] for t in range(tiles)]
        return [
            jnp.concatenate([parts[t - 1], parts[t], parts[(t + 1) % tiles]], axis=1)
            for t in range(tiles)
        ]

    high, low = (jnp.concatenate(windows(part), axis=0) for part in halves(rows))
    result = dot3(high, low, block_high, block_low)
    lane = lax.broadcasted_iota(jnp.int32, (count, LANES), 1)
    ordered = [jnp.zeros((count, LANES), jnp.float32)] * tiles
    source, target = 0, 0
    for size in (LANES // 2, LANES // 4, LANES // 8, LANES // 8):
        for t in range(tiles):
            tile, offset = divmod(target + size * t, LANES)
            piece = result[count * t : count * (t + 1)]
            shift = (offset - source) % LANES
            if shift:
                piece = pltpu.roll(piece, shift, 1)
            inside = (lane >= offset) & (lane < offset + size)
            ordered[tile] = jnp.where(inside, piece, ordered[tile])
        source += size
        target += size * tiles
    return jnp.concatenate(ordered, axis=1)


def pressure_of(h_one, total, gain_a, gain_b, base):
    top = lax.broadcasted_iota(jnp.int32, h_one.shape, 0) < 4
    mixed = jnp.where(top, total - h_one, h_one)
    return base + gain_a * mixed + gain_b * pltpu.roll(mixed, 4, 0)


def depth_neighbours(own, far, lower):
    layer = lax.broadcasted_iota(jnp.int32, own.shape, 0) & 3
    up = far * jnp.where(lower, 1.0, 0.0)
    down = far * jnp.where(lower, 0.0, 1.0)
    ahead, behind = [], []
    for k in range(1, 4):
        ahead.append(jnp.where(layer < 4 - k, pltpu.roll(own, 8 - k, 0), pltpu.roll(up, 4 - k, 0)))
        behind.append(jnp.where(layer >= k, pltpu.roll(own, k, 0), pltpu.roll(down, 4 + k, 0)))
    return ahead + [up], behind + [down]


def across(parts, taps):
    width = parts.shape[1]
    blocks = []
    for start in range(0, width, 2 * LANES):
        stop = min(start + 2 * LANES, width)
        first = start - LANES
        low, high = max(first, 0), min(stop + LANES, width)
        block = taps[low - first : high - first, : stop - start]
        blocks.append(jnp.dot(parts[:, low:high], block, preferred_element_type=jnp.float32))
    return jnp.concatenate(blocks, axis=1)


def joined(parts, rows):
    return parts[:rows] + parts[rows:]


def interior_kernel(
    waves,
    other,
    axis_x,
    axis_y,
    axis_z,
    gain_a,
    gain_b,
    base,
    taps_first,
    taps_second,
    block_high,
    block_low,
    h_own,
    sum_own,
    inside,
    crossline,
    dz,
    dzz,
    dy,
    dyy,
    dzy,
):
    rows, sub, width = waves.shape
    flat = rows * sub
    lower = lax.axis_index("gz") == 0
    for x in range(rows):
        own = waves[x]
        ahead, behind = depth_neighbours(own, other[x], lower)
        dz[x] = first_of(ahead, behind)
        dzz[x] = second_of(own, ahead, behind)
    field = jnp.concatenate(halves(waves[...].reshape(flat, width)), axis=0)
    slope = jnp.concatenate(halves(dz[...].reshape(flat, width)), axis=0)
    dyy[...] = joined(across(field, taps_second), flat).reshape(waves.shape)
    dy[...] = joined(across(field, taps_first), flat).reshape(waves.shape)
    dzy[...] = joined(across(slope, taps_first), flat).reshape(waves.shape)
    for x in range(rows):
        centre = waves[x]
        dxx = SECOND[0] * centre
        dxy = jnp.zeros_like(centre)
        dxz = jnp.zeros_like(centre)
        for k in range(1, 5):
            for step in (k, -k):
                if 0 <= x + step < rows:
                    weight = FIRST[k - 1] if step > 0 else -FIRST[k - 1]
                    dxx = dxx + SECOND[k] * waves[x + step]
                    dxy = dxy + (weight / SCALE_FIRST) * dy[x + step]
                    dxz = dxz + weight * dz[x + step]
        cross = SECOND[0] * centre + (1.0 / SCALE_SECOND) * dyy[x]
        n_x, n_y, n_z = axis_x[x], axis_y[x], axis_z[x]
        h_one = n_x * (n_x * dxx + 2.0 * (n_y * dxy + n_z * dxz))
        h_one = h_one + n_y * (n_y * cross + (2.0 / SCALE_FIRST) * (n_z * dzy[x]))
        h_one = h_one + n_z * (n_z * dzz[x])
        total = dxx + cross + dzz[x]
        if 4 <= x < rows - 4:
            inside[x - 4] = pressure_of(h_one, total, gain_a[x], gain_b[x], base[x])
        else:
            row = x if x < 4 else x - rows + 8
            h_own[row], sum_own[row] = h_one, total
    ready = packed_rows([inside[x] for x in range(rows - 8)])
    crossline[...] = crossline_of(ready, block_high[...], block_low[...])


def halo_rows(size, edges):
    place = lax.axis_index("xy")
    even = place % 2 == 0
    left_at, right_at = jnp.where(even, 0, 4), jnp.where(even, 4, 0)
    left_in = jnp.where(place > 0, 1.0, 0.0)
    right_in = jnp.where(place < size - 1, 1.0, 0.0)
    before = [edges[left_at + x] * left_in for x in range(4)]
    return before + [edges[right_at + x] * right_in for x in range(4)]


def reach(values, row, coefficients, sign):
    total = None
    for k in range(1, 5):
        at = row + 4 - k if row < 4 else row + k - 4
        if (row < 4 and 0 <= at < 4) or (row >= 4 and 4 <= at < 8):
            term = (coefficients[k - 1] * (sign if row < 4 else 1.0)) * values[at]
            total = term if total is None else total + term
    return total


def halo_kernel(size, edges, axis_x, axis_y, axis_z, h_own, sum_own, taps_first, h_edge, sum_edge):
    rows, sub, _ = axis_x.shape
    values = halo_rows(size, edges)
    parts = jnp.concatenate(halves(jnp.concatenate(values, axis=0)), axis=0)
    slopes = joined(across(parts, taps_first), 8 * sub)
    slopes = [slopes[sub * x : sub * x + sub] for x in range(8)]
    lower = lax.axis_index("gz") == 0
    depth = [first_of(*depth_neighbours(value, jnp.zeros_like(value), lower)) for value in values]
    for row in range(8):
        x = row if row < 4 else rows - 8 + row
        dxx = reach(values, row, SECOND[1:], 1.0)
        dxy = reach(slopes, row, [c / SCALE_FIRST for c in FIRST], -1.0)
        n_x = axis_x[x]
        dxz = reach(depth, row, FIRST, -1.0)
        h_edge[row] = h_own[row] + n_x * (n_x * dxx + 2.0 * (axis_y[x] * dxy + axis_z[x] * dxz))
        sum_edge[row] = sum_own[row] + dxx


def step_kernel(
    size,
    gives,
    edges_other,
    h_edge,
    sum_edge,
    axis_x,
    axis_z,
    gain_a,
    gain_b,
    base,
    block_high,
    block_low,
    crossline_inside,
    inline_high,
    inline_low,
    outside,
    crossline,
    *sends,
):
    rows = axis_x.shape[0]
    lower = lax.axis_index("gz") == 0
    place = lax.axis_index("xy")
    even, early = place % 2 == 0, place % 4 < 2

    slopes = [
        first_of(*depth_neighbours(jnp.zeros_like(far), far, lower))
        for far in halo_rows(size, edges_other)
    ]
    for row in range(8):
        x = row if row < 4 else rows - 8 + row
        dxz = reach(slopes, row, FIRST, -1.0)
        h_one = h_edge[row] + 2.0 * (axis_x[x] * axis_z[x] * dxz)
        outside[row] = pressure_of(h_one, sum_edge[row], gain_a[x], gain_b[x], base[x])
    ready = packed_rows([outside[row] for row in range(8)])
    edge = crossline_of(ready, block_high[...], block_low[...])
    transformed = jnp.concatenate([edge[:16], crossline_inside[...], edge[16:]], axis=0)
    crossline[...] = transformed
    parts = dot3(inline_high[...], inline_low[...], *halves(transformed))
    to_next, to_previous, to_second_next, to_second_previous = (
        parts[start : start + count] for start, count in gives
    )
    sends[0][...] = jnp.where(even, to_previous, to_next)
    sends[1][...] = jnp.where(even, to_next, to_previous)
    sends[2][...] = jnp.where(early, to_second_previous, to_second_next)
    sends[3][...] = jnp.where(early, to_second_next, to_second_previous)


def own_kernel(inside, outside, crossline, own_high, own_low, next_p, next_q, mine):
    rows = next_p.shape[0]
    for x in range(rows):
        if 4 <= x < rows - 4:
            value = inside[x - 4]
        else:
            value = outside[x if x < 4 else x - rows + 8]
        next_p[x] = value[:4]
        next_q[x] = value[4:]
    mine[...] = dot3(own_high[...], own_low[...], *halves(crossline[...]))


def finish_kernel(at, takes, mine, *rest):
    received, outs = [ref[...] for ref in rest[: len(takes)]], rest[len(takes) :]
    place = lax.axis_index("xy")
    for first, near in zip(range(0, len(takes), 2), (place % 2 == 0, place % 4 < 2)):
        outer, inner = received[first : first + 2]
        received[first : first + 2] = jnp.where(near, outer, inner), jnp.where(near, inner, outer)
    for out in outs:
        for row in range(out.shape[0]):
            total = mine[4 * at : 4 * at + 4]
            for take, got in zip(takes, received):
                for j in range(take.shape[1]):
                    factor = float(take[at, j])
                    if abs(factor) > 1e-13:
                        total = total + factor * got[4 * j : 4 * j + 4]
            out[row] = total
            at += 1


def pair_swaps(size):
    one = [1 if i % 2 == 0 else -1 for i in range(size)]
    two = [2 if i % 4 < 2 else -2 for i in range(size)]
    return [
        [(i, (i - one[i]) % size) for i in range(size)],
        [(i, i + one[i]) for i in range(size)],
        [(i, (i - two[i]) % size) for i in range(size)],
        [(i, i + two[i]) for i in range(size)],
    ]


def body(size, wave_p, wave_q, prior_p, prior_q, courant, epsilon, thomsen_delta, tilt_angle, azimuth):
    rows, layers, width = wave_p.shape
    f32 = jnp.float32
    even = lax.axis_index("xy") % 2 == 0
    pairs = pair_swaps(size)
    cores = [(0, 1), (1, 0)]
    stack = jax.ShapeDtypeStruct((rows, 8, width), f32)

    def parts(matrix):
        return [jnp.asarray(part) for part in split_bf16(matrix)]

    cells = rows * layers * width
    params = pltpu.CompilerParams(vmem_limit_bytes=16 * 1024 * 1024)

    def kernel(function, out_shape, work, name, scratch_shapes=()):
        cost = pl.CostEstimate(flops=work * cells, bytes_accessed=40 * cells, transcendentals=0)
        return pl.pallas_call(
            function,
            out_shape=out_shape,
            scratch_shapes=scratch_shapes,
            compiler_params=params,
            cost_estimate=cost,
            name=name,
        )

    waves = lax.optimization_barrier(jnp.concatenate([wave_p, wave_q], axis=1))
    leading, last = waves[:4], waves[rows - 4 :]
    open_outer = [
        (2 * i + g, 2 * i + 1 - g) if abs(i - j) > 1 else (2 * i + g, 2 * j + g)
        for i, j in pairs[0]
        for g in range(2)
    ]
    to_outer, to_inner = jnp.where(even, leading, last), jnp.where(even, last, leading)
    to_outer, to_inner, fields = lax.optimization_barrier((to_outer, to_inner, waves))
    outer = lax.ppermute(to_outer, ("xy", "gz"), open_outer)
    inner = lax.ppermute(to_inner, "xy", pairs[1])
    other = lax.ppermute(fields, "gz", cores)

    taps = jax.ShapeDtypeStruct((4 * LANES, 2 * LANES), jnp.bfloat16)
    taps_first, taps_second = kernel(taps_kernel, [taps] * 2, LONG, "taps")()
    axis_x, axis_y, axis_z, *gains = kernel(weights_kernel, [stack] * 6, 100, "weights")(
        waves, prior_p, prior_q, courant, epsilon, thomsen_delta, tilt_angle, azimuth
    )
    block = parts(crossline_block(width))
    work = pltpu.VMEM((rows, 8, width), f32)
    edge = jax.ShapeDtypeStruct((8, 8, width), f32)
    inside = jax.ShapeDtypeStruct((rows - 8, 8, width), f32)
    ready = jax.ShapeDtypeStruct((layers * (rows - 8), width), f32)
    h_own, sum_own, inside, crossline = kernel(
        interior_kernel, [edge, edge, inside, ready], 100, "interior", [work] * 5
    )(waves, other, axis_x, axis_y, axis_z, *gains, taps_first, taps_second, *block)
    h_own, sum_own, outer, inner = lax.optimization_barrier((h_own, sum_own, outer, inner))
    edges = jnp.concatenate([outer, inner], axis=0)
    edges_other = lax.ppermute(edges, "gz", cores)
    h_edge, sum_edge = kernel(functools.partial(halo_kernel, size), [edge] * 2, 100, "halo")(
        edges, axis_x, axis_y, axis_z, h_own, sum_own, taps_first
    )

    own, factors = inline_blocks(rows)
    offsets = (-1, 1, -2, 2)
    pieces, gives, start = [], [], 0
    for offset in offsets:
        give = factors[offset][1]
        pad = give.shape[0] % 2
        pieces.append(np.pad(give, ((0, pad), (0, 0))))
        gives.append((start, 4 * (give.shape[0] + pad)))
        start += gives[-1][1]

    inline = parts(np.kron(np.concatenate(pieces), np.eye(4)))
    inline_own = parts(np.kron(own, np.eye(4)))
    flat = jax.ShapeDtypeStruct((layers * rows, width), f32)
    sizes = [count for _, count in gives]
    outside, crossline, *sends = kernel(
        functools.partial(step_kernel, size, gives),
        [edge, flat] + [jax.ShapeDtypeStruct((count, width), f32) for count in sizes],
        400,
        "step",
    )(edges_other, h_edge, sum_edge, axis_x, axis_z, *gains, *block, crossline, *inline)
    received = [lax.ppermute(send, "xy", pair) for send, pair in zip(sends, pairs)]
    grid = jax.ShapeDtypeStruct(wave_p.shape, f32)
    next_p, next_q, mine = kernel(own_kernel, [grid, grid, flat], 100, "own")(
        inside, outside, crossline, *inline_own
    )
    takes = [factors[offset][0] for offset in offsets]
    counts = (rows // 2, rows // 4, rows // 8, rows // 8)
    outs = [jax.ShapeDtypeStruct((count, layers, width), f32) for count in counts]
    first, second = kernel(functools.partial(finish_kernel, 0, takes[:2]), outs[:2], 20, "fine")(
        mine, *received[:2]
    )
    first, *received[2:] = lax.optimization_barrier((first, *received[2:]))
    third, coarse = kernel(
        functools.partial(finish_kernel, counts[0] + counts[1], takes), outs[2:], 20, "coarse"
    )(mine, *received)
    return (next_p, next_q, first, second, third, coarse)


def solution(mesh):
    split = P(("shot", "xy"), "gz", None)
    shared = P("xy", "gz", None)
    return jax.shard_map(
        functools.partial(body, mesh.shape["xy"]),
        mesh=mesh,
        in_specs=(split,) * 4 + (shared,) * 5,
        out_specs=(split,) * 6,
        check_vma=False,
    )
```

```python
import functools

import jax
import jax.numpy as jnp
import numpy as np
from jax import lax
from jax.experimental import pallas as pl
from jax.experimental.pallas import tpu as pltpu
from jax.sharding import PartitionSpec as P

SECOND = (-205.0 / 72.0, 8.0 / 5.0, -1.0 / 5.0, 8.0 / 315.0, -1.0 / 560.0)
FIRST = (4.0 / 5.0, -1.0 / 5.0, 4.0 / 105.0, -1.0 / 280.0)
LIFT = (-1.586134342, -0.05298011854, 0.8829110762, 0.4435068522)
ZETA = 1.149604398
LANES = 128
SCALE_FIRST, SCALE_SECOND = 840.0, 5040.0


def lift_level(values):
    even, odd = values[0::2], values[1::2]
    odd = odd + LIFT[0] * (even + np.roll(even, -1, 0))
    even = even + LIFT[1] * (odd + np.roll(odd, 1, 0))
    odd = odd + LIFT[2] * (even + np.roll(even, -1, 0))
    even = even + LIFT[3] * (odd + np.roll(odd, 1, 0))
    return even * ZETA, odd * (1.0 / ZETA)


def three_levels(length):
    coarse, members = np.eye(length), []
    for _ in range(3):
        coarse, detail = lift_level(coarse)
        members.append(detail)
    return members + [coarse]


def crossline_block(width):
    tiles = width // LANES
    members = three_levels(width)
    tile = tiles // 2
    wanted = np.concatenate(
        [m[tile * len(m) // tiles : (tile + 1) * len(m) // tiles] for m in members]
    )
    return wanted[:, (tile - 1) * LANES : (tile + 2) * LANES].T


def split_bf16(matrix):
    high = matrix.astype(jnp.bfloat16)
    low = (matrix - high.astype(np.float64)).astype(jnp.bfloat16)
    return high, low


def inline_blocks(rows):
    bricks, brick = 8, 4
    members = three_levels(rows * bricks)
    wanted = np.concatenate(
        [m[brick * len(m) // bricks : (brick + 1) * len(m) // bricks] for m in members]
    )

    def block(offset):
        return wanted[:, rows * (brick + offset) : rows * (brick + offset + 1)]

    factors = {}
    for offset in (-1, 1, -2, 2):
        left, sizes, right = np.linalg.svd(block(offset))
        rank = int((sizes > 1e-12).sum())
        root = np.sqrt(sizes[:rank])
        factors[offset] = (left[:, :rank] * root, root[:, None] * right[:rank])
    return block(0), factors


def sine_cosine(angle):
    turns = jnp.round(angle * (2.0 / np.pi))
    rest = angle - turns * 1.5703125
    rest = rest - turns * 4.837512969970703125e-4
    rest = rest - turns * 7.549789948768648e-8
    square = rest * rest
    sine = rest + rest * square * (
        -1.6666654611e-1 + square * (8.3321608736e-3 + square * -1.9515295891e-4)
    )
    cosine = (
        1.0
        - 0.5 * square
        + square
        * square
        * (4.166664568298827e-2 + square * (-1.388731625493765e-3 + square * 2.443315711809948e-5))
    )
    quarter = turns.astype(jnp.int32)
    swapped = (quarter & 1) == 1
    out_sine = jnp.where(swapped, cosine, sine)
    out_cosine = jnp.where(swapped, sine, cosine)
    out_sine = jnp.where((quarter & 2) == 2, -out_sine, out_sine)
    out_cosine = jnp.where(((quarter + 1) & 2) == 2, -out_cosine, out_cosine)
    return out_sine, out_cosine


def band(shape, taps, sign, scale):
    offset = lax.broadcasted_iota(jnp.int32, shape, 0) - LANES
    offset = offset - lax.broadcasted_iota(jnp.int32, shape, 1)
    values = jnp.zeros(shape, jnp.float32)
    for k, tap in enumerate(taps, 1):
        values = jnp.where(jnp.abs(offset) == k, float(np.round(tap * scale)), values)
    if sign < 0:
        values = jnp.where(offset < 0, -values, values)
    return values.astype(jnp.bfloat16)


def weights_kernel(
    waves,
    prior_p,
    prior_q,
    courant,
    epsilon,
    delta,
    tilt,
    azimuth,
    axis_x,
    axis_y,
    axis_z,
    gain_a,
    gain_b,
    base,
    taps_first,
    taps_second,
):
    rows = waves.shape[0]
    taps_first[...] = band(taps_first.shape, FIRST, -1.0, SCALE_FIRST)
    taps_second[...] = band(taps_second.shape, SECOND[1:], 1.0, SCALE_SECOND)
    top = lax.broadcasted_iota(jnp.int32, waves.shape[1:], 0) < 4

    def swap(value):
        return pltpu.roll(value, 4, 0)

    for x in range(rows):
        angles = jnp.concatenate(
            [tilt[x].astype(jnp.float32), azimuth[x].astype(jnp.float32)], axis=0
        )
        sine, cosine = sine_cosine(angles)
        sine_other, cosine_other = swap(sine), swap(cosine)
        sine_tilt = jnp.where(top, sine, sine_other)
        axis_x[x] = sine_tilt * jnp.where(top, cosine_other, cosine)
        axis_y[x] = sine * sine_other
        axis_z[x] = jnp.where(top, cosine, cosine_other)
        speed = courant[x].astype(jnp.float32)
        root = jnp.sqrt(1.0 + 2.0 * delta[x].astype(jnp.float32))
        stretch = 1.0 + 2.0 * epsilon[x].astype(jnp.float32)
        gain_a[x] = jnp.concatenate([speed * stretch, speed], axis=0)
        across = speed * root
        gain_b[x] = jnp.concatenate([across, across], axis=0)
        base[x] = 2.0 * waves[x] - jnp.concatenate([prior_p[x], prior_q[x]], axis=0)


def first_of(ahead, behind):
    total = FIRST[0] * (ahead[0] - behind[0])
    for k in range(1, 4):
        total = total + FIRST[k] * (ahead[k] - behind[k])
    return total


def second_of(centre, ahead, behind):
    total = SECOND[0] * centre
    for k in range(4):
        total = total + SECOND[k + 1] * (ahead[k] + behind[k])
    return total


def dot3(a_high, a_low, b_high, b_low):
    def dot(a, b):
        return jnp.dot(a, b, preferred_element_type=jnp.float32)

    rows = a_high.shape[0]
    both = dot(jnp.concatenate([a_high, a_low], axis=0), b_high)
    return both[:rows] + (both[rows:] + dot(a_high, b_low))


def halves(value):
    high = value.astype(jnp.bfloat16)
    return high, (value - high.astype(jnp.float32)).astype(jnp.bfloat16)


def packed_rows(rows):
    top = lax.broadcasted_iota(jnp.int32, rows[0].shape, 0) < 4
    return jnp.concatenate(
        [
            jnp.where(top, rows[x], pltpu.roll(rows[x + 1], 4, 0))
            for x in range(0, len(rows), 2)
        ],
        axis=0,
    )


def crossline_of(rows, block_high, block_low):
    count, width = rows.shape
    tiles = width // LANES

    def windows(values):
        parts = [values[:, LANES * t : LANES * (t + 1)] for t in range(tiles)]
        return [
            jnp.concatenate([parts[t - 1], parts[t], parts[(t + 1) % tiles]], axis=1)
            for t in range(tiles)
        ]

    high, low = (jnp.concatenate(windows(part), axis=0) for part in halves(rows))
    result = dot3(high, low, block_high, block_low)
    lane = lax.broadcasted_iota(jnp.int32, (count, LANES), 1)
    ordered = [jnp.zeros((count, LANES), jnp.float32)] * tiles
    source, target = 0, 0
    for size in (LANES // 2, LANES // 4, LANES // 8, LANES // 8):
        for t in range(tiles):
            tile, offset = divmod(target + size * t, LANES)
            piece = result[count * t : count * (t + 1)]
            shift = (offset - source) % LANES
            if shift:
                piece = pltpu.roll(piece, shift, 1)
            inside = (lane >= offset) & (lane < offset + size)
            ordered[tile] = jnp.where(inside, piece, ordered[tile])
        source += size
        target += size * tiles
    return jnp.concatenate(ordered, axis=1)


def pressure_of(h_one, total, gain_a, gain_b, base):
    top = lax.broadcasted_iota(jnp.int32, h_one.shape, 0) < 4
    mixed = jnp.where(top, total - h_one, h_one)
    return base + gain_a * mixed + gain_b * pltpu.roll(mixed, 4, 0)


def depth_neighbours(own, far, lower):
    layer = lax.broadcasted_iota(jnp.int32, own.shape, 0) & 3
    up = far * jnp.where(lower, 1.0, 0.0)
    down = far * jnp.where(lower, 0.0, 1.0)
    ahead, behind = [], []
    for k in range(1, 4):
        ahead.append(jnp.where(layer < 4 - k, pltpu.roll(own, 8 - k, 0), pltpu.roll(up, 4 - k, 0)))
        behind.append(jnp.where(layer >= k, pltpu.roll(own, k, 0), pltpu.roll(down, 4 + k, 0)))
    return ahead + [up], behind + [down]


def across(parts, taps):
    width = parts.shape[1]
    blocks = []
    for start in range(0, width, 2 * LANES):
        stop = min(start + 2 * LANES, width)
        first = start - LANES
        low, high = max(first, 0), min(stop + LANES, width)
        block = taps[low - first : high - first, : stop - start]
        blocks.append(jnp.dot(parts[:, low:high], block, preferred_element_type=jnp.float32))
    return jnp.concatenate(blocks, axis=1)


def joined(parts, rows):
    return parts[:rows] + parts[rows:]


def interior_kernel(
    waves,
    other,
    axis_x,
    axis_y,
    axis_z,
    gain_a,
    gain_b,
    base,
    taps_first,
    taps_second,
    block_high,
    block_low,
    h_own,
    sum_own,
    inside,
    crossline,
    dz,
    dzz,
    dy,
    dyy,
    dzy,
):
    rows, sub, width = waves.shape
    flat = rows * sub
    lower = lax.axis_index("gz") == 0
    for x in range(rows):
        own = waves[x]
        ahead, behind = depth_neighbours(own, other[x], lower)
        dz[x] = first_of(ahead, behind)
        dzz[x] = second_of(own, ahead, behind)
    field = jnp.concatenate(halves(waves[...].reshape(flat, width)), axis=0)
    slope = jnp.concatenate(halves(dz[...].reshape(flat, width)), axis=0)
    dyy[...] = joined(across(field, taps_second), flat).reshape(waves.shape)
    dy[...] = joined(across(field, taps_first), flat).reshape(waves.shape)
    dzy[...] = joined(across(slope, taps_first), flat).reshape(waves.shape)
    for x in range(rows):
        centre = waves[x]
        dxx = SECOND[0] * centre
        dxy = jnp.zeros_like(centre)
        dxz = jnp.zeros_like(centre)
        for k in range(1, 5):
            for step in (k, -k):
                if 0 <= x + step < rows:
                    weight = FIRST[k - 1] if step > 0 else -FIRST[k - 1]
                    dxx = dxx + SECOND[k] * waves[x + step]
                    dxy = dxy + (weight / SCALE_FIRST) * dy[x + step]
                    dxz = dxz + weight * dz[x + step]
        cross = SECOND[0] * centre + (1.0 / SCALE_SECOND) * dyy[x]
        n_x, n_y, n_z = axis_x[x], axis_y[x], axis_z[x]
        h_one = n_x * (n_x * dxx + 2.0 * (n_y * dxy + n_z * dxz))
        h_one = h_one + n_y * (n_y * cross + (2.0 / SCALE_FIRST) * (n_z * dzy[x]))
        h_one = h_one + n_z * (n_z * dzz[x])
        total = dxx + cross + dzz[x]
        if 4 <= x < rows - 4:
            inside[x - 4] = pressure_of(h_one, total, gain_a[x], gain_b[x], base[x])
        else:
            row = x if x < 4 else x - rows + 8
            h_own[row], sum_own[row] = h_one, total
    ready = packed_rows([inside[x] for x in range(rows - 8)])
    crossline[...] = crossline_of(ready, block_high[...], block_low[...])


def halo_rows(size, edges, other_core=False):
    place = lax.axis_index("xy")
    first = (place % 2 == 0) == (lax.axis_index("gz") == (1 if other_core else 0))
    left_at, right_at = jnp.where(first, 0, 4), jnp.where(first, 4, 0)
    left_in = jnp.where(place > 0, 1.0, 0.0)
    right_in = jnp.where(place < size - 1, 1.0, 0.0)
    before = [edges[left_at + x] * left_in for x in range(4)]
    return before + [edges[right_at + x] * right_in for x in range(4)]


def reach(values, row, coefficients, sign):
    total = None
    for k in range(1, 5):
        at = row + 4 - k if row < 4 else row + k - 4
        if (row < 4 and 0 <= at < 4) or (row >= 4 and 4 <= at < 8):
            term = (coefficients[k - 1] * (sign if row < 4 else 1.0)) * values[at]
            total = term if total is None else total + term
    return total


def halo_kernel(size, edges, axis_x, axis_y, h_own, sum_own, taps_first, h_edge, sum_edge):
    rows, sub, _ = axis_x.shape
    values = halo_rows(size, edges)
    parts = jnp.concatenate(halves(jnp.concatenate(values, axis=0)), axis=0)
    slopes = joined(across(parts, taps_first), 8 * sub)
    slopes = [slopes[sub * x : sub * x + sub] for x in range(8)]
    for row in range(8):
        x = row if row < 4 else rows - 8 + row
        dxx = reach(values, row, SECOND[1:], 1.0)
        dxy = reach(slopes, row, [c / SCALE_FIRST for c in FIRST], -1.0)
        n_x = axis_x[x]
        h_edge[row] = h_own[row] + n_x * (n_x * dxx + 2.0 * (axis_y[x] * dxy))
        sum_edge[row] = sum_own[row] + dxx


def step_kernel(
    size,
    gives,
    edges,
    edges_other,
    h_edge,
    sum_edge,
    axis_x,
    axis_z,
    gain_a,
    gain_b,
    base,
    block_high,
    block_low,
    crossline_inside,
    inline_high,
    inline_low,
    outside,
    crossline,
    *sends,
):
    rows = axis_x.shape[0]
    lower = lax.axis_index("gz") == 0
    place = lax.axis_index("xy")
    even, early = place % 2 == 0, place % 4 < 2

    slopes = [
        first_of(*depth_neighbours(own, far, lower))
        for own, far in zip(halo_rows(size, edges), halo_rows(size, edges_other, True))
    ]
    for row in range(8):
        x = row if row < 4 else rows - 8 + row
        dxz = reach(slopes, row, FIRST, -1.0)
        h_one = h_edge[row] + 2.0 * (axis_x[x] * axis_z[x] * dxz)
        outside[row] = pressure_of(h_one, sum_edge[row], gain_a[x], gain_b[x], base[x])
    ready = packed_rows([outside[row] for row in range(8)])
    edge = crossline_of(ready, block_high[...], block_low[...])
    transformed = jnp.concatenate([edge[:16], crossline_inside[...], edge[16:]], axis=0)
    crossline[...] = transformed
    parts = dot3(inline_high[...], inline_low[...], *halves(transformed))
    to_next, to_previous, to_second_next, to_second_previous = (
        parts[start : start + count] for start, count in gives
    )
    sends[0][...] = jnp.where(even, to_previous, to_next)
    sends[1][...] = jnp.where(even, to_next, to_previous)
    sends[2][...] = jnp.where(early, to_second_previous, to_second_next)
    sends[3][...] = jnp.where(early, to_second_next, to_second_previous)


def own_kernel(inside, outside, crossline, own_high, own_low, next_p, next_q, mine):
    rows = next_p.shape[0]
    for x in range(rows):
        if 4 <= x < rows - 4:
            value = inside[x - 4]
        else:
            value = outside[x if x < 4 else x - rows + 8]
        next_p[x] = value[:4]
        next_q[x] = value[4:]
    mine[...] = dot3(own_high[...], own_low[...], *halves(crossline[...]))


def finish_kernel(at, takes, mine, *rest):
    received, outs = [ref[...] for ref in rest[: len(takes)]], rest[len(takes) :]
    place = lax.axis_index("xy")
    for first, near in zip(range(0, len(takes), 2), (place % 2 == 0, place % 4 < 2)):
        outer, inner = received[first : first + 2]
        received[first : first + 2] = jnp.where(near, outer, inner), jnp.where(near, inner, outer)
    for out in outs:
        for row in range(out.shape[0]):
            total = mine[4 * at : 4 * at + 4]
            for take, got in zip(takes, received):
                for j in range(take.shape[1]):
                    factor = float(take[at, j])
                    if abs(factor) > 1e-13:
                        total = total + factor * got[4 * j : 4 * j + 4]
            out[row] = total
            at += 1


def pair_swaps(size):
    one = [1 if i % 2 == 0 else -1 for i in range(size)]
    two = [2 if i % 4 < 2 else -2 for i in range(size)]
    return [
        [(i, (i - one[i]) % size) for i in range(size)],
        [(i, i + one[i]) for i in range(size)],
        [(i, (i - two[i]) % size) for i in range(size)],
        [(i, i + two[i]) for i in range(size)],
    ]


def body(size, wave_p, wave_q, prior_p, prior_q, courant, epsilon, thomsen_delta, tilt_angle, azimuth):
    rows, layers, width = wave_p.shape
    f32 = jnp.float32
    even = lax.axis_index("xy") % 2 == 0
    pairs = pair_swaps(size)
    cores = [(0, 1), (1, 0)]
    stack = jax.ShapeDtypeStruct((rows, 8, width), f32)

    def parts(matrix):
        return [jnp.asarray(part) for part in split_bf16(matrix)]

    cells = rows * layers * width
    params = pltpu.CompilerParams(vmem_limit_bytes=16 * 1024 * 1024)

    def kernel(function, out_shape, work, name, scratch_shapes=()):
        cost = pl.CostEstimate(flops=work * cells, bytes_accessed=40 * cells, transcendentals=0)
        return pl.pallas_call(
            function,
            out_shape=out_shape,
            scratch_shapes=scratch_shapes,
            compiler_params=params,
            cost_estimate=cost,
            name=name,
        )

    waves = lax.optimization_barrier(jnp.concatenate([wave_p, wave_q], axis=1))
    leading, last = waves[:4], waves[rows - 4 :]
    shots = lax.axis_size("shot")

    def mixed(outer_core):
        swaps = []
        for shot in range(shots):
            for i in range(size):
                for core in range(2):
                    j = pairs[0 if core == outer_core else 1][i][1]
                    to = (shot, j) if abs(i - j) == 1 else ((shot + 1) % shots, i)
                    swaps.append(((shot * size + i) * 2 + core, (to[0] * size + to[1]) * 2 + core))
        return swaps

    first = even == (lax.axis_index("gz") == 0)
    everywhere = ("shot", "xy", "gz")
    other = lax.ppermute(waves, "gz", cores)
    edges_first = lax.ppermute(jnp.where(first, leading, last), everywhere, mixed(0))
    edges_second = lax.ppermute(jnp.where(first, last, leading), everywhere, mixed(1))

    taps = jax.ShapeDtypeStruct((4 * LANES, 2 * LANES), jnp.bfloat16)
    axis_x, axis_y, axis_z, *gains, taps_first, taps_second = kernel(
        weights_kernel, [stack] * 6 + [taps] * 2, 100, "weights"
    )(waves, prior_p, prior_q, courant, epsilon, thomsen_delta, tilt_angle, azimuth)
    block = parts(crossline_block(width))
    work = pltpu.VMEM((rows, 8, width), f32)
    edge = jax.ShapeDtypeStruct((8, 8, width), f32)
    inside = jax.ShapeDtypeStruct((rows - 8, 8, width), f32)
    ready = jax.ShapeDtypeStruct((layers * (rows - 8), width), f32)
    h_own, sum_own, inside, crossline = kernel(
        interior_kernel, [edge, edge, inside, ready], 100, "interior", [work] * 5
    )(waves, other, axis_x, axis_y, axis_z, *gains, taps_first, taps_second, *block)
    h_own, sum_own, edges_first, edges_second = lax.optimization_barrier(
        (h_own, sum_own, edges_first, edges_second)
    )
    edges = jnp.concatenate([edges_first, edges_second], axis=0)
    edges_other = lax.ppermute(edges, "gz", cores)
    h_edge, sum_edge = kernel(functools.partial(halo_kernel, size), [edge] * 2, 100, "halo")(
        edges, axis_x, axis_y, h_own, sum_own, taps_first
    )

    own, factors = inline_blocks(rows)
    offsets = (-1, 1, -2, 2)
    pieces, gives, start = [], [], 0
    for offset in offsets:
        give = factors[offset][1]
        pad = give.shape[0] % 2
        pieces.append(np.pad(give, ((0, pad), (0, 0))))
        gives.append((start, 4 * (give.shape[0] + pad)))
        start += gives[-1][1]

    inline = parts(np.kron(np.concatenate(pieces), np.eye(4)))
    inline_own = parts(np.kron(own, np.eye(4)))
    flat = jax.ShapeDtypeStruct((layers * rows, width), f32)
    outside, crossline, *sends = kernel(
        functools.partial(step_kernel, size, gives),
        [edge, flat] + [jax.ShapeDtypeStruct((count, width), f32) for _, count in gives],
        400,
        "step",
    )(edges, edges_other, h_edge, sum_edge, axis_x, axis_z, *gains, *block, crossline, *inline)
    received = [lax.ppermute(send, "xy", pair) for send, pair in zip(sends, pairs)]
    grid = jax.ShapeDtypeStruct(wave_p.shape, f32)
    next_p, next_q, mine = kernel(own_kernel, [grid, grid, flat], 100, "own")(
        inside, outside, crossline, *inline_own
    )
    takes = [factors[offset][0] for offset in offsets]
    counts = (rows // 2, rows // 4, rows // 8, rows // 8)
    outs = [jax.ShapeDtypeStruct((count, layers, width), f32) for count in counts]
    first, second = kernel(functools.partial(finish_kernel, 0, takes[:2]), outs[:2], 20, "fine")(
        mine, *received[:2]
    )
    first, *received[2:] = lax.optimization_barrier((first, *received[2:]))
    third, coarse = kernel(
        functools.partial(finish_kernel, counts[0] + counts[1], takes), outs[2:], 20, "coarse"
    )(mine, *received)
    return (next_p, next_q, first, second, third, coarse)


def solution(mesh):
    split = P(("shot", "xy"), "gz", None)
    shared = P("xy", "gz", None)
    return jax.shard_map(
        functools.partial(body, mesh.shape["xy"]),
        mesh=mesh,
        in_specs=(split,) * 4 + (shared,) * 5,
        out_specs=(split,) * 6,
        check_vma=False,
    )
```

```python
import functools

import jax
import jax.numpy as jnp
import numpy as np
from jax import lax
from jax.experimental import pallas as pl
from jax.experimental.pallas import tpu as pltpu
from jax.sharding import PartitionSpec as P

SECOND = (-205.0 / 72.0, 8.0 / 5.0, -1.0 / 5.0, 8.0 / 315.0, -1.0 / 560.0)
FIRST = (4.0 / 5.0, -1.0 / 5.0, 4.0 / 105.0, -1.0 / 280.0)
LIFT = (-1.586134342, -0.05298011854, 0.8829110762, 0.4435068522)
ZETA = 1.149604398
LANES = 128
LONG = 250_000
SCALE_FIRST, SCALE_SECOND = 840.0, 5040.0


def lift_level(values):
    even, odd = values[0::2], values[1::2]
    odd = odd + LIFT[0] * (even + np.roll(even, -1, 0))
    even = even + LIFT[1] * (odd + np.roll(odd, 1, 0))
    odd = odd + LIFT[2] * (even + np.roll(even, -1, 0))
    even = even + LIFT[3] * (odd + np.roll(odd, 1, 0))
    return even * ZETA, odd * (1.0 / ZETA)


def three_levels(length):
    coarse, members = np.eye(length), []
    for _ in range(3):
        coarse, detail = lift_level(coarse)
        members.append(detail)
    return members + [coarse]


def crossline_block(width):
    tiles = width // LANES
    members = three_levels(width)
    tile = tiles // 2
    wanted = np.concatenate(
        [m[tile * len(m) // tiles : (tile + 1) * len(m) // tiles] for m in members]
    )
    return wanted[:, (tile - 1) * LANES : (tile + 2) * LANES].T


def split_bf16(matrix):
    high = matrix.astype(jnp.bfloat16)
    low = (matrix - high.astype(np.float64)).astype(jnp.bfloat16)
    return high, low


def inline_blocks(rows):
    bricks, brick = 8, 4
    members = three_levels(rows * bricks)
    wanted = np.concatenate(
        [m[brick * len(m) // bricks : (brick + 1) * len(m) // bricks] for m in members]
    )

    def block(offset):
        return wanted[:, rows * (brick + offset) : rows * (brick + offset + 1)]

    factors = {}
    for offset in (-1, 1, -2, 2):
        left, sizes, right = np.linalg.svd(block(offset))
        rank = int((sizes > 1e-12).sum())
        root = np.sqrt(sizes[:rank])
        factors[offset] = (left[:, :rank] * root, root[:, None] * right[:rank])
    return block(0), factors


def sine_cosine(angle):
    turns = jnp.round(angle * (2.0 / np.pi))
    rest = angle - turns * 1.5703125
    rest = rest - turns * 4.837512969970703125e-4
    rest = rest - turns * 7.549789948768648e-8
    square = rest * rest
    sine = rest + rest * square * (
        -1.6666654611e-1 + square * (8.3321608736e-3 + square * -1.9515295891e-4)
    )
    cosine = (
        1.0
        - 0.5 * square
        + square
        * square
        * (4.166664568298827e-2 + square * (-1.388731625493765e-3 + square * 2.443315711809948e-5))
    )
    quarter = turns.astype(jnp.int32)
    swapped = (quarter & 1) == 1
    out_sine = jnp.where(swapped, cosine, sine)
    out_cosine = jnp.where(swapped, sine, cosine)
    out_sine = jnp.where((quarter & 2) == 2, -out_sine, out_sine)
    out_cosine = jnp.where(((quarter + 1) & 2) == 2, -out_cosine, out_cosine)
    return out_sine, out_cosine


def band(shape, taps, sign, scale):
    offset = lax.broadcasted_iota(jnp.int32, shape, 0) - LANES
    offset = offset - lax.broadcasted_iota(jnp.int32, shape, 1)
    values = jnp.zeros(shape, jnp.float32)
    for k, tap in enumerate(taps, 1):
        values = jnp.where(jnp.abs(offset) == k, float(np.round(tap * scale)), values)
    if sign < 0:
        values = jnp.where(offset < 0, -values, values)
    return values.astype(jnp.bfloat16)


def taps_kernel(taps_first, taps_second):
    taps_first[...] = band(taps_first.shape, FIRST, -1.0, SCALE_FIRST)
    taps_second[...] = band(taps_second.shape, SECOND[1:], 1.0, SCALE_SECOND)


def weights_kernel(
    waves,
    prior_p,
    prior_q,
    courant,
    epsilon,
    delta,
    tilt,
    azimuth,
    axis_x,
    axis_y,
    axis_z,
    gain_a,
    gain_b,
    base,
):
    rows = waves.shape[0]
    top = lax.broadcasted_iota(jnp.int32, waves.shape[1:], 0) < 4

    def swap(value):
        return pltpu.roll(value, 4, 0)

    for x in range(rows):
        angles = jnp.concatenate(
            [tilt[x].astype(jnp.float32), azimuth[x].astype(jnp.float32)], axis=0
        )
        sine, cosine = sine_cosine(angles)
        sine_other, cosine_other = swap(sine), swap(cosine)
        sine_tilt = jnp.where(top, sine, sine_other)
        axis_x[x] = sine_tilt * jnp.where(top, cosine_other, cosine)
        axis_y[x] = sine * sine_other
        axis_z[x] = jnp.where(top, cosine, cosine_other)
        speed = courant[x].astype(jnp.float32)
        root = jnp.sqrt(1.0 + 2.0 * delta[x].astype(jnp.float32))
        stretch = 1.0 + 2.0 * epsilon[x].astype(jnp.float32)
        gain_a[x] = jnp.concatenate([speed * stretch, speed], axis=0)
        across = speed * root
        gain_b[x] = jnp.concatenate([across, across], axis=0)
        base[x] = 2.0 * waves[x] - jnp.concatenate([prior_p[x], prior_q[x]], axis=0)


def first_of(ahead, behind):
    total = FIRST[0] * (ahead[0] - behind[0])
    for k in range(1, 4):
        total = total + FIRST[k] * (ahead[k] - behind[k])
    return total


def second_of(centre, ahead, behind):
    total = SECOND[0] * centre
    for k in range(4):
        total = total + SECOND[k + 1] * (ahead[k] + behind[k])
    return total


def dot3(a_high, a_low, b_high, b_low):
    def dot(a, b):
        return jnp.dot(a, b, preferred_element_type=jnp.float32)

    rows = a_high.shape[0]
    both = dot(jnp.concatenate([a_high, a_low], axis=0), b_high)
    return both[:rows] + (both[rows:] + dot(a_high, b_low))


def halves(value):
    high = value.astype(jnp.bfloat16)
    return high, (value - high.astype(jnp.float32)).astype(jnp.bfloat16)


def packed_rows(rows):
    top = lax.broadcasted_iota(jnp.int32, rows[0].shape, 0) < 4
    return jnp.concatenate(
        [
            jnp.where(top, rows[x], pltpu.roll(rows[x + 1], 4, 0))
            for x in range(0, len(rows), 2)
        ],
        axis=0,
    )


def crossline_of(rows, block_high, block_low):
    count, width = rows.shape
    tiles = width // LANES

    def windows(values):
        parts = [values[:, LANES * t : LANES * (t + 1)] for t in range(tiles)]
        return [
            jnp.concatenate([parts[t - 1], parts[t], parts[(t + 1) % tiles]], axis=1)
            for t in range(tiles)
        ]

    high, low = (jnp.concatenate(windows(part), axis=0) for part in halves(rows))
    result = dot3(high, low, block_high, block_low)
    lane = lax.broadcasted_iota(jnp.int32, (count, LANES), 1)
    ordered = [jnp.zeros((count, LANES), jnp.float32)] * tiles
    source, target = 0, 0
    for size in (LANES // 2, LANES // 4, LANES // 8, LANES // 8):
        for t in range(tiles):
            tile, offset = divmod(target + size * t, LANES)
            piece = result[count * t : count * (t + 1)]
            shift = (offset - source) % LANES
            if shift:
                piece = pltpu.roll(piece, shift, 1)
            inside = (lane >= offset) & (lane < offset + size)
            ordered[tile] = jnp.where(inside, piece, ordered[tile])
        source += size
        target += size * tiles
    return jnp.concatenate(ordered, axis=1)


def pressure_of(h_one, total, gain_a, gain_b, base):
    top = lax.broadcasted_iota(jnp.int32, h_one.shape, 0) < 4
    mixed = jnp.where(top, total - h_one, h_one)
    return base + gain_a * mixed + gain_b * pltpu.roll(mixed, 4, 0)


def depth_neighbours(own, far, lower):
    layer = lax.broadcasted_iota(jnp.int32, own.shape, 0) & 3
    up = far * jnp.where(lower, 1.0, 0.0)
    down = far * jnp.where(lower, 0.0, 1.0)
    ahead, behind = [], []
    for k in range(1, 4):
        ahead.append(jnp.where(layer < 4 - k, pltpu.roll(own, 8 - k, 0), pltpu.roll(up, 4 - k, 0)))
        behind.append(jnp.where(layer >= k, pltpu.roll(own, k, 0), pltpu.roll(down, 4 + k, 0)))
    return ahead + [up], behind + [down]


def across(parts, taps):
    width = parts.shape[1]
    blocks = []
    for start in range(0, width, 2 * LANES):
        stop = min(start + 2 * LANES, width)
        first = start - LANES
        low, high = max(first, 0), min(stop + LANES, width)
        block = taps[low - first : high - first, : stop - start]
        blocks.append(jnp.dot(parts[:, low:high], block, preferred_element_type=jnp.float32))
    return jnp.concatenate(blocks, axis=1)


def joined(parts, rows):
    return parts[:rows] + parts[rows:]


def interior_kernel(
    waves,
    other,
    axis_x,
    axis_y,
    axis_z,
    gain_a,
    gain_b,
    base,
    taps_first,
    taps_second,
    block_high,
    block_low,
    h_own,
    sum_own,
    inside,
    crossline,
    dz,
    dzz,
    dy,
    dyy,
    dzy,
):
    rows, sub, width = waves.shape
    flat = rows * sub
    lower = lax.axis_index("gz") == 0
    for x in range(rows):
        own = waves[x]
        ahead, behind = depth_neighbours(own, other[x], lower)
        dz[x] = first_of(ahead, behind)
        dzz[x] = second_of(own, ahead, behind)
    field = jnp.concatenate(halves(waves[...].reshape(flat, width)), axis=0)
    slope = jnp.concatenate(halves(dz[...].reshape(flat, width)), axis=0)
    dyy[...] = joined(across(field, taps_second), flat).reshape(waves.shape)
    dy[...] = joined(across(field, taps_first), flat).reshape(waves.shape)
    dzy[...] = joined(across(slope, taps_first), flat).reshape(waves.shape)
    for x in range(rows):
        centre = waves[x]
        dxx = SECOND[0] * centre
        dxy = jnp.zeros_like(centre)
        dxz = jnp.zeros_like(centre)
        for k in range(1, 5):
            for step in (k, -k):
                if 0 <= x + step < rows:
                    weight = FIRST[k - 1] if step > 0 else -FIRST[k - 1]
                    dxx = dxx + SECOND[k] * waves[x + step]
                    dxy = dxy + (weight / SCALE_FIRST) * dy[x + step]
                    dxz = dxz + weight * dz[x + step]
        cross = SECOND[0] * centre + (1.0 / SCALE_SECOND) * dyy[x]
        n_x, n_y, n_z = axis_x[x], axis_y[x], axis_z[x]
        h_one = n_x * (n_x * dxx + 2.0 * (n_y * dxy + n_z * dxz))
        h_one = h_one + n_y * (n_y * cross + (2.0 / SCALE_FIRST) * (n_z * dzy[x]))
        h_one = h_one + n_z * (n_z * dzz[x])
        total = dxx + cross + dzz[x]
        if 4 <= x < rows - 4:
            inside[x - 4] = pressure_of(h_one, total, gain_a[x], gain_b[x], base[x])
        else:
            row = x if x < 4 else x - rows + 8
            h_own[row], sum_own[row] = h_one, total
    ready = packed_rows([inside[x] for x in range(rows - 8)])
    crossline[...] = crossline_of(ready, block_high[...], block_low[...])


def halo_rows(size, edges):
    place = lax.axis_index("xy")
    even = place % 2 == 0
    left_at, right_at = jnp.where(even, 0, 4), jnp.where(even, 4, 0)
    left_in = jnp.where(place > 0, 1.0, 0.0)
    right_in = jnp.where(place < size - 1, 1.0, 0.0)
    before = [edges[left_at + x] * left_in for x in range(4)]
    return before + [edges[right_at + x] * right_in for x in range(4)]


def reach(values, row, coefficients, sign):
    total = None
    for k in range(1, 5):
        at = row + 4 - k if row < 4 else row + k - 4
        if (row < 4 and 0 <= at < 4) or (row >= 4 and 4 <= at < 8):
            term = (coefficients[k - 1] * (sign if row < 4 else 1.0)) * values[at]
            total = term if total is None else total + term
    return total


def halo_kernel(size, edges, axis_x, axis_y, axis_z, h_own, sum_own, taps_first, h_edge, sum_edge):
    rows, sub, _ = axis_x.shape
    values = halo_rows(size, edges)
    parts = jnp.concatenate(halves(jnp.concatenate(values, axis=0)), axis=0)
    slopes = joined(across(parts, taps_first), 8 * sub)
    slopes = [slopes[sub * x : sub * x + sub] for x in range(8)]
    lower = lax.axis_index("gz") == 0
    depth = [first_of(*depth_neighbours(value, jnp.zeros_like(value), lower)) for value in values]
    for row in range(8):
        x = row if row < 4 else rows - 8 + row
        dxx = reach(values, row, SECOND[1:], 1.0)
        dxy = reach(slopes, row, [c / SCALE_FIRST for c in FIRST], -1.0)
        n_x = axis_x[x]
        dxz = reach(depth, row, FIRST, -1.0)
        h_edge[row] = h_own[row] + n_x * (n_x * dxx + 2.0 * (axis_y[x] * dxy + axis_z[x] * dxz))
        sum_edge[row] = sum_own[row] + dxx


def step_kernel(
    size,
    gives,
    edges_other,
    h_edge,
    sum_edge,
    axis_x,
    axis_z,
    gain_a,
    gain_b,
    base,
    block_high,
    block_low,
    crossline_inside,
    inline_high,
    inline_low,
    outside,
    crossline,
    *sends,
):
    rows = axis_x.shape[0]
    lower = lax.axis_index("gz") == 0
    place = lax.axis_index("xy")
    even, early = place % 2 == 0, place % 4 < 2

    slopes = [
        first_of(*depth_neighbours(jnp.zeros_like(far), far, lower))
        for far in halo_rows(size, edges_other)
    ]
    for row in range(8):
        x = row if row < 4 else rows - 8 + row
        dxz = reach(slopes, row, FIRST, -1.0)
        h_one = h_edge[row] + 2.0 * (axis_x[x] * axis_z[x] * dxz)
        outside[row] = pressure_of(h_one, sum_edge[row], gain_a[x], gain_b[x], base[x])
    ready = packed_rows([outside[row] for row in range(8)])
    edge = crossline_of(ready, block_high[...], block_low[...])
    transformed = jnp.concatenate([edge[:16], crossline_inside[...], edge[16:]], axis=0)
    crossline[...] = transformed
    parts = dot3(inline_high[...], inline_low[...], *halves(transformed))
    to_next, to_previous, to_second_next, to_second_previous = (
        parts[start : start + count] for start, count in gives
    )
    sends[0][...] = jnp.where(even, to_previous, to_next)
    sends[1][...] = jnp.where(even, to_next, to_previous)
    sends[2][...] = jnp.where(early, to_second_previous, to_second_next)
    sends[3][...] = jnp.where(early, to_second_next, to_second_previous)


def own_kernel(inside, outside, crossline, own_high, own_low, next_p, next_q, mine):
    rows = next_p.shape[0]
    for x in range(rows):
        if 4 <= x < rows - 4:
            value = inside[x - 4]
        else:
            value = outside[x if x < 4 else x - rows + 8]
        next_p[x] = value[:4]
        next_q[x] = value[4:]
    mine[...] = dot3(own_high[...], own_low[...], *halves(crossline[...]))


def finish_kernel(at, takes, mine, *rest):
    received, outs = [ref[...] for ref in rest[: len(takes)]], rest[len(takes) :]
    place = lax.axis_index("xy")
    for first, near in zip(range(0, len(takes), 2), (place % 2 == 0, place % 4 < 2)):
        outer, inner = received[first : first + 2]
        received[first : first + 2] = jnp.where(near, outer, inner), jnp.where(near, inner, outer)
    for out in outs:
        for row in range(out.shape[0]):
            total = mine[4 * at : 4 * at + 4]
            for take, got in zip(takes, received):
                for j in range(take.shape[1]):
                    factor = float(take[at, j])
                    if abs(factor) > 1e-13:
                        total = total + factor * got[4 * j : 4 * j + 4]
            out[row] = total
            at += 1


def pair_swaps(size):
    one = [1 if i % 2 == 0 else -1 for i in range(size)]
    two = [2 if i % 4 < 2 else -2 for i in range(size)]
    return [
        [(i, (i - one[i]) % size) for i in range(size)],
        [(i, i + one[i]) for i in range(size)],
        [(i, (i - two[i]) % size) for i in range(size)],
        [(i, i + two[i]) for i in range(size)],
    ]


def body(size, wave_p, wave_q, prior_p, prior_q, courant, epsilon, thomsen_delta, tilt_angle, azimuth):
    rows, layers, width = wave_p.shape
    f32 = jnp.float32
    even = lax.axis_index("xy") % 2 == 0
    pairs = pair_swaps(size)
    cores = [(0, 1), (1, 0)]
    stack = jax.ShapeDtypeStruct((rows, 8, width), f32)

    def parts(matrix):
        return [jnp.asarray(part) for part in split_bf16(matrix)]

    cells = rows * layers * width
    params = pltpu.CompilerParams(vmem_limit_bytes=16 * 1024 * 1024)

    def kernel(function, out_shape, work, name, scratch_shapes=()):
        cost = pl.CostEstimate(flops=work * cells, bytes_accessed=40 * cells, transcendentals=0)
        return pl.pallas_call(
            function,
            out_shape=out_shape,
            scratch_shapes=scratch_shapes,
            compiler_params=params,
            cost_estimate=cost,
            name=name,
        )

    waves = lax.optimization_barrier(jnp.concatenate([wave_p, wave_q], axis=1))
    leading, last = waves[:4], waves[rows - 4 :]
    open_outer = [
        (2 * i + g, 2 * i + 1 - g) if abs(i - j) > 1 else (2 * i + g, 2 * j + g)
        for i, j in pairs[0]
        for g in range(2)
    ]
    to_outer, to_inner = jnp.where(even, leading, last), jnp.where(even, last, leading)
    to_outer, to_inner, fields = lax.optimization_barrier((to_outer, to_inner, waves))
    outer = lax.ppermute(to_outer, ("xy", "gz"), open_outer)
    inner = lax.ppermute(to_inner, "xy", pairs[1])
    other = lax.ppermute(fields, "gz", cores)

    taps = jax.ShapeDtypeStruct((4 * LANES, 2 * LANES), jnp.bfloat16)
    taps_first, taps_second = kernel(taps_kernel, [taps] * 2, LONG, "taps")()
    axis_x, axis_y, axis_z, *gains = kernel(weights_kernel, [stack] * 6, 100, "weights")(
        waves, prior_p, prior_q, courant, epsilon, thomsen_delta, tilt_angle, azimuth
    )
    block = parts(crossline_block(width))
    work = pltpu.VMEM((rows, 8, width), f32)
    edge = jax.ShapeDtypeStruct((8, 8, width), f32)
    inside = jax.ShapeDtypeStruct((rows - 8, 8, width), f32)
    ready = jax.ShapeDtypeStruct((layers * (rows - 8), width), f32)
    h_own, sum_own, inside, crossline = kernel(
        interior_kernel, [edge, edge, inside, ready], 100, "interior", [work] * 5
    )(waves, other, axis_x, axis_y, axis_z, *gains, taps_first, taps_second, *block)
    h_own, sum_own, inner, outer = lax.optimization_barrier((h_own, sum_own, inner, outer))
    edges = jnp.concatenate([outer, inner], axis=0)
    edges_other = lax.ppermute(edges, "gz", cores)
    h_edge, sum_edge = kernel(functools.partial(halo_kernel, size), [edge] * 2, 100, "halo")(
        edges, axis_x, axis_y, axis_z, h_own, sum_own, taps_first
    )

    own, factors = inline_blocks(rows)
    offsets = (-1, 1, -2, 2)
    pieces, gives, start = [], [], 0
    for offset in offsets:
        give = factors[offset][1]
        pad = give.shape[0] % 2
        pieces.append(np.pad(give, ((0, pad), (0, 0))))
        gives.append((start, 4 * (give.shape[0] + pad)))
        start += gives[-1][1]

    inline = parts(np.kron(np.concatenate(pieces), np.eye(4)))
    inline_own = parts(np.kron(own, np.eye(4)))
    flat = jax.ShapeDtypeStruct((layers * rows, width), f32)
    sizes = [count for _, count in gives]
    outside, crossline, *sends = kernel(
        functools.partial(step_kernel, size, gives),
        [edge, flat] + [jax.ShapeDtypeStruct((count, width), f32) for count in sizes],
        400,
        "step",
    )(edges_other, h_edge, sum_edge, axis_x, axis_z, *gains, *block, crossline, *inline)
    received = [lax.ppermute(send, "xy", pair) for send, pair in zip(sends, pairs)]
    grid = jax.ShapeDtypeStruct(wave_p.shape, f32)
    next_p, next_q, mine = kernel(own_kernel, [grid, grid, flat], 100, "own")(
        inside, outside, crossline, *inline_own
    )
    takes = [factors[offset][0] for offset in offsets]
    counts = (rows // 2, rows // 4, rows // 8, rows // 8)
    outs = [jax.ShapeDtypeStruct((count, layers, width), f32) for count in counts]
    first, second = kernel(functools.partial(finish_kernel, 0, takes[:2]), outs[:2], 20, "fine")(
        mine, *received[:2]
    )
    first, *received[2:] = lax.optimization_barrier((first, *received[2:]))
    third, coarse = kernel(
        functools.partial(finish_kernel, counts[0] + counts[1], takes), outs[2:], 20, "coarse"
    )(mine, *received)
    return (next_p, next_q, first, second, third, coarse)


def solution(mesh):
    split = P(("shot", "xy"), "gz", None)
    shared = P("xy", "gz", None)
    return jax.shard_map(
        functools.partial(body, mesh.shape["xy"]),
        mesh=mesh,
        in_specs=(split,) * 4 + (shared,) * 5,
        out_specs=(split,) * 6,
        check_vma=False,
    )
```

```python
import functools

import jax
import jax.numpy as jnp
import numpy as np
from jax import lax
from jax.experimental import pallas as pl
from jax.experimental.pallas import tpu as pltpu
from jax.sharding import PartitionSpec as P

SECOND = (-205.0 / 72.0, 8.0 / 5.0, -1.0 / 5.0, 8.0 / 315.0, -1.0 / 560.0)
FIRST = (4.0 / 5.0, -1.0 / 5.0, 4.0 / 105.0, -1.0 / 280.0)
LIFT = (-1.586134342, -0.05298011854, 0.8829110762, 0.4435068522)
ZETA = 1.149604398
LANES = 128
LONG = 250_000
SCALE_FIRST, SCALE_SECOND = 840.0, 5040.0


def lift_level(values):
    even, odd = values[0::2], values[1::2]
    odd = odd + LIFT[0] * (even + np.roll(even, -1, 0))
    even = even + LIFT[1] * (odd + np.roll(odd, 1, 0))
    odd = odd + LIFT[2] * (even + np.roll(even, -1, 0))
    even = even + LIFT[3] * (odd + np.roll(odd, 1, 0))
    return even * ZETA, odd * (1.0 / ZETA)


def three_levels(length):
    coarse, members = np.eye(length), []
    for _ in range(3):
        coarse, detail = lift_level(coarse)
        members.append(detail)
    return members + [coarse]


def crossline_block(width):
    tiles = width // LANES
    members = three_levels(width)
    tile = tiles // 2
    wanted = np.concatenate(
        [m[tile * len(m) // tiles : (tile + 1) * len(m) // tiles] for m in members]
    )
    return wanted[:, (tile - 1) * LANES : (tile + 2) * LANES].T


def split_bf16(matrix):
    high = matrix.astype(jnp.bfloat16)
    low = (matrix - high.astype(np.float64)).astype(jnp.bfloat16)
    return high, low


def inline_blocks(rows):
    bricks, brick = 8, 4
    members = three_levels(rows * bricks)
    wanted = np.concatenate(
        [m[brick * len(m) // bricks : (brick + 1) * len(m) // bricks] for m in members]
    )

    def block(offset):
        return wanted[:, rows * (brick + offset) : rows * (brick + offset + 1)]

    factors = {}
    for offset in (-1, 1, -2, 2):
        left, sizes, right = np.linalg.svd(block(offset))
        rank = int((sizes > 1e-12).sum())
        root = np.sqrt(sizes[:rank])
        factors[offset] = (left[:, :rank] * root, root[:, None] * right[:rank])
    return block(0), factors


def sine_cosine(angle):
    turns = jnp.round(angle * (2.0 / np.pi))
    rest = angle - turns * 1.5703125
    rest = rest - turns * 4.837512969970703125e-4
    rest = rest - turns * 7.549789948768648e-8
    square = rest * rest
    sine = rest + rest * square * (
        -1.6666654611e-1 + square * (8.3321608736e-3 + square * -1.9515295891e-4)
    )
    cosine = (
        1.0
        - 0.5 * square
        + square
        * square
        * (4.166664568298827e-2 + square * (-1.388731625493765e-3 + square * 2.443315711809948e-5))
    )
    quarter = turns.astype(jnp.int32)
    swapped = (quarter & 1) == 1
    out_sine = jnp.where(swapped, cosine, sine)
    out_cosine = jnp.where(swapped, sine, cosine)
    out_sine = jnp.where((quarter & 2) == 2, -out_sine, out_sine)
    out_cosine = jnp.where(((quarter + 1) & 2) == 2, -out_cosine, out_cosine)
    return out_sine, out_cosine


def band(shape, taps, sign, scale):
    offset = lax.broadcasted_iota(jnp.int32, shape, 0) - LANES
    offset = offset - lax.broadcasted_iota(jnp.int32, shape, 1)
    values = jnp.zeros(shape, jnp.float32)
    for k, tap in enumerate(taps, 1):
        values = jnp.where(jnp.abs(offset) == k, float(np.round(tap * scale)), values)
    if sign < 0:
        values = jnp.where(offset < 0, -values, values)
    return values.astype(jnp.bfloat16)


def taps_kernel(taps_first, taps_second):
    taps_first[...] = band(taps_first.shape, FIRST, -1.0, SCALE_FIRST)
    taps_second[...] = band(taps_second.shape, SECOND[1:], 1.0, SCALE_SECOND)


def weights_kernel(
    waves,
    prior_p,
    prior_q,
    courant,
    epsilon,
    delta,
    tilt,
    azimuth,
    axis_x,
    axis_y,
    axis_z,
    gain_a,
    gain_b,
    base,
):
    rows = waves.shape[0]
    top = lax.broadcasted_iota(jnp.int32, waves.shape[1:], 0) < 4

    def swap(value):
        return pltpu.roll(value, 4, 0)

    for x in range(rows):
        angles = jnp.concatenate(
            [tilt[x].astype(jnp.float32), azimuth[x].astype(jnp.float32)], axis=0
        )
        sine, cosine = sine_cosine(angles)
        sine_other, cosine_other = swap(sine), swap(cosine)
        sine_tilt = jnp.where(top, sine, sine_other)
        axis_x[x] = sine_tilt * jnp.where(top, cosine_other, cosine)
        axis_y[x] = sine * sine_other
        axis_z[x] = jnp.where(top, cosine, cosine_other)
        speed = courant[x].astype(jnp.float32)
        root = jnp.sqrt(1.0 + 2.0 * delta[x].astype(jnp.float32))
        stretch = 1.0 + 2.0 * epsilon[x].astype(jnp.float32)
        gain_a[x] = jnp.concatenate([speed * stretch, speed], axis=0)
        across = speed * root
        gain_b[x] = jnp.concatenate([across, across], axis=0)
        base[x] = 2.0 * waves[x] - jnp.concatenate([prior_p[x], prior_q[x]], axis=0)


def first_of(ahead, behind):
    total = FIRST[0] * (ahead[0] - behind[0])
    for k in range(1, 4):
        total = total + FIRST[k] * (ahead[k] - behind[k])
    return total


def second_of(centre, ahead, behind):
    total = SECOND[0] * centre
    for k in range(4):
        total = total + SECOND[k + 1] * (ahead[k] + behind[k])
    return total


def dot3(a_high, a_low, b_high, b_low):
    def dot(a, b):
        return jnp.dot(a, b, preferred_element_type=jnp.float32)

    rows = a_high.shape[0]
    both = dot(jnp.concatenate([a_high, a_low], axis=0), b_high)
    return both[:rows] + (both[rows:] + dot(a_high, b_low))


def halves(value):
    high = value.astype(jnp.bfloat16)
    return high, (value - high.astype(jnp.float32)).astype(jnp.bfloat16)


def packed_rows(rows):
    top = lax.broadcasted_iota(jnp.int32, rows[0].shape, 0) < 4
    return jnp.concatenate(
        [
            jnp.where(top, rows[x], pltpu.roll(rows[x + 1], 4, 0))
            for x in range(0, len(rows), 2)
        ],
        axis=0,
    )


def crossline_of(rows, block_high, block_low):
    count, width = rows.shape
    tiles = width // LANES

    def windows(values):
        parts = [values[:, LANES * t : LANES * (t + 1)] for t in range(tiles)]
        return [
            jnp.concatenate([parts[t - 1], parts[t], parts[(t + 1) % tiles]], axis=1)
            for t in range(tiles)
        ]

    high, low = (jnp.concatenate(windows(part), axis=0) for part in halves(rows))
    result = dot3(high, low, block_high, block_low)
    lane = lax.broadcasted_iota(jnp.int32, (count, LANES), 1)
    ordered = [jnp.zeros((count, LANES), jnp.float32)] * tiles
    source, target = 0, 0
    for size in (LANES // 2, LANES // 4, LANES // 8, LANES // 8):
        for t in range(tiles):
            tile, offset = divmod(target + size * t, LANES)
            piece = result[count * t : count * (t + 1)]
            shift = (offset - source) % LANES
            if shift:
                piece = pltpu.roll(piece, shift, 1)
            inside = (lane >= offset) & (lane < offset + size)
            ordered[tile] = jnp.where(inside, piece, ordered[tile])
        source += size
        target += size * tiles
    return jnp.concatenate(ordered, axis=1)


def pressure_of(h_one, total, gain_a, gain_b, base):
    top = lax.broadcasted_iota(jnp.int32, h_one.shape, 0) < 4
    mixed = jnp.where(top, total - h_one, h_one)
    return base + gain_a * mixed + gain_b * pltpu.roll(mixed, 4, 0)


def depth_neighbours(own, far, lower):
    layer = lax.broadcasted_iota(jnp.int32, own.shape, 0) & 3
    up = far * jnp.where(lower, 1.0, 0.0)
    down = far * jnp.where(lower, 0.0, 1.0)
    ahead, behind = [], []
    for k in range(1, 4):
        ahead.append(jnp.where(layer < 4 - k, pltpu.roll(own, 8 - k, 0), pltpu.roll(up, 4 - k, 0)))
        behind.append(jnp.where(layer >= k, pltpu.roll(own, k, 0), pltpu.roll(down, 4 + k, 0)))
    return ahead + [up], behind + [down]


def across(parts, taps):
    width = parts.shape[1]
    blocks = []
    for start in range(0, width, 2 * LANES):
        stop = min(start + 2 * LANES, width)
        first = start - LANES
        low, high = max(first, 0), min(stop + LANES, width)
        block = taps[low - first : high - first, : stop - start]
        blocks.append(jnp.dot(parts[:, low:high], block, preferred_element_type=jnp.float32))
    return jnp.concatenate(blocks, axis=1)


def joined(parts, rows):
    return parts[:rows] + parts[rows:]


def interior_kernel(
    waves,
    other,
    axis_x,
    axis_y,
    axis_z,
    gain_a,
    gain_b,
    base,
    taps_first,
    taps_second,
    block_high,
    block_low,
    h_own,
    sum_own,
    inside,
    packed,
    crossline,
    dz,
    dzz,
    dy,
    dyy,
    dzy,
):
    rows, sub, width = waves.shape
    flat = rows * sub
    lower = lax.axis_index("gz") == 0
    for x in range(rows):
        own = waves[x]
        ahead, behind = depth_neighbours(own, other[x], lower)
        dz[x] = first_of(ahead, behind)
        dzz[x] = second_of(own, ahead, behind)
    field = jnp.concatenate(halves(waves[...].reshape(flat, width)), axis=0)
    slope = jnp.concatenate(halves(dz[...].reshape(flat, width)), axis=0)
    dyy[...] = joined(across(field, taps_second), flat).reshape(waves.shape)
    dy[...] = joined(across(field, taps_first), flat).reshape(waves.shape)
    dzy[...] = joined(across(slope, taps_first), flat).reshape(waves.shape)
    for x in range(rows):
        centre = waves[x]
        dxx = SECOND[0] * centre
        dxy = jnp.zeros_like(centre)
        dxz = jnp.zeros_like(centre)
        for k in range(1, 5):
            for step in (k, -k):
                if 0 <= x + step < rows:
                    weight = FIRST[k - 1] if step > 0 else -FIRST[k - 1]
                    dxx = dxx + SECOND[k] * waves[x + step]
                    dxy = dxy + (weight / SCALE_FIRST) * dy[x + step]
                    dxz = dxz + weight * dz[x + step]
        cross = SECOND[0] * centre + (1.0 / SCALE_SECOND) * dyy[x]
        n_x, n_y, n_z = axis_x[x], axis_y[x], axis_z[x]
        h_one = n_x * (n_x * dxx + 2.0 * (n_y * dxy + n_z * dxz))
        h_one = h_one + n_y * (n_y * cross + (2.0 / SCALE_FIRST) * (n_z * dzy[x]))
        h_one = h_one + n_z * (n_z * dzz[x])
        total = dxx + cross + dzz[x]
        if 4 <= x < rows - 4:
            inside[x - 4] = pressure_of(h_one, total, gain_a[x], gain_b[x], base[x])
        else:
            row = x if x < 4 else x - rows + 8
            h_own[row], sum_own[row] = h_one, total
    ready = packed_rows([inside[x] for x in range(rows - 8)])
    packed[...] = ready
    crossline[...] = crossline_of(ready, block_high[...], block_low[...])


def halo_rows(size, edges):
    place = lax.axis_index("xy")
    even = place % 2 == 0
    left_at, right_at = jnp.where(even, 0, 4), jnp.where(even, 4, 0)
    left_in = jnp.where(place > 0, 1.0, 0.0)
    right_in = jnp.where(place < size - 1, 1.0, 0.0)
    before = [edges[left_at + x] * left_in for x in range(4)]
    return before + [edges[right_at + x] * right_in for x in range(4)]


def reach(values, row, coefficients, sign):
    total = None
    for k in range(1, 5):
        at = row + 4 - k if row < 4 else row + k - 4
        if (row < 4 and 0 <= at < 4) or (row >= 4 and 4 <= at < 8):
            term = (coefficients[k - 1] * (sign if row < 4 else 1.0)) * values[at]
            total = term if total is None else total + term
    return total


def halo_kernel(size, edges, axis_x, axis_y, axis_z, h_own, sum_own, taps_first, h_edge, sum_edge):
    rows, sub, _ = axis_x.shape
    values = halo_rows(size, edges)
    parts = jnp.concatenate(halves(jnp.concatenate(values, axis=0)), axis=0)
    slopes = joined(across(parts, taps_first), 8 * sub)
    slopes = [slopes[sub * x : sub * x + sub] for x in range(8)]
    lower = lax.axis_index("gz") == 0
    depth = [first_of(*depth_neighbours(value, jnp.zeros_like(value), lower)) for value in values]
    for row in range(8):
        x = row if row < 4 else rows - 8 + row
        dxx = reach(values, row, SECOND[1:], 1.0)
        dxy = reach(slopes, row, [c / SCALE_FIRST for c in FIRST], -1.0)
        n_x = axis_x[x]
        dxz = reach(depth, row, FIRST, -1.0)
        h_edge[row] = h_own[row] + n_x * (n_x * dxx + 2.0 * (axis_y[x] * dxy + axis_z[x] * dxz))
        sum_edge[row] = sum_own[row] + dxx


def step_kernel(
    size,
    gives,
    edges_other,
    h_edge,
    sum_edge,
    axis_x,
    axis_z,
    gain_a,
    gain_b,
    base,
    packed_inside,
    inline_high,
    inline_low,
    outside,
    packed,
    *sends,
):
    rows = axis_x.shape[0]
    lower = lax.axis_index("gz") == 0
    place = lax.axis_index("xy")
    even, early = place % 2 == 0, place % 4 < 2

    slopes = [
        first_of(*depth_neighbours(jnp.zeros_like(far), far, lower))
        for far in halo_rows(size, edges_other)
    ]
    for row in range(8):
        x = row if row < 4 else rows - 8 + row
        dxz = reach(slopes, row, FIRST, -1.0)
        h_one = h_edge[row] + 2.0 * (axis_x[x] * axis_z[x] * dxz)
        outside[row] = pressure_of(h_one, sum_edge[row], gain_a[x], gain_b[x], base[x])
    ready = packed_rows([outside[row] for row in range(8)])
    packed[...] = ready
    ordered = jnp.concatenate([ready[:16], packed_inside[...], ready[16:]], axis=0)
    parts = dot3(inline_high[...], inline_low[...], *halves(ordered))
    to_next, to_previous, to_second_next, to_second_previous = (
        parts[start : start + count] for start, count in gives
    )
    sends[0][...] = jnp.where(even, to_previous, to_next)
    sends[1][...] = jnp.where(even, to_next, to_previous)
    sends[2][...] = jnp.where(early, to_second_previous, to_second_next)
    sends[3][...] = jnp.where(early, to_second_next, to_second_previous)


def own_kernel(
    inside, outside, packed, crossline, block_high, block_low, own_high, own_low, next_p, next_q, mine
):
    rows = next_p.shape[0]
    for x in range(rows):
        if 4 <= x < rows - 4:
            value = inside[x - 4]
        else:
            value = outside[x if x < 4 else x - rows + 8]
        next_p[x] = value[:4]
        next_q[x] = value[4:]
    edge = crossline_of(packed[...], block_high[...], block_low[...])
    ordered = jnp.concatenate([edge[:16], crossline[...], edge[16:]], axis=0)
    mine[...] = dot3(own_high[...], own_low[...], *halves(ordered))


def finish_kernel(at, takes, mine, block_high, block_low, *rest):
    received, outs = [ref[...] for ref in rest[: len(takes)]], rest[len(takes) :]
    place = lax.axis_index("xy")
    for first, near in zip(range(0, len(takes), 2), (place % 2 == 0, place % 4 < 2)):
        outer, inner = received[first : first + 2]
        received[first : first + 2] = jnp.where(near, outer, inner), jnp.where(near, inner, outer)
    wanted = range(at, at + sum(out.shape[0] for out in outs))
    given = {}
    for row in wanted:
        for take, got in zip(takes, received):
            for j in range(take.shape[1]):
                factor = float(take[row, j])
                if abs(factor) > 1e-13:
                    term = factor * got[4 * j : 4 * j + 4]
                    given[row] = given[row] + term if row in given else term
    places = {row: 4 * k for k, row in enumerate(given)}
    pieces = list(given.values())
    pieces += [jnp.zeros_like(pieces[0])] * (-len(pieces) % 4)
    pairs = [jnp.concatenate(pieces[k : k + 2], axis=0) for k in range(0, len(pieces), 2)]
    across_rows = crossline_of(jnp.concatenate(pairs, axis=0), block_high[...], block_low[...])
    for out in outs:
        for row in range(out.shape[0]):
            total = mine[4 * at : 4 * at + 4]
            if at in places:
                total = total + across_rows[places[at] : places[at] + 4]
            out[row] = total
            at += 1


def pair_swaps(size):
    one = [1 if i % 2 == 0 else -1 for i in range(size)]
    two = [2 if i % 4 < 2 else -2 for i in range(size)]
    return [
        [(i, (i - one[i]) % size) for i in range(size)],
        [(i, i + one[i]) for i in range(size)],
        [(i, (i - two[i]) % size) for i in range(size)],
        [(i, i + two[i]) for i in range(size)],
    ]


def body(size, wave_p, wave_q, prior_p, prior_q, courant, epsilon, thomsen_delta, tilt_angle, azimuth):
    rows, layers, width = wave_p.shape
    f32 = jnp.float32
    even = lax.axis_index("xy") % 2 == 0
    pairs = pair_swaps(size)
    cores = [(0, 1), (1, 0)]
    stack = jax.ShapeDtypeStruct((rows, 8, width), f32)

    def parts(matrix):
        return [jnp.asarray(part) for part in split_bf16(matrix)]

    cells = rows * layers * width
    params = pltpu.CompilerParams(vmem_limit_bytes=16 * 1024 * 1024)

    def kernel(function, out_shape, work, name, scratch_shapes=()):
        cost = pl.CostEstimate(flops=work * cells, bytes_accessed=40 * cells, transcendentals=0)
        return pl.pallas_call(
            function,
            out_shape=out_shape,
            scratch_shapes=scratch_shapes,
            compiler_params=params,
            cost_estimate=cost,
            name=name,
        )

    waves = lax.optimization_barrier(jnp.concatenate([wave_p, wave_q], axis=1))
    leading, last = waves[:4], waves[rows - 4 :]
    open_outer = [
        (2 * i + g, 2 * i + 1 - g) if abs(i - j) > 1 else (2 * i + g, 2 * j + g)
        for i, j in pairs[0]
        for g in range(2)
    ]
    to_outer, to_inner = jnp.where(even, leading, last), jnp.where(even, last, leading)
    to_outer, to_inner, fields = lax.optimization_barrier((to_outer, to_inner, waves))
    outer = lax.ppermute(to_outer, ("xy", "gz"), open_outer)
    inner = lax.ppermute(to_inner, "xy", pairs[1])
    other = lax.ppermute(fields, "gz", cores)

    taps = jax.ShapeDtypeStruct((4 * LANES, 2 * LANES), jnp.bfloat16)
    taps_first, taps_second = kernel(taps_kernel, [taps] * 2, LONG, "taps")()
    axis_x, axis_y, axis_z, *gains = kernel(weights_kernel, [stack] * 6, 100, "weights")(
        waves, prior_p, prior_q, courant, epsilon, thomsen_delta, tilt_angle, azimuth
    )
    block = parts(crossline_block(width))
    work = pltpu.VMEM((rows, 8, width), f32)
    edge = jax.ShapeDtypeStruct((8, 8, width), f32)
    inside = jax.ShapeDtypeStruct((rows - 8, 8, width), f32)
    ready = jax.ShapeDtypeStruct((layers * (rows - 8), width), f32)
    h_own, sum_own, inside, packed_inside, crossline = kernel(
        interior_kernel, [edge, edge, inside, ready, ready], 100, "interior", [work] * 5
    )(waves, other, axis_x, axis_y, axis_z, *gains, taps_first, taps_second, *block)
    h_own, sum_own, inner, outer = lax.optimization_barrier((h_own, sum_own, inner, outer))
    edges = jnp.concatenate([outer, inner], axis=0)
    edges_other = lax.ppermute(edges, "gz", cores)
    h_edge, sum_edge = kernel(functools.partial(halo_kernel, size), [edge] * 2, 100, "halo")(
        edges, axis_x, axis_y, axis_z, h_own, sum_own, taps_first
    )

    own, factors = inline_blocks(rows)
    offsets = (-1, 1, -2, 2)
    pieces, gives, start = [], [], 0
    for offset in offsets:
        give = factors[offset][1]
        pad = give.shape[0] % 2
        pieces.append(np.pad(give, ((0, pad), (0, 0))))
        gives.append((start, 4 * (give.shape[0] + pad)))
        start += gives[-1][1]

    inline = parts(np.kron(np.concatenate(pieces), np.eye(4)))
    inline_own = parts(np.kron(own, np.eye(4)))
    flat = jax.ShapeDtypeStruct((layers * rows, width), f32)
    sizes = [count for _, count in gives]
    packed_edge = jax.ShapeDtypeStruct((layers * 8, width), f32)
    outside, packed, *sends = kernel(
        functools.partial(step_kernel, size, gives),
        [edge, packed_edge] + [jax.ShapeDtypeStruct((count, width), f32) for count in sizes],
        400,
        "step",
    )(edges_other, h_edge, sum_edge, axis_x, axis_z, *gains, packed_inside, *inline)
    received = [lax.ppermute(send, "xy", pair) for send, pair in zip(sends, pairs)]
    grid = jax.ShapeDtypeStruct(wave_p.shape, f32)
    next_p, next_q, mine = kernel(own_kernel, [grid, grid, flat], 100, "own")(
        inside, outside, packed, crossline, *block, *inline_own
    )
    takes = [factors[offset][0] for offset in offsets]
    counts = (rows // 2, rows // 4, rows // 8, rows // 8)
    outs = [jax.ShapeDtypeStruct((count, layers, width), f32) for count in counts]
    first, second = kernel(functools.partial(finish_kernel, 0, takes[:2]), outs[:2], 20, "fine")(
        mine, *block, *received[:2]
    )
    first, *received[2:] = lax.optimization_barrier((first, *received[2:]))
    third, coarse = kernel(
        functools.partial(finish_kernel, counts[0] + counts[1], takes), outs[2:], 20, "coarse"
    )(mine, *block, *received)
    return (next_p, next_q, first, second, third, coarse)


def solution(mesh):
    split = P(("shot", "xy"), "gz", None)
    shared = P("xy", "gz", None)
    return jax.shard_map(
        functools.partial(body, mesh.shape["xy"]),
        mesh=mesh,
        in_specs=(split,) * 4 + (shared,) * 5,
        out_specs=(split,) * 6,
        check_vma=False,
    )
```

```python
import functools

import jax
import jax.numpy as jnp
import numpy as np
from jax import lax
from jax.experimental import pallas as pl
from jax.experimental.pallas import tpu as pltpu
from jax.sharding import PartitionSpec as P

SECOND = (-205.0 / 72.0, 8.0 / 5.0, -1.0 / 5.0, 8.0 / 315.0, -1.0 / 560.0)
FIRST = (4.0 / 5.0, -1.0 / 5.0, 4.0 / 105.0, -1.0 / 280.0)
LIFT = (-1.586134342, -0.05298011854, 0.8829110762, 0.4435068522)
ZETA = 1.149604398
LANES = 128
LONG = 250_000
SCALE_FIRST, SCALE_SECOND = 840.0, 5040.0


def lift_level(values):
    even, odd = values[0::2], values[1::2]
    odd = odd + LIFT[0] * (even + np.roll(even, -1, 0))
    even = even + LIFT[1] * (odd + np.roll(odd, 1, 0))
    odd = odd + LIFT[2] * (even + np.roll(even, -1, 0))
    even = even + LIFT[3] * (odd + np.roll(odd, 1, 0))
    return even * ZETA, odd * (1.0 / ZETA)


def three_levels(length):
    coarse, members = np.eye(length), []
    for _ in range(3):
        coarse, detail = lift_level(coarse)
        members.append(detail)
    return members + [coarse]


def crossline_block(width):
    tiles = width // LANES
    members = three_levels(width)
    tile = tiles // 2
    wanted = np.concatenate(
        [m[tile * len(m) // tiles : (tile + 1) * len(m) // tiles] for m in members]
    )
    return wanted[:, (tile - 1) * LANES : (tile + 2) * LANES].T


def split_bf16(matrix):
    high = matrix.astype(jnp.bfloat16)
    low = (matrix - high.astype(np.float64)).astype(jnp.bfloat16)
    return high, low


def inline_blocks(rows):
    bricks, brick = 8, 4
    members = three_levels(rows * bricks)
    wanted = np.concatenate(
        [m[brick * len(m) // bricks : (brick + 1) * len(m) // bricks] for m in members]
    )

    def block(offset):
        return wanted[:, rows * (brick + offset) : rows * (brick + offset + 1)]

    factors = {}
    for offset in (-1, 1, -2, 2):
        left, sizes, right = np.linalg.svd(block(offset))
        rank = int((sizes > 1e-12).sum())
        root = np.sqrt(sizes[:rank])
        factors[offset] = (left[:, :rank] * root, root[:, None] * right[:rank])
    return block(0), factors


def sine_cosine(angle):
    turns = jnp.round(angle * (2.0 / np.pi))
    rest = angle - turns * 1.5703125
    rest = rest - turns * 4.837512969970703125e-4
    rest = rest - turns * 7.549789948768648e-8
    square = rest * rest
    sine = rest + rest * square * (
        -1.6666654611e-1 + square * (8.3321608736e-3 + square * -1.9515295891e-4)
    )
    cosine = (
        1.0
        - 0.5 * square
        + square
        * square
        * (4.166664568298827e-2 + square * (-1.388731625493765e-3 + square * 2.443315711809948e-5))
    )
    quarter = turns.astype(jnp.int32)
    swapped = (quarter & 1) == 1
    out_sine = jnp.where(swapped, cosine, sine)
    out_cosine = jnp.where(swapped, sine, cosine)
    out_sine = jnp.where((quarter & 2) == 2, -out_sine, out_sine)
    out_cosine = jnp.where(((quarter + 1) & 2) == 2, -out_cosine, out_cosine)
    return out_sine, out_cosine


def band(shape, taps, sign, scale):
    offset = lax.broadcasted_iota(jnp.int32, shape, 0) - LANES
    offset = offset - lax.broadcasted_iota(jnp.int32, shape, 1)
    values = jnp.zeros(shape, jnp.float32)
    for k, tap in enumerate(taps, 1):
        values = jnp.where(jnp.abs(offset) == k, float(np.round(tap * scale)), values)
    if sign < 0:
        values = jnp.where(offset < 0, -values, values)
    return values.astype(jnp.bfloat16)


def taps_kernel(taps_first, taps_second):
    taps_first[...] = band(taps_first.shape, FIRST, -1.0, SCALE_FIRST)
    taps_second[...] = band(taps_second.shape, SECOND[1:], 1.0, SCALE_SECOND)


def weights_kernel(
    waves,
    prior_p,
    prior_q,
    courant,
    epsilon,
    delta,
    tilt,
    azimuth,
    axis_x,
    axis_y,
    axis_z,
    gain_a,
    gain_b,
    base,
):
    rows = waves.shape[0]
    top = lax.broadcasted_iota(jnp.int32, waves.shape[1:], 0) < 4

    def swap(value):
        return pltpu.roll(value, 4, 0)

    for x in range(rows):
        angles = jnp.concatenate(
            [tilt[x].astype(jnp.float32), azimuth[x].astype(jnp.float32)], axis=0
        )
        sine, cosine = sine_cosine(angles)
        sine_other, cosine_other = swap(sine), swap(cosine)
        sine_tilt = jnp.where(top, sine, sine_other)
        axis_x[x] = sine_tilt * jnp.where(top, cosine_other, cosine)
        axis_y[x] = sine * sine_other
        axis_z[x] = jnp.where(top, cosine, cosine_other)
        speed = courant[x].astype(jnp.float32)
        root = jnp.sqrt(1.0 + 2.0 * delta[x].astype(jnp.float32))
        stretch = 1.0 + 2.0 * epsilon[x].astype(jnp.float32)
        gain_a[x] = jnp.concatenate([speed * stretch, speed], axis=0)
        across = speed * root
        gain_b[x] = jnp.concatenate([across, across], axis=0)
        base[x] = 2.0 * waves[x] - jnp.concatenate([prior_p[x], prior_q[x]], axis=0)


def first_of(ahead, behind):
    total = FIRST[0] * (ahead[0] - behind[0])
    for k in range(1, 4):
        total = total + FIRST[k] * (ahead[k] - behind[k])
    return total


def second_of(centre, ahead, behind):
    total = SECOND[0] * centre
    for k in range(4):
        total = total + SECOND[k + 1] * (ahead[k] + behind[k])
    return total


def dot3(a_high, a_low, b_high, b_low):
    def dot(a, b):
        return jnp.dot(a, b, preferred_element_type=jnp.float32)

    rows = a_high.shape[0]
    both = dot(jnp.concatenate([a_high, a_low], axis=0), b_high)
    return both[:rows] + (both[rows:] + dot(a_high, b_low))


def halves(value):
    high = value.astype(jnp.bfloat16)
    return high, (value - high.astype(jnp.float32)).astype(jnp.bfloat16)


def packed_rows(rows):
    top = lax.broadcasted_iota(jnp.int32, rows[0].shape, 0) < 4
    return jnp.concatenate(
        [
            jnp.where(top, rows[x], pltpu.roll(rows[x + 1], 4, 0))
            for x in range(0, len(rows), 2)
        ],
        axis=0,
    )


def crossline_of(rows, block_high, block_low):
    count, width = rows.shape
    tiles = width // LANES

    def windows(values):
        parts = [values[:, LANES * t : LANES * (t + 1)] for t in range(tiles)]
        return [
            jnp.concatenate([parts[t - 1], parts[t], parts[(t + 1) % tiles]], axis=1)
            for t in range(tiles)
        ]

    high, low = (jnp.concatenate(windows(part), axis=0) for part in halves(rows))
    result = dot3(high, low, block_high, block_low)
    lane = lax.broadcasted_iota(jnp.int32, (count, LANES), 1)
    ordered = [jnp.zeros((count, LANES), jnp.float32)] * tiles
    source, target = 0, 0
    for size in (LANES // 2, LANES // 4, LANES // 8, LANES // 8):
        for t in range(tiles):
            tile, offset = divmod(target + size * t, LANES)
            piece = result[count * t : count * (t + 1)]
            shift = (offset - source) % LANES
            if shift:
                piece = pltpu.roll(piece, shift, 1)
            inside = (lane >= offset) & (lane < offset + size)
            ordered[tile] = jnp.where(inside, piece, ordered[tile])
        source += size
        target += size * tiles
    return jnp.concatenate(ordered, axis=1)


def pressure_of(h_one, total, gain_a, gain_b, base):
    top = lax.broadcasted_iota(jnp.int32, h_one.shape, 0) < 4
    mixed = jnp.where(top, total - h_one, h_one)
    return base + gain_a * mixed + gain_b * pltpu.roll(mixed, 4, 0)


def depth_neighbours(own, far, lower):
    layer = lax.broadcasted_iota(jnp.int32, own.shape, 0) & 3
    up = far * jnp.where(lower, 1.0, 0.0)
    down = far * jnp.where(lower, 0.0, 1.0)
    ahead, behind = [], []
    for k in range(1, 4):
        ahead.append(jnp.where(layer < 4 - k, pltpu.roll(own, 8 - k, 0), pltpu.roll(up, 4 - k, 0)))
        behind.append(jnp.where(layer >= k, pltpu.roll(own, k, 0), pltpu.roll(down, 4 + k, 0)))
    return ahead + [up], behind + [down]


def across(parts, taps):
    width = parts.shape[1]
    blocks = []
    for start in range(0, width, 2 * LANES):
        stop = min(start + 2 * LANES, width)
        first = start - LANES
        low, high = max(first, 0), min(stop + LANES, width)
        block = taps[low - first : high - first, : stop - start]
        blocks.append(jnp.dot(parts[:, low:high], block, preferred_element_type=jnp.float32))
    return jnp.concatenate(blocks, axis=1)


def joined(parts, rows):
    return parts[:rows] + parts[rows:]


def interior_kernel(
    waves,
    other,
    axis_x,
    axis_y,
    axis_z,
    gain_a,
    gain_b,
    base,
    taps_first,
    taps_second,
    block_high,
    block_low,
    h_own,
    sum_own,
    inside,
    packed,
    crossline,
    dz,
    dzz,
    dy,
    dyy,
    dzy,
):
    rows, sub, width = waves.shape
    flat = rows * sub
    lower = lax.axis_index("gz") == 0
    for x in range(rows):
        own = waves[x]
        ahead, behind = depth_neighbours(own, other[x], lower)
        dz[x] = first_of(ahead, behind)
        dzz[x] = second_of(own, ahead, behind)
    field = jnp.concatenate(halves(waves[...].reshape(flat, width)), axis=0)
    slope = jnp.concatenate(halves(dz[...].reshape(flat, width)), axis=0)
    dyy[...] = joined(across(field, taps_second), flat).reshape(waves.shape)
    dy[...] = joined(across(field, taps_first), flat).reshape(waves.shape)
    dzy[...] = joined(across(slope, taps_first), flat).reshape(waves.shape)
    for x in range(rows):
        centre = waves[x]
        dxx = SECOND[0] * centre
        dxy = jnp.zeros_like(centre)
        dxz = jnp.zeros_like(centre)
        for k in range(1, 5):
            for step in (k, -k):
                if 0 <= x + step < rows:
                    weight = FIRST[k - 1] if step > 0 else -FIRST[k - 1]
                    dxx = dxx + SECOND[k] * waves[x + step]
                    dxy = dxy + (weight / SCALE_FIRST) * dy[x + step]
                    dxz = dxz + weight * dz[x + step]
        cross = SECOND[0] * centre + (1.0 / SCALE_SECOND) * dyy[x]
        n_x, n_y, n_z = axis_x[x], axis_y[x], axis_z[x]
        h_one = n_x * (n_x * dxx + 2.0 * (n_y * dxy + n_z * dxz))
        h_one = h_one + n_y * (n_y * cross + (2.0 / SCALE_FIRST) * (n_z * dzy[x]))
        h_one = h_one + n_z * (n_z * dzz[x])
        total = dxx + cross + dzz[x]
        if 4 <= x < rows - 4:
            inside[x - 4] = pressure_of(h_one, total, gain_a[x], gain_b[x], base[x])
        else:
            row = x if x < 4 else x - rows + 8
            h_own[row], sum_own[row] = h_one, total
    ready = packed_rows([inside[x] for x in range(rows - 8)])
    packed[...] = ready
    crossline[...] = crossline_of(ready, block_high[...], block_low[...])


def halo_rows(size, edges):
    place = lax.axis_index("xy")
    even = place % 2 == 0
    left_at, right_at = jnp.where(even, 0, 4), jnp.where(even, 4, 0)
    left_in = jnp.where(place > 0, 1.0, 0.0)
    right_in = jnp.where(place < size - 1, 1.0, 0.0)
    before = [edges[left_at + x] * left_in for x in range(4)]
    return before + [edges[right_at + x] * right_in for x in range(4)]


def reach(values, row, coefficients, sign):
    total = None
    for k in range(1, 5):
        at = row + 4 - k if row < 4 else row + k - 4
        if (row < 4 and 0 <= at < 4) or (row >= 4 and 4 <= at < 8):
            term = (coefficients[k - 1] * (sign if row < 4 else 1.0)) * values[at]
            total = term if total is None else total + term
    return total


def halo_kernel(size, edges, axis_x, axis_y, axis_z, h_own, sum_own, taps_first, h_edge, sum_edge):
    rows, sub, _ = axis_x.shape
    values = halo_rows(size, edges)
    parts = jnp.concatenate(halves(jnp.concatenate(values, axis=0)), axis=0)
    slopes = joined(across(parts, taps_first), 8 * sub)
    slopes = [slopes[sub * x : sub * x + sub] for x in range(8)]
    lower = lax.axis_index("gz") == 0
    depth = [first_of(*depth_neighbours(value, jnp.zeros_like(value), lower)) for value in values]
    for row in range(8):
        x = row if row < 4 else rows - 8 + row
        dxx = reach(values, row, SECOND[1:], 1.0)
        dxy = reach(slopes, row, [c / SCALE_FIRST for c in FIRST], -1.0)
        n_x = axis_x[x]
        dxz = reach(depth, row, FIRST, -1.0)
        h_edge[row] = h_own[row] + n_x * (n_x * dxx + 2.0 * (axis_y[x] * dxy + axis_z[x] * dxz))
        sum_edge[row] = sum_own[row] + dxx


def step_kernel(
    size,
    gives,
    edges_other,
    h_edge,
    sum_edge,
    axis_x,
    axis_z,
    gain_a,
    gain_b,
    base,
    packed_inside,
    block_high,
    block_low,
    inline_high,
    inline_low,
    outside,
    packed,
    *sends,
):
    rows = axis_x.shape[0]
    lower = lax.axis_index("gz") == 0
    place = lax.axis_index("xy")
    even, early = place % 2 == 0, place % 4 < 2

    slopes = [
        first_of(*depth_neighbours(jnp.zeros_like(far), far, lower))
        for far in halo_rows(size, edges_other)
    ]
    for row in range(8):
        x = row if row < 4 else rows - 8 + row
        dxz = reach(slopes, row, FIRST, -1.0)
        h_one = h_edge[row] + 2.0 * (axis_x[x] * axis_z[x] * dxz)
        outside[row] = pressure_of(h_one, sum_edge[row], gain_a[x], gain_b[x], base[x])
    ready = packed_rows([outside[row] for row in range(8)])
    packed[...] = ready
    ordered = jnp.concatenate([ready[:16], packed_inside[...], ready[16:]], axis=0)
    parts = dot3(inline_high[...], inline_low[...], *halves(ordered))
    to_next, to_previous = (parts[start : start + count] for start, count in gives[:2])
    seconds = crossline_of(parts[gives[2][0] :], block_high[...], block_low[...])
    to_second_next, to_second_previous = seconds[: gives[2][1]], seconds[gives[2][1] :]
    sends[0][...] = jnp.where(even, to_previous, to_next)
    sends[1][...] = jnp.where(even, to_next, to_previous)
    sends[2][...] = jnp.where(early, to_second_previous, to_second_next)
    sends[3][...] = jnp.where(early, to_second_next, to_second_previous)


def own_kernel(
    inside, outside, packed, crossline, block_high, block_low, own_high, own_low, next_p, next_q, mine
):
    rows = next_p.shape[0]
    for x in range(rows):
        if 4 <= x < rows - 4:
            value = inside[x - 4]
        else:
            value = outside[x if x < 4 else x - rows + 8]
        next_p[x] = value[:4]
        next_q[x] = value[4:]
    edge = crossline_of(packed[...], block_high[...], block_low[...])
    ordered = jnp.concatenate([edge[:16], crossline[...], edge[16:]], axis=0)
    mine[...] = dot3(own_high[...], own_low[...], *halves(ordered))


def fine_kernel(takes, mine, block_high, block_low, outer, inner, first, second, rest):
    even = lax.axis_index("xy") % 2 == 0
    outer, inner = outer[...], inner[...]
    received = jnp.where(even, outer, inner), jnp.where(even, inner, outer)
    wanted = range(mine.shape[0] // 4)
    given = {}
    for row in wanted:
        for take, got in zip(takes, received):
            for j in range(take.shape[1]):
                factor = float(take[row, j])
                if abs(factor) > 1e-13:
                    term = factor * got[4 * j : 4 * j + 4]
                    given[row] = given[row] + term if row in given else term
    places = {row: 4 * k for k, row in enumerate(given)}
    pieces = list(given.values())
    pieces += [jnp.zeros_like(pieces[0])] * (-len(pieces) % 4)
    pairs = [jnp.concatenate(pieces[k : k + 2], axis=0) for k in range(0, len(pieces), 2)]
    across_rows = crossline_of(jnp.concatenate(pairs, axis=0), block_high[...], block_low[...])
    for row in wanted:
        total = mine[4 * row : 4 * row + 4]
        if row in places:
            total = total + across_rows[places[row] : places[row] + 4]
        at = row - first.shape[0]
        if at < 0:
            first[row] = total
        elif at < second.shape[0]:
            second[at] = total
        else:
            at = 4 * (at - second.shape[0])
            rest[at : at + 4] = total


def coarse_kernel(takes, begun, outer, inner, third, coarse):
    early = lax.axis_index("xy") % 4 < 2
    outer, inner = outer[...], inner[...]
    received = jnp.where(early, outer, inner), jnp.where(early, inner, outer)
    last = begun.shape[0] // 4
    for row in range(last):
        total = begun[4 * row : 4 * row + 4]
        for take, got in zip(takes, received):
            for j in range(take.shape[1]):
                factor = float(take[row - last, j])
                if abs(factor) > 1e-13:
                    total = total + factor * got[4 * j : 4 * j + 4]
        if row < third.shape[0]:
            third[row] = total
        else:
            coarse[row - third.shape[0]] = total


def pair_swaps(size):
    one = [1 if i % 2 == 0 else -1 for i in range(size)]
    two = [2 if i % 4 < 2 else -2 for i in range(size)]
    return [
        [(i, (i - one[i]) % size) for i in range(size)],
        [(i, i + one[i]) for i in range(size)],
        [(i, (i - two[i]) % size) for i in range(size)],
        [(i, i + two[i]) for i in range(size)],
    ]


def body(size, wave_p, wave_q, prior_p, prior_q, courant, epsilon, thomsen_delta, tilt_angle, azimuth):
    rows, layers, width = wave_p.shape
    f32 = jnp.float32
    even = lax.axis_index("xy") % 2 == 0
    pairs = pair_swaps(size)
    cores = [(0, 1), (1, 0)]
    stack = jax.ShapeDtypeStruct((rows, 8, width), f32)

    def parts(matrix):
        return [jnp.asarray(part) for part in split_bf16(matrix)]

    cells = rows * layers * width
    params = pltpu.CompilerParams(vmem_limit_bytes=16 * 1024 * 1024)

    def kernel(function, out_shape, work, name, scratch_shapes=()):
        cost = pl.CostEstimate(flops=work * cells, bytes_accessed=40 * cells, transcendentals=0)
        return pl.pallas_call(
            function,
            out_shape=out_shape,
            scratch_shapes=scratch_shapes,
            compiler_params=params,
            cost_estimate=cost,
            name=name,
        )

    waves = lax.optimization_barrier(jnp.concatenate([wave_p, wave_q], axis=1))
    leading, last = waves[:4], waves[rows - 4 :]
    open_outer = [
        (2 * i + g, 2 * i + 1 - g) if abs(i - j) > 1 else (2 * i + g, 2 * j + g)
        for i, j in pairs[0]
        for g in range(2)
    ]
    to_outer, to_inner = jnp.where(even, leading, last), jnp.where(even, last, leading)
    to_outer, to_inner, fields = lax.optimization_barrier((to_outer, to_inner, waves))
    outer = lax.ppermute(to_outer, ("xy", "gz"), open_outer)
    inner = lax.ppermute(to_inner, "xy", pairs[1])
    other = lax.ppermute(fields, "gz", cores)

    taps = jax.ShapeDtypeStruct((4 * LANES, 2 * LANES), jnp.bfloat16)
    taps_first, taps_second = kernel(taps_kernel, [taps] * 2, LONG, "taps")()
    axis_x, axis_y, axis_z, *gains = kernel(weights_kernel, [stack] * 6, 100, "weights")(
        waves, prior_p, prior_q, courant, epsilon, thomsen_delta, tilt_angle, azimuth
    )
    block = parts(crossline_block(width))
    work = pltpu.VMEM((rows, 8, width), f32)
    edge = jax.ShapeDtypeStruct((8, 8, width), f32)
    inside = jax.ShapeDtypeStruct((rows - 8, 8, width), f32)
    ready = jax.ShapeDtypeStruct((layers * (rows - 8), width), f32)
    h_own, sum_own, inside, packed_inside, crossline = kernel(
        interior_kernel, [edge, edge, inside, ready, ready], 100, "interior", [work] * 5
    )(waves, other, axis_x, axis_y, axis_z, *gains, taps_first, taps_second, *block)
    h_own, sum_own, inner, outer = lax.optimization_barrier((h_own, sum_own, inner, outer))
    edges = jnp.concatenate([outer, inner], axis=0)
    edges_other = lax.ppermute(edges, "gz", cores)
    h_edge, sum_edge = kernel(functools.partial(halo_kernel, size), [edge] * 2, 100, "halo")(
        edges, axis_x, axis_y, axis_z, h_own, sum_own, taps_first
    )

    own, factors = inline_blocks(rows)
    offsets = (-1, 1, -2, 2)
    pieces, gives, start = [], [], 0
    for offset in offsets:
        give = factors[offset][1]
        pad = give.shape[0] % 2
        pieces.append(np.pad(give, ((0, pad), (0, 0))))
        gives.append((start, 4 * (give.shape[0] + pad)))
        start += gives[-1][1]

    inline = parts(np.kron(np.concatenate(pieces), np.eye(4)))
    inline_own = parts(np.kron(own, np.eye(4)))
    flat = jax.ShapeDtypeStruct((layers * rows, width), f32)
    sizes = [count for _, count in gives]
    packed_edge = jax.ShapeDtypeStruct((layers * 8, width), f32)
    outside, packed, *sends = kernel(
        functools.partial(step_kernel, size, gives),
        [edge, packed_edge] + [jax.ShapeDtypeStruct((count, width), f32) for count in sizes],
        400,
        "step",
    )(edges_other, h_edge, sum_edge, axis_x, axis_z, *gains, packed_inside, *block, *inline)
    received = [lax.ppermute(send, "xy", pair) for send, pair in zip(sends, pairs)]
    grid = jax.ShapeDtypeStruct(wave_p.shape, f32)
    next_p, next_q, mine = kernel(own_kernel, [grid, grid, flat], 100, "own")(
        inside, outside, packed, crossline, *block, *inline_own
    )
    takes = [factors[offset][0] for offset in offsets]
    counts = (rows // 2, rows // 4, rows // 8, rows // 8)
    outs = [jax.ShapeDtypeStruct((count, layers, width), f32) for count in counts]
    begun = jax.ShapeDtypeStruct((layers * (counts[2] + counts[3]), width), f32)
    first, second, begun = kernel(
        functools.partial(fine_kernel, takes[:2]), [*outs[:2], begun], 20, "fine"
    )(mine, *block, *received[:2])
    begun, *received[2:] = lax.optimization_barrier((begun, *received[2:]))
    third, coarse = kernel(functools.partial(coarse_kernel, takes[2:]), outs[2:], 20, "coarse")(
        begun, *received[2:]
    )
    return (next_p, next_q, first, second, third, coarse)


def solution(mesh):
    split = P(("shot", "xy"), "gz", None)
    shared = P("xy", "gz", None)
    return jax.shard_map(
        functools.partial(body, mesh.shape["xy"]),
        mesh=mesh,
        in_specs=(split,) * 4 + (shared,) * 5,
        out_specs=(split,) * 6,
        check_vma=False,
    )
```

```python
import functools

import jax
import jax.numpy as jnp
import numpy as np
from jax import lax
from jax.experimental import pallas as pl
from jax.experimental.pallas import tpu as pltpu
from jax.sharding import PartitionSpec as P

SECOND = (-205.0 / 72.0, 8.0 / 5.0, -1.0 / 5.0, 8.0 / 315.0, -1.0 / 560.0)
FIRST = (4.0 / 5.0, -1.0 / 5.0, 4.0 / 105.0, -1.0 / 280.0)
LIFT = (-1.586134342, -0.05298011854, 0.8829110762, 0.4435068522)
ZETA = 1.149604398
LANES = 128
LONG = 250_000
SCALE_FIRST, SCALE_SECOND = 840.0, 5040.0


def lift_level(values):
    even, odd = values[0::2], values[1::2]
    odd = odd + LIFT[0] * (even + np.roll(even, -1, 0))
    even = even + LIFT[1] * (odd + np.roll(odd, 1, 0))
    odd = odd + LIFT[2] * (even + np.roll(even, -1, 0))
    even = even + LIFT[3] * (odd + np.roll(odd, 1, 0))
    return even * ZETA, odd * (1.0 / ZETA)


def three_levels(length):
    coarse, members = np.eye(length), []
    for _ in range(3):
        coarse, detail = lift_level(coarse)
        members.append(detail)
    return members + [coarse]


def crossline_block(width):
    tiles = width // LANES
    members = three_levels(width)
    tile = tiles // 2
    wanted = np.concatenate(
        [m[tile * len(m) // tiles : (tile + 1) * len(m) // tiles] for m in members]
    )
    return wanted[:, (tile - 1) * LANES : (tile + 2) * LANES].T


def split_bf16(matrix):
    high = matrix.astype(jnp.bfloat16)
    low = (matrix - high.astype(np.float64)).astype(jnp.bfloat16)
    return high, low


def inline_blocks(rows):
    bricks, brick = 8, 4
    members = three_levels(rows * bricks)
    wanted = np.concatenate(
        [m[brick * len(m) // bricks : (brick + 1) * len(m) // bricks] for m in members]
    )

    def block(offset):
        return wanted[:, rows * (brick + offset) : rows * (brick + offset + 1)]

    factors = {}
    for offset in (-1, 1, -2, 2):
        left, sizes, right = np.linalg.svd(block(offset))
        rank = int((sizes > 1e-12).sum())
        root = np.sqrt(sizes[:rank])
        factors[offset] = (left[:, :rank] * root, root[:, None] * right[:rank])
    return block(0), factors


def sine_cosine(angle):
    turns = jnp.round(angle * (2.0 / np.pi))
    rest = angle - turns * 1.5703125
    rest = rest - turns * 4.837512969970703125e-4
    rest = rest - turns * 7.549789948768648e-8
    square = rest * rest
    sine = rest + rest * square * (
        -1.6666654611e-1 + square * (8.3321608736e-3 + square * -1.9515295891e-4)
    )
    cosine = (
        1.0
        - 0.5 * square
        + square
        * square
        * (4.166664568298827e-2 + square * (-1.388731625493765e-3 + square * 2.443315711809948e-5))
    )
    quarter = turns.astype(jnp.int32)
    swapped = (quarter & 1) == 1
    out_sine = jnp.where(swapped, cosine, sine)
    out_cosine = jnp.where(swapped, sine, cosine)
    out_sine = jnp.where((quarter & 2) == 2, -out_sine, out_sine)
    out_cosine = jnp.where(((quarter + 1) & 2) == 2, -out_cosine, out_cosine)
    return out_sine, out_cosine


def band(shape, taps, sign, scale):
    offset = lax.broadcasted_iota(jnp.int32, shape, 0) - LANES
    offset = offset - lax.broadcasted_iota(jnp.int32, shape, 1)
    values = jnp.zeros(shape, jnp.float32)
    for k, tap in enumerate(taps, 1):
        values = jnp.where(jnp.abs(offset) == k, float(np.round(tap * scale)), values)
    if sign < 0:
        values = jnp.where(offset < 0, -values, values)
    return values.astype(jnp.bfloat16)


def taps_kernel(taps_first, taps_second):
    taps_first[...] = band(taps_first.shape, FIRST, -1.0, SCALE_FIRST)
    taps_second[...] = band(taps_second.shape, SECOND[1:], 1.0, SCALE_SECOND)


def weights_kernel(
    waves,
    prior_p,
    prior_q,
    courant,
    epsilon,
    delta,
    tilt,
    azimuth,
    axis_x,
    axis_y,
    axis_z,
    gain_a,
    gain_b,
    base,
):
    rows = waves.shape[0]
    top = lax.broadcasted_iota(jnp.int32, waves.shape[1:], 0) < 4

    def swap(value):
        return pltpu.roll(value, 4, 0)

    for x in range(rows):
        angles = jnp.concatenate(
            [tilt[x].astype(jnp.float32), azimuth[x].astype(jnp.float32)], axis=0
        )
        sine, cosine = sine_cosine(angles)
        sine_other, cosine_other = swap(sine), swap(cosine)
        sine_tilt = jnp.where(top, sine, sine_other)
        axis_x[x] = sine_tilt * jnp.where(top, cosine_other, cosine)
        axis_y[x] = sine * sine_other
        axis_z[x] = jnp.where(top, cosine, cosine_other)
        speed = courant[x].astype(jnp.float32)
        root = jnp.sqrt(1.0 + 2.0 * delta[x].astype(jnp.float32))
        stretch = 1.0 + 2.0 * epsilon[x].astype(jnp.float32)
        gain_a[x] = jnp.concatenate([speed * stretch, speed], axis=0)
        across = speed * root
        gain_b[x] = jnp.concatenate([across, across], axis=0)
        base[x] = 2.0 * waves[x] - jnp.concatenate([prior_p[x], prior_q[x]], axis=0)


def first_of(ahead, behind):
    total = FIRST[0] * (ahead[0] - behind[0])
    for k in range(1, 4):
        total = total + FIRST[k] * (ahead[k] - behind[k])
    return total


def second_of(centre, ahead, behind):
    total = SECOND[0] * centre
    for k in range(4):
        total = total + SECOND[k + 1] * (ahead[k] + behind[k])
    return total


def dot3(a_high, a_low, b_high, b_low):
    def dot(a, b):
        return jnp.dot(a, b, preferred_element_type=jnp.float32)

    rows = a_high.shape[0]
    both = dot(jnp.concatenate([a_high, a_low], axis=0), b_high)
    return both[:rows] + (both[rows:] + dot(a_high, b_low))


def halves(value):
    high = value.astype(jnp.bfloat16)
    return high, (value - high.astype(jnp.float32)).astype(jnp.bfloat16)


def packed_rows(rows):
    top = lax.broadcasted_iota(jnp.int32, rows[0].shape, 0) < 4
    return jnp.concatenate(
        [
            jnp.where(top, rows[x], pltpu.roll(rows[x + 1], 4, 0))
            for x in range(0, len(rows), 2)
        ],
        axis=0,
    )


def crossline_of(rows, block_high, block_low):
    count, width = rows.shape
    tiles = width // LANES

    def windows(values):
        parts = [values[:, LANES * t : LANES * (t + 1)] for t in range(tiles)]
        return [
            jnp.concatenate([parts[t - 1], parts[t], parts[(t + 1) % tiles]], axis=1)
            for t in range(tiles)
        ]

    high, low = (jnp.concatenate(windows(part), axis=0) for part in halves(rows))
    result = dot3(high, low, block_high, block_low)
    lane = lax.broadcasted_iota(jnp.int32, (count, LANES), 1)
    ordered = [jnp.zeros((count, LANES), jnp.float32)] * tiles
    source, target = 0, 0
    for size in (LANES // 2, LANES // 4, LANES // 8, LANES // 8):
        for t in range(tiles):
            tile, offset = divmod(target + size * t, LANES)
            piece = result[count * t : count * (t + 1)]
            shift = (offset - source) % LANES
            if shift:
                piece = pltpu.roll(piece, shift, 1)
            inside = (lane >= offset) & (lane < offset + size)
            ordered[tile] = jnp.where(inside, piece, ordered[tile])
        source += size
        target += size * tiles
    return jnp.concatenate(ordered, axis=1)


def pressure_of(h_one, total, gain_a, gain_b, base):
    top = lax.broadcasted_iota(jnp.int32, h_one.shape, 0) < 4
    mixed = jnp.where(top, total - h_one, h_one)
    return base + gain_a * mixed + gain_b * pltpu.roll(mixed, 4, 0)


def depth_neighbours(own, far, lower):
    layer = lax.broadcasted_iota(jnp.int32, own.shape, 0) & 3
    up = far * jnp.where(lower, 1.0, 0.0)
    down = far * jnp.where(lower, 0.0, 1.0)
    ahead, behind = [], []
    for k in range(1, 4):
        ahead.append(jnp.where(layer < 4 - k, pltpu.roll(own, 8 - k, 0), pltpu.roll(up, 4 - k, 0)))
        behind.append(jnp.where(layer >= k, pltpu.roll(own, k, 0), pltpu.roll(down, 4 + k, 0)))
    return ahead + [up], behind + [down]


def across(parts, taps):
    width = parts.shape[1]
    blocks = []
    for start in range(0, width, 2 * LANES):
        stop = min(start + 2 * LANES, width)
        first = start - LANES
        low, high = max(first, 0), min(stop + LANES, width)
        block = taps[low - first : high - first, : stop - start]
        blocks.append(jnp.dot(parts[:, low:high], block, preferred_element_type=jnp.float32))
    return jnp.concatenate(blocks, axis=1)


def joined(parts, rows):
    return parts[:rows] + parts[rows:]


def interior_kernel(
    waves,
    other,
    axis_x,
    axis_y,
    axis_z,
    gain_a,
    gain_b,
    base,
    taps_first,
    taps_second,
    block_high,
    block_low,
    h_own,
    sum_own,
    inside,
    packed,
    crossline,
    dz,
    dzz,
    dy,
    dyy,
    dzy,
):
    rows, sub, width = waves.shape
    flat = rows * sub
    lower = lax.axis_index("gz") == 0
    for x in range(rows):
        own = waves[x]
        ahead, behind = depth_neighbours(own, other[x], lower)
        dz[x] = first_of(ahead, behind)
        dzz[x] = second_of(own, ahead, behind)
    field = jnp.concatenate(halves(waves[...].reshape(flat, width)), axis=0)
    slope = jnp.concatenate(halves(dz[...].reshape(flat, width)), axis=0)
    dyy[...] = joined(across(field, taps_second), flat).reshape(waves.shape)
    dy[...] = joined(across(field, taps_first), flat).reshape(waves.shape)
    dzy[...] = joined(across(slope, taps_first), flat).reshape(waves.shape)
    for x in range(rows):
        centre = waves[x]
        dxx = SECOND[0] * centre
        dxy = jnp.zeros_like(centre)
        dxz = jnp.zeros_like(centre)
        for k in range(1, 5):
            for step in (k, -k):
                if 0 <= x + step < rows:
                    weight = FIRST[k - 1] if step > 0 else -FIRST[k - 1]
                    dxx = dxx + SECOND[k] * waves[x + step]
                    dxy = dxy + (weight / SCALE_FIRST) * dy[x + step]
                    dxz = dxz + weight * dz[x + step]
        cross = SECOND[0] * centre + (1.0 / SCALE_SECOND) * dyy[x]
        n_x, n_y, n_z = axis_x[x], axis_y[x], axis_z[x]
        h_one = n_x * (n_x * dxx + 2.0 * (n_y * dxy + n_z * dxz))
        h_one = h_one + n_y * (n_y * cross + (2.0 / SCALE_FIRST) * (n_z * dzy[x]))
        h_one = h_one + n_z * (n_z * dzz[x])
        total = dxx + cross + dzz[x]
        if 4 <= x < rows - 4:
            inside[x - 4] = pressure_of(h_one, total, gain_a[x], gain_b[x], base[x])
        else:
            row = x if x < 4 else x - rows + 8
            h_own[row], sum_own[row] = h_one, total
    ready = packed_rows([inside[x] for x in range(rows - 8)])
    packed[...] = ready
    crossline[...] = crossline_of(ready, block_high[...], block_low[...])


def halo_rows(size, edges):
    place = lax.axis_index("xy")
    even = place % 2 == 0
    left_at, right_at = jnp.where(even, 0, 4), jnp.where(even, 4, 0)
    left_in = jnp.where(place > 0, 1.0, 0.0)
    right_in = jnp.where(place < size - 1, 1.0, 0.0)
    before = [edges[left_at + x] * left_in for x in range(4)]
    return before + [edges[right_at + x] * right_in for x in range(4)]


def reach(values, row, coefficients, sign):
    total = None
    for k in range(1, 5):
        at = row + 4 - k if row < 4 else row + k - 4
        if (row < 4 and 0 <= at < 4) or (row >= 4 and 4 <= at < 8):
            term = (coefficients[k - 1] * (sign if row < 4 else 1.0)) * values[at]
            total = term if total is None else total + term
    return total


def halo_kernel(size, edges, axis_x, axis_y, axis_z, h_own, sum_own, taps_first, h_edge, sum_edge):
    rows, sub, _ = axis_x.shape
    values = halo_rows(size, edges)
    parts = jnp.concatenate(halves(jnp.concatenate(values, axis=0)), axis=0)
    slopes = joined(across(parts, taps_first), 8 * sub)
    slopes = [slopes[sub * x : sub * x + sub] for x in range(8)]
    lower = lax.axis_index("gz") == 0
    depth = [first_of(*depth_neighbours(value, jnp.zeros_like(value), lower)) for value in values]
    for row in range(8):
        x = row if row < 4 else rows - 8 + row
        dxx = reach(values, row, SECOND[1:], 1.0)
        dxy = reach(slopes, row, [c / SCALE_FIRST for c in FIRST], -1.0)
        n_x = axis_x[x]
        dxz = reach(depth, row, FIRST, -1.0)
        h_edge[row] = h_own[row] + n_x * (n_x * dxx + 2.0 * (axis_y[x] * dxy + axis_z[x] * dxz))
        sum_edge[row] = sum_own[row] + dxx


def step_kernel(
    size,
    gives,
    edges_other,
    h_edge,
    sum_edge,
    axis_x,
    axis_z,
    gain_a,
    gain_b,
    base,
    packed_inside,
    block_high,
    block_low,
    inline_high,
    inline_low,
    outside,
    packed,
    *sends,
):
    rows = axis_x.shape[0]
    lower = lax.axis_index("gz") == 0
    place = lax.axis_index("xy")
    even, early = place % 2 == 0, place % 4 < 2

    slopes = [
        first_of(*depth_neighbours(jnp.zeros_like(far), far, lower))
        for far in halo_rows(size, edges_other)
    ]
    for row in range(8):
        x = row if row < 4 else rows - 8 + row
        dxz = reach(slopes, row, FIRST, -1.0)
        h_one = h_edge[row] + 2.0 * (axis_x[x] * axis_z[x] * dxz)
        outside[row] = pressure_of(h_one, sum_edge[row], gain_a[x], gain_b[x], base[x])
    ready = packed_rows([outside[row] for row in range(8)])
    packed[...] = ready
    ordered = jnp.concatenate([ready[:16], packed_inside[...], ready[16:]], axis=0)
    parts = dot3(inline_high[...], inline_low[...], *halves(ordered))
    to_next, to_previous = (parts[start : start + count] for start, count in gives[:2])
    seconds = crossline_of(parts[gives[2][0] :], block_high[...], block_low[...])
    to_second_next, to_second_previous = seconds[: gives[2][1]], seconds[gives[2][1] :]
    sends[0][...] = jnp.where(even, to_previous, to_next)
    sends[1][...] = jnp.where(even, to_next, to_previous)
    sends[2][...] = jnp.where(early, to_second_previous, to_second_next)
    sends[3][...] = jnp.where(early, to_second_next, to_second_previous)


def own_kernel(
    packed, crossline, block_high, block_low, own_high, own_low, mine
):
    edge = crossline_of(packed[...], block_high[...], block_low[...])
    ordered = jnp.concatenate([edge[:16], crossline[...], edge[16:]], axis=0)
    mine[...] = dot3(own_high[...], own_low[...], *halves(ordered))


def fine_kernel(
    takes, mine, inside, outside, block_high, block_low, outer, inner, first, second, rest, next_p, next_q
):
    rows = next_p.shape[0]
    for x in range(rows):
        if 4 <= x < rows - 4:
            value = inside[x - 4]
        else:
            value = outside[x if x < 4 else x - rows + 8]
        next_p[x] = value[:4]
        next_q[x] = value[4:]
    even = lax.axis_index("xy") % 2 == 0
    outer, inner = outer[...], inner[...]
    received = jnp.where(even, outer, inner), jnp.where(even, inner, outer)
    wanted = range(mine.shape[0] // 4)
    given = {}
    for row in wanted:
        for take, got in zip(takes, received):
            for j in range(take.shape[1]):
                factor = float(take[row, j])
                if abs(factor) > 1e-13:
                    term = factor * got[4 * j : 4 * j + 4]
                    given[row] = given[row] + term if row in given else term
    places = {row: 4 * k for k, row in enumerate(given)}
    pieces = list(given.values())
    pieces += [jnp.zeros_like(pieces[0])] * (-len(pieces) % 4)
    pairs = [jnp.concatenate(pieces[k : k + 2], axis=0) for k in range(0, len(pieces), 2)]
    across_rows = crossline_of(jnp.concatenate(pairs, axis=0), block_high[...], block_low[...])
    for row in wanted:
        total = mine[4 * row : 4 * row + 4]
        if row in places:
            total = total + across_rows[places[row] : places[row] + 4]
        at = row - first.shape[0]
        if at < 0:
            first[row] = total
        elif at < second.shape[0]:
            second[at] = total
        else:
            at = 4 * (at - second.shape[0])
            rest[at : at + 4] = total


def coarse_kernel(takes, begun, outer, inner, third, coarse):
    early = lax.axis_index("xy") % 4 < 2
    outer, inner = outer[...], inner[...]
    received = jnp.where(early, outer, inner), jnp.where(early, inner, outer)
    last = begun.shape[0] // 4
    for row in range(last):
        total = begun[4 * row : 4 * row + 4]
        for take, got in zip(takes, received):
            for j in range(take.shape[1]):
                factor = float(take[row - last, j])
                if abs(factor) > 1e-13:
                    total = total + factor * got[4 * j : 4 * j + 4]
        if row < third.shape[0]:
            third[row] = total
        else:
            coarse[row - third.shape[0]] = total


def pair_swaps(size):
    one = [1 if i % 2 == 0 else -1 for i in range(size)]
    two = [2 if i % 4 < 2 else -2 for i in range(size)]
    return [
        [(i, (i - one[i]) % size) for i in range(size)],
        [(i, i + one[i]) for i in range(size)],
        [(i, (i - two[i]) % size) for i in range(size)],
        [(i, i + two[i]) for i in range(size)],
    ]


def body(size, wave_p, wave_q, prior_p, prior_q, courant, epsilon, thomsen_delta, tilt_angle, azimuth):
    rows, layers, width = wave_p.shape
    f32 = jnp.float32
    even = lax.axis_index("xy") % 2 == 0
    pairs = pair_swaps(size)
    cores = [(0, 1), (1, 0)]
    stack = jax.ShapeDtypeStruct((rows, 8, width), f32)

    def parts(matrix):
        return [jnp.asarray(part) for part in split_bf16(matrix)]

    cells = rows * layers * width
    params = pltpu.CompilerParams(vmem_limit_bytes=16 * 1024 * 1024)

    def kernel(function, out_shape, work, name, scratch_shapes=()):
        cost = pl.CostEstimate(flops=work * cells, bytes_accessed=40 * cells, transcendentals=0)
        return pl.pallas_call(
            function,
            out_shape=out_shape,
            scratch_shapes=scratch_shapes,
            compiler_params=params,
            cost_estimate=cost,
            name=name,
        )

    waves = lax.optimization_barrier(jnp.concatenate([wave_p, wave_q], axis=1))
    leading, last = waves[:4], waves[rows - 4 :]
    open_outer = [
        (2 * i + g, 2 * i + 1 - g) if abs(i - j) > 1 else (2 * i + g, 2 * j + g)
        for i, j in pairs[0]
        for g in range(2)
    ]
    to_outer, to_inner = jnp.where(even, leading, last), jnp.where(even, last, leading)
    to_outer, to_inner, fields = lax.optimization_barrier((to_outer, to_inner, waves))
    outer = lax.ppermute(to_outer, ("xy", "gz"), open_outer)
    inner = lax.ppermute(to_inner, "xy", pairs[1])
    other = lax.ppermute(fields, "gz", cores)

    taps = jax.ShapeDtypeStruct((4 * LANES, 2 * LANES), jnp.bfloat16)
    taps_first, taps_second = kernel(taps_kernel, [taps] * 2, LONG, "taps")()
    axis_x, axis_y, axis_z, *gains = kernel(weights_kernel, [stack] * 6, 100, "weights")(
        waves, prior_p, prior_q, courant, epsilon, thomsen_delta, tilt_angle, azimuth
    )
    block = parts(crossline_block(width))
    work = pltpu.VMEM((rows, 8, width), f32)
    edge = jax.ShapeDtypeStruct((8, 8, width), f32)
    inside = jax.ShapeDtypeStruct((rows - 8, 8, width), f32)
    ready = jax.ShapeDtypeStruct((layers * (rows - 8), width), f32)
    h_own, sum_own, inside, packed_inside, crossline = kernel(
        interior_kernel, [edge, edge, inside, ready, ready], 100, "interior", [work] * 5
    )(waves, other, axis_x, axis_y, axis_z, *gains, taps_first, taps_second, *block)
    h_own, sum_own, inner, outer = lax.optimization_barrier((h_own, sum_own, inner, outer))
    edges = jnp.concatenate([outer, inner], axis=0)
    edges_other = lax.ppermute(edges, "gz", cores)
    h_edge, sum_edge = kernel(functools.partial(halo_kernel, size), [edge] * 2, 100, "halo")(
        edges, axis_x, axis_y, axis_z, h_own, sum_own, taps_first
    )

    own, factors = inline_blocks(rows)
    offsets = (-1, 1, -2, 2)
    pieces, gives, start = [], [], 0
    for offset in offsets:
        give = factors[offset][1]
        pad = give.shape[0] % 2
        pieces.append(np.pad(give, ((0, pad), (0, 0))))
        gives.append((start, 4 * (give.shape[0] + pad)))
        start += gives[-1][1]

    inline = parts(np.kron(np.concatenate(pieces), np.eye(4)))
    inline_own = parts(np.kron(own, np.eye(4)))
    flat = jax.ShapeDtypeStruct((layers * rows, width), f32)
    sizes = [count for _, count in gives]
    packed_edge = jax.ShapeDtypeStruct((layers * 8, width), f32)
    outside, packed, *sends = kernel(
        functools.partial(step_kernel, size, gives),
        [edge, packed_edge] + [jax.ShapeDtypeStruct((count, width), f32) for count in sizes],
        400,
        "step",
    )(edges_other, h_edge, sum_edge, axis_x, axis_z, *gains, packed_inside, *block, *inline)
    received = [lax.ppermute(send, "xy", pair) for send, pair in zip(sends, pairs)]
    grid = jax.ShapeDtypeStruct(wave_p.shape, f32)
    mine = kernel(own_kernel, flat, 100, "own")(
        packed, crossline, *block, *inline_own
    )
    takes = [factors[offset][0] for offset in offsets]
    counts = (rows // 2, rows // 4, rows // 8, rows // 8)
    outs = [jax.ShapeDtypeStruct((count, layers, width), f32) for count in counts]
    begun = jax.ShapeDtypeStruct((layers * (counts[2] + counts[3]), width), f32)
    first, second, begun, next_p, next_q = kernel(
        functools.partial(fine_kernel, takes[:2]), [*outs[:2], begun, grid, grid], 20, "fine"
    )(mine, inside, outside, *block, *received[:2])
    begun, *received[2:] = lax.optimization_barrier((begun, *received[2:]))
    third, coarse = kernel(functools.partial(coarse_kernel, takes[2:]), outs[2:], 20, "coarse")(
        begun, *received[2:]
    )
    return (next_p, next_q, first, second, third, coarse)


def solution(mesh):
    split = P(("shot", "xy"), "gz", None)
    shared = P("xy", "gz", None)
    return jax.shard_map(
        functools.partial(body, mesh.shape["xy"]),
        mesh=mesh,
        in_specs=(split,) * 4 + (shared,) * 5,
        out_specs=(split,) * 6,
        check_vma=False,
    )
```
